32 devices in a mesh: seq: 8 (over z, core), rows: 4 (over y, x).
Axes of the slice: x: 2, y: 2, z: 4, core: 2. Of those that a mesh axis runs over, the one named last changes fastest.
Arguments:
- tokens: bfloat16 [2, 4, 1024, 2048], P(None, 'rows', 'seq'), may hold values from -6 to 6
- w_query: bfloat16 [2048, 2048], P(('seq', 'rows')), may hold values from -0.125 to 0.125
- w_key: bfloat16 [2048, 256], P(('seq', 'rows')), may hold values from -0.125 to 0.125
- w_value: bfloat16 [2048, 256], P(('seq', 'rows')), may hold values from -0.125 to 0.125
- w_out: bfloat16 [2048, 2048], P(('seq', 'rows')), may hold values from -0.75 to 0.75
- w_gate: bfloat16 [2048, 5632], P(('seq', 'rows')), may hold values from -0.125 to 0.125
- w_up: bfloat16 [2048, 5632], P(('seq', 'rows')), may hold values from -0.125 to 0.125
- w_down: bfloat16 [5632, 2048], P(('seq', 'rows')), may hold values from -0.078125 to 0.078125
- gain_attn: bfloat16 [2048], P(('seq', 'rows')), may hold values from 0.5 to 1.5
- gain_ffn: bfloat16 [2048], P(('seq', 'rows')), may hold values from 0.5 to 1.5
- lengths: int32 [2, 4, 2], P(None, 'rows'), may hold values from 512 to 512, as said below
- order: int32 [16], replicated, may hold values from 0 to 15, each once
- cotangent: bfloat16 [2, 4, 1024, 2048], P(None, 'rows', 'seq'), may hold values from -6 to 6
Outputs:
- output: bfloat16 [2, 4, 1024, 2048], P(None, 'rows', 'seq')
- x_grad: bfloat16 [2, 4, 1024, 2048], P(None, 'rows', 'seq')
- w_query_grad: float32 [2048, 2048], P(('seq', 'rows'))
- w_key_grad: float32 [2048, 256], P(('seq', 'rows'))
- w_value_grad: float32 [2048, 256], P(('seq', 'rows'))
- w_out_grad: float32 [2048, 2048], P(('seq', 'rows'))
- w_gate_grad: float32 [2048, 5632], P(('seq', 'rows'))
- w_up_grad: float32 [2048, 5632], P(('seq', 'rows'))
- w_down_grad: float32 [5632, 2048], P(('seq', 'rows'))
- gain_attn_grad: float32 [2048], P(('seq', 'rows'))
- gain_ffn_grad: float32 [2048], P(('seq', 'rows'))
The draws below stay inside these ranges and needn't reach their ends.
Inputs may be any that keep to these rules, and one draw needn't show every extreme that they name: lengths[m, r] holds the first then the second sequence of row r of micro-batch m; the two add up to 1024. `order`: each block number appears once; index i of seq holds slot blocks 2 i and 2 i + 1.
All inputs are finite; a program needn't handle non-finite values.
Results may differ from the reference program's by a relative error of at most 0.022.
Values may be sent and summed in bfloat16 or wider, within the bound.
A program may use at most 384 MiB of HBM per device.

```python
import math
import jax
import jax.numpy as jnp
from jax import lax

D = 2048
HEADS = 32
KV_HEADS = 4
HEAD_DIM = 64
FF = 5632
MICRO = 2
GROUP = 8
KVW = 256
HALF = 64
SLOTS = 16
ROW_LEN = 1024
ROWS = 4
LEAST = 512


def draw_lengths(key, part):
    key = jax.random.fold_in(key, 11)
    first_len = jax.random.randint(key, (MICRO, ROWS), LEAST, ROW_LEN - LEAST + 1)
    corner = jnp.arange(MICRO)[:, None] + jnp.arange(ROWS)[None, :] == 0
    first_len = jnp.where(corner, LEAST, first_len)
    return jnp.stack([first_len, ROW_LEN - first_len], axis=-1).astype(jnp.int32)


def block_levels(rng, dims, split, least, high):
    def one(dim, shards_of):
        draws = jax.random.uniform(jax.random.fold_in(jax.random.fold_in(rng, 6), dim), (shards_of,), jnp.float32, least / len(split), high / len(split))
        return jnp.repeat(jnp.exp(draws), dims[dim] // shards_of).reshape((-1,) + (1,) * (len(dims) - dim - 1))

    loudness = one(*split[0])
    for cut in split[1:]:
        loudness = loudness * one(*cut)
    return loudness


def scatter_about(rng, dims, scale, bound, cuts=(), held_as=jnp.bfloat16):
    values = scale * jax.random.normal(rng, dims, jnp.float32)
    if cuts:
        values = values * block_levels(rng, dims, cuts, -0.22, 0.18)
    return jnp.clip(values, -bound, bound).astype(held_as)


def setup_inputs(seed: int = 0) -> dict:
    streams_of = jax.random.split(jax.random.key(seed), 14)
    return {
        "tokens": scatter_about(streams_of[0], (MICRO, ROWS, ROW_LEN, D), 1.0, 6.0, ((1, 4), (2, 8))),
        "w_query": scatter_about(streams_of[1], (D, D), D ** -0.5, 0.125, ((0, 32),)),
        "w_key": scatter_about(streams_of[2], (D, KVW), D ** -0.5, 0.125, ((0, 32),)),
        "w_value": scatter_about(streams_of[3], (D, KVW), D ** -0.5, 0.125, ((0, 32),)),
        "w_out": scatter_about(streams_of[4], (D, D), (D // 32) ** -0.5, 0.75, ((0, 32),)),
        "w_gate": scatter_about(streams_of[5], (D, FF), D ** -0.5, 0.125, ((0, 32),)),
        "w_up": scatter_about(streams_of[6], (D, FF), D ** -0.5, 0.125, ((0, 32),)),
        "w_down": scatter_about(streams_of[7], (FF, D), FF ** -0.5, 0.078125, ((0, 32),)),
        "gain_attn": jnp.clip(1.0 + 0.1 * jax.random.normal(streams_of[8], (D,), jnp.float32), 0.5, 1.5).astype(jnp.bfloat16),
        "gain_ffn": jnp.clip(1.0 + 0.1 * jax.random.normal(streams_of[9], (D,), jnp.float32), 0.5, 1.5).astype(jnp.bfloat16),
        "lengths": draw_lengths(jax.random.fold_in(streams_of[13], 71), 0),
        "order": jax.random.permutation(streams_of[11], SLOTS).astype(jnp.int32),
        "cotangent": scatter_about(streams_of[12], (MICRO, ROWS, ROW_LEN, D), 1.0, 6.0, ((1, 4), (2, 8))),
    }


@jax.custom_vjp
def low(v):
    return lax.optimization_barrier(v.astype(jnp.bfloat16)).astype(jnp.float32)

@jax.custom_vjp
def low_back(v):
    return v

def low_keep(v):
    return (low(v), None)

def low_pass(kept, grad):
    return (grad,)

def back_keep(v):
    return (v, None)

def back_low(kept, grad):
    return (low(grad),)
low.defvjp(low_keep, low_pass)
low_back.defvjp(back_keep, back_low)
EPSILON = 1e-05
NEG_LARGE = -1e+30

def rms_scaled(values, gain_vec):
    return values * lax.rsqrt(lax.optimization_barrier(jnp.mean(values * values, axis=-1, keepdims=True)) + EPSILON) * gain_vec

def angle_tables(position):
    width_half = HEAD_DIM // 2
    inverse = 10000.0 ** (-jnp.arange(width_half, dtype=jnp.float32) / width_half)
    angles = position[..., None] * inverse
    return (jnp.cos(angles), jnp.sin(angles))

def rotate_pairs(tensor, cosine, sine):
    width_half = tensor.shape[-1] // 2
    first_half = tensor[..., :width_half]
    second_half = tensor[..., width_half:]
    return jnp.concatenate([first_half * cosine - second_half * sine, second_half * cosine + first_half * sine], axis=-1)

def matmul(left, right):
    return jnp.dot(left, right, precision=lax.Precision.HIGHEST, preferred_element_type=jnp.float32)

def reference(tokens, w_query, w_key, w_value, w_out, w_gate, w_up, w_down, gain_attn, gain_ffn, lengths, order, cotangent):
    scale = 1.0 / math.sqrt(HEAD_DIM)
    batch_rows = MICRO * ROWS
    slot_ids = jnp.arange(ROW_LEN, dtype=jnp.int32)
    glob_place = (jnp.take(order, slot_ids // HALF) * HALF + slot_ids % HALF).astype(jnp.int32)
    first_len = lengths[..., 0].reshape(batch_rows).astype(jnp.int32)
    seq_start = jnp.where(glob_place[None, :] >= first_len[:, None], first_len[:, None], 0).astype(jnp.int32)
    cosine, sine = angle_tables((glob_place[None, :] - seq_start).astype(jnp.float32))
    cos_heads = cosine[:, :, None, :]
    sin_heads = sine[:, :, None, :]
    block_rows = min(512, ROW_LEN)
    block_count = ROW_LEN // block_rows

    def forward(x_float, query_w, key_w, value_w, out_w, gate_w, up_w, down_w, gain_one, gain_two):
        flat = x_float.reshape(batch_rows * ROW_LEN, D)
        attn_in = low(rms_scaled(flat, gain_one))
        q_lin = low_back(matmul(attn_in, query_w)).reshape(batch_rows, ROW_LEN, HEADS, HEAD_DIM)
        k_lin = low_back(matmul(attn_in, key_w)).reshape(batch_rows, ROW_LEN, KV_HEADS, HEAD_DIM)
        v_heads = low(low_back(matmul(attn_in, value_w))).reshape(batch_rows, ROW_LEN, KV_HEADS, HEAD_DIM)
        queries = low(rotate_pairs(q_lin, cos_heads, sin_heads))
        keys = low(rotate_pairs(k_lin, cos_heads, sin_heads))

        def attend_row(row_items):
            row_query, row_key, row_value, row_start = row_items

            def attend_block(block_items):
                block_query, block_place, block_start = block_items
                grouped = block_query.reshape(block_rows, KV_HEADS, GROUP, HEAD_DIM)
                scores = low_back(jnp.einsum('tkgd,skd->kgts', grouped, row_key, precision=lax.Precision.HIGHEST) * scale)
                allowed = (glob_place[None, :] <= block_place[:, None]) & (glob_place[None, :] >= block_start[:, None])
                scores = jnp.where(allowed[None, None], scores, NEG_LARGE)
                shifted = jnp.exp(scores - lax.optimization_barrier(jnp.max(scores, axis=-1, keepdims=True)))
                probs = shifted / lax.optimization_barrier(jnp.sum(shifted, axis=-1, keepdims=True))
                mixed = jnp.einsum('kgts,skd->tkgd', low(probs), row_value, precision=lax.Precision.HIGHEST)
                return mixed.reshape(block_rows, D)
            pieces = lax.map(jax.checkpoint(attend_block), (row_query.reshape(block_count, block_rows, HEADS, HEAD_DIM), glob_place.reshape(block_count, block_rows), row_start.reshape(block_count, block_rows)))
            return pieces.reshape(ROW_LEN, D)
        attended = lax.map(attend_row, (queries, keys, v_heads, seq_start))
        attended = low(low_back(attended.reshape(batch_rows * ROW_LEN, D)))
        middle = flat + low_back(matmul(attended, out_w))
        ffn_in = low(rms_scaled(middle, gain_two))
        gate = low_back(matmul(ffn_in, gate_w))
        upper = low_back(matmul(ffn_in, up_w))
        hidden = low(gate * jax.nn.sigmoid(gate) * upper)
        result = middle + low_back(matmul(hidden, down_w))
        return result.reshape(tokens.shape)
    inputs = (tokens, w_query, w_key, w_value, w_out, w_gate, w_up, w_down, gain_attn, gain_ffn)
    output, pullback = jax.vjp(forward, *[item.astype(jnp.float32) for item in inputs])
    grads = pullback(cotangent.astype(jnp.float32))
    return (output.astype(jnp.bfloat16), grads[0].astype(jnp.bfloat16), grads[1], grads[2], grads[3], grads[4], grads[5], grads[6], grads[7], grads[8], grads[9])
```

```python
import functools
import math

import jax
import jax.numpy as jnp
from jax import lax
from jax.experimental import pallas as pl
from jax.experimental.pallas import tpu as pltpu
from jax.sharding import PartitionSpec as P

D = 2048
HEADS = 32
KV_HEADS = 4
HEAD_DIM = 64
GROUP = 8
KVW = 256
QKV = D + 2 * KVW
PACK = QKV + D + 128

EPSILON = 1e-05
NEG_LARGE = -1e30
MESH = pl.DeviceIdType.MESH
MIB = 1 << 20


def product(left, right):
    return jnp.dot(left, right, preferred_element_type=jnp.float32)


def product_nt(left, right):
    return lax.dot_general(left, right, (((1,), (1,)), ((), ())), preferred_element_type=jnp.float32)


def product_tn(left, right):
    return lax.dot_general(left, right, (((0,), (0,)), ((), ())), preferred_element_type=jnp.float32)


def rms_factor(values):
    return lax.rsqrt(jnp.mean(values * values, axis=-1, keepdims=True) + EPSILON)


def norm_back(d_scaled, normed, factor, gain):
    inner = d_scaled * gain
    mean = jnp.mean(inner * normed, axis=-1, keepdims=True)
    return factor * (inner - normed * mean), jnp.sum(d_scaled * normed, axis=0)


def rotate(tensor, cosine, sine):
    half = tensor.shape[-1] // 2
    one, two = tensor[..., :half], tensor[..., half:]
    return jnp.concatenate([one * cosine - two * sine, two * cosine + one * sine], axis=-1)


def rotate_back(tensor, cosine, sine):
    return rotate(tensor, cosine, -sine)


def slot_places(order, half_len, slot_ids):
    matches = (slot_ids // half_len)[:, None] == jnp.arange(order.shape[0], dtype=jnp.int32)[None, :]
    return jnp.sum(jnp.where(matches, order[None, :], 0), axis=1) * half_len + slot_ids % half_len


def place():
    s, r = lax.axis_index("seq"), lax.axis_index("rows")
    return lax.div(s, 2), lax.rem(s, 2), r


def send(src, dst, ssem, rsem, device):
    return pltpu.make_async_remote_copy(
        src_ref=src, dst_ref=dst, send_sem=ssem, recv_sem=rsem, device_id=device, device_id_type=MESH
    )


def greet(devices):
    barrier = pltpu.get_barrier_semaphore()
    for device in devices:
        pl.semaphore_signal(barrier, inc=1, device_id=device, device_id_type=MESH)
    pl.semaphore_wait(barrier, len(devices))


def corners(r):
    return r, r + 1 - 2 * lax.rem(r, 2), lax.rem(r + 2, 4), 3 - r


def gather_kernel(zs, planes, z_flags, *refs):
    count = len(z_flags)
    own, out = refs[:count], refs[count : 2 * count]
    z_ssem, z_rsem, f_ssem, f_rsem, h_ssem, h_rsem, c_ssem, c_rsem, l_sem = refs[2 * count :]
    z, c, r = place()
    line = corners(r)
    s = z * 2 + c

    def at_z(other):
        return (other * 2 + c, r)

    twin = (z * 2 + 1 - c, r)
    shifts = range(1, zs) if any(z_flags) else ()
    partners = [twin] + ([(s, line[1]), (s, line[2])] if planes else [])
    partners += [at_z(lax.rem(z + k, zs)) for k in shifts]
    greet(partners)

    items = []
    for k in range(zs):
        for a in range(count):
            if k == 0 or z_flags[a]:
                items.append((a, k))
    pending = []

    def slot(a, k, core, row):
        zz = lax.rem(z - k + zs, zs) if z_flags[a] else 0
        return out[a].at[zz, core, row] if planes else out[a].at[zz, core]

    for i, (a, k) in enumerate(items):
        if k == 0:
            local = pltpu.make_async_copy(own[a], slot(a, 0, c, r), l_sem.at[a])
            local.start()
            pending.append(local.wait)
    for i, (a, k) in enumerate(items):
        if k:
            copy = send(own[a], out[a].at[(z, c, r) if planes else (z, c)], z_ssem.at[i], z_rsem.at[i], at_z(lax.rem(z + k, zs)))
            copy.start()
            pending.append(copy.wait_send)

    def to_twin(i, j, src, dst):
        copy = send(src, dst, c_ssem.at[i, j], c_rsem.at[i, j], twin)
        copy.start()
        pending.append(copy.wait_send)

    def begin(i):
        a, k = items[i]
        dst = slot(a, k, c, r)
        src = own[a]
        if k:
            send(dst, dst, z_ssem.at[i], z_rsem.at[i], at_z(lax.rem(z + k, zs))).wait_recv()
            src = dst
        if planes:
            for j in (1, 2):
                copy = send(src, dst, f_ssem.at[i, j - 1], f_rsem.at[i, j - 1], (s, line[j]))
                copy.start()
                pending.append(copy.wait_send)
        to_twin(i, 0, src, dst)

    def forward(i):
        a, k = items[i]
        half = own[a].shape[0] // 2
        for j in (1, 2):
            dst = slot(a, k, c, line[j])
            send(dst, dst, f_ssem.at[i, j - 1], f_rsem.at[i, j - 1], (s, line[j])).wait_recv()
            part = dst.at[pl.ds(half if j == 1 else 0, half)]
            copy = send(part, part, h_ssem.at[i, j - 1], h_rsem.at[i, j - 1], (s, line[3 - j]))
            copy.start()
            pending.append(copy.wait_send)
            to_twin(i, j, dst, dst)

    def finish(i):
        a, k = items[i]
        half = own[a].shape[0] // 2
        dst = slot(a, k, c, line[3])
        for j in (1, 2):
            part = dst.at[pl.ds(half if j == 1 else 0, half)]
            send(part, part, h_ssem.at[i, j - 1], h_rsem.at[i, j - 1], (s, line[3 - j])).wait_recv()
        to_twin(i, 3, dst, dst)

    total = len(items)
    for i in range(total + 2):
        if i < total:
            begin(i)
        if planes and 1 <= i <= total:
            forward(i - 1)
        if planes and i >= 2:
            finish(i - 2)
    for i, (a, k) in enumerate(items):
        for j in range(4 if planes else 1):
            dst = slot(a, k, 1 - c, line[j])
            send(dst, dst, c_ssem.at[i, j], c_rsem.at[i, j], twin).wait_recv()
    for wait in pending:
        wait()


def gather(arrays, z_flags, zs, collective_id, planes=True):
    n = sum(zs if f else 1 for f in z_flags)
    rows = (4,) if planes else ()
    sem = pltpu.SemaphoreType.DMA
    return pl.pallas_call(
        functools.partial(gather_kernel, zs, planes, tuple(z_flags)),
        out_shape=[
            jax.ShapeDtypeStruct((zs if f else 1, 2) + rows + a.shape, a.dtype) for a, f in zip(arrays, z_flags)
        ],
        in_specs=[pl.BlockSpec(memory_space=pl.ANY)] * len(arrays),
        out_specs=[pl.BlockSpec(memory_space=pl.ANY)] * len(arrays),
        scratch_shapes=[
            sem((n,)), sem((n,)), sem((n, 2)), sem((n, 2)), sem((n, 2)), sem((n, 2)), sem((n, 4)), sem((n, 4)),
            sem((len(arrays),)),
        ],
        compiler_params=pltpu.CompilerParams(collective_id=collective_id, has_side_effects=True),
    )(*arrays)


def exchange_kernel(own, out, ssem, rsem, l_sem):
    z, c, r = place()
    line = corners(r)
    others = [(cc, j) for j in (3, 1, 2, 0) for cc in range(2) if (cc, j) != (0, 0)]

    def core(flip):
        return 1 - c if flip else c

    devices = [(z * 2 + core(cc), line[j]) for cc, j in others]
    greet(devices)
    copies = []
    for i, (cc, j) in enumerate(others):
        copy = send(own.at[core(cc), line[j]], out.at[c, r], ssem.at[i], rsem.at[i], devices[i])
        copy.start()
        copies.append(copy)
    local = pltpu.make_async_copy(own.at[c, r], out.at[c, r], l_sem)
    local.start()
    for i, (cc, j) in enumerate(others):
        dst = out.at[core(cc), line[j]]
        send(dst, dst, ssem.at[i], rsem.at[i], devices[i]).wait_recv()
    for copy in copies:
        copy.wait_send()
    local.wait()


def exchange(blocks, collective_id):
    sem = pltpu.SemaphoreType.DMA
    return pl.pallas_call(
        exchange_kernel,
        out_shape=jax.ShapeDtypeStruct(blocks.shape, blocks.dtype),
        in_specs=[pl.BlockSpec(memory_space=pl.ANY)],
        out_specs=pl.BlockSpec(memory_space=pl.ANY),
        scratch_shapes=[sem((7,)), sem((7,)), sem],
        compiler_params=pltpu.CompilerParams(collective_id=collective_id, has_side_effects=True),
    )(blocks)


def scatter_kernel(zs, planes, given, out, own, twin_in, half_in, full_in, z_in, l_sem, c_ssem, c_rsem, h_ssem, h_rsem,
                   f_ssem, f_rsem, z_ssem, z_rsem):
    z, c, r = place()
    line = corners(r)
    s = z * 2 + c
    twin = (z * 2 + 1 - c, r)
    rows = out.shape[0]
    half = rows // 2
    step = 16
    spots = (3, 1, 2, 0) if planes else (0,)

    def at_z(other):
        return (other * 2 + c, r)

    partners = [twin] + ([(s, line[1]), (s, line[2])] if planes else [])
    partners += [at_z(lax.rem(z + k, zs)) for k in range(1, zs)]
    greet(partners)
    pending = []

    def block(k, core, row):
        zz = lax.rem(z + k, zs)
        return given.at[zz, core, row] if planes else given.at[zz, core]

    order = list(range(1, zs)) + [0]
    for k in order:
        for j in spots:
            copy = send(block(k, 1 - c, line[j]), twin_in.at[k, j], c_ssem.at[k, j], c_rsem.at[k, j], twin)
            copy.start()
            pending.append(copy.wait_send)
            pltpu.make_async_copy(block(k, c, line[j]), own.at[k, j], l_sem.at[k, j]).start()

    def settle(k, j):
        pltpu.make_async_copy(block(k, c, line[j]), own.at[k, j], l_sem.at[k, j]).wait()
        send(own.at[k, j], twin_in.at[k, j], c_ssem.at[k, j], c_rsem.at[k, j], twin).wait_recv()

    def add(first, last, k, j, *more):
        def body(n, carry):
            at = pl.ds(pl.multiple_of(first + n * step, step), step)
            value = own[k, j, at, :].astype(jnp.float32) + twin_in[k, j, at, :].astype(jnp.float32)
            for ref, offset in more:
                there = pl.ds(pl.multiple_of(first - offset + n * step, step), step)
                value = value + ref[there, :].astype(jnp.float32)
            own[k, j, at, :] = value.astype(own.dtype)
            return carry

        lax.fori_loop(0, (last - first) // step, body, 0)

    def start(copy):
        copy.start()
        pending.append(copy.wait_send)

    def stage_a(k):
        settle(k, 3)
        add(0, rows, k, 3)
        start(send(own.at[k, 3, pl.ds(half, half)], half_in.at[k, 1], h_ssem.at[k, 1], h_rsem.at[k, 1], (s, line[2])))
        start(send(own.at[k, 3, pl.ds(0, half)], half_in.at[k, 0], h_ssem.at[k, 0], h_rsem.at[k, 0], (s, line[1])))

    def stage_b(k):
        for j in (1, 2):
            settle(k, j)
            n = 1 if j == 1 else 0
            send(half_in.at[k, n], half_in.at[k, n], h_ssem.at[k, n], h_rsem.at[k, n], (s, line[2 - n])).wait_recv()
            if n:
                add(0, half, k, j)
                add(half, rows, k, j, (half_in.at[k, n], half))
            else:
                add(0, half, k, j, (half_in.at[k, n], 0))
                add(half, rows, k, j)
            start(send(own.at[k, j], full_in.at[k, j - 1], f_ssem.at[k, j - 1], f_rsem.at[k, j - 1], (s, line[j])))

    def stage_c(k):
        settle(k, 0)
        more = []
        if planes:
            for j in (1, 2):
                there = full_in.at[k, j - 1]
                send(there, there, f_ssem.at[k, j - 1], f_rsem.at[k, j - 1], (s, line[j])).wait_recv()
                more.append(there)
        if k:
            add(0, rows, k, 0, *[(ref, 0) for ref in more])
            start(send(own.at[k, 0], z_in.at[k], z_ssem.at[k], z_rsem.at[k], at_z(lax.rem(z + k, zs))))
            return
        for k2 in range(1, zs):
            there = z_in.at[k2]
            send(there, there, z_ssem.at[k2], z_rsem.at[k2], at_z(lax.rem(z + k2, zs))).wait_recv()
            more.append(there)

        def body(n, carry):
            at = pl.ds(pl.multiple_of(n * step, step), step)
            value = own[0, 0, at, :].astype(jnp.float32) + twin_in[0, 0, at, :].astype(jnp.float32)
            for ref in more:
                value = value + ref[at, :].astype(jnp.float32)
            out[at, :] = value
            return carry

        lax.fori_loop(0, rows // step, body, 0)

    total = len(order)
    for n in range(total + 2):
        if planes and n < total:
            stage_a(order[n])
        if planes and 1 <= n <= total:
            stage_b(order[n - 1])
        if n >= 2:
            stage_c(order[n - 2])
    for wait in pending:
        wait()


def scatter(blocks, zs, collective_id, planes=True):
    rows, columns = blocks.shape[-2:]
    spots = 4 if planes else 1
    low = blocks.dtype
    sem = pltpu.SemaphoreType.DMA
    size = rows * columns * 2
    used = size * (zs * (2 * spots + (3 if planes else 0) + 1) + 2)
    few = (zs, 2, 1 if planes else 1)
    return pl.pallas_call(
        functools.partial(scatter_kernel, zs, planes),
        out_shape=jax.ShapeDtypeStruct((rows, columns), jnp.float32),
        in_specs=[pl.BlockSpec(memory_space=pl.ANY)],
        out_specs=pl.BlockSpec(memory_space=pltpu.VMEM),
        scratch_shapes=[
            pltpu.VMEM((zs, spots, rows, columns), low),
            pltpu.VMEM((zs, spots, rows, columns), low),
            pltpu.VMEM((zs, 2, rows // 2, columns) if planes else (1, 2, 16, 128), low),
            pltpu.VMEM((zs, 2, rows, columns) if planes else (1, 2, 16, 128), low),
            pltpu.VMEM((zs, rows, columns) if zs > 1 else (1, 16, 128), low),
            sem((zs, 4)), sem((zs, 4)), sem((zs, 4)), sem((zs, 2)), sem((zs, 2)), sem((zs, 2)), sem((zs, 2)),
            sem((zs,)), sem((zs,)),
        ],
        compiler_params=pltpu.CompilerParams(
            collective_id=collective_id, has_side_effects=True, vmem_limit_bytes=used + 6 * MIB
        ),
    )(blocks)


class Links:
    def __init__(self, seq, rows):
        self.zs, self.rows = seq // 2, rows
        self.kernels = rows == 4 and self.zs == 4
        self.z_groups = [[2 * z + c for z in range(self.zs)] for c in range(2)]
        self.core_groups = [[2 * z, 2 * z + 1] for z in range(self.zs)]

    def gather_z(self, block):
        return lax.all_gather(block, "seq", axis=0, tiled=True, axis_index_groups=self.z_groups)

    def scatter_z(self, blocks):
        return lax.psum_scatter(blocks, "seq", scatter_dimension=0, tiled=True, axis_index_groups=self.z_groups)

    def exchange(self, blocks, collective_id):
        if self.kernels:
            return exchange(blocks, collective_id)
        moved = lax.all_to_all(blocks, "rows", split_axis=1, concat_axis=1, tiled=True)
        return lax.all_to_all(moved, "seq", split_axis=0, concat_axis=0, tiled=True, axis_index_groups=self.core_groups)

    def gather(self, arrays, z_flags, collective_id, planes=True):
        if self.kernels:
            return gather(arrays, z_flags, self.zs, collective_id, planes)
        results = []
        for array, flag in zip(arrays, z_flags):
            if planes:
                array = lax.all_gather(array, "rows", axis=0)
            array = lax.all_gather(array, "seq", axis=0, axis_index_groups=self.core_groups)[None]
            results.append(self.gather_z(array) if flag else array)
        return results

    def scatter(self, blocks, zs, collective_id, planes=True):
        if self.kernels:
            return scatter(blocks, zs, collective_id, planes)
        if zs > 1:
            blocks = self.scatter_z(blocks)
        blocks = lax.psum_scatter(
            blocks[0], "seq", scatter_dimension=0, tiled=True, axis_index_groups=self.core_groups
        )[0]
        if planes:
            blocks = lax.psum_scatter(blocks, "rows", scatter_dimension=0, tiled=True)[0]
        return blocks.astype(jnp.float32)


def on_device(seq, rows, tokens, w_query, w_key, w_value, w_out, w_gate, w_up, w_down, gain_attn, gain_ffn, lengths, order, cotangent):
    links = Links(seq, rows)
    zs = links.zs
    micro, _, span, _ = tokens.shape
    half_len = span // 2
    many = micro * span
    low = jnp.bfloat16
    scale = 1.0 / math.sqrt(HEAD_DIM)
    wide, part = w_gate.shape
    unit = w_down.shape[0]
    share = zs * unit

    both = jnp.stack([w_gate, w_up]).reshape(2, wide, zs, 2, rows, unit)
    both = jnp.transpose(both, (3, 4, 0, 1, 2, 5)).reshape(2, rows, 2, wide, share)
    both = links.exchange(both, 0)
    gate_w = links.gather_z(both[:, :, 0].reshape(2 * rows * wide, share))
    up_w = links.gather_z(both[:, :, 1].reshape(2 * rows * wide, share))
    down_w = links.gather_z(w_down)

    dy_own = cotangent.reshape(many, D)
    gains = jnp.pad(jnp.stack([gain_attn, gain_ffn], axis=1), ((0, 0), (0, 126)))
    pack = jnp.concatenate([w_query, w_key, w_value, w_out, gains], axis=1)
    packed, dy = links.gather([pack, dy_own], (True, False), 1)
    packed = packed.reshape(D, PACK)
    dy = dy.reshape(2 * rows * many, D)
    qkv_w, out_w = packed[:, :QKV], packed[:, QKV : QKV + D]
    gain_one = packed[:, QKV + D].astype(jnp.float32)
    gain_two = packed[:, QKV + D + 1].astype(jnp.float32)

    mine = slot_places(order, half_len, lax.axis_index("seq") * span + jnp.arange(span, dtype=jnp.int32))
    first = lengths[:, 0, 0]
    start = jnp.where(mine[None, :] >= first[:, None], first[:, None], 0)
    inverse = 10000.0 ** (-jnp.arange(HEAD_DIM // 2, dtype=jnp.float32) / (HEAD_DIM // 2))
    angles = (mine[None, :] - start).astype(jnp.float32)[..., None] * inverse
    cosine = jnp.cos(angles).reshape(many, 1, HEAD_DIM // 2)
    sine = jnp.sin(angles).reshape(many, 1, HEAD_DIM // 2)

    x = tokens.reshape(many, D).astype(jnp.float32)
    factor_one = rms_factor(x)
    attn_in = (x * factor_one * gain_one).astype(low)
    lin = product(attn_in, qkv_w)
    queries = rotate(lin[:, :D].reshape(many, HEADS, HEAD_DIM), cosine, sine).astype(low)
    queries = queries.reshape(micro, span, KV_HEADS, GROUP, HEAD_DIM)
    keys_own = rotate(lin[:, D : D + KVW].reshape(many, KV_HEADS, HEAD_DIM), cosine, sine).astype(low)
    kv_own = jnp.concatenate([keys_own.reshape(many, KVW), lin[:, D + KVW :].astype(low)], axis=1)
    (kv,) = links.gather([kv_own], (True,), 2, planes=False)
    count = seq * span
    kv = jnp.transpose(kv.reshape(seq, micro, span, 2 * KVW), (1, 0, 2, 3)).reshape(micro, count, 2, KV_HEADS, HEAD_DIM)
    keys, values = kv[:, :, 0], kv[:, :, 1]
    key_place = slot_places(order, half_len, jnp.arange(count, dtype=jnp.int32))
    allowed = (key_place[None, None, :] <= mine[None, :, None]) & (key_place[None, None, :] >= start[:, :, None])
    allowed = allowed[:, None, None]
    scores = jnp.einsum("mtkgd,mskd->mkgts", queries, keys, preferred_element_type=jnp.float32) * scale
    scores = jnp.where(allowed, scores, NEG_LARGE)
    top = jnp.max(scores, axis=-1, keepdims=True)
    exps = jnp.exp(scores - top)
    total = jnp.sum(exps, axis=-1, keepdims=True)
    probs = exps / total
    probs_low = probs.astype(low)
    attn_float = jnp.einsum("mkgts,mskd->mtkgd", probs_low, values, preferred_element_type=jnp.float32)
    attended = attn_float.astype(low).reshape(many, D)
    middle = x + product(attended, out_w)
    factor_two = rms_factor(middle)
    normed_two = middle * factor_two
    ffn_own = (normed_two * gain_two).astype(low)

    (ffn_in,) = links.gather([ffn_own], (False,), 3)
    ffn_in = ffn_in.reshape(2 * rows * many, D)
    gate = product(ffn_in, gate_w)
    upper = product(ffn_in, up_w)
    sig = jax.nn.sigmoid(gate)
    hidden = (gate * sig * upper).astype(low)
    d_hidden = product_nt(dy, down_w)
    d_gate = (d_hidden * upper * (sig * (1.0 + gate * (1.0 - sig)))).astype(low)
    d_upper = (d_hidden * gate * sig).astype(low)
    d_ffn_part = (product_nt(d_gate, gate_w) + product_nt(d_upper, up_w)).astype(low)
    result_part = product(hidden, down_w).astype(low)
    grad_down = product_tn(hidden, dy).astype(low)
    grad_gate = product_tn(ffn_in, d_gate).astype(low)
    grad_up = product_tn(ffn_in, d_upper).astype(low)

    d_ffn_in = links.scatter(d_ffn_part.reshape(1, 2, rows, many, D), 1, 4)
    result = (middle + links.scatter(result_part.reshape(1, 2, rows, many, D), 1, 4)).astype(low)
    grad_down = links.scatter_z(grad_down).astype(jnp.float32)
    grad_gate = links.scatter_z(grad_gate)
    grad_up = links.scatter_z(grad_up)
    grads = jnp.stack([grad_gate.reshape(2, rows, wide, share), grad_up.reshape(2, rows, wide, share)], axis=2)
    grads = links.exchange(grads, 0).reshape(2, rows, 2, wide, zs, unit)
    grads = jnp.transpose(grads, (2, 3, 4, 0, 1, 5)).reshape(2, wide, part).astype(jnp.float32)

    d_part, grad_gain_two = norm_back(d_ffn_in, normed_two, factor_two, gain_two)
    d_middle = dy_own.astype(jnp.float32) + d_part
    d_mid_low = d_middle.astype(low)
    grad_out = product_tn(attended, d_mid_low)
    d_heads = product_nt(d_mid_low, out_w).astype(low).reshape(micro, span, KV_HEADS, GROUP, HEAD_DIM)
    d_probs = jnp.einsum("mtkgd,mskd->mkgts", d_heads, values, preferred_element_type=jnp.float32)
    delta = jnp.sum(probs * d_probs, axis=-1, keepdims=True)
    d_scores = (probs * (d_probs - delta)).astype(low)
    d_query = jnp.einsum("mkgts,mskd->mtkgd", d_scores, keys, preferred_element_type=jnp.float32) * scale
    d_keys = jnp.einsum("mkgts,mtkgd->mskd", d_scores, queries, preferred_element_type=jnp.float32) * scale
    d_values = jnp.einsum("mkgts,mtkgd->mskd", probs_low, d_heads, preferred_element_type=jnp.float32)
    d_kv = jnp.concatenate([d_keys.reshape(micro, count, KVW), d_values.reshape(micro, count, KVW)], axis=-1).astype(low)
    d_kv = jnp.transpose(d_kv.reshape(micro, zs, 2, span, 2 * KVW), (1, 2, 0, 3, 4)).reshape(zs, 2, many, 2 * KVW)
    d_kv = links.scatter(d_kv, zs, 5, planes=False)
    d_lin = jnp.concatenate(
        [
            rotate_back(d_query.reshape(many, HEADS, HEAD_DIM), cosine, sine).reshape(many, D),
            rotate_back(d_kv[:, :KVW].reshape(many, KV_HEADS, HEAD_DIM), cosine, sine).reshape(many, KVW),
            d_kv[:, KVW:],
        ],
        axis=1,
    ).astype(low)
    grad_qkv = product_tn(attn_in, d_lin)
    d_attn_in = product_nt(d_lin, qkv_w)
    d_x, grad_gain_one = norm_back(d_attn_in, x * factor_one, factor_one, gain_one)
    x_grad = (d_middle + d_x).astype(low)
    gains_grad = jnp.pad(jnp.stack([grad_gain_one, grad_gain_two], axis=1), ((0, 0), (0, 126)))
    pack_grad = jnp.concatenate([grad_qkv, grad_out, gains_grad], axis=1).astype(low)
    pack_grad = links.scatter(pack_grad.reshape(zs, 2, rows, wide, PACK), zs, 6)

    return (
        result.reshape(tokens.shape),
        x_grad.reshape(tokens.shape),
        pack_grad[:, :D],
        pack_grad[:, D : D + KVW],
        pack_grad[:, D + KVW : QKV],
        pack_grad[:, QKV : QKV + D],
        grads[0],
        grads[1],
        grad_down,
        pack_grad[:, QKV + D],
        pack_grad[:, QKV + D + 1],
    )


def solution(mesh):
    both = ("seq", "rows")
    row = P(None, "rows", "seq", None)
    weight, gain = P(both, None), P(both)
    return jax.shard_map(
        functools.partial(on_device, mesh.shape["seq"], mesh.shape["rows"]),
        mesh=mesh,
        in_specs=(row,) + (weight,) * 7 + (gain, gain, P(None, "rows", None), P(), row),
        out_specs=(row, row) + (weight,) * 7 + (gain, gain),
        check_vma=False,
    )
```

```python
import functools

import jax
import jax.numpy as jnp
from jax import lax
from jax.experimental import pallas as pl
from jax.experimental.pallas import tpu as pltpu
from jax.sharding import PartitionSpec as P

D = 2048
HEADS = 32
KV_HEADS = 4
HEAD_DIM = 64
GROUP = 8
KVW = 256
QKV = D + 2 * KVW
PACK = QKV + 128

EPSILON = 1e-05
NEG_LARGE = -1e30
MESH = pl.DeviceIdType.MESH
MIB = 1 << 20
LONG = pl.CostEstimate(flops=50_000_000_000, bytes_accessed=150 * MIB, transcendentals=0)


def product(left, right):
    return jnp.dot(left, right, preferred_element_type=jnp.float32)


def product_nt(left, right):
    return lax.dot_general(left, right, (((1,), (1,)), ((), ())), preferred_element_type=jnp.float32)


def product_tn(left, right):
    return lax.dot_general(left, right, (((0,), (0,)), ((), ())), preferred_element_type=jnp.float32)


def rms_factor(values):
    return lax.rsqrt(jnp.mean(values * values, axis=-1, keepdims=True) + EPSILON)


def norm_back(d_scaled, normed, factor, gain):
    inner = d_scaled * gain
    mean = jnp.mean(inner * normed, axis=-1, keepdims=True)
    return factor * (inner - normed * mean), jnp.sum(d_scaled * normed, axis=0)


def slot_places(order, half_len, slot_ids):
    matches = (slot_ids // half_len)[:, None] == jnp.arange(order.shape[0], dtype=jnp.int32)[None, :]
    return jnp.sum(jnp.where(matches, order[None, :], 0), axis=1) * half_len + slot_ids % half_len


def place():
    s, r = lax.axis_index("seq"), lax.axis_index("rows")
    return lax.div(s, 2), lax.rem(s, 2), r


def send(src, dst, ssem, rsem, device):
    return pltpu.make_async_remote_copy(
        src_ref=src, dst_ref=dst, send_sem=ssem, recv_sem=rsem, device_id=device, device_id_type=MESH
    )


def greet(devices):
    barrier = pltpu.get_barrier_semaphore()
    for device in devices:
        pl.semaphore_signal(barrier, inc=1, device_id=device, device_id_type=MESH)
    pl.semaphore_wait(barrier, len(devices))


def corners(r):
    return r, r + 1 - 2 * lax.rem(r, 2), lax.rem(r + 2, 4), 3 - r


def exchange_others():
    return [(cc, j) for j in (3, 1, 2, 0) for cc in range(2) if (cc, j) != (0, 0)]


class Exchange:
    def __init__(self, own, out, ssem, rsem, l_sem):
        z, c, r = place()
        line = corners(r)
        self.own, self.out, self.ssem, self.rsem, self.here = own, out, ssem, rsem, (c, r)
        self.others = [(1 - c if cc else c, line[j]) for cc, j in exchange_others()]
        self.devices = [(z * 2 + core, row) for core, row in self.others]
        self.local = pltpu.make_async_copy(own.at[c, r], out.at[c, r], l_sem)

    def start(self):
        self.copies = []
        for i, other in enumerate(self.others):
            copy = send(self.own.at[other], self.out.at[self.here], self.ssem.at[i], self.rsem.at[i], self.devices[i])
            copy.start()
            self.copies.append(copy)
        self.local.start()

    def finish(self):
        for i, other in enumerate(self.others):
            dst = self.out.at[other]
            send(dst, dst, self.ssem.at[i], self.rsem.at[i], self.devices[i]).wait_recv()
        for copy in self.copies:
            copy.wait_send()
        self.local.wait()


class Line:
    def __init__(self, zs, way, lo, hi, src, dst, sems):
        z, c, r = place()
        lo, hi = (lo, min(hi, zs - 1)) if way == 1 else (max(lo, 1), hi)
        self.sends = (z >= lo) & (z < hi)
        self.gets = (z - way >= lo) & (z - way < hi)
        to = lax.rem(z + way + zs, zs)
        self.copy = send(src, dst, sems.at[0], sems.at[1], (to * 2 + c, r))

    def start(self):
        pl.when(self.sends)(self.copy.start)

    def finish(self):
        pl.when(self.sends)(self.copy.wait_send)
        pl.when(self.gets)(self.copy.wait_recv)


LINE_SEMS = pltpu.SemaphoreType.DMA((2,))
EXCHANGE_SEMS = [pltpu.SemaphoreType.DMA((7,)), pltpu.SemaphoreType.DMA((7,)), pltpu.SemaphoreType.DMA]


def neighbours(zs, planes, moved):
    z, c, r = place()
    line = corners(r)
    s = z * 2 + c
    devices = [(z * 2 + 1 - c, r)]
    if moved:
        devices = [(z * 2 + (1 - c if cc else c), line[j]) for cc, j in exchange_others()]
    elif planes:
        devices += [(s, line[1]), (s, line[2])]
    return devices + [(lax.rem(z + k, zs) * 2 + c, r) for k in range(1, zs)]


def gather_kernel(zs, flags, moves, lines, *refs):
    count = len(flags)
    carried = sum(not source for source, *_ in lines)
    taken = count + moves + carried
    own, line_own = refs[:count], refs[count + moves : taken]
    out, line_out = refs[taken : taken + count], refs[taken + count + moves : taken + count + moves + len(lines)]
    moved = [(refs[count + n], refs[taken + count + n]) for n in range(moves)]
    sems = refs[taken + count + moves + len(lines) :]
    z_ssem, z_rsem, f_ssem, f_rsem, h_ssem, h_rsem, c_ssem, c_rsem, l_sem = sems[:9]
    z, c, r = place()
    line = corners(r)
    s = z * 2 + c
    reach = zs if lines or any(flag[0] for flag in flags) else 1

    def at_z(other):
        return (other * 2 + c, r)

    twin = (z * 2 + 1 - c, r)
    greet(neighbours(reach, any(flag[1] for flag in flags), moves))
    exchanges = [Exchange(*pair, *sems[9 + 3 * n : 12 + 3 * n]) for n, pair in enumerate(moved)]
    waiting = list(line_own)
    going = [
        Line(zs, *way, moved[source - 1][1] if source else waiting.pop(0), dst, sems[9 + 3 * moves + n])
        for n, ((source, *way), dst) in enumerate(zip(lines, line_out))
    ]

    items = [(a, k) for k in range(zs) for a in range(count) if k == 0 or flags[a][0]]
    pending = []

    def slot(a, k, other, j):
        z_flag, planes = flags[a]
        if not z_flag:
            return out[a].at[other, j]
        core = 1 - c if other else c
        zz = lax.rem(z - k + zs, zs)
        return out[a].at[zz, core, line[j]] if planes else out[a].at[zz, core]

    def arrival(a, k, other, j):
        z_flag, planes = flags[a]
        if not z_flag:
            return out[a].at[other, j]
        zz = lax.rem(z - k + zs, zs)
        return out[a].at[zz, c, r] if planes else out[a].at[zz, c]

    for a in range(count):
        local = pltpu.make_async_copy(own[a], slot(a, 0, 0, 0), l_sem.at[a])
        local.start()
        pending.append(local.wait)
    for exchange_one in exchanges:
        exchange_one.start()
    for i, (a, k) in enumerate(items):
        if k:
            copy = send(own[a], arrival(a, 0, 0, 0), z_ssem.at[i], z_rsem.at[i], at_z(lax.rem(z + k, zs)))
            copy.start()
            pending.append(copy.wait_send)

    def to_twin(i, j, src):
        a, k = items[i]
        dst = slot(a, k, 0, j) if flags[a][0] else out[a].at[1, j]
        copy = send(src, dst, c_ssem.at[i, j], c_rsem.at[i, j], twin)
        copy.start()
        pending.append(copy.wait_send)

    def begin(i):
        a, k = items[i]
        src = own[a]
        if k:
            src = slot(a, k, 0, 0)
            send(src, src, z_ssem.at[i], z_rsem.at[i], at_z(lax.rem(z + k, zs))).wait_recv()
        if flags[a][1]:
            for j in (1, 2):
                copy = send(src, arrival(a, k, 0, j), f_ssem.at[i, j - 1], f_rsem.at[i, j - 1], (s, line[j]))
                copy.start()
                pending.append(copy.wait_send)
        to_twin(i, 0, src)

    def halves(a, ref, j):
        half = own[a].shape[0] // 2
        return ref.at[pl.ds(half if j == 1 else 0, half)]

    def forward(i):
        a, k = items[i]
        for j in (1, 2):
            src = slot(a, k, 0, j)
            send(src, src, f_ssem.at[i, j - 1], f_rsem.at[i, j - 1], (s, line[j])).wait_recv()
            there = slot(a, k, 0, j) if flags[a][0] else out[a].at[0, 3]
            copy = send(
                halves(a, src, j), halves(a, there, j), h_ssem.at[i, j - 1], h_rsem.at[i, j - 1], (s, line[3 - j])
            )
            copy.start()
            pending.append(copy.wait_send)
            to_twin(i, j, src)

    def finish(i):
        a, k = items[i]
        src = slot(a, k, 0, 3)
        for j in (1, 2):
            part = halves(a, src, j)
            send(part, part, h_ssem.at[i, j - 1], h_rsem.at[i, j - 1], (s, line[3 - j])).wait_recv()
        to_twin(i, 3, src)

    total = len(items)
    for i in range(total + 2):
        if i < total:
            begin(i)
        if i == total - 1:
            for exchange_one in exchanges:
                exchange_one.finish()
            for one in going:
                one.start()
        if 1 <= i <= total and flags[items[i - 1][0]][1]:
            forward(i - 1)
        if i >= 2 and flags[items[i - 2][0]][1]:
            finish(i - 2)
    for i, (a, k) in enumerate(items):
        for j in range(4 if flags[a][1] else 1):
            dst = slot(a, k, 1, j)
            send(dst, dst, c_ssem.at[i, j], c_rsem.at[i, j], twin).wait_recv()
    for one in going:
        one.finish()
    for wait in pending:
        wait()


def gather(arrays, flags, zs, collective_id, moved=(), lines=()):
    carried = [line[0] for line in lines if not isinstance(line[0], int)]
    plan = tuple((line[0] if isinstance(line[0], int) else 0,) + tuple(line[1:]) for line in lines)
    line_shapes = [moved[line[0] - 1] if isinstance(line[0], int) else line[0] for line in lines]
    n = sum(zs if z_flag else 1 for z_flag, _ in flags)
    sem = pltpu.SemaphoreType.DMA
    anywhere = pl.BlockSpec(memory_space=pl.ANY)
    shapes = [
        jax.ShapeDtypeStruct(((zs,) if z_flag else ()) + (2,) + ((4,) if planes else ()) + a.shape, a.dtype)
        for a, (z_flag, planes) in zip(arrays, flags)
    ] + [jax.ShapeDtypeStruct(m.shape, m.dtype) for m in (*moved, *line_shapes)]
    return pl.pallas_call(
        functools.partial(gather_kernel, zs, tuple(flags), len(moved), plan),
        out_shape=shapes,
        in_specs=[anywhere] * (len(arrays) + len(moved) + len(carried)),
        out_specs=[anywhere] * len(shapes),
        scratch_shapes=[
            sem((n,)), sem((n,)), sem((n, 2)), sem((n, 2)), sem((n, 2)), sem((n, 2)), sem((n, 4)), sem((n, 4)),
            sem((len(arrays),)),
        ] + EXCHANGE_SEMS * len(moved) + [LINE_SEMS] * len(lines),
        compiler_params=pltpu.CompilerParams(collective_id=collective_id, has_side_effects=True),
        cost_estimate=LONG,
    )(*arrays, *moved, *carried)


class Scatter:
    def __init__(self, zs, z_flag, planes, given, out, own, twin_in, half_in, full_in, z_in, l_sem, c_ssem, c_rsem, h_ssem, h_rsem,
                 f_ssem, f_rsem, z_ssem, z_rsem):
        self.__dict__.update(locals())
        self.z, self.c, self.r = place()
        self.line = corners(self.r)
        self.s = self.z * 2 + self.c
        self.twin = (self.z * 2 + 1 - self.c, self.r)
        self.rows = out.shape[0]
        self.step = 16
        self.spots = (3, 1, 2, 0) if planes else (0,)
        self.zs = zs if z_flag else 1
        self.order = list(range(1, self.zs)) + [0]
        self.pending = []

    def at_z(self, k):
        return (lax.rem(self.z + k, self.zs) * 2 + self.c, self.r)

    def block(self, k, other, j):
        if not self.z_flag:
            return self.given.at[other, j]
        zz, core = lax.rem(self.z + k, self.zs), 1 - self.c if other else self.c
        return self.given.at[zz, core, self.line[j]] if self.planes else self.given.at[zz, core]

    def start(self, copy):
        copy.start()
        self.pending.append(copy.wait_send)

    def local(self, k, j):
        return pltpu.make_async_copy(self.block(k, 0, j), self.own.at[k, j], self.l_sem.at[k, j])

    def begin(self):
        for k in self.order:
            for j in self.spots:
                block = self.block(k, 1, j)
                self.start(send(block, self.twin_in.at[k, j], self.c_ssem.at[k, j], self.c_rsem.at[k, j], self.twin))
                self.local(k, j).start()

    def settle(self, k, j):
        self.local(k, j).wait()
        send(self.own.at[k, j], self.twin_in.at[k, j], self.c_ssem.at[k, j], self.c_rsem.at[k, j], self.twin).wait_recv()

    def add(self, first, last, k, j, *more, final=False):
        step = self.step

        def body(n, carry):
            at = pl.ds(pl.multiple_of(first + n * step, step), step)
            value = self.own[k, j, at, :].astype(jnp.float32) + self.twin_in[k, j, at, :].astype(jnp.float32)
            for ref, offset in more:
                there = pl.ds(pl.multiple_of(first - offset + n * step, step), step)
                value = value + ref[there, :].astype(jnp.float32)
            if final:
                self.out[at, :] = value
            else:
                self.own[k, j, at, :] = value.astype(self.own.dtype)
            return carry

        lax.fori_loop(0, (last - first) // step, body, 0)

    def half_copy(self, k, n, src):
        dst = self.half_in.at[k, n]
        return send(dst if src is None else src, dst, self.h_ssem.at[k, n], self.h_rsem.at[k, n], (self.s, self.line[n + 1]))

    def full_copy(self, k, j, src):
        dst = self.full_in.at[k, j - 1]
        return send(dst if src is None else src, dst, self.f_ssem.at[k, j - 1], self.f_rsem.at[k, j - 1], (self.s, self.line[j]))

    def z_copy(self, k, src):
        dst = self.z_in.at[k]
        return send(dst if src is None else src, dst, self.z_ssem.at[k], self.z_rsem.at[k], self.at_z(k))

    def stage_a(self, k):
        half = self.rows // 2
        self.settle(k, 3)
        self.add(0, self.rows, k, 3)
        self.start(self.half_copy(k, 1, self.own.at[k, 3, pl.ds(half, half)]))
        self.start(self.half_copy(k, 0, self.own.at[k, 3, pl.ds(0, half)]))

    def stage_b(self, k):
        half = self.rows // 2
        for j in (1, 2):
            self.settle(k, j)
            n = 2 - j
            self.half_copy(k, n, None).wait_recv()
            more = (self.half_in.at[k, n], half if n else 0)
            self.add(0, half, k, j, *([] if n else [more]))
            self.add(half, self.rows, k, j, *([more] if n else []))
            self.start(self.full_copy(k, j, self.own.at[k, j]))

    def stage_c(self, k):
        self.settle(k, 0)
        more = []
        if self.planes:
            for j in (1, 2):
                self.full_copy(k, j, None).wait_recv()
                more.append((self.full_in.at[k, j - 1], 0))
        if k:
            self.add(0, self.rows, k, 0, *more)
            self.start(self.z_copy(k, self.own.at[k, 0]))
            return
        for k2 in range(1, self.zs):
            self.z_copy(k2, None).wait_recv()
            more.append((self.z_in.at[k2], 0))
        self.add(0, self.rows, 0, 0, *more, final=True)

    def end(self):
        for wait in self.pending:
            wait()


SCATTER_REFS = 14


def scatter_kernel(zs, flags, moves, lines, *refs):
    count, taken = len(flags), len(flags) + moves + len(lines)
    given, moved, line_own = refs[:count], refs[count : count + moves], refs[count + moves : taken]
    out, rest = refs[taken : taken + count], refs[taken + count :]
    moved_out, line_out, rest = rest[:moves], rest[moves : moves + len(lines)], rest[moves + len(lines) :]
    reach = zs if lines or any(flag[0] for flag in flags) else 1
    greet(neighbours(reach, any(flag[1] for flag in flags), moves))
    sums = [
        Scatter(zs, *flags[a], given[a], out[a], *rest[SCATTER_REFS * a : SCATTER_REFS * (a + 1)]) for a in range(count)
    ]
    rest = rest[SCATTER_REFS * count :]
    exchanges = [Exchange(moved[n], moved_out[n], *rest[3 * n : 3 * n + 3]) for n in range(moves)]
    rest = rest[3 * moves :]
    going = [Line(zs, *line, line_own[n], line_out[n], rest[n]) for n, line in enumerate(lines)]
    for one in sums:
        one.begin()
    for one in exchanges:
        one.start()
    for one in going:
        one.start()
    for one in sums:
        if not one.planes:
            for k in one.order[:-1]:
                one.stage_c(k)
    items = [(one, k) for k in list(range(1, zs)) + [0] for one in sums if one.planes and k < one.zs]
    total = len(items)
    for n in range(total + 2):
        for back, stage in enumerate((Scatter.stage_a, Scatter.stage_b, Scatter.stage_c)):
            if 0 <= n - back < total and (back < 2 or items[n - back][1]):
                stage(*items[n - back])
    for one in sums:
        one.stage_c(0)
    for one in exchanges + going:
        one.finish()
    for one in sums:
        one.end()


def scatter(arrays, flags, zs, collective_id, moved=(), lines=()):
    sem = pltpu.SemaphoreType.DMA
    anywhere = pl.BlockSpec(memory_space=pl.ANY)
    scratch, used, shapes = [], 0, []
    all_zs = zs
    for array, (z_flag, planes) in zip(arrays, flags):
        rows, columns = array.shape[-2:]
        zs = all_zs if z_flag else 1
        spots, low = 4 if planes else 1, array.dtype
        used += rows * columns * 2 * (zs * (2 * spots + (3 if planes else 0) + 1) + 4)
        shapes.append(jax.ShapeDtypeStruct((rows, columns), jnp.float32))
        scratch += [
            pltpu.VMEM((zs, spots, rows, columns), low),
            pltpu.VMEM((zs, spots, rows, columns), low),
            pltpu.VMEM((zs, 2, rows // 2, columns) if planes else (1, 2, 16, 128), low),
            pltpu.VMEM((zs, 2, rows, columns) if planes else (1, 2, 16, 128), low),
            pltpu.VMEM((zs, rows, columns) if zs > 1 else (1, 16, 128), low),
            sem((zs, 4)), sem((zs, 4)), sem((zs, 4)), sem((zs, 2)), sem((zs, 2)), sem((zs, 2)), sem((zs, 2)),
            sem((zs,)), sem((zs,)),
        ]
    count = len(arrays)
    return pl.pallas_call(
        functools.partial(scatter_kernel, all_zs, tuple(flags), len(moved), tuple(tuple(line[1:]) for line in lines)),
        out_shape=shapes + [jax.ShapeDtypeStruct(m.shape, m.dtype) for m in (*moved, *[line[0] for line in lines])],
        in_specs=[anywhere] * (count + len(moved) + len(lines)),
        out_specs=[pl.BlockSpec(memory_space=pltpu.VMEM)] * count + [anywhere] * (len(moved) + len(lines)),
        scratch_shapes=scratch + EXCHANGE_SEMS * len(moved) + [LINE_SEMS] * len(lines),
        compiler_params=pltpu.CompilerParams(
            collective_id=collective_id, has_side_effects=True, vmem_limit_bytes=used + 6 * MIB
        ),
        cost_estimate=LONG,
    )(*arrays, *moved, *[line[0] for line in lines])


def partner(tensor):
    lanes = tensor.shape[-1]
    half = HEAD_DIM // 2
    lane = lax.broadcasted_iota(jnp.int32, tensor.shape, tensor.ndim - 1)
    ahead = pltpu.roll(tensor, lanes - half, tensor.ndim - 1)
    behind = pltpu.roll(tensor, half, tensor.ndim - 1)
    return jnp.where(lax.rem(lane, HEAD_DIM) < half, ahead, behind)


def stack_heads(block, first):
    return jnp.concatenate(
        [block[:, (first + h) * HEAD_DIM : (first + h + 1) * HEAD_DIM] for h in range(GROUP)], axis=0
    )


def unstack_heads(stacked, span):
    return jnp.concatenate([stacked[h * span : (h + 1) * span] for h in range(GROUP)], axis=1)


def load_window(inverse_ref, kv_ref, window, first_block):
    half_len = kv_ref.shape[1] // 2
    for n in range(window.shape[0] // half_len):
        slot = inverse_ref[first_block + n]
        at = pl.ds(pl.multiple_of(lax.rem(slot, 2) * half_len, half_len), half_len)
        window[n * half_len : (n + 1) * half_len, :] = kv_ref[lax.div(slot, 2), at, :]


def window_of(order_ref, first_ref, count, half_len):
    m, half = pl.program_id(0), pl.program_id(1)
    my_block = order_ref[lax.axis_index("seq") * 2 + half]
    half_blocks = count // half_len // 2
    first_block = jnp.where(my_block >= half_blocks, half_blocks, 0)
    return first_block, my_block * half_len, first_ref[m]


def attend_kernel(order_ref, inverse_ref, first_ref, lin_ref, cos_ref, sin_ref, kv_ref, q_ref, out_ref, window, bias):
    span = lin_ref.shape[0]
    wide = window.shape[0]
    first_block, my_place, first = window_of(order_ref, first_ref, 2 * wide, span)
    load_window(inverse_ref, kv_ref, window, first_block)
    key_place = first_block * span + lax.broadcasted_iota(jnp.int32, (span, wide), 1)
    place_here = my_place + lax.broadcasted_iota(jnp.int32, (span, wide), 0)
    start = jnp.where(place_here >= first, first, 0)
    bias[...] = jnp.where((key_place <= place_here) & (key_place >= start), 0.0, NEG_LARGE)
    cosine, sine = cos_ref[...], sin_ref[...]
    width = GROUP * HEAD_DIM
    for g in range(KV_HEADS):
        at = slice(g * width, (g + 1) * width)
        lin = lin_ref[:, at]
        query = (lin * cosine + partner(lin) * sine).astype(jnp.bfloat16) * jnp.bfloat16(HEAD_DIM ** -0.5)
        q_ref[:, at] = query
        key = window[:, g * HEAD_DIM : (g + 1) * HEAD_DIM]
        value = window[:, KVW + g * HEAD_DIM : KVW + (g + 1) * HEAD_DIM]
        scores = product_nt(stack_heads(query, 0), key).reshape(GROUP, span, wide) + bias[...][None]
        exps = jnp.exp(scores - jnp.max(scores, axis=-1, keepdims=True))
        total = jnp.sum(exps, axis=-1, keepdims=True).reshape(GROUP * span, 1)
        mixed = product(exps.astype(jnp.bfloat16).reshape(GROUP * span, wide), value) / total
        out_ref[:, at] = unstack_heads(mixed, span).astype(jnp.bfloat16)


def attend_back_kernel(order_ref, inverse_ref, first_ref, q_ref, d_ref, cos_ref, sin_ref, kv_ref, dq_ref, dkv_ref, window, bias, sums):
    span = q_ref.shape[0]
    wide = window.shape[0]
    rows = GROUP * span
    half = pl.program_id(1)
    first_block, my_place, first = window_of(order_ref, first_ref, 2 * wide, span)
    load_window(inverse_ref, kv_ref, window, first_block)
    key_place = first_block * span + lax.broadcasted_iota(jnp.int32, (wide, rows), 0)
    place_here = my_place + lax.rem(lax.broadcasted_iota(jnp.int32, (wide, rows), 1), span)
    start = jnp.where(place_here >= first, first, 0)
    bias[...] = jnp.where((key_place <= place_here) & (key_place >= start), 0.0, NEG_LARGE)

    @pl.when(half == 0)
    def _():
        sums[...] = jnp.zeros_like(sums)

    cosine, sine = cos_ref[...], sin_ref[...]
    width = GROUP * HEAD_DIM
    d_keys, d_values = [], []
    for g in range(KV_HEADS):
        at = slice(g * width, (g + 1) * width)
        key = window[:, g * HEAD_DIM : (g + 1) * HEAD_DIM]
        value = window[:, KVW + g * HEAD_DIM : KVW + (g + 1) * HEAD_DIM]
        query = stack_heads(q_ref[:, at], 0)
        d_mixed = stack_heads(d_ref[:, at], 0)
        scores = product_nt(key, query) + bias[...]
        exps = jnp.exp(scores - jnp.max(scores, axis=0, keepdims=True))
        probs = exps * (1.0 / jnp.sum(exps, axis=0, keepdims=True))
        d_probs = product_nt(value, d_mixed)
        weighted = probs * d_probs
        delta = jnp.sum(weighted, axis=0, keepdims=True)
        d_scores = (weighted - probs * delta).astype(jnp.bfloat16)
        d_keys.append(product(d_scores, query))
        d_values.append(product(probs.astype(jnp.bfloat16), d_mixed))
        d_query = unstack_heads(product_tn(d_scores, key) * HEAD_DIM ** -0.5, span)
        dq_ref[:, at] = (d_query * cosine - partner(d_query) * sine).astype(jnp.bfloat16)
    d_window = jnp.concatenate(d_keys + d_values, axis=1)
    for n in range(wide // span):
        slot = inverse_ref[first_block + n]
        to = pl.ds(pl.multiple_of(lax.rem(slot, 2) * span, span), span)
        sums[lax.div(slot, 2), to, :] += d_window[n * span : (n + 1) * span]

    @pl.when(half == 1)
    def _():
        dkv_ref[...] = sums[...].astype(jnp.bfloat16)


def attention_specs(seq, micro, span):
    half_len = span // 2

    def rows(width):
        return pl.BlockSpec((half_len, width), lambda m, h, *_: (m * 2 + h, 0))

    whole = pl.BlockSpec((seq, span, 2 * KVW), lambda m, h, *_: (0, m, 0))
    return half_len, rows, whole


def attend(order, inverse, first, lin, cosine, sine, kv):
    seq, many, _ = kv.shape
    micro = first.shape[0]
    span = many // micro
    half_len, rows, whole = attention_specs(seq, micro, span)
    wide = seq * span // 2
    return pl.pallas_call(
        attend_kernel,
        grid_spec=pltpu.PrefetchScalarGridSpec(
            num_scalar_prefetch=3,
            grid=(micro, 2),
            in_specs=[rows(D), rows(GROUP * HEAD_DIM), rows(GROUP * HEAD_DIM), whole],
            out_specs=[rows(D), rows(D)],
            scratch_shapes=[pltpu.VMEM((wide, 2 * KVW), jnp.bfloat16), pltpu.VMEM((half_len, wide), jnp.float32)],
        ),
        out_shape=[jax.ShapeDtypeStruct((many, D), jnp.bfloat16)] * 2,
        compiler_params=pltpu.CompilerParams(vmem_limit_bytes=48 * MIB),
        cost_estimate=pl.CostEstimate(flops=8 * many * wide * D, bytes_accessed=16 * MIB, transcendentals=many * wide * HEADS),
    )(order, inverse, first, lin, cosine, sine, kv)


def attend_back(order, inverse, first, queries, d_heads, cosine, sine, kv):
    seq, many, _ = kv.shape
    micro = first.shape[0]
    span = many // micro
    half_len, rows, whole = attention_specs(seq, micro, span)
    wide = seq * span // 2
    return pl.pallas_call(
        attend_back_kernel,
        grid_spec=pltpu.PrefetchScalarGridSpec(
            num_scalar_prefetch=3,
            grid=(micro, 2),
            in_specs=[rows(D), rows(D), rows(GROUP * HEAD_DIM), rows(GROUP * HEAD_DIM), whole],
            out_specs=[rows(D), whole],
            scratch_shapes=[
                pltpu.VMEM((wide, 2 * KVW), jnp.bfloat16),
                pltpu.VMEM((wide, GROUP * half_len), jnp.float32),
                pltpu.VMEM((seq, span, 2 * KVW), jnp.float32),
            ],
        ),
        out_shape=[jax.ShapeDtypeStruct((many, D), jnp.bfloat16), jax.ShapeDtypeStruct(kv.shape, jnp.bfloat16)],
        compiler_params=pltpu.CompilerParams(vmem_limit_bytes=56 * MIB),
        cost_estimate=pl.CostEstimate(flops=20 * many * wide * D, bytes_accessed=24 * MIB, transcendentals=many * wide * HEADS),
    )(order, inverse, first, queries, d_heads, cosine, sine, kv)


def assemble(zs, pieces, whole, sem):
    if len(pieces) == 1:
        copy = pltpu.make_async_copy(pieces[0], whole, sem.at[0])
        copy.start()
        return [copy]
    z = lax.div(lax.axis_index("seq"), 2)
    size = whole.shape[0] // zs

    def rows(zz):
        return whole.at[pl.ds(pl.multiple_of(zz * size, size), size)]

    copies = [pltpu.make_async_copy(pieces[0], rows(z), sem.at[0])]
    copies[0].start()
    for k in range(1, zs):
        below = pltpu.make_async_copy(pieces[k], rows(lax.rem(z - k + zs, zs)), sem.at[k])
        above = pltpu.make_async_copy(pieces[2 * zs - 1 - k], rows(lax.rem(z - k + zs, zs)), sem.at[k])
        pl.when(z >= k)(below.start)
        pl.when(z < k)(above.start)
        copies.append(below)
    return copies


def ffn_kernel(zs, count, *refs):
    x_ref, dy_ref = refs[:2]
    both_pieces, down_pieces = refs[2 : 2 + count], refs[2 + count : 2 + 2 * count]
    out_ref, dx_ref, g_both_ref, g_down_ref, both_w, down_w, both_sum, down_sum, sem = refs[2 + 2 * count :]
    n = down_w.shape[0]
    step, last = pl.program_id(0), pl.num_programs(0) - 1

    @pl.when(step == 0)
    def _():
        copies = assemble(zs, both_pieces, both_w, sem.at[0]) + assemble(zs, down_pieces, down_w, sem.at[1])
        both_sum[...] = jnp.zeros_like(both_sum)
        down_sum[...] = jnp.zeros_like(down_sum)
        for copy in copies:
            copy.wait()

    x, dy = x_ref[...], dy_ref[...]
    lin = product(x, both_w[...])
    gate, upper = lin[:, :n], lin[:, n:]
    sig = 1.0 / (1.0 + jnp.exp(-gate))
    act = gate * sig
    hidden = (act * upper).astype(jnp.bfloat16)
    d_hidden = product_nt(dy, down_w[...])
    d_gate = d_hidden * upper * (sig * (1.0 + gate * (1.0 - sig)))
    d_both = jnp.concatenate([d_gate.astype(jnp.bfloat16), (d_hidden * act).astype(jnp.bfloat16)], axis=1)
    dx_ref[...] = product_nt(d_both, both_w[...]).astype(jnp.bfloat16)
    out_ref[...] = product(hidden, down_w[...]).astype(jnp.bfloat16)
    for at in range(0, D, 256):
        both_sum[at : at + 256, :] += product_tn(x[:, at : at + 256], d_both)
    part = n // 4
    for at in range(0, n, part):
        down_sum[at : at + part, :] += product_tn(hidden[:, at : at + part], dy)

    @pl.when(step == last)
    def _():
        both_w[...] = both_sum[...].astype(jnp.bfloat16)
        down_w[...] = down_sum[...].astype(jnp.bfloat16)
        copies = [
            pltpu.make_async_copy(both_w, g_both_ref, sem.at[0, 0]),
            pltpu.make_async_copy(down_w, g_down_ref, sem.at[1, 0]),
        ]
        for copy in copies:
            copy.start()
        for copy in copies:
            copy.wait()


def feed_forward(x, dy, both_pieces, down_pieces, zs):
    count = x.shape[0]
    spread_over = zs if len(both_pieces) > 1 else 1
    n = down_pieces[0].shape[0] * spread_over
    block = 256
    low = jnp.bfloat16
    tokens = pl.BlockSpec((block, D), lambda i: (i, 0))
    anywhere = pl.BlockSpec(memory_space=pl.ANY)
    return pl.pallas_call(
        functools.partial(ffn_kernel, zs, len(both_pieces)),
        grid=(count // block,),
        in_specs=[tokens, tokens] + [anywhere] * (2 * len(both_pieces)),
        out_specs=[tokens, tokens, anywhere, anywhere],
        out_shape=[jax.ShapeDtypeStruct(x.shape, low)] * 2
        + [jax.ShapeDtypeStruct((D, 2 * n), low), jax.ShapeDtypeStruct((n, D), low)],
        scratch_shapes=[
            pltpu.VMEM((D, 2 * n), low),
            pltpu.VMEM((n, D), low),
            pltpu.VMEM((D, 2 * n), jnp.float32),
            pltpu.VMEM((n, D), jnp.float32),
            pltpu.SemaphoreType.DMA((2, zs)),
        ],
        compiler_params=pltpu.CompilerParams(vmem_limit_bytes=60 * MIB),
        cost_estimate=pl.CostEstimate(flops=18 * count * D * n, bytes_accessed=60 * MIB, transcendentals=count * n),
    )(x, dy, *both_pieces, *down_pieces)


def spread_kernel(zs, rows, unit, gate_ref, up_ref, out):
    for c in range(2):
        for r in range(rows):
            for n, weight in enumerate((gate_ref, up_ref)):
                for z in range(zs):
                    at = ((z * 2 + c) * rows + r) * unit
                    to = (n * zs + z) * unit
                    out[c, r, :, to : to + unit] = weight[:, at : at + unit]


def spread(gate, up, zs, rows):
    wide, part = gate.shape
    unit = part // (zs * 2 * rows)
    return pl.pallas_call(
        functools.partial(spread_kernel, zs, rows, unit),
        out_shape=jax.ShapeDtypeStruct((2, rows, wide, 2 * zs * unit), gate.dtype),
    )(gate, up)


def collect_kernel(zs, rows, unit, given, *outs):
    for n, out in enumerate(outs):
        for c in range(2):
            for r in range(rows):
                for z in range(zs):
                    at = ((z * 2 + c) * rows + r) * unit
                    to = (n * zs + z) * unit
                    out[:, at : at + unit] = given[c, r, :, to : to + unit].astype(jnp.float32)


def collect(blocks, zs, rows, unit):
    shape = jax.ShapeDtypeStruct((blocks.shape[2], unit * zs * 2 * rows), jnp.float32)
    return pl.pallas_call(functools.partial(collect_kernel, zs, rows, unit), out_shape=[shape, shape])(blocks)


class Links:
    def __init__(self, seq, rows):
        self.zs, self.rows = seq // 2, rows
        self.kernels = rows == 4 and self.zs == 4
        self.z_groups = [[2 * z + c for z in range(self.zs)] for c in range(2)]
        self.core_groups = [[2 * z, 2 * z + 1] for z in range(self.zs)]

    def gather_z(self, block):
        return lax.all_gather(block, "seq", axis=0, tiled=True, axis_index_groups=self.z_groups)

    def scatter_z(self, blocks):
        return lax.psum_scatter(blocks, "seq", scatter_dimension=0, tiled=True, axis_index_groups=self.z_groups)

    def exchange_xla(self, blocks):
        moved = lax.all_to_all(blocks, "rows", split_axis=1, concat_axis=1, tiled=True)
        return lax.all_to_all(moved, "seq", split_axis=0, concat_axis=0, tiled=True, axis_index_groups=self.core_groups)

    def along(self, way, lo, hi):
        return [(2 * z + c, 2 * (z + way) + c) for z in range(lo, hi) for c in range(2) if 0 <= z + way < self.zs]

    def permute(self, lines):
        return [lax.ppermute(array, "seq", self.along(way, lo, hi)) for array, way, lo, hi in lines]

    def gather_lines(self, k, up, down):
        return [(up, 1, k - 1, self.zs), (down, -1, 0, self.zs - k + 1)]

    def part(self, blocks, to, held):
        z = lax.div(lax.axis_index("seq"), 2)
        found = lax.dynamic_index_in_dim(blocks, lax.rem(z + to + self.zs, self.zs), 0, keepdims=False)
        for other, there in held:
            found = found.astype(jnp.float32) + jnp.where(there, other.astype(jnp.float32), 0.0)
        return found

    def scatter_lines(self, k, blocks, held=None):
        up, down = self.held(held)
        low = blocks.dtype
        return [
            (self.part(blocks, -k, up).astype(low), 1, 0, k),
            (self.part(blocks, k, down).astype(low), -1, self.zs - k, self.zs),
        ]

    def scatter_end(self, blocks, held):
        up, down = self.held(held)
        return self.part(blocks, 0, up + down)

    def held(self, held):
        z = lax.div(lax.axis_index("seq"), 2)
        return ([(held[0], z > 0)], [(held[1], z < self.zs - 1)]) if held else ([], [])

    @staticmethod
    def tie(arrays, *others):
        if not others:
            return arrays
        return lax.optimization_barrier((*arrays, *others))[: len(arrays)]

    def gather(self, arrays, flags, collective_id, moved=(), lines=()):
        if self.kernels:
            return gather(arrays, flags, self.zs, collective_id, moved, lines)
        results = []
        for array, (z_flag, planes) in zip(arrays, flags):
            if planes:
                array = lax.all_gather(array, "rows", axis=0)
            array = lax.all_gather(array, "seq", axis=0, axis_index_groups=self.core_groups)
            results.append(self.gather_z(array[None]) if z_flag else array)
        return results + [self.exchange_xla(blocks) for blocks in moved] + [line[0] for line in lines]

    def scatter(self, arrays, flags, collective_id, moved=(), lines=()):
        if self.kernels:
            return scatter(arrays, flags, self.zs, collective_id, moved, lines)
        return (
            [
                self.scatter_one(self.scatter_z(blocks)[0] if z_flag else blocks, planes)
                for blocks, (z_flag, planes) in zip(arrays, flags)
            ]
            + [self.exchange_xla(blocks) for blocks in moved]
            + [line[0] for line in lines]
        )

    def scatter_one(self, blocks, planes):
        blocks = lax.psum_scatter(blocks, "seq", scatter_dimension=0, tiled=True, axis_index_groups=self.core_groups)[0]
        if planes:
            blocks = lax.psum_scatter(blocks, "rows", scatter_dimension=0, tiled=True)[0]
        return blocks.astype(jnp.float32)


def on_device(seq, rows, tokens, w_query, w_key, w_value, w_out, w_gate, w_up, w_down, gain_attn, gain_ffn, lengths, order, cotangent):
    links = Links(seq, rows)
    zs = links.zs
    micro, _, span, _ = tokens.shape
    half_len = span // 2
    many = micro * span
    low = jnp.bfloat16
    wide = w_gate.shape[0]
    unit = w_down.shape[0]

    chained = links.kernels
    both = spread(w_gate, w_up, zs, rows)
    gains = jnp.pad(jnp.stack([gain_attn, gain_ffn], axis=1), ((0, 0), (0, 126)))
    pack = jnp.concatenate([w_query, w_key, w_value, gains], axis=1)
    lines = [(1, 1, 0, zs), (1, -1, 0, zs)] if chained else []
    packed, both_own, *both_got = links.gather([pack], [(True, True)], 0, [both], lines)
    flat = (2 * rows * wide, 2 * zs * unit)
    both_own = both_own.reshape(flat)
    both_w, down_w = [both_own], [w_down]
    if chained:
        both_w += [None] * (2 * zs - 2)
        down_w += [None] * (2 * zs - 2)
        both_w[1], both_w[zs] = (b.reshape(flat) for b in both_got)
        down_w[1], down_w[zs] = links.permute(links.gather_lines(1, *links.tie([w_down, w_down], packed)))
    else:
        both_w, down_w = [links.gather_z(both_own)], [links.gather_z(w_down)]
    packed = packed.reshape(D, PACK)
    gain_one = packed[:, QKV].astype(jnp.float32)
    gain_two = packed[:, QKV + 1].astype(jnp.float32)
    dy_own = cotangent.reshape(many, D)

    mine = slot_places(order, half_len, lax.axis_index("seq") * span + jnp.arange(span, dtype=jnp.int32))
    first = lengths[:, 0, 0]
    start = jnp.where(mine[None, :] >= first[:, None], first[:, None], 0)
    inverse = 10000.0 ** (-jnp.arange(HEAD_DIM // 2, dtype=jnp.float32) / (HEAD_DIM // 2))
    angles = ((mine[None, :] - start).astype(jnp.float32)[..., None] * inverse).reshape(many, HEAD_DIM // 2)
    cosine, sine = jnp.cos(angles), jnp.sin(angles)
    cosine = jnp.tile(cosine, (1, 2 * GROUP))
    sine = jnp.tile(jnp.concatenate([-sine, sine], axis=1), (1, GROUP))
    slot_of = jnp.argmax(order[None, :] == jnp.arange(order.shape[0], dtype=jnp.int32)[:, None], axis=1).astype(jnp.int32)

    def turn(tensor, sign):
        swapped = jnp.flip(tensor.reshape(many, KV_HEADS, 2, HEAD_DIM // 2), axis=2).reshape(many, KVW)
        return tensor * cosine[:, :KVW] + sign * swapped * sine[:, :KVW]

    x = tokens.reshape(many, D).astype(jnp.float32)
    factor_one = rms_factor(x)
    attn_in = (x * factor_one * gain_one).astype(low)
    lin = product(attn_in, packed)
    kv_own = jnp.concatenate([turn(lin[:, D : D + KVW], 1.0), lin[:, D + KVW : QKV]], axis=1).astype(low)
    lines = []
    if chained:
        (kv_own,) = links.tie([kv_own], down_w[1], down_w[zs])
        lines = links.gather_lines(2, both_w[1], both_w[zs])
    kv, out_w, dy, *got = links.gather([kv_own, w_out, dy_own], [(True, False), (True, True), (False, True)], 1, (), lines)
    kv = kv.reshape(seq, many, 2 * KVW)
    out_w = out_w.reshape(D, D)
    dy = dy.reshape(2 * rows * many, D)
    if chained:
        both_w[2], both_w[zs + 1] = got
        down_w[2], down_w[zs + 1] = links.permute(links.gather_lines(2, *links.tie([down_w[1], down_w[zs]], kv)))
    queries, attended = attend(order, slot_of, first, lin, cosine, sine, kv)
    middle = x + product(attended, out_w)
    factor_two = rms_factor(middle)
    normed_two = middle * factor_two
    ffn_own = (normed_two * gain_two).astype(low)

    lines = []
    if chained:
        (ffn_own,) = links.tie([ffn_own], down_w[2], down_w[zs + 1])
        lines = links.gather_lines(3, both_w[2], both_w[zs + 1]) + links.gather_lines(3, down_w[2], down_w[zs + 1])
    ffn_in, *got = links.gather([ffn_own], [(False, True)], 2, (), lines)
    if chained:
        both_w[3], both_w[zs + 2], down_w[3], down_w[zs + 2] = got
    ffn_in = ffn_in.reshape(2 * rows * many, D)
    result_part, d_ffn_part, grad_both, grad_down = feed_forward(ffn_in, dy, both_w, down_w, zs)
    grad_both = grad_both.reshape(zs, *flat)
    grad_down = grad_down.reshape(zs, unit, D)
    lines = []
    if chained:
        lines = links.scatter_lines(1, grad_both) + links.scatter_lines(1, grad_down)
    d_ffn_in, *got = links.scatter([d_ffn_part.reshape(2, rows, many, D)], [(False, True)], 3, (), lines)
    if chained:
        lines = links.scatter_lines(2, grad_both, got[:2]) + links.scatter_lines(2, grad_down, got[2:])
        got = links.permute(lines)

    d_part, grad_gain_two = norm_back(d_ffn_in, normed_two, factor_two, gain_two)
    d_middle = dy_own.astype(jnp.float32) + d_part
    d_mid_low = d_middle.astype(low)
    grad_out = product_tn(attended, d_mid_low).astype(low)
    d_heads = product_nt(d_mid_low, out_w).astype(low)
    d_query, d_kv = attend_back(order, slot_of, first, queries, d_heads, cosine, sine, kv)
    shards = (zs, 2, rows, wide)
    lines = []
    if chained:
        d_query, d_kv, *got = lax.optimization_barrier((d_query, d_kv, *got))
        lines = links.scatter_lines(3, grad_both, got[:2])
        down_lines = links.scatter_lines(3, grad_down, got[2:])
    grad_query = product_tn(attn_in, d_query).astype(low)
    d_kv, grad_out, grad_query, result_sum, *got = links.scatter(
        [
            d_kv.reshape(zs, 2, many, 2 * KVW),
            grad_out.reshape(*shards, D),
            grad_query.reshape(*shards, D),
            result_part.reshape(2, rows, many, D),
        ],
        [(True, False), (True, True), (True, True), (False, True)],
        4,
        (),
        lines,
    )
    if chained:
        grad_both = links.scatter_end(grad_both, got).astype(low)
    else:
        grad_both, grad_down = links.scatter_z(grad_both)[0], links.scatter_z(grad_down)[0]
        down_lines = []
    result = (middle + result_sum).astype(low)
    d_key = turn(d_kv[:, :KVW], -1.0)
    d_kv = jnp.concatenate([d_key.astype(low), d_kv[:, KVW:].astype(low)], axis=1)
    d_attn_in = product_nt(d_query, packed[:, :D]) + product_nt(d_kv, packed[:, D:QKV])
    d_x, grad_gain_one = norm_back(d_attn_in, x * factor_one, factor_one, gain_one)
    x_grad = (d_middle + d_x).astype(low)
    gains_grad = jnp.pad(jnp.stack([grad_gain_one, grad_gain_two], axis=1), ((0, 0), (0, 126)))
    pack_grad = jnp.concatenate([product_tn(attn_in, d_kv), gains_grad], axis=1).astype(low)
    pack_grad, grad_both, *got = links.scatter(
        [pack_grad.reshape(*shards, 2 * KVW + 128)],
        [(True, True)],
        5,
        [grad_both.reshape(2, rows, wide, 2 * zs * unit)],
        down_lines,
    )
    if chained:
        grad_down = links.scatter_end(grad_down, got)
    grad_down = grad_down.astype(jnp.float32)
    grad_gate, grad_up = collect(grad_both, zs, rows, unit)

    return (
        result.reshape(tokens.shape),
        x_grad.reshape(tokens.shape),
        grad_query,
        pack_grad[:, :KVW],
        pack_grad[:, KVW : 2 * KVW],
        grad_out,
        grad_gate,
        grad_up,
        grad_down,
        pack_grad[:, 2 * KVW],
        pack_grad[:, 2 * KVW + 1],
    )


def solution(mesh):
    both = ("seq", "rows")
    row = P(None, "rows", "seq", None)
    weight, gain = P(both, None), P(both)
    return jax.shard_map(
        functools.partial(on_device, mesh.shape["seq"], mesh.shape["rows"]),
        mesh=mesh,
        in_specs=(row,) + (weight,) * 7 + (gain, gain, P(None, "rows", None), P(), row),
        out_specs=(row, row) + (weight,) * 7 + (gain, gain),
        check_vma=False,
    )
```

```python
import functools

import jax
import jax.numpy as jnp
from jax import lax
from jax.experimental import pallas as pl
from jax.experimental.pallas import tpu as pltpu
from jax.sharding import PartitionSpec as P

D = 2048
HEADS = 32
KV_HEADS = 4
HEAD_DIM = 64
GROUP = 8
KVW = 256
QKV = D + 2 * KVW
PACK = QKV + 128

EPSILON = 1e-05
NEG_LARGE = -1e30
MESH = pl.DeviceIdType.MESH
MIB = 1 << 20
LONG = pl.CostEstimate(flops=50_000_000_000, bytes_accessed=150 * MIB, transcendentals=0)


def product(left, right):
    return jnp.dot(left, right, preferred_element_type=jnp.float32)


def product_nt(left, right):
    return lax.dot_general(left, right, (((1,), (1,)), ((), ())), preferred_element_type=jnp.float32)


def product_tn(left, right):
    return lax.dot_general(left, right, (((0,), (0,)), ((), ())), preferred_element_type=jnp.float32)


def rms_factor(values):
    return lax.rsqrt(jnp.mean(values * values, axis=-1, keepdims=True) + EPSILON)


def norm_back(d_scaled, normed, factor, gain):
    inner = d_scaled * gain
    mean = jnp.mean(inner * normed, axis=-1, keepdims=True)
    return factor * (inner - normed * mean), jnp.sum(d_scaled * normed, axis=0)


def turn(tensor, cosine, sine):
    rows, lanes = tensor.shape
    half = HEAD_DIM // 2
    swapped = jnp.flip(tensor.reshape(rows, lanes // HEAD_DIM, 2, half), axis=2).reshape(rows, lanes)
    return tensor * jnp.tile(cosine, (1, lanes // 128)) + swapped * jnp.tile(sine, (1, lanes // 128))


def slot_places(order, half_len, slot_ids):
    matches = (slot_ids // half_len)[:, None] == jnp.arange(order.shape[0], dtype=jnp.int32)[None, :]
    return jnp.sum(jnp.where(matches, order[None, :], 0), axis=1) * half_len + slot_ids % half_len


def place():
    s, r = lax.axis_index("seq"), lax.axis_index("rows")
    return lax.div(s, 2), lax.rem(s, 2), r


def send(src, dst, ssem, rsem, device):
    return pltpu.make_async_remote_copy(
        src_ref=src, dst_ref=dst, send_sem=ssem, recv_sem=rsem, device_id=device, device_id_type=MESH
    )


def greet(devices):
    barrier = pltpu.get_barrier_semaphore()
    for device in devices:
        pl.semaphore_signal(barrier, inc=1, device_id=device, device_id_type=MESH)
    pl.semaphore_wait(barrier, len(devices))


def corners(r):
    return r, r + 1 - 2 * lax.rem(r, 2), lax.rem(r + 2, 4), 3 - r


def exchange_others():
    return [(cc, j) for j in (3, 1, 2, 0) for cc in range(2) if (cc, j) != (0, 0)]


class Exchange:
    def __init__(self, own, out, ssem, rsem, l_sem):
        z, c, r = place()
        line = corners(r)
        self.own, self.out, self.ssem, self.rsem, self.here = own, out, ssem, rsem, (c, r)
        self.others = [(1 - c if cc else c, line[j]) for cc, j in exchange_others()]
        self.devices = [(z * 2 + core, row) for core, row in self.others]
        self.local = pltpu.make_async_copy(own.at[c, r], out.at[c, r], l_sem)

    def start(self):
        self.copies = []
        for i, other in enumerate(self.others):
            copy = send(self.own.at[other], self.out.at[self.here], self.ssem.at[i], self.rsem.at[i], self.devices[i])
            copy.start()
            self.copies.append(copy)
        self.local.start()

    def finish(self):
        for i, other in enumerate(self.others):
            dst = self.out.at[other]
            send(dst, dst, self.ssem.at[i], self.rsem.at[i], self.devices[i]).wait_recv()
        self.local.wait()

    def end(self):
        for copy in self.copies:
            copy.wait_send()


class Line:
    def __init__(self, zs, way, lo, hi, src, dst, sems):
        z, c, r = place()
        lo, hi = (lo, min(hi, zs - 1)) if way == 1 else (max(lo, 1), hi)
        self.sends = (z >= lo) & (z < hi)
        self.gets = (z - way >= lo) & (z - way < hi)
        to = lax.rem(z + way + zs, zs)
        self.copy = send(src, dst, sems.at[0], sems.at[1], (to * 2 + c, r))

    def start(self):
        pl.when(self.sends)(self.copy.start)

    def finish(self):
        pl.when(self.sends)(self.copy.wait_send)
        pl.when(self.gets)(self.copy.wait_recv)


LINE_SEMS = pltpu.SemaphoreType.DMA((2,))
EXCHANGE_SEMS = [pltpu.SemaphoreType.DMA((7,)), pltpu.SemaphoreType.DMA((7,)), pltpu.SemaphoreType.DMA]


def neighbours(zs, planes, moved):
    z, c, r = place()
    line = corners(r)
    s = z * 2 + c
    devices = [(z * 2 + 1 - c, r)]
    if moved:
        devices = [(z * 2 + (1 - c if cc else c), line[j]) for cc, j in exchange_others()]
    elif planes:
        devices += [(s, line[1]), (s, line[2])]
    return devices + [(lax.rem(z + k, zs) * 2 + c, r) for k in range(1, zs)]


class Gather:
    def __init__(self, zs, z_flag, planes, own, out, z_ssem, z_rsem, f_ssem, f_rsem, h_ssem, h_rsem, c_ssem, c_rsem, l_sem):
        self.__dict__.update(locals())
        self.z, self.c, self.r = place()
        self.line = corners(self.r)
        self.s = self.z * 2 + self.c
        self.twin = (self.z * 2 + 1 - self.c, self.r)
        self.count = zs if z_flag else 1
        self.half = own.shape[0] // 2
        self.pending = []

    def start(self, copy):
        copy.start()
        self.pending.append(copy.wait_send)

    def slot(self, k, other, j):
        if not self.z_flag:
            return self.out.at[other, j]
        core = 1 - self.c if other else self.c
        zz = lax.rem(self.z - k + self.zs, self.zs)
        return self.out.at[zz, core, self.line[j]] if self.planes else self.out.at[zz, core]

    def z_copy(self, k, dst):
        src = self.own if dst is None else dst
        dst = self.slot(0, 0, 0) if dst is None else dst
        to = (lax.rem(self.z + k, self.zs) * 2 + self.c, self.r)
        return send(src, dst, self.z_ssem.at[k], self.z_rsem.at[k], to)

    def near(self, k, j, src):
        dst = self.slot(k, 0, j) if src is None or not self.z_flag else self.slot(k, 0, 0)
        return send(dst if src is None else src, dst, self.f_ssem.at[k, j - 1], self.f_rsem.at[k, j - 1], (self.s, self.line[j]))

    def part(self, ref, j):
        return ref.at[pl.ds(self.half if j == 1 else 0, self.half)]

    def far(self, k, j, src):
        if src is None:
            src = dst = self.part(self.slot(k, 0, 3), j)
        else:
            dst = self.part(src if self.z_flag else self.out.at[0, 3], j)
            src = self.part(src, j)
        return send(src, dst, self.h_ssem.at[k, j - 1], self.h_rsem.at[k, j - 1], (self.s, self.line[3 - j]))

    def to_twin(self, k, j, src):
        dst = self.slot(k, 0, j) if self.z_flag else self.out.at[1, j]
        self.start(send(src, dst, self.c_ssem.at[k, j], self.c_rsem.at[k, j], self.twin))

    def launch(self):
        self.local = pltpu.make_async_copy(self.own, self.slot(0, 0, 0), self.l_sem)
        self.local.start()
        for k in range(1, self.count):
            self.start(self.z_copy(k, None))

    def begin(self, k):
        src = self.own
        if k:
            src = self.slot(k, 0, 0)
            self.z_copy(k, src).wait_recv()
        if self.planes:
            for j in (1, 2):
                self.start(self.near(k, j, src))
        self.to_twin(k, 0, src)

    def forward(self, k):
        for j in (1, 2):
            self.near(k, j, None).wait_recv()
            src = self.slot(k, 0, j)
            self.start(self.far(k, j, src))
            self.to_twin(k, j, src)

    def finish(self, k):
        for j in (1, 2):
            self.far(k, j, None).wait_recv()
        self.to_twin(k, 3, self.slot(k, 0, 3))

    def complete(self, k):
        if k == 0:
            self.local.wait()
        for j in range(4 if self.planes else 1):
            dst = self.slot(k, 1, j)
            send(dst, dst, self.c_ssem.at[k, j], self.c_rsem.at[k, j], self.twin).wait_recv()

    def end(self):
        for wait in self.pending:
            wait()


def gather_sems(zs, z_flag):
    sem = pltpu.SemaphoreType.DMA
    n = zs if z_flag else 1
    return [sem((n,)), sem((n,)), sem((n, 2)), sem((n, 2)), sem((n, 2)), sem((n, 2)), sem((n, 4)), sem((n, 4)), sem]


class Chain:
    def __init__(self, zs, own, got, sems):
        self.zs, self.own, self.got, self.sems = zs, own, got, sems
        self.lines = []

    def start(self, k):
        zs = self.zs
        up, down = (self.own, self.own) if k == 1 else (self.got[k - 2], self.got[zs + k - 3])
        self.lines = [
            Line(zs, 1, k - 1, zs, up, self.got[k - 1], self.sems.at[k - 1]),
            Line(zs, -1, 0, zs - k + 1, down, self.got[zs + k - 2], self.sems.at[zs + k - 2]),
        ]
        for line in self.lines:
            line.start()

    def finish(self):
        for line in self.lines:
            line.finish()


class Scatter:
    def __init__(self, zs, z_flag, planes, given, out, own, twin_in, half_in, full_in, z_in, l_sem, c_ssem, c_rsem, h_ssem, h_rsem,
                 f_ssem, f_rsem, z_ssem, z_rsem):
        self.__dict__.update(locals())
        self.z, self.c, self.r = place()
        self.line = corners(self.r)
        self.s = self.z * 2 + self.c
        self.twin = (self.z * 2 + 1 - self.c, self.r)
        self.rows = out.shape[0]
        self.step = 16
        self.spots = (3, 1, 2, 0) if planes else (0,)
        self.zs = zs if z_flag else 1
        self.order = list(range(1, self.zs)) + [0]
        self.pending = []

    def at_z(self, k):
        return (lax.rem(self.z + k, self.zs) * 2 + self.c, self.r)

    def block(self, k, other, j):
        if not self.z_flag:
            return self.given.at[other, j]
        zz, core = lax.rem(self.z + k, self.zs), 1 - self.c if other else self.c
        return self.given.at[zz, core, self.line[j]] if self.planes else self.given.at[zz, core]

    def start(self, copy):
        copy.start()
        self.pending.append(copy.wait_send)

    def local(self, k, j):
        return pltpu.make_async_copy(self.block(k, 0, j), self.own.at[k, j], self.l_sem.at[k, j])

    def begin(self):
        for k in self.order:
            for j in self.spots:
                block = self.block(k, 1, j)
                self.start(send(block, self.twin_in.at[k, j], self.c_ssem.at[k, j], self.c_rsem.at[k, j], self.twin))
                self.local(k, j).start()

    def settle(self, k, j):
        self.local(k, j).wait()
        send(self.own.at[k, j], self.twin_in.at[k, j], self.c_ssem.at[k, j], self.c_rsem.at[k, j], self.twin).wait_recv()

    def add(self, first, last, k, j, *more, final=False):
        step = self.step

        def body(n, carry):
            at = pl.ds(pl.multiple_of(first + n * step, step), step)
            value = self.own[k, j, at, :].astype(jnp.float32) + self.twin_in[k, j, at, :].astype(jnp.float32)
            for ref, offset in more:
                there = pl.ds(pl.multiple_of(first - offset + n * step, step), step)
                value = value + ref[there, :].astype(jnp.float32)
            if final:
                self.out[at, :] = value
            else:
                self.own[k, j, at, :] = value.astype(self.own.dtype)
            return carry

        lax.fori_loop(0, (last - first) // step, body, 0)

    def half_copy(self, k, n, src):
        dst = self.half_in.at[k, n]
        return send(dst if src is None else src, dst, self.h_ssem.at[k, n], self.h_rsem.at[k, n], (self.s, self.line[n + 1]))

    def full_copy(self, k, j, src):
        dst = self.full_in.at[k, j - 1]
        return send(dst if src is None else src, dst, self.f_ssem.at[k, j - 1], self.f_rsem.at[k, j - 1], (self.s, self.line[j]))

    def z_copy(self, k, src):
        dst = self.z_in.at[k]
        return send(dst if src is None else src, dst, self.z_ssem.at[k], self.z_rsem.at[k], self.at_z(k))

    def stage_a(self, k):
        half = self.rows // 2
        self.settle(k, 3)
        self.add(0, self.rows, k, 3)
        self.start(self.half_copy(k, 1, self.own.at[k, 3, pl.ds(half, half)]))
        self.start(self.half_copy(k, 0, self.own.at[k, 3, pl.ds(0, half)]))

    def stage_b(self, k):
        half = self.rows // 2
        for j in (1, 2):
            self.settle(k, j)
            n = 2 - j
            self.half_copy(k, n, None).wait_recv()
            more = (self.half_in.at[k, n], half if n else 0)
            self.add(0, half, k, j, *([] if n else [more]))
            self.add(half, self.rows, k, j, *([more] if n else []))
            self.start(self.full_copy(k, j, self.own.at[k, j]))

    def stage_c(self, k):
        self.settle(k, 0)
        more = []
        if self.planes:
            for j in (1, 2):
                self.full_copy(k, j, None).wait_recv()
                more.append((self.full_in.at[k, j - 1], 0))
        if k:
            self.add(0, self.rows, k, 0, *more)
            self.start(self.z_copy(k, self.own.at[k, 0]))
            return
        for k2 in range(1, self.zs):
            self.z_copy(k2, None).wait_recv()
            more.append((self.z_in.at[k2], 0))
        self.add(0, self.rows, 0, 0, *more, final=True)

    def end(self):
        for wait in self.pending:
            wait()


SCATTER_REFS = 14


def scatter_kernel(zs, flags, moves, lines, *refs):
    count, taken = len(flags), len(flags) + moves + len(lines)
    given, moved, line_own = refs[:count], refs[count : count + moves], refs[count + moves : taken]
    out, rest = refs[taken : taken + count], refs[taken + count :]
    moved_out, line_out, rest = rest[:moves], rest[moves : moves + len(lines)], rest[moves + len(lines) :]
    reach = zs if lines or any(flag[0] for flag in flags) else 1
    greet(neighbours(reach, any(flag[1] for flag in flags), moves))
    sums = [
        Scatter(zs, *flags[a], given[a], out[a], *rest[SCATTER_REFS * a : SCATTER_REFS * (a + 1)]) for a in range(count)
    ]
    rest = rest[SCATTER_REFS * count :]
    exchanges = [Exchange(moved[n], moved_out[n], *rest[3 * n : 3 * n + 3]) for n in range(moves)]
    rest = rest[3 * moves :]
    going = [Line(zs, *line, line_own[n], line_out[n], rest[n]) for n, line in enumerate(lines)]
    for one in sums:
        one.begin()
    for one in exchanges:
        one.start()
    for one in going:
        one.start()
    for one in sums:
        if not one.planes:
            for k in one.order[:-1]:
                one.stage_c(k)
    items = [(one, k) for k in list(range(1, zs)) + [0] for one in sums if one.planes and k < one.zs]
    total = len(items)
    for n in range(total + 2):
        for back, stage in enumerate((Scatter.stage_a, Scatter.stage_b, Scatter.stage_c)):
            if 0 <= n - back < total and (back < 2 or items[n - back][1]):
                stage(*items[n - back])
    for one in sums:
        one.stage_c(0)
    for one in exchanges + going:
        one.finish()
    for one in exchanges + sums:
        one.end()


def scatter(arrays, flags, zs, collective_id, moved=(), lines=()):
    sem = pltpu.SemaphoreType.DMA
    anywhere = pl.BlockSpec(memory_space=pl.ANY)
    scratch, used, shapes = [], 0, []
    all_zs = zs
    for array, (z_flag, planes) in zip(arrays, flags):
        rows, columns = array.shape[-2:]
        zs = all_zs if z_flag else 1
        spots, low = 4 if planes else 1, array.dtype
        used += rows * columns * 2 * (zs * (2 * spots + (3 if planes else 0) + 1) + 4)
        shapes.append(jax.ShapeDtypeStruct((rows, columns), jnp.float32))
        scratch += [
            pltpu.VMEM((zs, spots, rows, columns), low),
            pltpu.VMEM((zs, spots, rows, columns), low),
            pltpu.VMEM((zs, 2, rows // 2, columns) if planes else (1, 2, 16, 128), low),
            pltpu.VMEM((zs, 2, rows, columns) if planes else (1, 2, 16, 128), low),
            pltpu.VMEM((zs, rows, columns) if zs > 1 else (1, 16, 128), low),
            sem((zs, 4)), sem((zs, 4)), sem((zs, 4)), sem((zs, 2)), sem((zs, 2)), sem((zs, 2)), sem((zs, 2)),
            sem((zs,)), sem((zs,)),
        ]
    count = len(arrays)
    return pl.pallas_call(
        functools.partial(scatter_kernel, all_zs, tuple(flags), len(moved), tuple(tuple(line[1:]) for line in lines)),
        out_shape=shapes + [jax.ShapeDtypeStruct(m.shape, m.dtype) for m in (*moved, *[line[0] for line in lines])],
        in_specs=[anywhere] * (count + len(moved) + len(lines)),
        out_specs=[pl.BlockSpec(memory_space=pltpu.VMEM)] * count + [anywhere] * (len(moved) + len(lines)),
        scratch_shapes=scratch + EXCHANGE_SEMS * len(moved) + [LINE_SEMS] * len(lines),
        compiler_params=pltpu.CompilerParams(
            collective_id=collective_id, has_side_effects=True, vmem_limit_bytes=used + 6 * MIB
        ),
        cost_estimate=LONG,
    )(*arrays, *moved, *[line[0] for line in lines])


def partner(tensor):
    lanes = tensor.shape[-1]
    half = HEAD_DIM // 2
    lane = lax.broadcasted_iota(jnp.int32, tensor.shape, tensor.ndim - 1)
    ahead = pltpu.roll(tensor, lanes - half, tensor.ndim - 1)
    behind = pltpu.roll(tensor, half, tensor.ndim - 1)
    return jnp.where(lax.rem(lane, HEAD_DIM) < half, ahead, behind)


def stack_heads(block, first):
    return jnp.concatenate(
        [block[:, (first + h) * HEAD_DIM : (first + h + 1) * HEAD_DIM] for h in range(GROUP)], axis=0
    )


def unstack_heads(stacked, span):
    return jnp.concatenate([stacked[h * span : (h + 1) * span] for h in range(GROUP)], axis=1)


def load_window(inverse_ref, kv_ref, window, first_block):
    half_len = kv_ref.shape[1] // 2
    for n in range(window.shape[0] // half_len):
        slot = inverse_ref[first_block + n]
        at = pl.ds(pl.multiple_of(lax.rem(slot, 2) * half_len, half_len), half_len)
        window[n * half_len : (n + 1) * half_len, :] = kv_ref[lax.div(slot, 2), at, :]


def window_of(order_ref, first_ref, count, half_len):
    m, half = pl.program_id(0), pl.program_id(1)
    my_block = order_ref[lax.axis_index("seq") * 2 + half]
    half_blocks = count // half_len // 2
    first_block = jnp.where(my_block >= half_blocks, half_blocks, 0)
    return first_block, my_block * half_len, first_ref[m]


def attend_kernel(order_ref, inverse_ref, first_ref, lin_ref, cos_ref, sin_ref, kv_ref, q_ref, out_ref, window, bias):
    span = lin_ref.shape[0]
    wide = window.shape[0]
    first_block, my_place, first = window_of(order_ref, first_ref, 2 * wide, span)
    load_window(inverse_ref, kv_ref, window, first_block)
    key_place = first_block * span + lax.broadcasted_iota(jnp.int32, (span, wide), 1)
    place_here = my_place + lax.broadcasted_iota(jnp.int32, (span, wide), 0)
    start = jnp.where(place_here >= first, first, 0)
    bias[...] = jnp.where((key_place <= place_here) & (key_place >= start), 0.0, NEG_LARGE)
    width = GROUP * HEAD_DIM
    cosine = jnp.concatenate([cos_ref[...]] * (width // 128), axis=1)
    sine = jnp.concatenate([sin_ref[...]] * (width // 128), axis=1)
    for g in range(KV_HEADS):
        at = slice(g * width, (g + 1) * width)
        lin = lin_ref[:, at]
        query = (lin * cosine + partner(lin) * sine).astype(jnp.bfloat16) * jnp.bfloat16(HEAD_DIM ** -0.5)
        q_ref[:, at] = query
        key = window[:, g * HEAD_DIM : (g + 1) * HEAD_DIM]
        value = window[:, KVW + g * HEAD_DIM : KVW + (g + 1) * HEAD_DIM]
        scores = product_nt(stack_heads(query, 0), key).reshape(GROUP, span, wide) + bias[...][None]
        exps = jnp.exp(scores - jnp.max(scores, axis=-1, keepdims=True))
        total = jnp.sum(exps, axis=-1, keepdims=True).reshape(GROUP * span, 1)
        mixed = product(exps.astype(jnp.bfloat16).reshape(GROUP * span, wide), value) / total
        out_ref[:, at] = unstack_heads(mixed, span).astype(jnp.bfloat16)


def attend_back_kernel(order_ref, inverse_ref, first_ref, q_ref, d_ref, cos_ref, sin_ref, kv_ref, dq_ref, dkv_ref, window, bias, sums):
    span = q_ref.shape[0]
    wide = window.shape[0]
    rows = GROUP * span
    half = pl.program_id(1)
    first_block, my_place, first = window_of(order_ref, first_ref, 2 * wide, span)
    load_window(inverse_ref, kv_ref, window, first_block)
    key_place = first_block * span + lax.broadcasted_iota(jnp.int32, (wide, rows), 0)
    place_here = my_place + lax.rem(lax.broadcasted_iota(jnp.int32, (wide, rows), 1), span)
    start = jnp.where(place_here >= first, first, 0)
    bias[...] = jnp.where((key_place <= place_here) & (key_place >= start), 0.0, NEG_LARGE)

    @pl.when(half == 0)
    def _():
        sums[...] = jnp.zeros_like(sums)

    width = GROUP * HEAD_DIM
    cosine = jnp.concatenate([cos_ref[...]] * (width // 128), axis=1)
    sine = jnp.concatenate([sin_ref[...]] * (width // 128), axis=1)
    d_keys, d_values = [], []
    for g in range(KV_HEADS):
        at = slice(g * width, (g + 1) * width)
        key = window[:, g * HEAD_DIM : (g + 1) * HEAD_DIM]
        value = window[:, KVW + g * HEAD_DIM : KVW + (g + 1) * HEAD_DIM]
        query = stack_heads(q_ref[:, at], 0)
        d_mixed = stack_heads(d_ref[:, at], 0)
        scores = product_nt(key, query) + bias[...]
        exps = jnp.exp(scores - jnp.max(scores, axis=0, keepdims=True))
        probs = exps * (1.0 / jnp.sum(exps, axis=0, keepdims=True))
        d_probs = product_nt(value, d_mixed)
        weighted = probs * d_probs
        delta = jnp.sum(weighted, axis=0, keepdims=True)
        d_scores = (weighted - probs * delta).astype(jnp.bfloat16)
        d_keys.append(product(d_scores, query))
        d_values.append(product(probs.astype(jnp.bfloat16), d_mixed))
        d_query = unstack_heads(product_tn(d_scores, key) * HEAD_DIM ** -0.5, span)
        dq_ref[:, at] = (d_query * cosine - partner(d_query) * sine).astype(jnp.bfloat16)
    d_window = jnp.concatenate(d_keys + d_values, axis=1)
    for n in range(wide // span):
        slot = inverse_ref[first_block + n]
        to = pl.ds(pl.multiple_of(lax.rem(slot, 2) * span, span), span)
        sums[lax.div(slot, 2), to, :] += d_window[n * span : (n + 1) * span]

    @pl.when(half == 1)
    def _():
        dkv_ref[...] = sums[...].astype(jnp.bfloat16)


def attention_specs(seq, micro, span):
    half_len = span // 2

    def rows(width):
        return pl.BlockSpec((half_len, width), lambda m, h, *_: (m * 2 + h, 0))

    whole = pl.BlockSpec((seq, span, 2 * KVW), lambda m, h, *_: (0, m, 0))
    return half_len, rows, whole


def attend(order, inverse, first, lin, cosine, sine, kv):
    seq, many, _ = kv.shape
    micro = first.shape[0]
    span = many // micro
    half_len, rows, whole = attention_specs(seq, micro, span)
    wide = seq * span // 2
    return pl.pallas_call(
        attend_kernel,
        grid_spec=pltpu.PrefetchScalarGridSpec(
            num_scalar_prefetch=3,
            grid=(micro, 2),
            in_specs=[rows(D), rows(128), rows(128), whole],
            out_specs=[rows(D), rows(D)],
            scratch_shapes=[pltpu.VMEM((wide, 2 * KVW), jnp.bfloat16), pltpu.VMEM((half_len, wide), jnp.float32)],
        ),
        out_shape=[jax.ShapeDtypeStruct((many, D), jnp.bfloat16)] * 2,
        compiler_params=pltpu.CompilerParams(vmem_limit_bytes=48 * MIB),
        cost_estimate=pl.CostEstimate(flops=8 * many * wide * D, bytes_accessed=16 * MIB, transcendentals=many * wide * HEADS),
    )(order, inverse, first, lin, cosine, sine, kv)


def attend_back(order, inverse, first, queries, d_heads, cosine, sine, kv):
    seq, many, _ = kv.shape
    micro = first.shape[0]
    span = many // micro
    half_len, rows, whole = attention_specs(seq, micro, span)
    wide = seq * span // 2
    return pl.pallas_call(
        attend_back_kernel,
        grid_spec=pltpu.PrefetchScalarGridSpec(
            num_scalar_prefetch=3,
            grid=(micro, 2),
            in_specs=[rows(D), rows(D), rows(128), rows(128), whole],
            out_specs=[rows(D), whole],
            scratch_shapes=[
                pltpu.VMEM((wide, 2 * KVW), jnp.bfloat16),
                pltpu.VMEM((wide, GROUP * half_len), jnp.float32),
                pltpu.VMEM((seq, span, 2 * KVW), jnp.float32),
            ],
        ),
        out_shape=[jax.ShapeDtypeStruct((many, D), jnp.bfloat16), jax.ShapeDtypeStruct(kv.shape, jnp.bfloat16)],
        compiler_params=pltpu.CompilerParams(vmem_limit_bytes=56 * MIB),
        cost_estimate=pl.CostEstimate(flops=20 * many * wide * D, bytes_accessed=24 * MIB, transcendentals=many * wide * HEADS),
    )(order, inverse, first, queries, d_heads, cosine, sine, kv)


def assemble(zs, pieces, whole, sem):
    if len(pieces) == 1:
        copy = pltpu.make_async_copy(pieces[0], whole, sem.at[0])
        copy.start()
        return [copy]
    z = lax.div(lax.axis_index("seq"), 2)
    size = whole.shape[0] // zs

    def rows(zz):
        return whole.at[pl.ds(pl.multiple_of(zz * size, size), size)]

    copies = [pltpu.make_async_copy(pieces[0], rows(z), sem.at[0])]
    copies[0].start()
    for k in range(1, zs):
        below = pltpu.make_async_copy(pieces[k], rows(lax.rem(z - k + zs, zs)), sem.at[k])
        above = pltpu.make_async_copy(pieces[2 * zs - 1 - k], rows(lax.rem(z - k + zs, zs)), sem.at[k])
        pl.when(z >= k)(below.start)
        pl.when(z < k)(above.start)
        copies.append(below)
    return copies


def ffn_kernel(zs, count, *refs):
    x_ref, dy_ref = refs[:2]
    both_pieces, down_pieces = refs[2 : 2 + count], refs[2 + count : 2 + 2 * count]
    out_ref, dx_ref, g_both_ref, g_down_ref, both_w, down_w, both_sum, down_sum, sem = refs[2 + 2 * count :]
    n = down_w.shape[0]
    step, last = pl.program_id(0), pl.num_programs(0) - 1

    @pl.when(step == 0)
    def _():
        copies = assemble(zs, both_pieces, both_w, sem.at[0]) + assemble(zs, down_pieces, down_w, sem.at[1])
        both_sum[...] = jnp.zeros_like(both_sum)
        down_sum[...] = jnp.zeros_like(down_sum)
        for copy in copies:
            copy.wait()

    x, dy = x_ref[...], dy_ref[...]
    lin = product(x, both_w[...])
    gate, upper = lin[:, :n], lin[:, n:]
    sig = 1.0 / (1.0 + jnp.exp(-gate))
    act = gate * sig
    hidden = (act * upper).astype(jnp.bfloat16)
    d_hidden = product_nt(dy, down_w[...])
    d_gate = d_hidden * upper * (sig * (1.0 + gate * (1.0 - sig)))
    d_both = jnp.concatenate([d_gate.astype(jnp.bfloat16), (d_hidden * act).astype(jnp.bfloat16)], axis=1)
    dx_ref[...] = product_nt(d_both, both_w[...]).astype(jnp.bfloat16)
    out_ref[...] = product(hidden, down_w[...]).astype(jnp.bfloat16)
    for at in range(0, D, 256):
        both_sum[at : at + 256, :] += product_tn(x[:, at : at + 256], d_both)
    part = n // 4
    for at in range(0, n, part):
        down_sum[at : at + part, :] += product_tn(hidden[:, at : at + part], dy)

    @pl.when(step == last)
    def _():
        both_w[...] = both_sum[...].astype(jnp.bfloat16)
        down_w[...] = down_sum[...].astype(jnp.bfloat16)
        copies = [
            pltpu.make_async_copy(both_w, g_both_ref, sem.at[0, 0]),
            pltpu.make_async_copy(down_w, g_down_ref, sem.at[1, 0]),
        ]
        for copy in copies:
            copy.start()
        for copy in copies:
            copy.wait()


def feed_forward(x, dy, both_pieces, down_pieces, zs):
    count = x.shape[0]
    spread_over = zs if len(both_pieces) > 1 else 1
    n = down_pieces[0].shape[0] * spread_over
    block = 256
    low = jnp.bfloat16
    tokens = pl.BlockSpec((block, D), lambda i: (i, 0))
    anywhere = pl.BlockSpec(memory_space=pl.ANY)
    return pl.pallas_call(
        functools.partial(ffn_kernel, zs, len(both_pieces)),
        grid=(count // block,),
        in_specs=[tokens, tokens] + [anywhere] * (2 * len(both_pieces)),
        out_specs=[tokens, tokens, anywhere, anywhere],
        out_shape=[jax.ShapeDtypeStruct(x.shape, low)] * 2
        + [jax.ShapeDtypeStruct((D, 2 * n), low), jax.ShapeDtypeStruct((n, D), low)],
        scratch_shapes=[
            pltpu.VMEM((D, 2 * n), low),
            pltpu.VMEM((n, D), low),
            pltpu.VMEM((D, 2 * n), jnp.float32),
            pltpu.VMEM((n, D), jnp.float32),
            pltpu.SemaphoreType.DMA((2, zs)),
        ],
        compiler_params=pltpu.CompilerParams(vmem_limit_bytes=60 * MIB),
        cost_estimate=pl.CostEstimate(flops=18 * count * D * n, bytes_accessed=60 * MIB, transcendentals=count * n),
    )(x, dy, *both_pieces, *down_pieces)


def spread_kernel(zs, rows, unit, gate_ref, up_ref, out):
    for c in range(2):
        for r in range(rows):
            for n, weight in enumerate((gate_ref, up_ref)):
                for z in range(zs):
                    at = ((z * 2 + c) * rows + r) * unit
                    to = (n * zs + z) * unit
                    out[c, r, :, to : to + unit] = weight[:, at : at + unit]


def spread(gate, up, zs, rows):
    wide, part = gate.shape
    unit = part // (zs * 2 * rows)
    return pl.pallas_call(
        functools.partial(spread_kernel, zs, rows, unit),
        out_shape=jax.ShapeDtypeStruct((2, rows, wide, 2 * zs * unit), gate.dtype),
    )(gate, up)


def collect_kernel(zs, rows, unit, given, *outs):
    for n, out in enumerate(outs):
        for c in range(2):
            for r in range(rows):
                for z in range(zs):
                    at = ((z * 2 + c) * rows + r) * unit
                    to = (n * zs + z) * unit
                    out[:, at : at + unit] = given[c, r, :, to : to + unit].astype(jnp.float32)


def collect(blocks, zs, rows, unit):
    shape = jax.ShapeDtypeStruct((blocks.shape[2], unit * zs * 2 * rows), jnp.float32)
    return pl.pallas_call(functools.partial(collect_kernel, zs, rows, unit), out_shape=[shape, shape])(blocks)


def forward_kernel(zs, micro, *refs):
    order_ref, places_ref, first_ref, freq_ref, x_ref, pack_ref, both_ref, down_ref, out_ref, dy_ref = refs[:10]
    packed, both_own, kv_all, out_all, dy_all, ffn_all = refs[10:16]
    steps = 2 * zs - 2
    both_got, down_got = refs[16 : 16 + steps], refs[16 + steps : 16 + 2 * steps]
    q_ref, attn_ref, attended_ref, middle_ref, gains_ref, cos_ref, sin_ref = refs[16 + 2 * steps : 23 + 2 * steps]
    (staged, lin, kv_own, kv_here, window, bias, out_w, ffn_own, sems, *more) = refs[23 + 2 * steps :]
    low = jnp.bfloat16
    z, c, r = place()
    many = x_ref.shape[0]
    span = many // micro
    half_len = span // 2
    rows = D // zs
    greet(neighbours(zs, True, True))

    exchange = Exchange(both_ref, both_own, *more[:3])
    both_chain, down_chain = Chain(zs, both_own, both_got, more[3]), Chain(zs, down_ref, down_got, more[4])
    more = more[5:]
    weights = Gather(zs, True, True, pack_ref, packed, *more[:9])
    outs = Gather(zs, True, True, out_ref, out_all, *more[9:18])
    pairs = Gather(zs, True, False, kv_own, kv_all, *more[18:27])
    dys = Gather(zs, False, True, dy_ref, dy_all, *more[27:36])
    ffns = Gather(zs, False, True, ffn_own, ffn_all, *more[36:45])

    weights.launch()
    exchange.start()
    weights.begin(0)
    outs.launch()

    lane = lax.broadcasted_iota(jnp.int32, (half_len, 128), 1)
    for i in range(2 * micro):
        place_here = order_ref[(z * 2 + c) * 2 + i % 2] * half_len + lax.broadcasted_iota(jnp.int32, (half_len, 128), 0)
        start = jnp.where(place_here >= first_ref[i // 2], first_ref[i // 2], 0)
        angle = (place_here - start).astype(jnp.float32) * freq_ref[...]
        cos_ref[i * half_len : (i + 1) * half_len, :] = jnp.cos(angle)
        sine = jnp.sin(angle)
        sin_ref[i * half_len : (i + 1) * half_len, :] = jnp.where(lax.rem(lane, HEAD_DIM) < HEAD_DIM // 2, -sine, sine)
    x = x_ref[...].astype(jnp.float32)
    factor = rms_factor(x)

    loads = {}

    def load(k):
        weights.complete(k)
        zz = lax.rem(z - k + zs, zs)
        loads[k] = pltpu.make_async_copy(packed.at[zz], staged.at[k % 2], sems.at[k % 2])
        loads[k].start()

    def project(k):
        loads[k].wait()
        zz = lax.rem(z - k + zs, zs)
        at = pl.ds(pl.multiple_of(zz * rows, rows), rows)
        block = staged[k % 2].reshape(rows, PACK)
        gains = block[:, QKV:].astype(jnp.float32).T[:8]
        gains_ref[:, at] = gains
        attn_in = (x_ref[:, at].astype(jnp.float32) * factor * gains[0:1]).astype(low)
        attn_ref[:, at] = attn_in
        value = product(attn_in, block[:, :QKV])
        lin[...] = value if k == 0 else lin[...] + value

    weights.begin(1)
    weights.forward(0)
    weights.begin(2)
    weights.forward(1)
    weights.finish(0)
    weights.begin(3)
    down_chain.start(1)
    exchange.finish()
    both_chain.start(1)
    weights.forward(2)
    weights.finish(1)
    load(0)
    weights.forward(3)
    weights.finish(2)
    outs.begin(0)
    load(1)
    project(0)
    outs.begin(1)
    project(1)
    weights.finish(3)
    dys.launch()
    dys.begin(0)
    load(2)
    load(3)
    project(2)
    project(3)

    width = GROUP * HEAD_DIM
    cosine = jnp.concatenate([cos_ref[...]] * (width // 128), axis=1)
    sine = jnp.concatenate([sin_ref[...]] * (width // 128), axis=1)

    def turned(block, w):
        return block * cosine[:, :w] + partner(block) * sine[:, :w]

    kv_own[:, :KVW] = turned(lin[:, D : D + KVW], KVW).astype(low)
    kv_own[:, KVW:] = lin[:, D + KVW :].astype(low)
    pairs.launch()
    pairs.begin(0)
    for g in range(KV_HEADS):
        at = slice(g * width, (g + 1) * width)
        q_ref[:, at] = turned(lin[:, at], width).astype(low) * low(HEAD_DIM ** -0.5)
    outs.forward(0)
    outs.begin(2)
    for k in range(1, zs):
        pairs.begin(k)
    outs.forward(1)
    outs.finish(0)
    outs.begin(3)
    for k in range(zs):
        pairs.complete(k)
    both_chain.finish()
    down_chain.finish()
    both_chain.start(2)
    down_chain.start(2)
    kv_load = pltpu.make_async_copy(kv_all, kv_here, sems.at[2])
    kv_load.start()
    outs.forward(2)
    outs.finish(1)
    kv_load.wait()

    wide = window.shape[0]
    half_blocks = wide // half_len

    def attend_some(i, carry):
        m, half = lax.div(i, 2), lax.rem(i, 2)
        my_block = order_ref[(z * 2 + c) * 2 + half]
        first_block = jnp.where(my_block >= half_blocks, half_blocks, 0)
        wanted = first_block * half_len + lax.broadcasted_iota(jnp.int32, (wide, 2 * wide), 0)
        chosen = jnp.where(places_ref[...] == wanted, 1.0, 0.0).astype(low)
        at = pl.ds(pl.multiple_of(m * span, span), span)
        window[...] = product(chosen, kv_here[:, :, at, :].reshape(2 * wide, 2 * KVW)).astype(low)
        key_place = first_block * half_len + lax.broadcasted_iota(jnp.int32, (half_len, wide), 1)
        place_here = my_block * half_len + lax.broadcasted_iota(jnp.int32, (half_len, wide), 0)
        first = first_ref[m]
        start = jnp.where(place_here >= first, first, 0)
        bias[...] = jnp.where((key_place <= place_here) & (key_place >= start), 0.0, NEG_LARGE)
        here = pl.ds(pl.multiple_of(i * half_len, half_len), half_len)
        for g in range(KV_HEADS):
            at = slice(g * width, (g + 1) * width)
            key = window[:, g * HEAD_DIM : (g + 1) * HEAD_DIM]
            value = window[:, KVW + g * HEAD_DIM : KVW + (g + 1) * HEAD_DIM]
            scores = product_nt(stack_heads(q_ref[here, at], 0), key).reshape(GROUP, half_len, wide) + bias[...][None]
            exps = jnp.exp(scores - jnp.max(scores, axis=-1, keepdims=True))
            total = jnp.sum(exps, axis=-1, keepdims=True).reshape(GROUP * half_len, 1)
            mixed = product(exps.astype(low).reshape(GROUP * half_len, wide), value) / total
            attended_ref[here, at] = unstack_heads(mixed, half_len).astype(low)
        return carry

    lax.fori_loop(0, 2 * micro, attend_some, 0)
    outs.forward(3)
    outs.finish(2)
    outs.finish(3)
    dys.forward(0)
    for k in range(zs):
        outs.complete(k)
    out_load = pltpu.make_async_copy(out_all, out_w, sems.at[3])
    out_load.start()
    dys.finish(0)
    out_load.wait()
    middle = x_ref[...].astype(jnp.float32) + product(attended_ref[...], out_w[...].reshape(D, D))
    middle_ref[...] = middle
    ffn_own[...] = (middle * rms_factor(middle) * gains_ref[1:2, :]).astype(low)
    ffns.launch()
    ffns.begin(0)
    dys.complete(0)
    ffns.forward(0)
    both_chain.finish()
    down_chain.finish()
    both_chain.start(3)
    down_chain.start(3)
    ffns.finish(0)
    ffns.complete(0)
    both_chain.finish()
    down_chain.finish()
    exchange.end()
    for one in (weights, outs, pairs, dys, ffns):
        one.end()


def forward(order, first, tokens, pack, both, down, w_out, dy, zs, collective_id):
    many = tokens.shape[0]
    micro = first.shape[0]
    seq = 2 * zs
    wide = seq * (many // micro) // 2
    low, full = jnp.bfloat16, jnp.float32
    places = (order[:, None] * (many // micro // 2) + jnp.arange(many // micro // 2, dtype=jnp.int32)).reshape(1, 2 * wide)
    freq = 10000.0 ** (-(jnp.arange(128, dtype=jnp.int32) % (HEAD_DIM // 2)).astype(full) / (HEAD_DIM // 2))
    anywhere, here, smem = (pl.BlockSpec(memory_space=m) for m in (pl.ANY, pltpu.VMEM, pltpu.SMEM))
    shape = jax.ShapeDtypeStruct
    out_any = [
        shape((zs, 2, 4) + pack.shape, low),
        shape(both.shape, low),
        shape((zs, 2, many, 2 * KVW), low),
        shape((zs, 2, 4) + w_out.shape, low),
        shape((2, 4) + dy.shape, low),
        shape((2, 4, many, D), low),
    ] + [shape(both.shape, low)] * (2 * zs - 2) + [shape(down.shape, low)] * (2 * zs - 2)
    out_here = [shape((many, D), t) for t in (low, low, low, full)] + [shape((8, D), full)] + [shape((many, 128), full)] * 2
    sem = pltpu.SemaphoreType.DMA
    found = pl.pallas_call(
        functools.partial(forward_kernel, zs, micro),
        out_shape=out_any + out_here,
        in_specs=[smem, here, smem] + [here] * 2 + [anywhere] * 5,
        out_specs=[anywhere] * len(out_any) + [here] * len(out_here),
        scratch_shapes=[
            pltpu.VMEM((2, 2, 4) + pack.shape, low),
            pltpu.VMEM((many, QKV), full),
            pltpu.VMEM((many, 2 * KVW), low),
            pltpu.VMEM((zs, 2, many, 2 * KVW), low),
            pltpu.VMEM((wide, 2 * KVW), low),
            pltpu.VMEM((many // micro // 2, wide), full),
            pltpu.VMEM((zs, 2, 4) + w_out.shape, low),
            pltpu.VMEM((many, D), low),
            sem((4,)),
        ] + EXCHANGE_SEMS + [sem((2 * zs - 2, 2))] * 2 + gather_sems(zs, True) * 3 + gather_sems(zs, False) * 2,
        compiler_params=pltpu.CompilerParams(
            collective_id=collective_id, has_side_effects=True, vmem_limit_bytes=56 * MIB
        ),
        cost_estimate=LONG,
    )(order, places, first, freq.reshape(1, 128), tokens, pack, both, down, w_out, dy)
    return found


class Links:
    def __init__(self, seq, rows):
        self.zs, self.rows = seq // 2, rows
        self.kernels = rows == 4 and self.zs == 4
        self.z_groups = [[2 * z + c for z in range(self.zs)] for c in range(2)]
        self.core_groups = [[2 * z, 2 * z + 1] for z in range(self.zs)]

    def gather_z(self, block):
        return lax.all_gather(block, "seq", axis=0, tiled=True, axis_index_groups=self.z_groups)

    def scatter_z(self, blocks):
        return lax.psum_scatter(blocks, "seq", scatter_dimension=0, tiled=True, axis_index_groups=self.z_groups)

    def exchange_xla(self, blocks):
        moved = lax.all_to_all(blocks, "rows", split_axis=1, concat_axis=1, tiled=True)
        return lax.all_to_all(moved, "seq", split_axis=0, concat_axis=0, tiled=True, axis_index_groups=self.core_groups)

    def along(self, way, lo, hi):
        return [(2 * z + c, 2 * (z + way) + c) for z in range(lo, hi) for c in range(2) if 0 <= z + way < self.zs]

    def permute(self, lines):
        return [lax.ppermute(array, "seq", self.along(way, lo, hi)) for array, way, lo, hi in lines]

    def part(self, blocks, to, held):
        z = lax.div(lax.axis_index("seq"), 2)
        found = lax.dynamic_index_in_dim(blocks, lax.rem(z + to + self.zs, self.zs), 0, keepdims=False)
        for other, there in held:
            found = found.astype(jnp.float32) + jnp.where(there, other.astype(jnp.float32), 0.0)
        return found

    def scatter_lines(self, k, blocks, held=None):
        up, down = self.held(held)
        low = blocks.dtype
        return [
            (self.part(blocks, -k, up).astype(low), 1, 0, k),
            (self.part(blocks, k, down).astype(low), -1, self.zs - k, self.zs),
        ]

    def scatter_end(self, blocks, held):
        up, down = self.held(held)
        return self.part(blocks, 0, up + down)

    def held(self, held):
        z = lax.div(lax.axis_index("seq"), 2)
        return ([(held[0], z > 0)], [(held[1], z < self.zs - 1)]) if held else ([], [])

    @staticmethod
    def tie(arrays, *others):
        if not others:
            return arrays
        return lax.optimization_barrier((*arrays, *others))[: len(arrays)]

    def gather(self, array, z_flag, planes):
        if planes:
            array = lax.all_gather(array, "rows", axis=0)
        array = lax.all_gather(array, "seq", axis=0, axis_index_groups=self.core_groups)
        return self.gather_z(array[None]) if z_flag else array

    def scatter(self, arrays, flags, collective_id, moved=(), lines=()):
        if self.kernels:
            return scatter(arrays, flags, self.zs, collective_id, moved, lines)
        return (
            [
                self.scatter_one(self.scatter_z(blocks)[0] if z_flag else blocks, planes)
                for blocks, (z_flag, planes) in zip(arrays, flags)
            ]
            + [self.exchange_xla(blocks) for blocks in moved]
            + [line[0] for line in lines]
        )

    def scatter_one(self, blocks, planes):
        blocks = lax.psum_scatter(blocks, "seq", scatter_dimension=0, tiled=True, axis_index_groups=self.core_groups)[0]
        if planes:
            blocks = lax.psum_scatter(blocks, "rows", scatter_dimension=0, tiled=True)[0]
        return blocks.astype(jnp.float32)


def on_device(seq, rows, tokens, w_query, w_key, w_value, w_out, w_gate, w_up, w_down, gain_attn, gain_ffn, lengths, order, cotangent):
    links = Links(seq, rows)
    zs = links.zs
    micro, _, span, _ = tokens.shape
    half_len = span // 2
    many = micro * span
    low = jnp.bfloat16
    wide = w_gate.shape[0]
    unit = w_down.shape[0]

    both = spread(w_gate, w_up, zs, rows)
    flat = (2 * rows * wide, 2 * zs * unit)
    gains = jnp.pad(jnp.stack([gain_attn, gain_ffn], axis=1), ((0, 0), (0, 126)))
    pack = jnp.concatenate([w_query, w_key, w_value, gains], axis=1)
    dy_own = cotangent.reshape(many, D)
    own_tokens = tokens.reshape(many, D)
    x = own_tokens.astype(jnp.float32)
    factor_one = rms_factor(x)
    first = lengths[:, 0, 0]
    slot_of = jnp.argmax(order[None, :] == jnp.arange(order.shape[0], dtype=jnp.int32)[:, None], axis=1).astype(jnp.int32)
    chained = links.kernels
    if chained:
        found = forward(order, first, own_tokens, pack, both, w_down, w_out, dy_own, zs, 0)
        packed, both_own, kv, out_w, dy, ffn_in = found[:6]
        both_w = [b.reshape(flat) for b in (both_own, *found[6 : 4 + 2 * zs])]
        down_w = [w_down, *found[4 + 2 * zs : 2 + 4 * zs]]
        queries, attn_in, attended, middle, gains, cosine, sine = found[2 + 4 * zs :]
        packed = packed.reshape(D, PACK)
        gain_one, gain_two = gains[0], gains[1]
    else:
        both_w = [links.gather_z(links.exchange_xla(both).reshape(flat))]
        down_w = [links.gather_z(w_down)]
        packed, dy = links.gather(pack, True, True).reshape(D, PACK), links.gather(dy_own, False, True)
        gain_one, gain_two = packed[:, QKV].astype(jnp.float32), packed[:, QKV + 1].astype(jnp.float32)
        mine = slot_places(order, half_len, lax.axis_index("seq") * span + jnp.arange(span, dtype=jnp.int32))
        start = jnp.where(mine[None, :] >= first[:, None], first[:, None], 0)
        inverse = 10000.0 ** (-jnp.arange(HEAD_DIM // 2, dtype=jnp.float32) / (HEAD_DIM // 2))
        angles = ((mine[None, :] - start).astype(jnp.float32)[..., None] * inverse).reshape(many, HEAD_DIM // 2)
        cosine, sine = jnp.cos(angles), jnp.sin(angles)
        cosine, sine = jnp.tile(cosine, (1, 4)), jnp.tile(jnp.concatenate([-sine, sine], axis=1), (1, 2))
        attn_in = (x * factor_one * gain_one).astype(low)
        lin = product(attn_in, packed)
        kv_own = jnp.concatenate([turn(lin[:, D : D + KVW], cosine, sine), lin[:, D + KVW : QKV]], axis=1).astype(low)
        kv, out_w = links.gather(kv_own, True, False), links.gather(w_out, True, True)
        queries, attended = attend(order, slot_of, first, lin, cosine, sine, kv.reshape(seq, many, 2 * KVW))
        middle = x + product(attended, out_w.reshape(D, D))
        ffn_in = links.gather((middle * rms_factor(middle) * gain_two).astype(low), False, True)
    kv = kv.reshape(seq, many, 2 * KVW)
    out_w = out_w.reshape(D, D)
    dy = dy.reshape(2 * rows * many, D)
    factor_two = rms_factor(middle)
    normed_two = middle * factor_two

    ffn_in = ffn_in.reshape(2 * rows * many, D)
    result_part, d_ffn_part, grad_both, grad_down = feed_forward(ffn_in, dy, both_w, down_w, zs)
    grad_both = grad_both.reshape(zs, *flat)
    grad_down = grad_down.reshape(zs, unit, D)
    lines = []
    if chained:
        lines = links.scatter_lines(1, grad_both) + links.scatter_lines(1, grad_down)
    d_ffn_in, *got = links.scatter([d_ffn_part.reshape(2, rows, many, D)], [(False, True)], 3, (), lines)
    if chained:
        lines = links.scatter_lines(2, grad_both, got[:2]) + links.scatter_lines(2, grad_down, got[2:])
        got = links.permute(lines)

    d_part, grad_gain_two = norm_back(d_ffn_in, normed_two, factor_two, gain_two)
    d_middle = dy_own.astype(jnp.float32) + d_part
    d_mid_low = d_middle.astype(low)
    grad_out = product_tn(attended, d_mid_low).astype(low)
    d_heads = product_nt(d_mid_low, out_w).astype(low)
    d_query, d_kv = attend_back(order, slot_of, first, queries, d_heads, cosine, sine, kv)
    shards = (zs, 2, rows, wide)
    lines = []
    if chained:
        d_query, d_kv, *got = lax.optimization_barrier((d_query, d_kv, *got))
        lines = links.scatter_lines(3, grad_both, got[:2])
        down_lines = links.scatter_lines(3, grad_down, got[2:])
    grad_query = product_tn(attn_in, d_query).astype(low)
    d_kv, grad_out, grad_query, result_sum, *got = links.scatter(
        [
            d_kv.reshape(zs, 2, many, 2 * KVW),
            grad_out.reshape(*shards, D),
            grad_query.reshape(*shards, D),
            result_part.reshape(2, rows, many, D),
        ],
        [(True, False), (True, True), (True, True), (False, True)],
        4,
        (),
        lines,
    )
    if chained:
        grad_both = links.scatter_end(grad_both, got).astype(low)
    else:
        grad_both, grad_down = links.scatter_z(grad_both)[0], links.scatter_z(grad_down)[0]
        down_lines = []
    result = (middle + result_sum).astype(low)
    d_key = turn(d_kv[:, :KVW], cosine, -sine)
    d_kv = jnp.concatenate([d_key.astype(low), d_kv[:, KVW:].astype(low)], axis=1)
    d_attn_in = product_nt(d_query, packed[:, :D]) + product_nt(d_kv, packed[:, D:QKV])
    d_x, grad_gain_one = norm_back(d_attn_in, x * factor_one, factor_one, gain_one)
    x_grad = (d_middle + d_x).astype(low)
    gains_grad = jnp.pad(jnp.stack([grad_gain_one, grad_gain_two], axis=1), ((0, 0), (0, 126)))
    pack_grad = jnp.concatenate([product_tn(attn_in, d_kv), gains_grad], axis=1).astype(low)
    pack_grad, grad_both, *got = links.scatter(
        [pack_grad.reshape(*shards, 2 * KVW + 128)],
        [(True, True)],
        5,
        [grad_both.reshape(2, rows, wide, 2 * zs * unit)],
        down_lines,
    )
    if chained:
        grad_down = links.scatter_end(grad_down, got)
    grad_down = grad_down.astype(jnp.float32)
    grad_gate, grad_up = collect(grad_both, zs, rows, unit)

    return (
        result.reshape(tokens.shape),
        x_grad.reshape(tokens.shape),
        grad_query,
        pack_grad[:, :KVW],
        pack_grad[:, KVW : 2 * KVW],
        grad_out,
        grad_gate,
        grad_up,
        grad_down,
        pack_grad[:, 2 * KVW],
        pack_grad[:, 2 * KVW + 1],
    )


def solution(mesh):
    both = ("seq", "rows")
    row = P(None, "rows", "seq", None)
    weight, gain = P(both, None), P(both)
    return jax.shard_map(
        functools.partial(on_device, mesh.shape["seq"], mesh.shape["rows"]),
        mesh=mesh,
        in_specs=(row,) + (weight,) * 7 + (gain, gain, P(None, "rows", None), P(), row),
        out_specs=(row, row) + (weight,) * 7 + (gain, gain),
        check_vma=False,
    )
```

```python
import functools

import jax
import jax.numpy as jnp
from jax import lax
from jax.experimental import pallas as pl
from jax.experimental.pallas import tpu as pltpu
from jax.sharding import PartitionSpec as P

D = 2048
HEADS = 32
KV_HEADS = 4
HEAD_DIM = 64
GROUP = 8
KVW = 256
QKV = D + 2 * KVW
PACK = QKV + 128

EPSILON = 1e-05
NEG_LARGE = -1e30
MESH = pl.DeviceIdType.MESH
MIB = 1 << 20
LONG = pl.CostEstimate(flops=50_000_000_000, bytes_accessed=150 * MIB, transcendentals=0)


def product(left, right):
    return jnp.dot(left, right, preferred_element_type=jnp.float32)


def product_nt(left, right):
    return lax.dot_general(left, right, (((1,), (1,)), ((), ())), preferred_element_type=jnp.float32)


def product_tn(left, right):
    return lax.dot_general(left, right, (((0,), (0,)), ((), ())), preferred_element_type=jnp.float32)


def rms_factor(values):
    return lax.rsqrt(jnp.mean(values * values, axis=-1, keepdims=True) + EPSILON)


def norm_back(d_scaled, normed, factor, gain):
    inner = d_scaled * gain
    mean = jnp.mean(inner * normed, axis=-1, keepdims=True)
    return factor * (inner - normed * mean), jnp.sum(d_scaled * normed, axis=0)


def turn(tensor, cosine, sine):
    rows, lanes = tensor.shape
    half = HEAD_DIM // 2
    swapped = jnp.flip(tensor.reshape(rows, lanes // HEAD_DIM, 2, half), axis=2).reshape(rows, lanes)
    return tensor * jnp.tile(cosine, (1, lanes // 128)) + swapped * jnp.tile(sine, (1, lanes // 128))


def slot_places(order, half_len, slot_ids):
    matches = (slot_ids // half_len)[:, None] == jnp.arange(order.shape[0], dtype=jnp.int32)[None, :]
    return jnp.sum(jnp.where(matches, order[None, :], 0), axis=1) * half_len + slot_ids % half_len


def place():
    s, r = lax.axis_index("seq"), lax.axis_index("rows")
    return lax.div(s, 2), lax.rem(s, 2), r


def send(src, dst, ssem, rsem, device):
    return pltpu.make_async_remote_copy(
        src_ref=src, dst_ref=dst, send_sem=ssem, recv_sem=rsem, device_id=device, device_id_type=MESH
    )


def greet(devices):
    barrier = pltpu.get_barrier_semaphore()
    for device in devices:
        pl.semaphore_signal(barrier, inc=1, device_id=device, device_id_type=MESH)
    pl.semaphore_wait(barrier, len(devices))


def corners(r):
    return r, r + 1 - 2 * lax.rem(r, 2), lax.rem(r + 2, 4), 3 - r


def exchange_others():
    return [(cc, j) for j in (3, 1, 2, 0) for cc in range(2) if (cc, j) != (0, 0)]


class Exchange:
    def __init__(self, own, out, ssem, rsem, l_sem):
        z, c, r = place()
        line = corners(r)
        self.own, self.out, self.ssem, self.rsem, self.here = own, out, ssem, rsem, (c, r)
        self.others = [(1 - c if cc else c, line[j]) for cc, j in exchange_others()]
        self.devices = [(z * 2 + core, row) for core, row in self.others]
        self.local = pltpu.make_async_copy(own.at[c, r], out.at[c, r], l_sem)

    def start(self):
        self.copies = []
        for i, other in enumerate(self.others):
            copy = send(self.own.at[other], self.out.at[self.here], self.ssem.at[i], self.rsem.at[i], self.devices[i])
            copy.start()
            self.copies.append(copy)
        self.local.start()

    def finish(self):
        for i, other in enumerate(self.others):
            dst = self.out.at[other]
            send(dst, dst, self.ssem.at[i], self.rsem.at[i], self.devices[i]).wait_recv()
        self.local.wait()

    def end(self):
        for copy in self.copies:
            copy.wait_send()


class Line:
    def __init__(self, zs, way, lo, hi, src, dst, sems):
        z, c, r = place()
        lo, hi = (lo, min(hi, zs - 1)) if way == 1 else (max(lo, 1), hi)
        self.sends = (z >= lo) & (z < hi)
        self.gets = (z - way >= lo) & (z - way < hi)
        to = lax.rem(z + way + zs, zs)
        self.copy = send(src, dst, sems.at[0], sems.at[1], (to * 2 + c, r))

    def start(self):
        pl.when(self.sends)(self.copy.start)

    def finish(self):
        pl.when(self.sends)(self.copy.wait_send)
        pl.when(self.gets)(self.copy.wait_recv)


LINE_SEMS = pltpu.SemaphoreType.DMA((2,))
EXCHANGE_SEMS = [pltpu.SemaphoreType.DMA((7,)), pltpu.SemaphoreType.DMA((7,)), pltpu.SemaphoreType.DMA]


def neighbours(zs, planes, moved):
    z, c, r = place()
    line = corners(r)
    s = z * 2 + c
    devices = [(z * 2 + 1 - c, r)]
    if moved:
        devices = [(z * 2 + (1 - c if cc else c), line[j]) for cc, j in exchange_others()]
    elif planes:
        devices += [(s, line[1]), (s, line[2])]
    return devices + [(lax.rem(z + k, zs) * 2 + c, r) for k in range(1, zs)]


class Gather:
    def __init__(self, zs, z_flag, planes, own, out, z_ssem, z_rsem, f_ssem, f_rsem, h_ssem, h_rsem, c_ssem, c_rsem, l_sem):
        self.__dict__.update(locals())
        self.z, self.c, self.r = place()
        self.line = corners(self.r)
        self.s = self.z * 2 + self.c
        self.twin = (self.z * 2 + 1 - self.c, self.r)
        self.count = zs if z_flag else 1
        self.half = own.shape[0] // 2
        self.pending = []

    def start(self, copy):
        copy.start()
        self.pending.append(copy.wait_send)

    def slot(self, k, other, j):
        if not self.z_flag:
            return self.out.at[other, j]
        core = 1 - self.c if other else self.c
        zz = lax.rem(self.z - k + self.zs, self.zs)
        return self.out.at[zz, core, self.line[j]] if self.planes else self.out.at[zz, core]

    def z_copy(self, k, dst):
        src = self.own if dst is None else dst
        dst = self.slot(0, 0, 0) if dst is None else dst
        to = (lax.rem(self.z + k, self.zs) * 2 + self.c, self.r)
        return send(src, dst, self.z_ssem.at[k], self.z_rsem.at[k], to)

    def near(self, k, j, src):
        dst = self.slot(k, 0, j) if src is None or not self.z_flag else self.slot(k, 0, 0)
        return send(dst if src is None else src, dst, self.f_ssem.at[k, j - 1], self.f_rsem.at[k, j - 1], (self.s, self.line[j]))

    def part(self, ref, j):
        return ref.at[pl.ds(self.half if j == 1 else 0, self.half)]

    def far(self, k, j, src):
        if src is None:
            src = dst = self.part(self.slot(k, 0, 3), j)
        else:
            dst = self.part(src if self.z_flag else self.out.at[0, 3], j)
            src = self.part(src, j)
        return send(src, dst, self.h_ssem.at[k, j - 1], self.h_rsem.at[k, j - 1], (self.s, self.line[3 - j]))

    def to_twin(self, k, j, src):
        dst = self.slot(k, 0, j) if self.z_flag else self.out.at[1, j]
        self.start(send(src, dst, self.c_ssem.at[k, j], self.c_rsem.at[k, j], self.twin))

    def launch(self):
        self.local = pltpu.make_async_copy(self.own, self.slot(0, 0, 0), self.l_sem)
        self.local.start()
        for k in range(1, self.count):
            self.start(self.z_copy(k, None))

    def begin(self, k):
        src = self.own
        if k:
            src = self.slot(k, 0, 0)
            self.z_copy(k, src).wait_recv()
        if self.planes:
            for j in (1, 2):
                self.start(self.near(k, j, src))
        self.to_twin(k, 0, src)

    def forward(self, k):
        for j in (1, 2):
            self.near(k, j, None).wait_recv()
            src = self.slot(k, 0, j)
            self.start(self.far(k, j, src))
            self.to_twin(k, j, src)

    def finish(self, k):
        for j in (1, 2):
            self.far(k, j, None).wait_recv()
        self.to_twin(k, 3, self.slot(k, 0, 3))

    def complete(self, k):
        if k == 0:
            self.local.wait()
        for j in range(4 if self.planes else 1):
            dst = self.slot(k, 1, j)
            send(dst, dst, self.c_ssem.at[k, j], self.c_rsem.at[k, j], self.twin).wait_recv()

    def end(self):
        for wait in self.pending:
            wait()


def gather_sems(zs, z_flag):
    sem = pltpu.SemaphoreType.DMA
    n = zs if z_flag else 1
    return [sem((n,)), sem((n,)), sem((n, 2)), sem((n, 2)), sem((n, 2)), sem((n, 2)), sem((n, 4)), sem((n, 4)), sem]


class Chain:
    def __init__(self, zs, own, got, sems):
        self.zs, self.own, self.got, self.sems = zs, own, got, sems
        self.lines = []

    def start(self, k):
        zs = self.zs
        up, down = (self.own, self.own) if k == 1 else (self.got[k - 2], self.got[zs + k - 3])
        self.lines = [
            Line(zs, 1, k - 1, zs, up, self.got[k - 1], self.sems.at[k - 1]),
            Line(zs, -1, 0, zs - k + 1, down, self.got[zs + k - 2], self.sems.at[zs + k - 2]),
        ]
        for line in self.lines:
            line.start()

    def finish(self):
        for line in self.lines:
            line.finish()


class Scatter:
    def __init__(self, zs, z_flag, planes, given, final, stage, twin_in, half_in, full_in, z_in, l_sem, c_ssem, c_rsem, h_ssem,
                 h_rsem, f_ssem, f_rsem, z_ssem, z_rsem):
        self.__dict__.update(locals())
        self.z, self.c, self.r = place()
        self.line = corners(self.r)
        self.s = self.z * 2 + self.c
        self.twin = (self.z * 2 + 1 - self.c, self.r)
        self.rows = twin_in.shape[2]
        self.step = 16
        self.spots = (3, 1, 2, 0) if planes else (0,)
        self.zs = zs if z_flag else 1
        self.order = list(range(1, self.zs)) + [0]
        self.pending = []
        self.loads = []
        self.settled = 0

    def at_z(self, k):
        return (lax.rem(self.z + k, self.zs) * 2 + self.c, self.r)

    def block(self, k, other, j):
        if not self.z_flag:
            return self.given.at[other, j]
        zz, core = lax.rem(self.z + k, self.zs), 1 - self.c if other else self.c
        return self.given.at[zz, core, self.line[j]] if self.planes else self.given.at[zz, core]

    def start(self, copy):
        copy.start()
        self.pending.append(copy.wait_send)

    def begin(self, schedule):
        for k in self.order:
            for j in self.spots:
                self.start(self.twin_copy(k, j, self.block(k, 1, j)))
        if self.stage is not None:
            self.loads = [
                pltpu.make_async_copy(self.block(k, 0, j), self.stage.at[n % 2], self.l_sem.at[n % 2])
                for n, (k, j) in enumerate(schedule)
            ]
            for load in self.loads[:2]:
                load.start()

    def twin_copy(self, k, j, src):
        dst = self.twin_in.at[k, j]
        return send(dst if src is None else src, dst, self.c_ssem.at[k, j], self.c_rsem.at[k, j], self.twin)

    def settle(self, k, j, parts):
        own = self.block(k, 0, j)
        n = self.settled
        if self.stage is not None:
            self.loads[n].wait()
            own = self.stage.at[n % 2]
        self.twin_copy(k, j, None).wait_recv()
        step = self.step
        for first, last, more in parts:

            def body(i, carry, first=first, more=more):
                at = pl.ds(pl.multiple_of(first + i * step, step), step)
                value = own[at, :].astype(jnp.float32) + self.twin_in[k, j, at, :].astype(jnp.float32)
                for ref, offset in more:
                    there = pl.ds(pl.multiple_of(first - offset + i * step, step), step)
                    value = value + ref[there, :].astype(jnp.float32)
                if k == 0 and j == 0:
                    self.final(at, value)
                else:
                    self.twin_in[k, j, at, :] = value.astype(self.twin_in.dtype)
                return carry

            lax.fori_loop(0, (last - first) // step, body, 0)
        if n + 2 < len(self.loads):
            self.loads[n + 2].start()
        self.settled = n + 1

    def half_copy(self, k, n, src):
        dst = self.half_in.at[k, n]
        return send(dst if src is None else src, dst, self.h_ssem.at[k, n], self.h_rsem.at[k, n], (self.s, self.line[n + 1]))

    def full_copy(self, k, j, src):
        dst = self.full_in.at[k, j - 1]
        return send(dst if src is None else src, dst, self.f_ssem.at[k, j - 1], self.f_rsem.at[k, j - 1], (self.s, self.line[j]))

    def z_copy(self, k, src):
        dst = self.z_in.at[k]
        return send(dst if src is None else src, dst, self.z_ssem.at[k], self.z_rsem.at[k], self.at_z(k))

    def stage_a(self, k):
        half = self.rows // 2
        self.settle(k, 3, [(0, self.rows, [])])
        self.start(self.half_copy(k, 1, self.twin_in.at[k, 3, pl.ds(half, half)]))
        self.start(self.half_copy(k, 0, self.twin_in.at[k, 3, pl.ds(0, half)]))

    def stage_b(self, k):
        half = self.rows // 2
        for j in (1, 2):
            n = 2 - j
            self.half_copy(k, n, None).wait_recv()
            more = [(self.half_in.at[k, n], half if n else 0)]
            self.settle(k, j, [(0, half, [] if n else more), (half, self.rows, more if n else [])])
            self.start(self.full_copy(k, j, self.twin_in.at[k, j]))

    def stage_c(self, k):
        more = []
        if self.planes:
            for j in (1, 2):
                self.full_copy(k, j, None).wait_recv()
                more.append((self.full_in.at[k, j - 1], 0))
        if not k:
            for other in range(1, self.zs):
                self.z_copy(other, None).wait_recv()
                more.append((self.z_in.at[other], 0))
        self.settle(k, 0, [(0, self.rows, more)])
        if k:
            self.start(self.z_copy(k, self.twin_in.at[k, 0]))

    def end(self):
        for wait in self.pending:
            wait()


def scatter_scratch(zs, planes, rows, columns, staged):
    sem = pltpu.SemaphoreType.DMA
    low, least = jnp.bfloat16, (1, 2, 16, 128)
    spots = 4 if planes else 1
    return [
        pltpu.VMEM((2, rows, columns) if staged else (16, 128), low),
        pltpu.VMEM((zs, spots, rows, columns), low),
        pltpu.VMEM((zs, 2, rows // 2, columns) if planes else least, low),
        pltpu.VMEM((zs, 2, rows, columns) if planes else least, low),
        pltpu.VMEM((zs, rows, columns) if zs > 1 else least[1:], low),
        sem((2,)), sem((zs, 4)), sem((zs, 4)), sem((zs, 2)), sem((zs, 2)), sem((zs, 2)), sem((zs, 2)), sem((zs,)), sem((zs,)),
    ]


SCATTER_REFS = 14


def scatter_plan(items):
    rounds = []
    for n in range(len(items) + 2):
        rounds.append([])
        for back, stage in enumerate(("a", "b", "c")):
            if 0 <= n - back < len(items):
                name, k = items[n - back]
                if stage != "c" or k:
                    rounds[-1].append((name, stage, k))
    rounds.append([(name, "c", 0) for name, k in items if not k])
    places = {"a": (3,), "b": (1, 2), "c": (0,)}
    schedules = {}
    for name, stage, k in sum(rounds, []):
        schedules.setdefault(name, []).extend((k, j) for j in places[stage])
    return rounds, schedules


def run_stage(scatters, name, stage, k):
    {"a": Scatter.stage_a, "b": Scatter.stage_b, "c": Scatter.stage_c}[stage](scatters[name], k)


class SumChain:
    def __init__(self, zs, parts, got, held, sems, l_sem):
        self.__dict__.update(locals())
        self.z = place()[0]

    def own(self, to):
        return self.parts.at[lax.rem(self.z + to + self.zs, self.zs)]

    def fetch(self, k):
        self.loads = [
            pltpu.make_async_copy(self.own(-k), self.held.at[0], self.l_sem.at[0]),
            pltpu.make_async_copy(self.own(k), self.held.at[1], self.l_sem.at[1]),
        ]
        for load in self.loads:
            load.start()

    def add(self, into, more):
        self.got[into] = (self.got[into].astype(jnp.float32) + self.held[more].astype(jnp.float32)).astype(self.got.dtype)

    def start(self, k):
        zs, z, got = self.zs, self.z, self.got
        up, down = k - 1, zs - 2 + k
        self.lines = [
            Line(zs, 1, 0, 1, self.own(-k), got.at[up], self.sems.at[up]),
            Line(zs, -1, zs - 1, zs, self.own(k), got.at[down], self.sems.at[down]),
        ]
        if k > 1:
            for load in self.loads:
                load.wait()
            pl.when((z >= 1) & (z < k))(functools.partial(self.add, up - 1, 0))
            pl.when((z >= zs - k) & (z < zs - 1))(functools.partial(self.add, down - 1, 1))
            self.lines += [
                Line(zs, 1, 1, k, got.at[up - 1], got.at[up], self.sems.at[up]),
                Line(zs, -1, zs - k, zs - 1, got.at[down - 1], got.at[down], self.sems.at[down]),
            ]
        for line in self.lines:
            line.start()
        if k < zs - 1:
            self.fetch(k + 1)
        else:
            self.loads = [pltpu.make_async_copy(self.own(0), self.held.at[0], self.l_sem.at[0])]
            self.loads[0].start()

    def finish(self):
        for line in self.lines:
            line.finish()

    def total(self):
        zs, z = self.zs, self.z
        self.loads[0].wait()

        def add(come):
            self.held[0] = (self.held[0].astype(jnp.float32) + self.got[come].astype(jnp.float32)).astype(self.held.dtype)

        pl.when(z > 0)(functools.partial(add, zs - 2))
        pl.when(z < zs - 1)(functools.partial(add, 2 * zs - 3))


def partner(tensor):
    lanes = tensor.shape[-1]
    half = HEAD_DIM // 2
    lane = lax.broadcasted_iota(jnp.int32, tensor.shape, tensor.ndim - 1)
    ahead = pltpu.roll(tensor, lanes - half, tensor.ndim - 1)
    behind = pltpu.roll(tensor, half, tensor.ndim - 1)
    return jnp.where(lax.rem(lane, HEAD_DIM) < half, ahead, behind)


def stack_heads(block, first):
    return jnp.concatenate(
        [block[:, (first + h) * HEAD_DIM : (first + h + 1) * HEAD_DIM] for h in range(GROUP)], axis=0
    )


def unstack_heads(stacked, span):
    return jnp.concatenate([stacked[h * span : (h + 1) * span] for h in range(GROUP)], axis=1)


def load_window(inverse_ref, kv_ref, window, first_block):
    half_len = kv_ref.shape[1] // 2
    for n in range(window.shape[0] // half_len):
        slot = inverse_ref[first_block + n]
        at = pl.ds(pl.multiple_of(lax.rem(slot, 2) * half_len, half_len), half_len)
        window[n * half_len : (n + 1) * half_len, :] = kv_ref[lax.div(slot, 2), at, :]


def window_of(order_ref, first_ref, count, half_len):
    m, half = pl.program_id(0), pl.program_id(1)
    my_block = order_ref[lax.axis_index("seq") * 2 + half]
    half_blocks = count // half_len // 2
    first_block = jnp.where(my_block >= half_blocks, half_blocks, 0)
    return first_block, my_block * half_len, first_ref[m]


def attend_kernel(order_ref, inverse_ref, first_ref, lin_ref, cos_ref, sin_ref, kv_ref, q_ref, out_ref, window, bias):
    span = lin_ref.shape[0]
    wide = window.shape[0]
    first_block, my_place, first = window_of(order_ref, first_ref, 2 * wide, span)
    load_window(inverse_ref, kv_ref, window, first_block)
    key_place = first_block * span + lax.broadcasted_iota(jnp.int32, (span, wide), 1)
    place_here = my_place + lax.broadcasted_iota(jnp.int32, (span, wide), 0)
    start = jnp.where(place_here >= first, first, 0)
    bias[...] = jnp.where((key_place <= place_here) & (key_place >= start), 0.0, NEG_LARGE)
    width = GROUP * HEAD_DIM
    cosine = jnp.concatenate([cos_ref[...]] * (width // 128), axis=1)
    sine = jnp.concatenate([sin_ref[...]] * (width // 128), axis=1)
    for g in range(KV_HEADS):
        at = slice(g * width, (g + 1) * width)
        lin = lin_ref[:, at]
        query = (lin * cosine + partner(lin) * sine).astype(jnp.bfloat16) * jnp.bfloat16(HEAD_DIM ** -0.5)
        q_ref[:, at] = query
        key = window[:, g * HEAD_DIM : (g + 1) * HEAD_DIM]
        value = window[:, KVW + g * HEAD_DIM : KVW + (g + 1) * HEAD_DIM]
        scores = product_nt(stack_heads(query, 0), key).reshape(GROUP, span, wide) + bias[...][None]
        exps = jnp.exp(scores - jnp.max(scores, axis=-1, keepdims=True))
        total = jnp.sum(exps, axis=-1, keepdims=True).reshape(GROUP * span, 1)
        mixed = product(exps.astype(jnp.bfloat16).reshape(GROUP * span, wide), value) / total
        out_ref[:, at] = unstack_heads(mixed, span).astype(jnp.bfloat16)


def attend_back_heads(queries, d_heads, key, value, bias, span):
    query, d_mixed = stack_heads(queries, 0), stack_heads(d_heads, 0)
    scores = product_nt(key, query) + bias[...]
    exps = jnp.exp(scores - jnp.max(scores, axis=0, keepdims=True))
    probs = exps * (1.0 / jnp.sum(exps, axis=0, keepdims=True))
    weighted = probs * product_nt(value, d_mixed)
    delta = jnp.sum(weighted, axis=0, keepdims=True)
    d_scores = (weighted - probs * delta).astype(jnp.bfloat16)
    d_query = unstack_heads(product_tn(d_scores, key) * HEAD_DIM ** -0.5, span)
    return product(d_scores, query), product(probs.astype(jnp.bfloat16), d_mixed), d_query


def attend_back_kernel(order_ref, inverse_ref, first_ref, q_ref, d_ref, cos_ref, sin_ref, kv_ref, dq_ref, dkv_ref, window, bias, sums):
    span = q_ref.shape[0]
    wide = window.shape[0]
    rows = GROUP * span
    half = pl.program_id(1)
    first_block, my_place, first = window_of(order_ref, first_ref, 2 * wide, span)
    load_window(inverse_ref, kv_ref, window, first_block)
    key_place = first_block * span + lax.broadcasted_iota(jnp.int32, (wide, rows), 0)
    place_here = my_place + lax.rem(lax.broadcasted_iota(jnp.int32, (wide, rows), 1), span)
    start = jnp.where(place_here >= first, first, 0)
    bias[...] = jnp.where((key_place <= place_here) & (key_place >= start), 0.0, NEG_LARGE)

    @pl.when(half == 0)
    def _():
        sums[...] = jnp.zeros_like(sums)

    width = GROUP * HEAD_DIM
    cosine = jnp.concatenate([cos_ref[...]] * (width // 128), axis=1)
    sine = jnp.concatenate([sin_ref[...]] * (width // 128), axis=1)
    d_keys, d_values = [], []
    for g in range(KV_HEADS):
        at = slice(g * width, (g + 1) * width)
        key = window[:, g * HEAD_DIM : (g + 1) * HEAD_DIM]
        value = window[:, KVW + g * HEAD_DIM : KVW + (g + 1) * HEAD_DIM]
        d_key, d_value, d_query = attend_back_heads(q_ref[:, at], d_ref[:, at], key, value, bias, span)
        d_keys.append(d_key)
        d_values.append(d_value)
        dq_ref[:, at] = (d_query * cosine - partner(d_query) * sine).astype(jnp.bfloat16)
    d_window = jnp.concatenate(d_keys + d_values, axis=1)
    for n in range(wide // span):
        slot = inverse_ref[first_block + n]
        to = pl.ds(pl.multiple_of(lax.rem(slot, 2) * span, span), span)
        sums[lax.div(slot, 2), to, :] += d_window[n * span : (n + 1) * span]

    @pl.when(half == 1)
    def _():
        dkv_ref[...] = sums[...].astype(jnp.bfloat16)


def attention_specs(seq, micro, span):
    half_len = span // 2

    def rows(width):
        return pl.BlockSpec((half_len, width), lambda m, h, *_: (m * 2 + h, 0))

    whole = pl.BlockSpec((seq, span, 2 * KVW), lambda m, h, *_: (0, m, 0))
    return half_len, rows, whole


def attend(order, inverse, first, lin, cosine, sine, kv):
    seq, many, _ = kv.shape
    micro = first.shape[0]
    span = many // micro
    half_len, rows, whole = attention_specs(seq, micro, span)
    wide = seq * span // 2
    return pl.pallas_call(
        attend_kernel,
        grid_spec=pltpu.PrefetchScalarGridSpec(
            num_scalar_prefetch=3,
            grid=(micro, 2),
            in_specs=[rows(D), rows(128), rows(128), whole],
            out_specs=[rows(D), rows(D)],
            scratch_shapes=[pltpu.VMEM((wide, 2 * KVW), jnp.bfloat16), pltpu.VMEM((half_len, wide), jnp.float32)],
        ),
        out_shape=[jax.ShapeDtypeStruct((many, D), jnp.bfloat16)] * 2,
        compiler_params=pltpu.CompilerParams(vmem_limit_bytes=48 * MIB),
        cost_estimate=pl.CostEstimate(flops=8 * many * wide * D, bytes_accessed=16 * MIB, transcendentals=many * wide * HEADS),
    )(order, inverse, first, lin, cosine, sine, kv)


def attend_back(order, inverse, first, queries, d_heads, cosine, sine, kv):
    seq, many, _ = kv.shape
    micro = first.shape[0]
    span = many // micro
    half_len, rows, whole = attention_specs(seq, micro, span)
    wide = seq * span // 2
    return pl.pallas_call(
        attend_back_kernel,
        grid_spec=pltpu.PrefetchScalarGridSpec(
            num_scalar_prefetch=3,
            grid=(micro, 2),
            in_specs=[rows(D), rows(D), rows(128), rows(128), whole],
            out_specs=[rows(D), whole],
            scratch_shapes=[
                pltpu.VMEM((wide, 2 * KVW), jnp.bfloat16),
                pltpu.VMEM((wide, GROUP * half_len), jnp.float32),
                pltpu.VMEM((seq, span, 2 * KVW), jnp.float32),
            ],
        ),
        out_shape=[jax.ShapeDtypeStruct((many, D), jnp.bfloat16), jax.ShapeDtypeStruct(kv.shape, jnp.bfloat16)],
        compiler_params=pltpu.CompilerParams(vmem_limit_bytes=56 * MIB),
        cost_estimate=pl.CostEstimate(flops=20 * many * wide * D, bytes_accessed=24 * MIB, transcendentals=many * wide * HEADS),
    )(order, inverse, first, queries, d_heads, cosine, sine, kv)


def assemble(zs, pieces, whole, sem):
    if len(pieces) == 1:
        copy = pltpu.make_async_copy(pieces[0], whole, sem.at[0])
        copy.start()
        return [copy]
    z = lax.div(lax.axis_index("seq"), 2)
    size = whole.shape[0] // zs

    def rows(zz):
        return whole.at[pl.ds(pl.multiple_of(zz * size, size), size)]

    copies = [pltpu.make_async_copy(pieces[0], rows(z), sem.at[0])]
    copies[0].start()
    for k in range(1, zs):
        below = pltpu.make_async_copy(pieces[k], rows(lax.rem(z - k + zs, zs)), sem.at[k])
        above = pltpu.make_async_copy(pieces[2 * zs - 1 - k], rows(lax.rem(z - k + zs, zs)), sem.at[k])
        pl.when(z >= k)(below.start)
        pl.when(z < k)(above.start)
        copies.append(below)
    return copies


def ffn_kernel(zs, count, *refs):
    x_ref, dy_ref = refs[:2]
    both_pieces, down_pieces = refs[2 : 2 + count], refs[2 + count : 2 + 2 * count]
    out_ref, dx_ref, g_both_ref, g_down_ref, both_w, down_w, both_sum, down_sum, sem = refs[2 + 2 * count :]
    n = down_w.shape[0]
    step, last = pl.program_id(0), pl.num_programs(0) - 1

    @pl.when(step == 0)
    def _():
        copies = assemble(zs, both_pieces, both_w, sem.at[0]) + assemble(zs, down_pieces, down_w, sem.at[1])
        both_sum[...] = jnp.zeros_like(both_sum)
        down_sum[...] = jnp.zeros_like(down_sum)
        for copy in copies:
            copy.wait()

    x, dy = x_ref[...], dy_ref[...]
    lin = product(x, both_w[...])
    gate, upper = lin[:, :n], lin[:, n:]
    sig = 1.0 / (1.0 + jnp.exp(-gate))
    act = gate * sig
    hidden = (act * upper).astype(jnp.bfloat16)
    d_hidden = product_nt(dy, down_w[...])
    d_gate = d_hidden * upper * (sig * (1.0 + gate * (1.0 - sig)))
    d_both = jnp.concatenate([d_gate.astype(jnp.bfloat16), (d_hidden * act).astype(jnp.bfloat16)], axis=1)
    dx_ref[...] = product_nt(d_both, both_w[...]).astype(jnp.bfloat16)
    out_ref[...] = product(hidden, down_w[...]).astype(jnp.bfloat16)
    for at in range(0, D, 256):
        both_sum[at : at + 256, :] += product_tn(x[:, at : at + 256], d_both)
    part = n // 4
    for at in range(0, n, part):
        down_sum[at : at + part, :] += product_tn(hidden[:, at : at + part], dy)

    @pl.when(step == last)
    def _():
        both_w[...] = both_sum[...].astype(jnp.bfloat16)
        down_w[...] = down_sum[...].astype(jnp.bfloat16)
        copies = [
            pltpu.make_async_copy(both_w, g_both_ref, sem.at[0, 0]),
            pltpu.make_async_copy(down_w, g_down_ref, sem.at[1, 0]),
        ]
        for copy in copies:
            copy.start()
        for copy in copies:
            copy.wait()


def feed_forward(x, dy, both_pieces, down_pieces, zs):
    count = x.shape[0]
    spread_over = zs if len(both_pieces) > 1 else 1
    n = down_pieces[0].shape[0] * spread_over
    block = 256
    low = jnp.bfloat16
    tokens = pl.BlockSpec((block, D), lambda i: (i, 0))
    anywhere = pl.BlockSpec(memory_space=pl.ANY)
    return pl.pallas_call(
        functools.partial(ffn_kernel, zs, len(both_pieces)),
        grid=(count // block,),
        in_specs=[tokens, tokens] + [anywhere] * (2 * len(both_pieces)),
        out_specs=[tokens, tokens, anywhere, anywhere],
        out_shape=[jax.ShapeDtypeStruct(x.shape, low)] * 2
        + [jax.ShapeDtypeStruct((D, 2 * n), low), jax.ShapeDtypeStruct((n, D), low)],
        scratch_shapes=[
            pltpu.VMEM((D, 2 * n), low),
            pltpu.VMEM((n, D), low),
            pltpu.VMEM((D, 2 * n), jnp.float32),
            pltpu.VMEM((n, D), jnp.float32),
            pltpu.SemaphoreType.DMA((2, zs)),
        ],
        compiler_params=pltpu.CompilerParams(vmem_limit_bytes=60 * MIB),
        cost_estimate=pl.CostEstimate(flops=18 * count * D * n, bytes_accessed=60 * MIB, transcendentals=count * n),
    )(x, dy, *both_pieces, *down_pieces)


def spread_kernel(zs, rows, unit, gate_ref, up_ref, out):
    for c in range(2):
        for r in range(rows):
            for n, weight in enumerate((gate_ref, up_ref)):
                for z in range(zs):
                    at = ((z * 2 + c) * rows + r) * unit
                    to = (n * zs + z) * unit
                    out[c, r, :, to : to + unit] = weight[:, at : at + unit]


def spread(gate, up, zs, rows):
    wide, part = gate.shape
    unit = part // (zs * 2 * rows)
    return pl.pallas_call(
        functools.partial(spread_kernel, zs, rows, unit),
        out_shape=jax.ShapeDtypeStruct((2, rows, wide, 2 * zs * unit), gate.dtype),
    )(gate, up)


def collect_kernel(zs, rows, unit, given, *outs):
    for n, out in enumerate(outs):
        for c in range(2):
            for r in range(rows):
                for z in range(zs):
                    at = ((z * 2 + c) * rows + r) * unit
                    to = (n * zs + z) * unit
                    out[:, at : at + unit] = given[c, r, :, to : to + unit].astype(jnp.float32)


def collect(blocks, zs, rows, unit):
    shape = jax.ShapeDtypeStruct((blocks.shape[2], unit * zs * 2 * rows), jnp.float32)
    return pl.pallas_call(functools.partial(collect_kernel, zs, rows, unit), out_shape=[shape, shape])(blocks)


def forward_kernel(zs, micro, *refs):
    order_ref, places_ref, first_ref, freq_ref, x_ref, pack_ref, both_ref, down_ref, out_ref, dy_ref = refs[:10]
    packed, both_own, kv_all, out_all, dy_all, ffn_all = refs[10:16]
    steps = 2 * zs - 2
    both_got, down_got = refs[16 : 16 + steps], refs[16 + steps : 16 + 2 * steps]
    q_ref, attn_ref, attended_ref, middle_ref, gains_ref, cos_ref, sin_ref = refs[16 + 2 * steps : 23 + 2 * steps]
    (staged, lin, kv_own, kv_here, window, bias, out_w, ffn_own, sems, *more) = refs[23 + 2 * steps :]
    low = jnp.bfloat16
    z, c, r = place()
    many = x_ref.shape[0]
    span = many // micro
    half_len = span // 2
    rows = D // zs
    greet(neighbours(zs, True, True))

    exchange = Exchange(both_ref, both_own, *more[:3])
    both_chain, down_chain = Chain(zs, both_own, both_got, more[3]), Chain(zs, down_ref, down_got, more[4])
    more = more[5:]
    weights = Gather(zs, True, True, pack_ref, packed, *more[:9])
    outs = Gather(zs, True, True, out_ref, out_all, *more[9:18])
    pairs = Gather(zs, True, False, kv_own, kv_all, *more[18:27])
    dys = Gather(zs, False, True, dy_ref, dy_all, *more[27:36])
    ffns = Gather(zs, False, True, ffn_own, ffn_all, *more[36:45])

    weights.launch()
    exchange.start()
    weights.begin(0)
    outs.launch()

    lane = lax.broadcasted_iota(jnp.int32, (half_len, 128), 1)
    for i in range(2 * micro):
        place_here = order_ref[(z * 2 + c) * 2 + i % 2] * half_len + lax.broadcasted_iota(jnp.int32, (half_len, 128), 0)
        start = jnp.where(place_here >= first_ref[i // 2], first_ref[i // 2], 0)
        angle = (place_here - start).astype(jnp.float32) * freq_ref[...]
        cos_ref[i * half_len : (i + 1) * half_len, :] = jnp.cos(angle)
        sine = jnp.sin(angle)
        sin_ref[i * half_len : (i + 1) * half_len, :] = jnp.where(lax.rem(lane, HEAD_DIM) < HEAD_DIM // 2, -sine, sine)
    x = x_ref[...].astype(jnp.float32)
    factor = rms_factor(x)

    loads = {}

    def load(k):
        weights.complete(k)
        zz = lax.rem(z - k + zs, zs)
        loads[k] = pltpu.make_async_copy(packed.at[zz], staged.at[k % 2], sems.at[k % 2])
        loads[k].start()

    def project(k):
        loads[k].wait()
        zz = lax.rem(z - k + zs, zs)
        at = pl.ds(pl.multiple_of(zz * rows, rows), rows)
        block = staged[k % 2].reshape(rows, PACK)
        gains = block[:, QKV:].astype(jnp.float32).T[:8]
        gains_ref[:, at] = gains
        attn_in = (x_ref[:, at].astype(jnp.float32) * factor * gains[0:1]).astype(low)
        attn_ref[:, at] = attn_in
        value = product(attn_in, block[:, :QKV])
        lin[...] = value if k == 0 else lin[...] + value

    weights.begin(1)
    weights.forward(0)
    weights.begin(2)
    weights.forward(1)
    weights.finish(0)
    weights.begin(3)
    down_chain.start(1)
    exchange.finish()
    both_chain.start(1)
    weights.forward(2)
    weights.finish(1)
    load(0)
    weights.forward(3)
    weights.finish(2)
    outs.begin(0)
    load(1)
    project(0)
    outs.begin(1)
    project(1)
    weights.finish(3)
    dys.launch()
    dys.begin(0)
    load(2)
    load(3)
    project(2)
    project(3)

    width = GROUP * HEAD_DIM
    cosine = jnp.concatenate([cos_ref[...]] * (width // 128), axis=1)
    sine = jnp.concatenate([sin_ref[...]] * (width // 128), axis=1)

    def turned(block, w):
        return block * cosine[:, :w] + partner(block) * sine[:, :w]

    kv_own[:, :KVW] = turned(lin[:, D : D + KVW], KVW).astype(low)
    kv_own[:, KVW:] = lin[:, D + KVW :].astype(low)
    pairs.launch()
    pairs.begin(0)
    for g in range(KV_HEADS):
        at = slice(g * width, (g + 1) * width)
        q_ref[:, at] = turned(lin[:, at], width).astype(low) * low(HEAD_DIM ** -0.5)
    outs.forward(0)
    outs.begin(2)
    both_chain.finish()
    down_chain.finish()
    both_chain.start(2)
    down_chain.start(2)
    for k in range(1, zs):
        pairs.begin(k)
    outs.forward(1)
    outs.finish(0)
    outs.begin(3)
    for k in range(zs):
        pairs.complete(k)
    kv_load = pltpu.make_async_copy(kv_all, kv_here, sems.at[2])
    kv_load.start()
    outs.forward(2)
    outs.finish(1)
    kv_load.wait()

    wide = window.shape[0]
    half_blocks = wide // half_len

    def attend_some(i, carry):
        m, half = lax.div(i, 2), lax.rem(i, 2)
        my_block = order_ref[(z * 2 + c) * 2 + half]
        first_block = jnp.where(my_block >= half_blocks, half_blocks, 0)
        wanted = first_block * half_len + lax.broadcasted_iota(jnp.int32, (wide, 2 * wide), 0)
        chosen = jnp.where(places_ref[...] == wanted, 1.0, 0.0).astype(low)
        at = pl.ds(pl.multiple_of(m * span, span), span)
        window[...] = product(chosen, kv_here[:, :, at, :].reshape(2 * wide, 2 * KVW)).astype(low)
        key_place = first_block * half_len + lax.broadcasted_iota(jnp.int32, (half_len, wide), 1)
        place_here = my_block * half_len + lax.broadcasted_iota(jnp.int32, (half_len, wide), 0)
        first = first_ref[m]
        start = jnp.where(place_here >= first, first, 0)
        bias[...] = jnp.where((key_place <= place_here) & (key_place >= start), 0.0, NEG_LARGE)
        here = pl.ds(pl.multiple_of(i * half_len, half_len), half_len)
        for g in range(KV_HEADS):
            at = slice(g * width, (g + 1) * width)
            key = window[:, g * HEAD_DIM : (g + 1) * HEAD_DIM]
            value = window[:, KVW + g * HEAD_DIM : KVW + (g + 1) * HEAD_DIM]
            scores = product_nt(stack_heads(q_ref[here, at], 0), key).reshape(GROUP, half_len, wide) + bias[...][None]
            exps = jnp.exp(scores - jnp.max(scores, axis=-1, keepdims=True))
            total = jnp.sum(exps, axis=-1, keepdims=True).reshape(GROUP * half_len, 1)
            mixed = product(exps.astype(low).reshape(GROUP * half_len, wide), value) / total
            attended_ref[here, at] = unstack_heads(mixed, half_len).astype(low)
        return carry

    lax.fori_loop(0, 2 * micro, attend_some, 0)
    outs.forward(3)
    outs.finish(2)
    outs.finish(3)
    dys.forward(0)
    for k in range(zs):
        outs.complete(k)
    out_load = pltpu.make_async_copy(out_all, out_w, sems.at[3])
    out_load.start()
    dys.finish(0)
    out_load.wait()
    middle = x_ref[...].astype(jnp.float32) + product(attended_ref[...], out_w[...].reshape(D, D))
    middle_ref[...] = middle
    ffn_own[...] = (middle * rms_factor(middle) * gains_ref[1:2, :]).astype(low)
    ffns.launch()
    ffns.begin(0)
    both_chain.finish()
    down_chain.finish()
    both_chain.start(3)
    down_chain.start(3)
    dys.complete(0)
    ffns.forward(0)
    ffns.finish(0)
    ffns.complete(0)
    both_chain.finish()
    down_chain.finish()
    exchange.end()
    for one in (weights, outs, pairs, dys, ffns):
        one.end()


def places_of(order, span):
    return (order[:, None] * (span // 2) + jnp.arange(span // 2, dtype=jnp.int32)).reshape(1, -1)


def forward(order, first, tokens, pack, both, down, w_out, dy, zs, collective_id):
    many = tokens.shape[0]
    micro = first.shape[0]
    seq = 2 * zs
    wide = seq * (many // micro) // 2
    low, full = jnp.bfloat16, jnp.float32
    freq = 10000.0 ** (-(jnp.arange(128, dtype=jnp.int32) % (HEAD_DIM // 2)).astype(full) / (HEAD_DIM // 2))
    anywhere, here, smem = (pl.BlockSpec(memory_space=m) for m in (pl.ANY, pltpu.VMEM, pltpu.SMEM))
    shape = jax.ShapeDtypeStruct
    out_any = [
        shape((zs, 2, 4) + pack.shape, low),
        shape(both.shape, low),
        shape((zs, 2, many, 2 * KVW), low),
        shape((zs, 2, 4) + w_out.shape, low),
        shape((2, 4) + dy.shape, low),
        shape((2, 4, many, D), low),
    ] + [shape(both.shape, low)] * (2 * zs - 2) + [shape(down.shape, low)] * (2 * zs - 2)
    out_here = [shape((many, D), t) for t in (low, low, low, full)] + [shape((8, D), full)] + [shape((many, 128), full)] * 2
    sem = pltpu.SemaphoreType.DMA
    found = pl.pallas_call(
        functools.partial(forward_kernel, zs, micro),
        out_shape=out_any + out_here,
        in_specs=[smem, here, smem] + [here] * 2 + [anywhere] * 5,
        out_specs=[anywhere] * len(out_any) + [here] * len(out_here),
        scratch_shapes=[
            pltpu.VMEM((2, 2, 4) + pack.shape, low),
            pltpu.VMEM((many, QKV), full),
            pltpu.VMEM((many, 2 * KVW), low),
            pltpu.VMEM((zs, 2, many, 2 * KVW), low),
            pltpu.VMEM((wide, 2 * KVW), low),
            pltpu.VMEM((many // micro // 2, wide), full),
            pltpu.VMEM((zs, 2, 4) + w_out.shape, low),
            pltpu.VMEM((many, D), low),
            sem((4,)),
        ] + EXCHANGE_SEMS + [sem((2 * zs - 2, 2))] * 2 + gather_sems(zs, True) * 3 + gather_sems(zs, False) * 2,
        compiler_params=pltpu.CompilerParams(
            collective_id=collective_id, has_side_effects=True, vmem_limit_bytes=56 * MIB
        ),
        cost_estimate=LONG,
    )(order, places_of(order, many // micro), first, freq.reshape(1, 128), tokens, pack, both, down, w_out, dy)
    return found


def back_kernel(zs, micro, *refs):
    (order_ref, places_ref, first_ref, dy_ref, middle_ref, gains_ref, q_ref, cos_ref, sin_ref) = refs[:9]
    dx_part, out_part, both_part, down_part, out_all, kv_all = refs[9:15]
    result_ref, d_middle_ref, dq_ref, dkv_ref, gain_ref, down_ref, both_up, both_down = refs[15:23]
    out_w, kv_here, d_heads, chosen, window, bias, d_places, sems, got, held, d_sems, dl_sem, b_sems, *more = refs[23:]
    low, full = jnp.bfloat16, jnp.float32
    z, c, r = place()
    many = dy_ref.shape[0]
    span = many // micro
    half_len = span // 2
    greet(neighbours(zs, True, False))

    def take_d_ffn(at, value):
        d_middle_ref[at, :] = value

    def take_result(at, value):
        result_ref[at, :] = (middle_ref[at, :] + value).astype(low)

    scatters = {
        "dx": Scatter(1, False, True, dx_part, take_d_ffn, *more[:SCATTER_REFS]),
        "out": Scatter(1, False, True, out_part, take_result, *more[SCATTER_REFS : 2 * SCATTER_REFS]),
    }
    down = SumChain(zs, down_part, got, held, d_sems, dl_sem)
    lines = [
        Line(zs, 1, 0, 1, both_part.at[lax.rem(z + zs - 1, zs)], both_up, b_sems.at[0]),
        Line(zs, -1, zs - 1, zs, both_part.at[lax.rem(z + 1, zs)], both_down, b_sems.at[1]),
    ]
    schedule = [(0, 3), (0, 1), (0, 2), (0, 0)]
    scatters["dx"].begin(schedule)
    down.start(1)
    for line in lines:
        line.start()
    loads = [pltpu.make_async_copy(out_all, out_w, sems.at[0]), pltpu.make_async_copy(kv_all, kv_here, sems.at[1])]
    for load in loads:
        load.start()
    scatters["dx"].stage_a(0)
    scatters["out"].begin(schedule)
    scatters["dx"].stage_b(0)
    scatters["out"].stage_a(0)
    scatters["dx"].stage_c(0)
    scatters["out"].stage_b(0)
    down.finish()
    down.start(2)

    gain_ref[0:1, :] = jnp.zeros((1, D), full)

    def norm_some(i, carry):
        at = pl.ds(pl.multiple_of(i * half_len, half_len), half_len)
        middle, d_ffn = middle_ref[at, :], d_middle_ref[at, :]
        factor = rms_factor(middle)
        normed = middle * factor
        inner = d_ffn * gains_ref[1:2, :]
        d_norm = factor * (inner - normed * jnp.mean(inner * normed, axis=-1, keepdims=True))
        d_middle_ref[at, :] = dy_ref[at, :].astype(full) + d_norm
        gain_ref[0:1, :] += jnp.sum(d_ffn * normed, axis=0, keepdims=True)
        return carry

    lax.fori_loop(0, many // half_len, norm_some, 0)
    for load in loads:
        load.wait()
    d_heads[...] = product_nt(d_middle_ref[...].astype(low), out_w[...].reshape(D, D)).astype(low)

    wide = window.shape[0]
    half_blocks = wide // half_len
    width = GROUP * HEAD_DIM

    def attend_some(i, carry):
        m, half = lax.div(i, 2), lax.rem(i, 2)
        my_block = order_ref[(z * 2 + c) * 2 + half]
        first_block = jnp.where(my_block >= half_blocks, half_blocks, 0)
        wanted = first_block * half_len + lax.broadcasted_iota(jnp.int32, (wide, 2 * wide), 0)
        chosen[...] = jnp.where(places_ref[...] == wanted, 1.0, 0.0).astype(low)
        rows = pl.ds(pl.multiple_of(m * span, span), span)
        window[...] = product(chosen[...], kv_here[:, :, rows, :].reshape(2 * wide, 2 * KVW)).astype(low)
        key_place = first_block * half_len + lax.broadcasted_iota(jnp.int32, bias.shape, 0)
        place_here = my_block * half_len + lax.rem(lax.broadcasted_iota(jnp.int32, bias.shape, 1), half_len)
        first = first_ref[m]
        start = jnp.where(place_here >= first, first, 0)
        bias[...] = jnp.where((key_place <= place_here) & (key_place >= start), 0.0, NEG_LARGE)
        here = pl.ds(pl.multiple_of(i * half_len, half_len), half_len)
        cosine = jnp.concatenate([cos_ref[here, :]] * (width // 128), axis=1)
        sine = jnp.concatenate([sin_ref[here, :]] * (width // 128), axis=1)
        d_keys, d_values = [], []
        for g in range(KV_HEADS):
            at = slice(g * width, (g + 1) * width)
            key = window[:, g * HEAD_DIM : (g + 1) * HEAD_DIM]
            value = window[:, KVW + g * HEAD_DIM : KVW + (g + 1) * HEAD_DIM]
            d_key, d_value, d_query = attend_back_heads(q_ref[here, at], d_heads[here, at], key, value, bias, half_len)
            d_keys.append(d_key)
            d_values.append(d_value)
            dq_ref[here, at] = (d_query * cosine - partner(d_query) * sine).astype(low)
        d_window = jnp.concatenate(d_keys + d_values, axis=1).astype(low)
        spread_back = product_tn(chosen[...], d_window)

        @pl.when(half == 0)
        def _():
            d_places[...] = spread_back

        @pl.when(half == 1)
        def _():
            both = (d_places[...] + spread_back).astype(low)
            dkv_ref[:, :, rows, :] = both.reshape(zs, 2, span, 2 * KVW)

        return carry

    lax.fori_loop(0, micro, attend_some, 0)
    down.finish()
    down.start(3)
    lax.fori_loop(micro, 2 * micro, attend_some, 0)
    scatters["out"].stage_c(0)
    down.finish()
    down.total()
    down_ref[...] = held[0].astype(full)
    for line in lines:
        line.finish()
    for one in scatters.values():
        one.end()


def back(order, first, dy, middle, gains, queries, cosine, sine, dx_part, out_part, both_part, down_part, out_all, kv_all,
         zs, collective_id):
    many = dy.shape[0]
    micro = first.shape[0]
    span = many // micro
    wide = zs * span
    low, full = jnp.bfloat16, jnp.float32
    anywhere, here, smem = (pl.BlockSpec(memory_space=m) for m in (pl.ANY, pltpu.VMEM, pltpu.SMEM))
    shape, sem = jax.ShapeDtypeStruct, pltpu.SemaphoreType.DMA
    unit = down_part.shape[1]
    piece = shape(both_part.shape[1:], low)
    return pl.pallas_call(
        functools.partial(back_kernel, zs, micro),
        out_shape=[
            shape((many, D), low), shape((many, D), full), shape((many, D), low), shape(kv_all.shape, low),
            shape((8, D), full), shape((unit, D), full), piece, piece,
        ],
        in_specs=[smem, here, smem] + [here] * 6 + [anywhere] * 6,
        out_specs=[here] * 6 + [anywhere] * 2,
        scratch_shapes=[
            pltpu.VMEM(out_all.shape, low),
            pltpu.VMEM(kv_all.shape, low),
            pltpu.VMEM((many, D), low),
            pltpu.VMEM((wide, 2 * wide), low),
            pltpu.VMEM((wide, 2 * KVW), low),
            pltpu.VMEM((wide, GROUP * span // 2), full),
            pltpu.VMEM((2 * wide, 2 * KVW), full),
            sem((2,)),
            pltpu.VMEM((2 * zs - 2, unit, D), low),
            pltpu.VMEM((2, unit, D), low),
            sem((2 * zs - 2, 2)), sem((2,)), sem((2, 2)),
        ] + scatter_scratch(1, True, many, D, True) * 2,
        compiler_params=pltpu.CompilerParams(
            collective_id=collective_id, has_side_effects=True, vmem_limit_bytes=62 * MIB
        ),
        cost_estimate=LONG,
    )(order, places_of(order, span), first, dy, middle, gains, queries, cosine, sine, dx_part, out_part, both_part, down_part,
      out_all, kv_all)


def weights_kernel(zs, *refs):
    x_ref, attn_ref, d_middle_ref, d_attn_ref, gains_ref, gain_two_ref, cos_ref, sin_ref, dkv_ref = refs[:9]
    packed, both_part, both_up, both_down, g_out, g_query = refs[9:15]
    x_grad_ref, out_ref, query_ref, pack_ref, moved_ref = refs[15:20]
    kv_w, d_kv, pack_g, sems, got, held, b_sems, bl_sem, *more = refs[20:]
    exchange_sems, more = more[:3], more[3:]
    low, full = jnp.bfloat16, jnp.float32
    greet(neighbours(zs, True, True))

    def into(ref):
        def take(at, value):
            ref[at, :] = value

        return take

    def next_refs(staged):
        nonlocal more
        mine, more = more[:SCATTER_REFS], more[SCATTER_REFS:]
        return mine if staged else [None, *mine[1:]]

    pairs = Scatter(zs, True, False, dkv_ref, into(d_kv), *next_refs(False))
    scatters = {
        "out": Scatter(zs, True, True, g_out, into(out_ref), *next_refs(True)),
        "query": Scatter(zs, True, True, g_query, into(query_ref), *next_refs(True)),
        "pack": Scatter(zs, True, True, pack_g, into(pack_ref), *next_refs(False)),
    }
    items = [(name, k) for k in range(1, zs) for name in ("out", "query")]
    items[4:4] = [("pack", 1)]
    items += [("pack", k) for k in range(2, zs)] + [("out", 0), ("query", 0), ("pack", 0)]
    rounds, schedules = scatter_plan(items)

    chain = SumChain(zs, both_part, got, held, b_sems, bl_sem)
    loads = [
        pltpu.make_async_copy(both_up, got.at[0], sems.at[0]),
        pltpu.make_async_copy(both_down, got.at[zs - 1], sems.at[1]),
        pltpu.make_async_copy(packed.at[:, :, :, :, pl.ds(D, 2 * KVW)], kv_w, sems.at[2]),
    ]
    for load in loads:
        load.start()
    chain.fetch(2)
    pairs.begin([])
    scatters["out"].begin(schedules["out"])
    scatters["query"].begin(schedules["query"])
    for k in range(1, zs):
        pairs.stage_c(k)
    for load in loads:
        load.wait()
    chain.start(2)

    def keys_and_norm():
        pairs.stage_c(0)
        lanes = KVW // 128
        cosine = jnp.concatenate([cos_ref[...]] * lanes, axis=1)
        sine = jnp.concatenate([sin_ref[...]] * lanes, axis=1)
        d_key = d_kv[:, :KVW]
        d_lin = jnp.concatenate([d_key * cosine - partner(d_key) * sine, d_kv[:, KVW:]], axis=1).astype(low)
        d_attn = d_attn_ref[...] + product_nt(d_lin, kv_w[...].reshape(D, 2 * KVW))
        x = x_ref[...].astype(full)
        factor = rms_factor(x)
        normed = x * factor
        inner = d_attn * gains_ref[0:1, :]
        d_x = factor * (inner - normed * jnp.mean(inner * normed, axis=-1, keepdims=True))
        x_grad_ref[...] = (d_middle_ref[...] + d_x).astype(low)
        gain_one = jnp.sum(d_attn * normed, axis=0, keepdims=True)
        rows = lax.broadcasted_iota(jnp.int32, (128, D), 0)
        both = jnp.where(rows == 0, gain_one, jnp.where(rows == 1, gain_two_ref[0:1, :], 0.0))
        pack = jnp.concatenate([product_tn(attn_ref[...], d_lin), both.T], axis=1).astype(low)
        pack_g[...] = pack.reshape(pack_g.shape)
        scatters["pack"].begin([])

    for n, stages in enumerate(rounds):
        if n == 3:
            keys_and_norm()
        if n == 6:
            chain.finish()
            chain.start(3)
        if n == len(rounds) - 1:
            chain.finish()
            chain.total()
            exchange = Exchange(held.at[0], moved_ref, *exchange_sems)
            exchange.start()
        for stage in stages:
            run_stage(scatters, *stage)
    exchange.finish()
    exchange.end()
    for one in (pairs, *scatters.values()):
        one.end()


def weight_sums(x, attn_in, d_middle, d_attn, gains, gain_two, cosine, sine, d_kv, packed, both_part, both_up, both_down, g_out,
                g_query, zs, collective_id):
    many = x.shape[0]
    low, full = jnp.bfloat16, jnp.float32
    anywhere, here = (pl.BlockSpec(memory_space=m) for m in (pl.ANY, pltpu.VMEM))
    shape, sem = jax.ShapeDtypeStruct, pltpu.SemaphoreType.DMA
    wide = packed.shape[3]
    narrow = 2 * KVW + 128
    block = both_part.shape[1:]
    return pl.pallas_call(
        functools.partial(weights_kernel, zs),
        out_shape=[
            shape((many, D), low), shape((wide, D), full), shape((wide, D), full), shape((wide, narrow), full), shape(block, low),
        ],
        in_specs=[here] * 9 + [anywhere] * 6,
        out_specs=[here] * 4 + [anywhere],
        scratch_shapes=[
            pltpu.VMEM(packed.shape[:4] + (2 * KVW,), low),
            pltpu.VMEM((many, 2 * KVW), full),
            pltpu.VMEM((zs, 2, 4, wide, narrow), low),
            sem((3,)),
            pltpu.VMEM((2 * zs - 2,) + block, low),
            pltpu.VMEM((2,) + block, low),
            sem((2 * zs - 2, 2)), sem((2,)),
        ] + EXCHANGE_SEMS
        + scatter_scratch(zs, False, many, 2 * KVW, False)
        + scatter_scratch(zs, True, wide, D, True) * 2
        + scatter_scratch(zs, True, wide, narrow, False),
        compiler_params=pltpu.CompilerParams(
            collective_id=collective_id, has_side_effects=True, vmem_limit_bytes=62 * MIB
        ),
        cost_estimate=LONG,
    )(x, attn_in, d_middle, d_attn, gains, gain_two, cosine, sine, d_kv, packed, both_part, both_up, both_down, g_out,
      g_query)


class Links:
    def __init__(self, seq, rows):
        self.zs, self.rows = seq // 2, rows
        self.kernels = rows == 4 and self.zs == 4
        self.z_groups = [[2 * z + c for z in range(self.zs)] for c in range(2)]
        self.core_groups = [[2 * z, 2 * z + 1] for z in range(self.zs)]

    def gather_z(self, block):
        return lax.all_gather(block, "seq", axis=0, tiled=True, axis_index_groups=self.z_groups)

    def scatter_z(self, blocks):
        return lax.psum_scatter(blocks, "seq", scatter_dimension=0, tiled=True, axis_index_groups=self.z_groups)

    def exchange_xla(self, blocks):
        moved = lax.all_to_all(blocks, "rows", split_axis=1, concat_axis=1, tiled=True)
        return lax.all_to_all(moved, "seq", split_axis=0, concat_axis=0, tiled=True, axis_index_groups=self.core_groups)

    def gather(self, array, z_flag, planes):
        if planes:
            array = lax.all_gather(array, "rows", axis=0)
        array = lax.all_gather(array, "seq", axis=0, axis_index_groups=self.core_groups)
        return self.gather_z(array[None]) if z_flag else array

    def scatter(self, blocks, z_flag, planes):
        blocks = self.scatter_z(blocks)[0] if z_flag else blocks
        blocks = lax.psum_scatter(blocks, "seq", scatter_dimension=0, tiled=True, axis_index_groups=self.core_groups)[0]
        if planes:
            blocks = lax.psum_scatter(blocks, "rows", scatter_dimension=0, tiled=True)[0]
        return blocks.astype(jnp.float32)


def on_device(seq, rows, tokens, w_query, w_key, w_value, w_out, w_gate, w_up, w_down, gain_attn, gain_ffn, lengths, order, cotangent):
    links = Links(seq, rows)
    zs = links.zs
    micro, _, span, _ = tokens.shape
    half_len = span // 2
    many = micro * span
    low = jnp.bfloat16
    wide = w_gate.shape[0]
    unit = w_down.shape[0]

    both = spread(w_gate, w_up, zs, rows)
    flat = (2 * rows * wide, 2 * zs * unit)
    gains = jnp.pad(jnp.stack([gain_attn, gain_ffn], axis=1), ((0, 0), (0, 126)))
    pack = jnp.concatenate([w_query, w_key, w_value, gains], axis=1)
    dy_own = cotangent.reshape(many, D)
    own_tokens = tokens.reshape(many, D)
    x = own_tokens.astype(jnp.float32)
    first = lengths[:, 0, 0]
    slot_of = jnp.argmax(order[None, :] == jnp.arange(order.shape[0], dtype=jnp.int32)[:, None], axis=1).astype(jnp.int32)
    chained = links.kernels
    if chained:
        found = forward(order, first, own_tokens, pack, both, w_down, w_out, dy_own, zs, 0)
        packed, both_own, kv, out_w, dy, ffn_in = found[:6]
        both_w = [b.reshape(flat) for b in (both_own, *found[6 : 4 + 2 * zs])]
        down_w = [w_down, *found[4 + 2 * zs : 2 + 4 * zs]]
        queries, attn_in, attended, middle, gains, cosine, sine = found[2 + 4 * zs :]
        packed = packed.reshape(D, PACK)
    else:
        both_w = [links.gather_z(links.exchange_xla(both).reshape(flat))]
        down_w = [links.gather_z(w_down)]
        packed, dy = links.gather(pack, True, True).reshape(D, PACK), links.gather(dy_own, False, True)
        gain_one, gain_two = packed[:, QKV].astype(jnp.float32), packed[:, QKV + 1].astype(jnp.float32)
        mine = slot_places(order, half_len, lax.axis_index("seq") * span + jnp.arange(span, dtype=jnp.int32))
        start = jnp.where(mine[None, :] >= first[:, None], first[:, None], 0)
        inverse = 10000.0 ** (-jnp.arange(HEAD_DIM // 2, dtype=jnp.float32) / (HEAD_DIM // 2))
        angles = ((mine[None, :] - start).astype(jnp.float32)[..., None] * inverse).reshape(many, HEAD_DIM // 2)
        cosine, sine = jnp.cos(angles), jnp.sin(angles)
        cosine, sine = jnp.tile(cosine, (1, 4)), jnp.tile(jnp.concatenate([-sine, sine], axis=1), (1, 2))
        attn_in = (x * rms_factor(x) * gain_one).astype(low)
        lin = product(attn_in, packed)
        kv_own = jnp.concatenate([turn(lin[:, D : D + KVW], cosine, sine), lin[:, D + KVW : QKV]], axis=1).astype(low)
        kv, out_w = links.gather(kv_own, True, False), links.gather(w_out, True, True)
        queries, attended = attend(order, slot_of, first, lin, cosine, sine, kv.reshape(seq, many, 2 * KVW))
        middle = x + product(attended, out_w.reshape(D, D))
        ffn_in = links.gather((middle * rms_factor(middle) * gain_two).astype(low), False, True)
    kv = kv.reshape(seq, many, 2 * KVW)
    out_w = out_w.reshape(D, D)
    dy = dy.reshape(2 * rows * many, D)

    ffn_in = ffn_in.reshape(2 * rows * many, D)
    result_part, d_ffn_part, grad_both, grad_down = feed_forward(ffn_in, dy, both_w, down_w, zs)
    shards = (zs, 2, rows, wide)
    grad_both = grad_both.reshape(*shards, 2 * zs * unit)
    grad_down = grad_down.reshape(zs, unit, D)
    d_ffn_part, result_part = (part.reshape(2, rows, many, D) for part in (d_ffn_part, result_part))
    if chained:
        out_all, kv_all = out_w.reshape(*shards, D), kv.reshape(zs, 2, many, 2 * KVW)
        result, d_middle, d_query, d_kv, gain_two_grad, grad_down, both_up, both_down = back(
            order, first, dy_own, middle, gains, queries, cosine, sine, d_ffn_part, result_part, grad_both, grad_down,
            out_all, kv_all, zs, 1,
        )
        grad_out = product_tn(attended, d_middle.astype(low)).astype(low).reshape(*shards, D)
        grad_query = product_tn(attn_in, d_query).astype(low).reshape(*shards, D)
        d_attn = product_nt(d_query, packed[:, :D])
        x_grad, grad_out, grad_query, pack_grad, grad_both = weight_sums(
            own_tokens, attn_in, d_middle, d_attn, gains, gain_two_grad, cosine, sine, d_kv, packed.reshape(*shards, PACK),
            grad_both, both_up, both_down, grad_out, grad_query, zs, 2,
        )
    else:
        d_ffn_in = links.scatter(d_ffn_part, False, True)
        result = (middle + links.scatter(result_part, False, True)).astype(low)
        grad_both = links.exchange_xla(links.scatter_z(grad_both)[0])
        grad_down = links.scatter_z(grad_down)[0].astype(jnp.float32)
        factor_two = rms_factor(middle)
        d_part, grad_gain_two = norm_back(d_ffn_in, middle * factor_two, factor_two, gain_two)
        d_middle = dy_own.astype(jnp.float32) + d_part
        d_mid_low = d_middle.astype(low)
        grad_out = links.scatter(product_tn(attended, d_mid_low).astype(low).reshape(*shards, D), True, True)
        d_heads = product_nt(d_mid_low, out_w).astype(low)
        d_query, d_kv = attend_back(order, slot_of, first, queries, d_heads, cosine, sine, kv)
        grad_query = links.scatter(product_tn(attn_in, d_query).astype(low).reshape(*shards, D), True, True)
        d_kv = links.scatter(d_kv.reshape(zs, 2, many, 2 * KVW), True, False)
        d_key = turn(d_kv[:, :KVW], cosine, -sine)
        d_kv = jnp.concatenate([d_key.astype(low), d_kv[:, KVW:].astype(low)], axis=1)
        d_attn_in = product_nt(d_query, packed[:, :D]) + product_nt(d_kv, packed[:, D:QKV])
        factor_one = rms_factor(x)
        d_x, grad_gain_one = norm_back(d_attn_in, x * factor_one, factor_one, gain_one)
        x_grad = (d_middle + d_x).astype(low)
        gains_grad = jnp.pad(jnp.stack([grad_gain_one, grad_gain_two], axis=1), ((0, 0), (0, 126)))
        pack_grad = jnp.concatenate([product_tn(attn_in, d_kv), gains_grad], axis=1).astype(low)
        pack_grad = links.scatter(pack_grad.reshape(*shards, 2 * KVW + 128), True, True)
    grad_gate, grad_up = collect(grad_both, zs, rows, unit)

    return (
        result.reshape(tokens.shape),
        x_grad.reshape(tokens.shape),
        grad_query,
        pack_grad[:, :KVW],
        pack_grad[:, KVW : 2 * KVW],
        grad_out,
        grad_gate,
        grad_up,
        grad_down,
        pack_grad[:, 2 * KVW],
        pack_grad[:, 2 * KVW + 1],
    )


def solution(mesh):
    both = ("seq", "rows")
    row = P(None, "rows", "seq", None)
    weight, gain = P(both, None), P(both)
    return jax.shard_map(
        functools.partial(on_device, mesh.shape["seq"], mesh.shape["rows"]),
        mesh=mesh,
        in_specs=(row,) + (weight,) * 7 + (gain, gain, P(None, "rows", None), P(), row),
        out_specs=(row, row) + (weight,) * 7 + (gain, gain),
        check_vma=False,
    )
```

```python
import functools

import jax
import jax.numpy as jnp
from jax import lax
from jax.experimental import pallas as pl
from jax.experimental.pallas import tpu as pltpu
from jax.sharding import PartitionSpec as P

D = 2048
HEADS = 32
KV_HEADS = 4
HEAD_DIM = 64
GROUP = 8
KVW = 256
QKV = D + 2 * KVW
PACK = QKV + 128

EPSILON = 1e-05
NEG_LARGE = -1e30
MESH = pl.DeviceIdType.MESH
MIB = 1 << 20
LONG = pl.CostEstimate(flops=50_000_000_000, bytes_accessed=150 * MIB, transcendentals=0)


def product(left, right):
    return jnp.dot(left, right, preferred_element_type=jnp.float32)


def product_nt(left, right):
    return lax.dot_general(left, right, (((1,), (1,)), ((), ())), preferred_element_type=jnp.float32)


def product_tn(left, right):
    return lax.dot_general(left, right, (((0,), (0,)), ((), ())), preferred_element_type=jnp.float32)


def rms_factor(values):
    return lax.rsqrt(jnp.mean(values * values, axis=-1, keepdims=True) + EPSILON)


def norm_back(d_scaled, normed, factor, gain):
    inner = d_scaled * gain
    mean = jnp.mean(inner * normed, axis=-1, keepdims=True)
    return factor * (inner - normed * mean), jnp.sum(d_scaled * normed, axis=0)


def turn(tensor, cosine, sine):
    rows, lanes = tensor.shape
    half = HEAD_DIM // 2
    swapped = jnp.flip(tensor.reshape(rows, lanes // HEAD_DIM, 2, half), axis=2).reshape(rows, lanes)
    return tensor * jnp.tile(cosine, (1, lanes // 128)) + swapped * jnp.tile(sine, (1, lanes // 128))


def slot_places(order, half_len, slot_ids):
    matches = (slot_ids // half_len)[:, None] == jnp.arange(order.shape[0], dtype=jnp.int32)[None, :]
    return jnp.sum(jnp.where(matches, order[None, :], 0), axis=1) * half_len + slot_ids % half_len


def place():
    s, r = lax.axis_index("seq"), lax.axis_index("rows")
    return lax.div(s, 2), lax.rem(s, 2), r


def send(src, dst, ssem, rsem, device):
    return pltpu.make_async_remote_copy(
        src_ref=src, dst_ref=dst, send_sem=ssem, recv_sem=rsem, device_id=device, device_id_type=MESH
    )


def greet(devices):
    barrier = pltpu.get_barrier_semaphore()
    for device in devices:
        pl.semaphore_signal(barrier, inc=1, device_id=device, device_id_type=MESH)
    pl.semaphore_wait(barrier, len(devices))


def corners(r):
    return r, r + 1 - 2 * lax.rem(r, 2), lax.rem(r + 2, 4), 3 - r


def exchange_others():
    return [(cc, j) for j in (3, 1, 2, 0) for cc in range(2) if (cc, j) != (0, 0)]


class Exchange:
    def __init__(self, own, out, ssem, rsem, l_sem):
        z, c, r = place()
        line = corners(r)
        self.own, self.out, self.ssem, self.rsem, self.here = own, out, ssem, rsem, (c, r)
        self.others = [(1 - c if cc else c, line[j]) for cc, j in exchange_others()]
        self.devices = [(z * 2 + core, row) for core, row in self.others]
        self.local = pltpu.make_async_copy(own.at[c, r], out.at[c, r], l_sem)

    def start(self):
        self.copies = []
        for i, other in enumerate(self.others):
            copy = send(self.own.at[other], self.out.at[self.here], self.ssem.at[i], self.rsem.at[i], self.devices[i])
            copy.start()
            self.copies.append(copy)
        self.local.start()

    def finish(self):
        for i, other in enumerate(self.others):
            dst = self.out.at[other]
            send(dst, dst, self.ssem.at[i], self.rsem.at[i], self.devices[i]).wait_recv()
        self.local.wait()

    def end(self):
        for copy in self.copies:
            copy.wait_send()


class Line:
    def __init__(self, zs, way, lo, hi, src, dst, sems):
        z, c, r = place()
        lo, hi = (lo, min(hi, zs - 1)) if way == 1 else (max(lo, 1), hi)
        self.sends = (z >= lo) & (z < hi)
        self.gets = (z - way >= lo) & (z - way < hi)
        to = lax.rem(z + way + zs, zs)
        self.copy = send(src, dst, sems.at[0], sems.at[1], (to * 2 + c, r))

    def start(self):
        pl.when(self.sends)(self.copy.start)

    def finish(self):
        pl.when(self.sends)(self.copy.wait_send)
        pl.when(self.gets)(self.copy.wait_recv)


LINE_SEMS = pltpu.SemaphoreType.DMA((2,))
EXCHANGE_SEMS = [pltpu.SemaphoreType.DMA((7,)), pltpu.SemaphoreType.DMA((7,)), pltpu.SemaphoreType.DMA]


def neighbours(zs, planes, moved):
    z, c, r = place()
    line = corners(r)
    s = z * 2 + c
    devices = [(z * 2 + 1 - c, r)]
    if moved:
        devices = [(z * 2 + (1 - c if cc else c), line[j]) for cc, j in exchange_others()]
    elif planes:
        devices += [(s, line[1]), (s, line[2])]
    return devices + [(lax.rem(z + k, zs) * 2 + c, r) for k in range(1, zs)]


class Gather:
    def __init__(self, zs, z_flag, planes, own, out, z_ssem, z_rsem, f_ssem, f_rsem, h_ssem, h_rsem, c_ssem, c_rsem, l_sem):
        self.__dict__.update(locals())
        self.z, self.c, self.r = place()
        self.line = corners(self.r)
        self.s = self.z * 2 + self.c
        self.twin = (self.z * 2 + 1 - self.c, self.r)
        self.count = zs if z_flag else 1
        self.half = own.shape[0] // 2
        self.pending = []
        self.sent = []
        z = self.z
        self.kth = [0, jnp.where(z == 0, 3, 1), jnp.where((z == 0) | (z == 3), 2, 3), jnp.where(z == 0, 1, jnp.where(z == 3, 3, 2))]

    def start(self, copy):
        copy.start()
        self.pending.append(copy.wait_send)

    def slot(self, k, other, j):
        if not self.z_flag:
            return self.out.at[other, j]
        core = 1 - self.c if other else self.c
        zz = lax.rem(self.z - k + self.zs, self.zs)
        return self.out.at[zz, core, self.line[j]] if self.planes else self.out.at[zz, core]

    def z_copy(self, n, way, k, src, dst):
        to = (lax.rem(self.z + way + self.zs, self.zs) * 2 + self.c, self.r)
        return send(src, dst, self.z_ssem.at[n, 0 if way == 1 else 1], self.z_rsem.at[k], to)

    def hand_on(self, n, src, dst):
        z, k, zs = self.z, self.kth[n], self.zs
        up, down = (z < zs - 1, z > 0) if n == 0 else ((z >= k) & (z < zs - 1), (z < k) & (z > 0))
        for way, goes, step in ((1, up, 1), (-1, down, zs - 1)):
            copy = self.z_copy(n, way, lax.rem(k + step, zs), src, dst)
            pl.when(goes)(copy.start)
            self.sent.append((goes, copy))

    def near(self, k, j, src):
        dst = self.slot(k, 0, j) if src is None or not self.z_flag else self.slot(k, 0, 0)
        return send(dst if src is None else src, dst, self.f_ssem.at[k, j - 1], self.f_rsem.at[k, j - 1], (self.s, self.line[j]))

    def part(self, ref, j):
        return ref.at[pl.ds(self.half if j == 1 else 0, self.half)]

    def far(self, k, j, src):
        if src is None:
            src = dst = self.part(self.slot(k, 0, 3), j)
        else:
            dst = self.part(src if self.z_flag else self.out.at[0, 3], j)
            src = self.part(src, j)
        return send(src, dst, self.h_ssem.at[k, j - 1], self.h_rsem.at[k, j - 1], (self.s, self.line[3 - j]))

    def to_twin(self, k, j, src):
        dst = self.slot(k, 0, j) if self.z_flag else self.out.at[1, j]
        self.start(send(src, dst, self.c_ssem.at[k, j], self.c_rsem.at[k, j], self.twin))

    def launch(self):
        self.local = pltpu.make_async_copy(self.own, self.slot(0, 0, 0), self.l_sem)
        self.local.start()
        if self.count > 1 and self.planes:
            self.hand_on(0, self.own, self.slot(0, 0, 0))
        elif self.count > 1:
            for k in range(1, self.count):
                self.start(self.z_copy(k, k, k, self.own, self.slot(0, 0, 0)))

    def arrive(self, n):
        k = self.kth[n]
        src = self.slot(k, 0, 0)
        self.z_copy(n, 1, k, src, src).wait_recv()
        if self.planes:
            self.hand_on(n, src, src)

    def begin(self, n):
        k = self.kth[n]
        src = self.slot(k, 0, 0) if n else self.own
        if self.planes:
            for j in (1, 2):
                self.start(self.near(k, j, src))
        self.to_twin(k, 0, src)

    def forward(self, n):
        k = self.kth[n]
        for j in (1, 2):
            self.near(k, j, None).wait_recv()
            src = self.slot(k, 0, j)
            self.start(self.far(k, j, src))
            self.to_twin(k, j, src)

    def finish(self, n):
        k = self.kth[n]
        for j in (1, 2):
            self.far(k, j, None).wait_recv()
        self.to_twin(k, 3, self.slot(k, 0, 3))

    def complete(self, n):
        k = self.kth[n]
        if n == 0:
            self.local.wait()
        for j in range(4 if self.planes else 1):
            dst = self.slot(k, 1, j)
            send(dst, dst, self.c_ssem.at[k, j], self.c_rsem.at[k, j], self.twin).wait_recv()

    def end(self):
        for goes, copy in self.sent:
            pl.when(goes)(copy.wait_send)
        for wait in self.pending:
            wait()


def gather_sems(zs, z_flag):
    sem = pltpu.SemaphoreType.DMA
    n = zs if z_flag else 1
    return [sem((n, 2)), sem((n,)), sem((n, 2)), sem((n, 2)), sem((n, 2)), sem((n, 2)), sem((n, 4)), sem((n, 4)), sem]


class Chain:
    def __init__(self, zs, own, got, sems):
        self.zs, self.own, self.got, self.sems = zs, own, got, sems
        self.lines = []

    def start(self, k):
        zs = self.zs
        up, down = (self.own, self.own) if k == 1 else (self.got[k - 2], self.got[zs + k - 3])
        self.lines = [
            Line(zs, 1, k - 1, zs, up, self.got[k - 1], self.sems.at[k - 1]),
            Line(zs, -1, 0, zs - k + 1, down, self.got[zs + k - 2], self.sems.at[zs + k - 2]),
        ]
        for line in self.lines:
            line.start()

    def finish(self):
        for line in self.lines:
            line.finish()


class Scatter:
    def __init__(self, zs, z_flag, planes, given, final, stage, twin_in, half_in, full_in, z_in, l_sem, c_ssem, c_rsem, h_ssem,
                 h_rsem, f_ssem, f_rsem, z_ssem, z_rsem):
        self.__dict__.update(locals())
        self.z, self.c, self.r = place()
        self.line = corners(self.r)
        self.s = self.z * 2 + self.c
        self.twin = (self.z * 2 + 1 - self.c, self.r)
        self.rows = twin_in.shape[2]
        self.step = 16
        self.spots = (3, 1, 2, 0) if planes else (0,)
        self.zs = zs if z_flag else 1
        self.order = list(range(1, self.zs)) + [0]
        self.pending = []
        self.loads = []
        self.settled = 0

    def at_z(self, k):
        return (lax.rem(self.z + k, self.zs) * 2 + self.c, self.r)

    def block(self, k, other, j):
        if not self.z_flag:
            return self.given.at[other, j]
        zz, core = lax.rem(self.z + k, self.zs), 1 - self.c if other else self.c
        return self.given.at[zz, core, self.line[j]] if self.planes else self.given.at[zz, core]

    def start(self, copy):
        copy.start()
        self.pending.append(copy.wait_send)

    def begin(self, schedule):
        for k in self.order:
            for j in self.spots:
                self.start(self.twin_copy(k, j, self.block(k, 1, j)))
        if self.stage is not None:
            self.loads = [
                pltpu.make_async_copy(self.block(k, 0, j), self.stage.at[n % 2], self.l_sem.at[n % 2])
                for n, (k, j) in enumerate(schedule)
            ]
            for load in self.loads[:2]:
                load.start()

    def twin_copy(self, k, j, src):
        dst = self.twin_in.at[k, j]
        return send(dst if src is None else src, dst, self.c_ssem.at[k, j], self.c_rsem.at[k, j], self.twin)

    def settle(self, k, j, parts):
        own = self.block(k, 0, j)
        n = self.settled
        if self.stage is not None:
            self.loads[n].wait()
            own = self.stage.at[n % 2]
        self.twin_copy(k, j, None).wait_recv()
        step = self.step
        for first, last, more in parts:

            def body(i, carry, first=first, more=more):
                at = pl.ds(pl.multiple_of(first + i * step, step), step)
                value = own[at, :].astype(jnp.float32) + self.twin_in[k, j, at, :].astype(jnp.float32)
                for ref, offset in more:
                    there = pl.ds(pl.multiple_of(first - offset + i * step, step), step)
                    value = value + ref[there, :].astype(jnp.float32)
                if k == 0 and j == 0:
                    self.final(at, value)
                else:
                    self.twin_in[k, j, at, :] = value.astype(self.twin_in.dtype)
                return carry

            lax.fori_loop(0, (last - first) // step, body, 0)
        if n + 2 < len(self.loads):
            self.loads[n + 2].start()
        self.settled = n + 1

    def half_copy(self, k, n, src):
        dst = self.half_in.at[k, n]
        return send(dst if src is None else src, dst, self.h_ssem.at[k, n], self.h_rsem.at[k, n], (self.s, self.line[n + 1]))

    def full_copy(self, k, j, src):
        dst = self.full_in.at[k, j - 1]
        return send(dst if src is None else src, dst, self.f_ssem.at[k, j - 1], self.f_rsem.at[k, j - 1], (self.s, self.line[j]))

    def z_copy(self, k, src):
        dst = self.z_in.at[k]
        return send(dst if src is None else src, dst, self.z_ssem.at[k], self.z_rsem.at[k], self.at_z(k))

    def stage_a(self, k):
        half = self.rows // 2
        self.settle(k, 3, [(0, self.rows, [])])
        self.start(self.half_copy(k, 1, self.twin_in.at[k, 3, pl.ds(half, half)]))
        self.start(self.half_copy(k, 0, self.twin_in.at[k, 3, pl.ds(0, half)]))

    def stage_b(self, k):
        half = self.rows // 2
        for j in (1, 2):
            n = 2 - j
            self.half_copy(k, n, None).wait_recv()
            more = [(self.half_in.at[k, n], half if n else 0)]
            self.settle(k, j, [(0, half, [] if n else more), (half, self.rows, more if n else [])])
            self.start(self.full_copy(k, j, self.twin_in.at[k, j]))

    def stage_c(self, k):
        more = []
        if self.planes:
            for j in (1, 2):
                self.full_copy(k, j, None).wait_recv()
                more.append((self.full_in.at[k, j - 1], 0))
        if not k:
            for other in range(1, self.zs):
                self.z_copy(other, None).wait_recv()
                more.append((self.z_in.at[other], 0))
        self.settle(k, 0, [(0, self.rows, more)])
        if k:
            self.start(self.z_copy(k, self.twin_in.at[k, 0]))

    def end(self):
        for wait in self.pending:
            wait()


def scatter_scratch(zs, planes, rows, columns, staged):
    sem = pltpu.SemaphoreType.DMA
    low, least = jnp.bfloat16, (1, 2, 16, 128)
    spots = 4 if planes else 1
    return [
        pltpu.VMEM((2, rows, columns) if staged else (16, 128), low),
        pltpu.VMEM((zs, spots, rows, columns), low),
        pltpu.VMEM((zs, 2, rows // 2, columns) if planes else least, low),
        pltpu.VMEM((zs, 2, rows, columns) if planes else least, low),
        pltpu.VMEM((zs, rows, columns) if zs > 1 else least[1:], low),
        sem((2,)), sem((zs, 4)), sem((zs, 4)), sem((zs, 2)), sem((zs, 2)), sem((zs, 2)), sem((zs, 2)), sem((zs,)), sem((zs,)),
    ]


SCATTER_REFS = 14


def scatter_plan(items):
    rounds = []
    for n in range(len(items) + 2):
        rounds.append([])
        for back, stage in enumerate(("a", "b", "c")):
            if 0 <= n - back < len(items):
                name, k = items[n - back]
                if stage != "c" or k:
                    rounds[-1].append((name, stage, k))
    rounds.append([(name, "c", 0) for name, k in items if not k])
    places = {"a": (3,), "b": (1, 2), "c": (0,)}
    schedules = {}
    for name, stage, k in sum(rounds, []):
        schedules.setdefault(name, []).extend((k, j) for j in places[stage])
    return rounds, schedules


def run_stage(scatters, name, stage, k):
    {"a": Scatter.stage_a, "b": Scatter.stage_b, "c": Scatter.stage_c}[stage](scatters[name], k)


class SumChain:
    def __init__(self, zs, parts, got, held, sems, l_sem):
        self.__dict__.update(locals())
        self.z = place()[0]

    def own(self, to):
        return self.parts.at[lax.rem(self.z + to + self.zs, self.zs)]

    def fetch(self, k):
        self.loads = [
            pltpu.make_async_copy(self.own(-k), self.held.at[0], self.l_sem.at[0]),
            pltpu.make_async_copy(self.own(k), self.held.at[1], self.l_sem.at[1]),
        ]
        for load in self.loads:
            load.start()

    def add(self, into, more):
        ref = self.got[into]
        ref[...] = (ref[...].astype(jnp.float32) + self.held[more].astype(jnp.float32)).astype(ref.dtype)

    def start(self, k):
        zs, z, got = self.zs, self.z, self.got
        up, down = k - 1, zs - 2 + k
        self.lines = [
            Line(zs, 1, 0, 1, self.own(-k), got[up], self.sems.at[up]),
            Line(zs, -1, zs - 1, zs, self.own(k), got[down], self.sems.at[down]),
        ]
        if k > 1:
            for load in self.loads:
                load.wait()
            pl.when((z >= 1) & (z < k))(functools.partial(self.add, up - 1, 0))
            pl.when((z >= zs - k) & (z < zs - 1))(functools.partial(self.add, down - 1, 1))
            self.lines += [
                Line(zs, 1, 1, k, got[up - 1], got[up], self.sems.at[up]),
                Line(zs, -1, zs - k, zs - 1, got[down - 1], got[down], self.sems.at[down]),
            ]
        for line in self.lines:
            line.start()
        if k < zs - 1 and self.got[up + 1] is not None:
            self.fetch(k + 1)
        elif k == zs - 1:
            self.loads = [pltpu.make_async_copy(self.own(0), self.held.at[0], self.l_sem.at[0])]
            self.loads[0].start()

    def finish(self):
        for line in self.lines:
            line.finish()

    def total(self):
        zs, z = self.zs, self.z
        self.loads[0].wait()

        def add(come):
            self.held[0] = (self.held[0].astype(jnp.float32) + self.got[come][...].astype(jnp.float32)).astype(self.held.dtype)

        pl.when(z > 0)(functools.partial(add, zs - 2))
        pl.when(z < zs - 1)(functools.partial(add, 2 * zs - 3))


def partner(tensor):
    lanes = tensor.shape[-1]
    half = HEAD_DIM // 2
    lane = lax.broadcasted_iota(jnp.int32, tensor.shape, tensor.ndim - 1)
    ahead = pltpu.roll(tensor, lanes - half, tensor.ndim - 1)
    behind = pltpu.roll(tensor, half, tensor.ndim - 1)
    return jnp.where(lax.rem(lane, HEAD_DIM) < half, ahead, behind)


def stack_heads(block, first):
    return jnp.concatenate(
        [block[:, (first + h) * HEAD_DIM : (first + h + 1) * HEAD_DIM] for h in range(GROUP)], axis=0
    )


def unstack_heads(stacked, span):
    return jnp.concatenate([stacked[h * span : (h + 1) * span] for h in range(GROUP)], axis=1)


def load_window(inverse_ref, kv_ref, window, first_block):
    half_len = kv_ref.shape[1] // 2
    for n in range(window.shape[0] // half_len):
        slot = inverse_ref[first_block + n]
        at = pl.ds(pl.multiple_of(lax.rem(slot, 2) * half_len, half_len), half_len)
        window[n * half_len : (n + 1) * half_len, :] = kv_ref[lax.div(slot, 2), at, :]


def window_of(order_ref, first_ref, count, half_len):
    m, half = pl.program_id(0), pl.program_id(1)
    my_block = order_ref[lax.axis_index("seq") * 2 + half]
    half_blocks = count // half_len // 2
    first_block = jnp.where(my_block >= half_blocks, half_blocks, 0)
    return first_block, my_block * half_len, first_ref[m]


def attend_kernel(order_ref, inverse_ref, first_ref, lin_ref, cos_ref, sin_ref, kv_ref, q_ref, out_ref, window, bias):
    span = lin_ref.shape[0]
    wide = window.shape[0]
    first_block, my_place, first = window_of(order_ref, first_ref, 2 * wide, span)
    load_window(inverse_ref, kv_ref, window, first_block)
    key_place = first_block * span + lax.broadcasted_iota(jnp.int32, (span, wide), 1)
    place_here = my_place + lax.broadcasted_iota(jnp.int32, (span, wide), 0)
    start = jnp.where(place_here >= first, first, 0)
    bias[...] = jnp.where((key_place <= place_here) & (key_place >= start), 0.0, NEG_LARGE)
    width = GROUP * HEAD_DIM
    cosine = jnp.concatenate([cos_ref[...]] * (width // 128), axis=1)
    sine = jnp.concatenate([sin_ref[...]] * (width // 128), axis=1)
    for g in range(KV_HEADS):
        at = slice(g * width, (g + 1) * width)
        lin = lin_ref[:, at]
        query = (lin * cosine + partner(lin) * sine).astype(jnp.bfloat16) * jnp.bfloat16(HEAD_DIM ** -0.5)
        q_ref[:, at] = query
        key = window[:, g * HEAD_DIM : (g + 1) * HEAD_DIM]
        value = window[:, KVW + g * HEAD_DIM : KVW + (g + 1) * HEAD_DIM]
        scores = product_nt(stack_heads(query, 0), key).reshape(GROUP, span, wide) + bias[...][None]
        exps = jnp.exp(scores - jnp.max(scores, axis=-1, keepdims=True))
        total = jnp.sum(exps, axis=-1, keepdims=True).reshape(GROUP * span, 1)
        mixed = product(exps.astype(jnp.bfloat16).reshape(GROUP * span, wide), value) / total
        out_ref[:, at] = unstack_heads(mixed, span).astype(jnp.bfloat16)


def attend_back_heads(queries, d_heads, key, value, bias, span):
    query, d_mixed = stack_heads(queries, 0), stack_heads(d_heads, 0)
    scores = product_nt(key, query) + bias[...]
    exps = jnp.exp(scores - jnp.max(scores, axis=0, keepdims=True))
    probs = exps * (1.0 / jnp.sum(exps, axis=0, keepdims=True))
    weighted = probs * product_nt(value, d_mixed)
    delta = jnp.sum(weighted, axis=0, keepdims=True)
    d_scores = (weighted - probs * delta).astype(jnp.bfloat16)
    d_query = unstack_heads(product_tn(d_scores, key) * HEAD_DIM ** -0.5, span)
    return product(d_scores, query), product(probs.astype(jnp.bfloat16), d_mixed), d_query


def attend_back_kernel(order_ref, inverse_ref, first_ref, q_ref, d_ref, cos_ref, sin_ref, kv_ref, dq_ref, dkv_ref, window, bias, sums):
    span = q_ref.shape[0]
    wide = window.shape[0]
    rows = GROUP * span
    half = pl.program_id(1)
    first_block, my_place, first = window_of(order_ref, first_ref, 2 * wide, span)
    load_window(inverse_ref, kv_ref, window, first_block)
    key_place = first_block * span + lax.broadcasted_iota(jnp.int32, (wide, rows), 0)
    place_here = my_place + lax.rem(lax.broadcasted_iota(jnp.int32, (wide, rows), 1), span)
    start = jnp.where(place_here >= first, first, 0)
    bias[...] = jnp.where((key_place <= place_here) & (key_place >= start), 0.0, NEG_LARGE)

    @pl.when(half == 0)
    def _():
        sums[...] = jnp.zeros_like(sums)

    width = GROUP * HEAD_DIM
    cosine = jnp.concatenate([cos_ref[...]] * (width // 128), axis=1)
    sine = jnp.concatenate([sin_ref[...]] * (width // 128), axis=1)
    d_keys, d_values = [], []
    for g in range(KV_HEADS):
        at = slice(g * width, (g + 1) * width)
        key = window[:, g * HEAD_DIM : (g + 1) * HEAD_DIM]
        value = window[:, KVW + g * HEAD_DIM : KVW + (g + 1) * HEAD_DIM]
        d_key, d_value, d_query = attend_back_heads(q_ref[:, at], d_ref[:, at], key, value, bias, span)
        d_keys.append(d_key)
        d_values.append(d_value)
        dq_ref[:, at] = (d_query * cosine - partner(d_query) * sine).astype(jnp.bfloat16)
    d_window = jnp.concatenate(d_keys + d_values, axis=1)
    for n in range(wide // span):
        slot = inverse_ref[first_block + n]
        to = pl.ds(pl.multiple_of(lax.rem(slot, 2) * span, span), span)
        sums[lax.div(slot, 2), to, :] += d_window[n * span : (n + 1) * span]

    @pl.when(half == 1)
    def _():
        dkv_ref[...] = sums[...].astype(jnp.bfloat16)


def attention_specs(seq, micro, span):
    half_len = span // 2

    def rows(width):
        return pl.BlockSpec((half_len, width), lambda m, h, *_: (m * 2 + h, 0))

    whole = pl.BlockSpec((seq, span, 2 * KVW), lambda m, h, *_: (0, m, 0))
    return half_len, rows, whole


def attend(order, inverse, first, lin, cosine, sine, kv):
    seq, many, _ = kv.shape
    micro = first.shape[0]
    span = many // micro
    half_len, rows, whole = attention_specs(seq, micro, span)
    wide = seq * span // 2
    return pl.pallas_call(
        attend_kernel,
        grid_spec=pltpu.PrefetchScalarGridSpec(
            num_scalar_prefetch=3,
            grid=(micro, 2),
            in_specs=[rows(D), rows(128), rows(128), whole],
            out_specs=[rows(D), rows(D)],
            scratch_shapes=[pltpu.VMEM((wide, 2 * KVW), jnp.bfloat16), pltpu.VMEM((half_len, wide), jnp.float32)],
        ),
        out_shape=[jax.ShapeDtypeStruct((many, D), jnp.bfloat16)] * 2,
        compiler_params=pltpu.CompilerParams(vmem_limit_bytes=48 * MIB),
        cost_estimate=pl.CostEstimate(flops=8 * many * wide * D, bytes_accessed=16 * MIB, transcendentals=many * wide * HEADS),
    )(order, inverse, first, lin, cosine, sine, kv)


def attend_back(order, inverse, first, queries, d_heads, cosine, sine, kv):
    seq, many, _ = kv.shape
    micro = first.shape[0]
    span = many // micro
    half_len, rows, whole = attention_specs(seq, micro, span)
    wide = seq * span // 2
    return pl.pallas_call(
        attend_back_kernel,
        grid_spec=pltpu.PrefetchScalarGridSpec(
            num_scalar_prefetch=3,
            grid=(micro, 2),
            in_specs=[rows(D), rows(D), rows(128), rows(128), whole],
            out_specs=[rows(D), whole],
            scratch_shapes=[
                pltpu.VMEM((wide, 2 * KVW), jnp.bfloat16),
                pltpu.VMEM((wide, GROUP * half_len), jnp.float32),
                pltpu.VMEM((seq, span, 2 * KVW), jnp.float32),
            ],
        ),
        out_shape=[jax.ShapeDtypeStruct((many, D), jnp.bfloat16), jax.ShapeDtypeStruct(kv.shape, jnp.bfloat16)],
        compiler_params=pltpu.CompilerParams(vmem_limit_bytes=56 * MIB),
        cost_estimate=pl.CostEstimate(flops=20 * many * wide * D, bytes_accessed=24 * MIB, transcendentals=many * wide * HEADS),
    )(order, inverse, first, queries, d_heads, cosine, sine, kv)


def assemble(zs, pieces, whole, sem):
    if len(pieces) == 1:
        copy = pltpu.make_async_copy(pieces[0], whole, sem.at[0])
        copy.start()
        return [copy]
    z = lax.div(lax.axis_index("seq"), 2)
    size = whole.shape[0] // zs

    def rows(zz):
        return whole.at[pl.ds(pl.multiple_of(zz * size, size), size)]

    if len(pieces) == 2:
        pieces = [pieces[0], *(pieces[1].at[k] for k in range(zs - 1))]
    copies = [pltpu.make_async_copy(pieces[0], rows(z), sem.at[0])]
    copies[0].start()
    for k in range(1, zs):
        to = rows(lax.rem(z - k + zs, zs))
        below = pltpu.make_async_copy(pieces[k], to, sem.at[k])
        if len(pieces) == zs:
            below.start()
        else:
            above = pltpu.make_async_copy(pieces[2 * zs - 1 - k], to, sem.at[k])
            pl.when(z >= k)(below.start)
            pl.when(z < k)(above.start)
        copies.append(below)
    return copies


class Around:
    def __init__(self, zs, block, got, sems):
        z, c, r = place()
        self.copies = [
            send(block(k), got.at[k - 1], sems.at[k - 1, 0], sems.at[k - 1, 1], (lax.rem(z + k, zs) * 2 + c, r))
            for k in range(1, zs)
        ]

    def start(self):
        for copy in self.copies:
            copy.start()

    def finish(self):
        for copy in self.copies:
            copy.wait()


def swiglu(lin, d_hidden):
    n = d_hidden.shape[1]
    gate, upper = lin[:, :n], lin[:, n:]
    sig = 1.0 / (1.0 + jnp.exp(-gate))
    act = gate * sig
    d_gate = d_hidden * upper * (sig * (1.0 + gate * (1.0 - sig)))
    d_both = jnp.concatenate([d_gate.astype(jnp.bfloat16), (d_hidden * act).astype(jnp.bfloat16)], axis=1)
    return (act * upper).astype(jnp.bfloat16), d_both


def add_gradients(x, dy, hidden, d_both, both_sum, down_sum):
    for at in range(0, D, 256):
        both_sum[at : at + 256, :] += product_tn(x[:, at : at + 256], d_both)
    part = hidden.shape[1] // 4
    for at in range(0, hidden.shape[1], part):
        down_sum[at : at + part, :] += product_tn(hidden[:, at : at + part], dy)


def put_gradients(sums, staged, out, sem):
    copies = []
    for n in range(2):
        staged[n][...] = sums[n][...].astype(jnp.bfloat16)
        copies.append(pltpu.make_async_copy(staged[n], out[n], sem.at[n, 0]))
        copies[-1].start()
    for copy in copies:
        copy.wait()


def ffn_first_kernel(zs, count, *refs):
    x_ref, dy_ref = refs[:2]
    both_pieces, down_pieces = refs[2 : 2 + count], refs[2 + count : 2 + 2 * count]
    hidden_ref, d_both_ref, g_both_ref, g_down_ref, both_w, down_w, both_sum, down_sum, sem = refs[2 + 2 * count :]
    step, last = pl.program_id(0), pl.num_programs(0) - 1

    @pl.when(step == 0)
    def _():
        copies = assemble(zs, both_pieces, both_w, sem.at[0]) + assemble(zs, down_pieces, down_w, sem.at[1])
        both_sum[...] = jnp.zeros_like(both_sum)
        down_sum[...] = jnp.zeros_like(down_sum)
        for copy in copies:
            copy.wait()

    x, dy = x_ref[...], dy_ref[...]
    hidden, d_both = swiglu(product(x, both_w[...]), product_nt(dy, down_w[...]))
    hidden_ref[...] = hidden
    d_both_ref[...] = d_both
    add_gradients(x, dy, hidden, d_both, both_sum, down_sum)

    @pl.when(step == last)
    def _():
        put_gradients((both_sum, down_sum), (both_w, down_w), (g_both_ref, g_down_ref), sem)


def ffn_second_kernel(zs, counts, linked, *refs):
    x_ref, dy_ref, hidden_ref, d_both_ref = refs[:4]
    refs = refs[4:]
    pieces = []
    for count in counts:
        pieces += [refs[:count], refs[count : 2 * count]]
        refs = refs[2 * count :]
    if linked:
        g_both_one, g_down_one, *refs = refs
    out_ref, dx_ref, g_both_ref, g_down_ref, *refs = refs
    if linked:
        *got, both_one, down_one, both_w, down_w, both_sum, down_sum, stage, sem, z_sem = refs
    else:
        got, (both_one, down_one, both_w, down_w, both_sum, down_sum, stage, sem) = [], refs
    n, wide = stage.shape[1] // 2, down_w.shape[0]
    down_rows = down_w.at[pl.ds(0, n)]
    step, last = pl.program_id(0), pl.num_programs(0) - 1
    lines = []
    if linked:
        z = lax.div(lax.axis_index("seq"), 2)
        for at, parts in ((0, g_both_one), (2, g_down_one)):
            lines += [
                Line(zs, 1, 0, 1, parts.at[lax.rem(z + zs - 1, zs)], got[at], z_sem.at[at]),
                Line(zs, -1, zs - 1, zs, parts.at[lax.rem(z + 1, zs)], got[at + 1], z_sem.at[at + 1]),
            ]

    @pl.when(step == 0)
    def _():
        copies = []
        for which, whole in enumerate((both_one, down_one, stage, down_rows)):
            copies += assemble(zs, pieces[which], whole, sem.at[which])
        if linked:
            greet(neighbours(zs, False, False))
            for line in lines:
                line.start()
        both_sum[...] = jnp.zeros_like(both_sum)
        down_sum[...] = jnp.zeros_like(down_sum)
        if wide > n:
            both_w[...] = jnp.zeros_like(both_w)
            down_w[n:, :] = jnp.zeros((wide - n, D), down_w.dtype)
        for copy in copies:
            copy.wait()
        both_w[:, :n] = stage[:, :n]
        both_w[:, wide : wide + n] = stage[:, n:]

    x, dy = x_ref[...], dy_ref[...]
    hidden, d_both = swiglu(product(x, both_w[...]), product_nt(dy, down_w[...]))
    dx_ref[...] = (product_nt(d_both_ref[...], both_one[...]) + product_nt(d_both, both_w[...])).astype(jnp.bfloat16)
    out_ref[...] = (product(hidden_ref[...], down_one[...]) + product(hidden, down_w[...])).astype(jnp.bfloat16)
    add_gradients(x, dy, hidden, d_both, both_sum, down_sum)

    @pl.when(step == last)
    def _():
        stage[:, :n] = both_sum[:, :n].astype(jnp.bfloat16)
        stage[:, n:] = both_sum[:, wide : wide + n].astype(jnp.bfloat16)
        down_w[...] = down_sum[...].astype(jnp.bfloat16)
        copies = [
            pltpu.make_async_copy(stage, g_both_ref, sem.at[0, 0]), pltpu.make_async_copy(down_rows, g_down_ref, sem.at[1, 0])
        ]
        for copy in copies:
            copy.start()
        for copy in copies:
            copy.wait()
        for line in lines:
            line.finish()


def ffn_first(x, dy, both_pieces, down_pieces, zs):
    count, n = len(both_pieces), down_pieces[0].shape[0] * (zs if len(down_pieces) > 1 else 1)
    block, low, full = 256, jnp.bfloat16, jnp.float32
    sem, shape = pltpu.SemaphoreType.DMA, jax.ShapeDtypeStruct
    anywhere = pl.BlockSpec(memory_space=pl.ANY)

    def tokens(width):
        return pl.BlockSpec((block, width), lambda i: (i, 0))

    return pl.pallas_call(
        functools.partial(ffn_first_kernel, zs, count),
        grid=(x.shape[0] // block,),
        in_specs=[tokens(D)] * 2 + [anywhere] * (2 * count),
        out_specs=[tokens(n), tokens(2 * n)] + [anywhere] * 2,
        out_shape=[shape((x.shape[0], n), low), shape((x.shape[0], 2 * n), low), shape((D, 2 * n), low), shape((n, D), low)],
        scratch_shapes=[
            pltpu.VMEM((D, 2 * n), low), pltpu.VMEM((n, D), low), pltpu.VMEM((D, 2 * n), full), pltpu.VMEM((n, D), full),
            sem((2, zs)),
        ],
        compiler_params=pltpu.CompilerParams(vmem_limit_bytes=56 * MIB),
        cost_estimate=LONG,
    )(x, dy, *both_pieces, *down_pieces)


def ffn_second(x, dy, hidden, d_both, one, two, zs, parts=(), collective_id=None):
    counts = (len(one[0]), len(two[0]))
    wides = [down[0].shape[0] * (zs if len(down) > 1 else 1) for _, down in (one, two)]
    n = wides[1]
    wide = -(-n // 128) * 128
    block, low, full = 256, jnp.bfloat16, jnp.float32
    sem, shape = pltpu.SemaphoreType.DMA, jax.ShapeDtypeStruct
    anywhere = pl.BlockSpec(memory_space=pl.ANY)

    def tokens(width):
        return pl.BlockSpec((block, width), lambda i: (i, 0))

    linked = bool(parts)
    params = dict(collective_id=collective_id, has_side_effects=True) if linked else {}
    return pl.pallas_call(
        functools.partial(ffn_second_kernel, zs, counts, linked),
        grid=(x.shape[0] // block,),
        in_specs=[tokens(D)] * 2 + [tokens(wides[0]), tokens(2 * wides[0])] + [anywhere] * (2 * sum(counts) + len(parts)),
        out_specs=[tokens(D)] * 2 + [anywhere] * (2 + 2 * len(parts)),
        out_shape=[shape(x.shape, low)] * 2 + [shape((D, 2 * n), low), shape((n, D), low)]
        + [shape(part.shape[1:], low) for part in parts for _ in range(2)],
        scratch_shapes=[
            pltpu.VMEM((D, 2 * wides[0]), low), pltpu.VMEM((wides[0], D), low),
            pltpu.VMEM((D, 2 * wide), low), pltpu.VMEM((wide, D), low),
            pltpu.VMEM((D, 2 * wide), full), pltpu.VMEM((wide, D), full), pltpu.VMEM((D, 2 * n), low),
            sem((4, zs)),
        ] + [sem((4, 2))] * linked,
        compiler_params=pltpu.CompilerParams(vmem_limit_bytes=56 * MIB, **params),
        cost_estimate=LONG,
    )(x, dy, hidden, d_both, *one[0], *one[1], *two[0], *two[1], *parts)


def split_unit(unit):
    return unit * 3 // 4 // 16 * 16


def portions(unit):
    first = split_unit(unit)
    return (0, first), (first, unit - first)


def spread_kernel(zs, rows, unit, gate_ref, up_ref, *out):
    for (begin, size), ref in zip(portions(unit), out):
        for c in range(2):
            for r in range(rows):
                for n, weight in enumerate((gate_ref, up_ref)):
                    for z in range(zs):
                        at = ((z * 2 + c) * rows + r) * unit + begin
                        to = (n * zs + z) * size
                        ref[c, r, :, to : to + size] = weight[:, at : at + size]


def spread(gate, up, zs, rows):
    wide, part = gate.shape
    unit = part // (zs * 2 * rows)
    return pl.pallas_call(
        functools.partial(spread_kernel, zs, rows, unit),
        out_shape=[jax.ShapeDtypeStruct((2, rows, wide, 2 * zs * size), gate.dtype) for _, size in portions(unit)],
    )(gate, up)


def collect_kernel(zs, rows, unit, *refs):
    given, outs = refs[:2], refs[2:]
    for n, out in enumerate(outs):
        for (begin, size), ref in zip(portions(unit), given):
            for c in range(2):
                for r in range(rows):
                    for z in range(zs):
                        at = ((z * 2 + c) * rows + r) * unit + begin
                        to = (n * zs + z) * size
                        out[:, at : at + size] = ref[c, r, :, to : to + size].astype(jnp.float32)


def collect(blocks, zs, rows, unit):
    shape = jax.ShapeDtypeStruct((blocks[0].shape[2], unit * zs * 2 * rows), jnp.float32)
    return pl.pallas_call(functools.partial(collect_kernel, zs, rows, unit), out_shape=[shape, shape])(*blocks)


def forward_kernel(zs, micro, *refs):
    order_ref, places_ref, first_ref, freq_ref, x_ref, pack_ref, both_ref, down_ref, out_ref, dy_ref, rest_ref, last_ref = refs[:12]
    refs = refs[2:]
    packed, both_own, kv_all, out_all, dy_all, ffn_all, rest_own, rest_got, last_got = refs[10:19]
    refs = refs[3:]
    steps = 2 * zs - 2
    both_got, down_got = refs[16 : 16 + steps], refs[16 + steps : 16 + 2 * steps]
    q_ref, attn_ref, attended_ref, middle_ref, gains_ref, cos_ref, sin_ref = refs[16 + 2 * steps : 23 + 2 * steps]
    (staged, lin, kv_own, kv_here, window, bias, out_w, ffn_own, sems, *more) = refs[23 + 2 * steps :]
    low = jnp.bfloat16
    z, c, r = place()
    many = x_ref.shape[0]
    span = many // micro
    half_len = span // 2
    rows = D // zs
    greet(neighbours(zs, True, True))

    exchange = Exchange(both_ref, both_own, *more[:3])
    rest = Exchange(rest_ref, rest_own, *more[3:6])
    arounds = [Around(zs, lambda k: rest_own, rest_got, more[6].at[0]), Around(zs, lambda k: last_ref, last_got, more[6].at[1])]
    more = more[:3] + more[7:]
    both_chain, down_chain = Chain(zs, both_own, both_got, more[3]), Chain(zs, down_ref, down_got, more[4])
    more = more[5:]
    weights = Gather(zs, True, True, pack_ref, packed, *more[:9])
    outs = Gather(zs, True, True, out_ref, out_all, *more[9:18])
    pairs = Gather(zs, True, False, kv_own, kv_all, *more[18:27])
    dys = Gather(zs, False, True, dy_ref, dy_all, *more[27:36])
    ffns = Gather(zs, False, True, ffn_own, ffn_all, *more[36:45])

    weights.launch()
    exchange.start()
    weights.begin(0)
    outs.launch()
    rest.start()

    lane = lax.broadcasted_iota(jnp.int32, (half_len, 128), 1)
    for i in range(2 * micro):
        place_here = order_ref[(z * 2 + c) * 2 + i % 2] * half_len + lax.broadcasted_iota(jnp.int32, (half_len, 128), 0)
        start = jnp.where(place_here >= first_ref[i // 2], first_ref[i // 2], 0)
        angle = (place_here - start).astype(jnp.float32) * freq_ref[...]
        cos_ref[i * half_len : (i + 1) * half_len, :] = jnp.cos(angle)
        sine = jnp.sin(angle)
        sin_ref[i * half_len : (i + 1) * half_len, :] = jnp.where(lax.rem(lane, HEAD_DIM) < HEAD_DIM // 2, -sine, sine)
    x = x_ref[...].astype(jnp.float32)
    factor = rms_factor(x)

    loads = {}

    def load(n):
        weights.complete(n)
        zz = lax.rem(z - weights.kth[n] + zs, zs)
        loads[n] = pltpu.make_async_copy(packed.at[zz], staged.at[n % 2], sems.at[n % 2])
        loads[n].start()

    def project(n):
        loads[n].wait()
        zz = lax.rem(z - weights.kth[n] + zs, zs)
        at = pl.ds(pl.multiple_of(zz * rows, rows), rows)
        block = staged[n % 2].reshape(rows, PACK)
        gains = block[:, QKV:].astype(jnp.float32).T[:8]
        gains_ref[:, at] = gains
        attn_in = (x_ref[:, at].astype(jnp.float32) * factor * gains[0:1]).astype(low)
        attn_ref[:, at] = attn_in
        value = product(attn_in, block[:, :QKV])
        lin[...] = value if n == 0 else lin[...] + value

    weights.arrive(1)
    weights.begin(1)
    weights.forward(0)
    weights.arrive(2)
    weights.begin(2)
    weights.forward(1)
    weights.finish(0)
    weights.arrive(3)
    weights.begin(3)
    down_chain.start(1)
    exchange.finish()
    both_chain.start(1)
    outs.arrive(1)
    weights.forward(2)
    weights.finish(1)
    load(0)
    outs.arrive(2)
    weights.forward(3)
    weights.finish(2)
    outs.begin(0)
    load(1)
    project(0)
    outs.arrive(3)
    outs.begin(1)
    project(1)
    weights.finish(3)
    dys.launch()
    dys.begin(0)
    load(2)
    load(3)
    project(2)
    project(3)

    width = GROUP * HEAD_DIM
    cosine = jnp.concatenate([cos_ref[...]] * (width // 128), axis=1)
    sine = jnp.concatenate([sin_ref[...]] * (width // 128), axis=1)

    def turned(block, w):
        return block * cosine[:, :w] + partner(block) * sine[:, :w]

    kv_own[:, :KVW] = turned(lin[:, D : D + KVW], KVW).astype(low)
    kv_own[:, KVW:] = lin[:, D + KVW :].astype(low)
    pairs.launch()
    pairs.begin(0)
    for g in range(KV_HEADS):
        at = slice(g * width, (g + 1) * width)
        q_ref[:, at] = turned(lin[:, at], width).astype(low) * low(HEAD_DIM ** -0.5)
    outs.forward(0)
    outs.begin(2)
    both_chain.finish()
    down_chain.finish()
    both_chain.start(2)
    down_chain.start(2)
    rest.finish()
    for one in arounds:
        one.start()
    for k in range(1, zs):
        pairs.arrive(k)
        pairs.begin(k)
    outs.forward(1)
    outs.finish(0)
    outs.begin(3)
    for k in range(zs):
        pairs.complete(k)
    kv_load = pltpu.make_async_copy(kv_all, kv_here, sems.at[2])
    kv_load.start()
    outs.forward(2)
    outs.finish(1)
    kv_load.wait()

    wide = window.shape[0]
    half_blocks = wide // half_len

    def attend_some(i, carry):
        m, half = lax.div(i, 2), lax.rem(i, 2)
        my_block = order_ref[(z * 2 + c) * 2 + half]
        first_block = jnp.where(my_block >= half_blocks, half_blocks, 0)
        wanted = first_block * half_len + lax.broadcasted_iota(jnp.int32, (wide, 2 * wide), 0)
        chosen = jnp.where(places_ref[...] == wanted, 1.0, 0.0).astype(low)
        at = pl.ds(pl.multiple_of(m * span, span), span)
        window[...] = product(chosen, kv_here[:, :, at, :].reshape(2 * wide, 2 * KVW)).astype(low)
        key_place = first_block * half_len + lax.broadcasted_iota(jnp.int32, (half_len, wide), 1)
        place_here = my_block * half_len + lax.broadcasted_iota(jnp.int32, (half_len, wide), 0)
        first = first_ref[m]
        start = jnp.where(place_here >= first, first, 0)
        bias[...] = jnp.where((key_place <= place_here) & (key_place >= start), 0.0, NEG_LARGE)
        here = pl.ds(pl.multiple_of(i * half_len, half_len), half_len)
        for g in range(KV_HEADS):
            at = slice(g * width, (g + 1) * width)
            key = window[:, g * HEAD_DIM : (g + 1) * HEAD_DIM]
            value = window[:, KVW + g * HEAD_DIM : KVW + (g + 1) * HEAD_DIM]
            scores = product_nt(stack_heads(q_ref[here, at], 0), key).reshape(GROUP, half_len, wide) + bias[...][None]
            exps = jnp.exp(scores - jnp.max(scores, axis=-1, keepdims=True))
            total = jnp.sum(exps, axis=-1, keepdims=True).reshape(GROUP * half_len, 1)
            mixed = product(exps.astype(low).reshape(GROUP * half_len, wide), value) / total
            attended_ref[here, at] = unstack_heads(mixed, half_len).astype(low)
        return carry

    lax.fori_loop(0, 2 * micro, attend_some, 0)
    outs.forward(3)
    outs.finish(2)
    outs.finish(3)
    dys.forward(0)
    for k in range(zs):
        outs.complete(k)
    out_load = pltpu.make_async_copy(out_all, out_w, sems.at[3])
    out_load.start()
    dys.finish(0)
    out_load.wait()
    middle = x_ref[...].astype(jnp.float32) + product(attended_ref[...], out_w[...].reshape(D, D))
    middle_ref[...] = middle
    ffn_own[...] = (middle * rms_factor(middle) * gains_ref[1:2, :]).astype(low)
    ffns.launch()
    ffns.begin(0)
    both_chain.finish()
    down_chain.finish()
    both_chain.start(3)
    down_chain.start(3)
    dys.complete(0)
    ffns.forward(0)
    ffns.finish(0)
    ffns.complete(0)
    both_chain.finish()
    down_chain.finish()
    for one in arounds:
        one.finish()
    rest.end()
    exchange.end()
    for one in (weights, outs, pairs, dys, ffns):
        one.end()


def places_of(order, span):
    return (order[:, None] * (span // 2) + jnp.arange(span // 2, dtype=jnp.int32)).reshape(1, -1)


def forward(order, first, tokens, pack, both, rest, down, last, w_out, dy, zs, collective_id):
    many = tokens.shape[0]
    micro = first.shape[0]
    seq = 2 * zs
    wide = seq * (many // micro) // 2
    low, full = jnp.bfloat16, jnp.float32
    freq = 10000.0 ** (-(jnp.arange(128, dtype=jnp.int32) % (HEAD_DIM // 2)).astype(full) / (HEAD_DIM // 2))
    anywhere, here, smem = (pl.BlockSpec(memory_space=m) for m in (pl.ANY, pltpu.VMEM, pltpu.SMEM))
    shape = jax.ShapeDtypeStruct
    out_any = [
        shape((zs, 2, 4) + pack.shape, low),
        shape(both.shape, low),
        shape((zs, 2, many, 2 * KVW), low),
        shape((zs, 2, 4) + w_out.shape, low),
        shape((2, 4) + dy.shape, low),
        shape((2, 4, many, D), low),
        shape(rest.shape, low),
        shape((zs - 1,) + rest.shape, low),
        shape((zs - 1,) + last.shape, low),
    ] + [shape(both.shape, low)] * (2 * zs - 2) + [shape(down.shape, low)] * (2 * zs - 2)
    out_here = [shape((many, D), t) for t in (low, low, low, full)] + [shape((8, D), full)] + [shape((many, 128), full)] * 2
    sem = pltpu.SemaphoreType.DMA
    found = pl.pallas_call(
        functools.partial(forward_kernel, zs, micro),
        out_shape=out_any + out_here,
        in_specs=[smem, here, smem] + [here] * 2 + [anywhere] * 7,
        out_specs=[anywhere] * len(out_any) + [here] * len(out_here),
        scratch_shapes=[
            pltpu.VMEM((2, 2, 4) + pack.shape, low),
            pltpu.VMEM((many, QKV), full),
            pltpu.VMEM((many, 2 * KVW), low),
            pltpu.VMEM((zs, 2, many, 2 * KVW), low),
            pltpu.VMEM((wide, 2 * KVW), low),
            pltpu.VMEM((many // micro // 2, wide), full),
            pltpu.VMEM((zs, 2, 4) + w_out.shape, low),
            pltpu.VMEM((many, D), low),
            sem((4,)),
        ] + EXCHANGE_SEMS * 2 + [sem((2, zs - 1, 2))] + [sem((2 * zs - 2, 2))] * 2 + gather_sems(zs, True) * 3 + gather_sems(zs, False) * 2,
        compiler_params=pltpu.CompilerParams(
            collective_id=collective_id, has_side_effects=True, vmem_limit_bytes=56 * MIB
        ),
        cost_estimate=LONG,
    )(order, places_of(order, many // micro), first, freq.reshape(1, 128), tokens, pack, both, down, w_out, dy, rest, last)
    return found


def back_kernel(zs, micro, *refs):
    (order_ref, places_ref, first_ref, dy_ref, middle_ref, gains_ref, q_ref, cos_ref, sin_ref) = refs[:9]
    dx_part, out_part, both_part, down_part, out_all, kv_all, rest_part, last_part, *come = refs[9:21]
    result_ref, d_middle_ref, dq_ref, dkv_ref, gain_ref, down_ref, both_up, both_down, rest_in, last_in = refs[21:31]
    out_w, kv_here, d_heads, chosen, window, bias, d_places, sems, got, held, d_sems, dl_sem, *more = refs[31:]
    b_got, b_held, b_sems, bl_sem, r_sems, *more = more
    low, full = jnp.bfloat16, jnp.float32
    z, c, r = place()
    many = dy_ref.shape[0]
    span = many // micro
    half_len = span // 2
    greet(neighbours(zs, True, False))

    def take_d_ffn(at, value):
        d_middle_ref[at, :] = value

    def take_result(at, value):
        result_ref[at, :] = (middle_ref[at, :] + value).astype(low)

    scatters = {
        "dx": Scatter(1, False, True, dx_part, take_d_ffn, *more[:SCATTER_REFS]),
        "out": Scatter(1, False, True, out_part, take_result, *more[SCATTER_REFS : 2 * SCATTER_REFS]),
    }
    down = SumChain(zs, down_part, [got.at[n] for n in range(2 * zs - 2)], held, d_sems, dl_sem)
    none = [None] * (zs - 3)
    both = SumChain(
        zs, both_part, [b_got.at[0], both_up, *none, b_got.at[1], both_down, *none], b_held, b_sems, bl_sem
    )
    arounds = [
        Around(zs, lambda k: rest_part.at[lax.rem(z + k, zs)], rest_in, r_sems.at[0]),
        Around(zs, lambda k: last_part.at[lax.rem(z + k, zs)], last_in, r_sems.at[1]),
    ]
    comes = [
        pltpu.make_async_copy(src, dst, sems.at[2 + n])
        for n, (src, dst) in enumerate(zip(come, (b_got.at[0], b_got.at[1], got.at[0], got.at[zs - 1])))
    ]
    for copy in comes:
        copy.start()
    both.fetch(2)
    down.fetch(2)
    schedule = [(0, 3), (0, 1), (0, 2), (0, 0)]
    scatters["dx"].begin(schedule)
    for one in arounds:
        one.start()
    loads = [pltpu.make_async_copy(out_all, out_w, sems.at[0]), pltpu.make_async_copy(kv_all, kv_here, sems.at[1])]
    for load in loads:
        load.start()
    scatters["dx"].stage_a(0)
    for copy in comes:
        copy.wait()
    both.start(2)
    down.start(2)
    scatters["out"].begin(schedule)
    scatters["dx"].stage_b(0)
    scatters["out"].stage_a(0)
    scatters["dx"].stage_c(0)
    scatters["out"].stage_b(0)

    gain_ref[0:1, :] = jnp.zeros((1, D), full)

    def norm_some(i, carry):
        at = pl.ds(pl.multiple_of(i * half_len, half_len), half_len)
        middle, d_ffn = middle_ref[at, :], d_middle_ref[at, :]
        factor = rms_factor(middle)
        normed = middle * factor
        inner = d_ffn * gains_ref[1:2, :]
        d_norm = factor * (inner - normed * jnp.mean(inner * normed, axis=-1, keepdims=True))
        d_middle_ref[at, :] = dy_ref[at, :].astype(full) + d_norm
        gain_ref[0:1, :] += jnp.sum(d_ffn * normed, axis=0, keepdims=True)
        return carry

    lax.fori_loop(0, many // half_len, norm_some, 0)
    for load in loads:
        load.wait()
    d_heads[...] = product_nt(d_middle_ref[...].astype(low), out_w[...].reshape(D, D)).astype(low)

    wide = window.shape[0]
    half_blocks = wide // half_len
    width = GROUP * HEAD_DIM

    def attend_some(i, carry):
        m, half = lax.div(i, 2), lax.rem(i, 2)
        my_block = order_ref[(z * 2 + c) * 2 + half]
        first_block = jnp.where(my_block >= half_blocks, half_blocks, 0)
        wanted = first_block * half_len + lax.broadcasted_iota(jnp.int32, (wide, 2 * wide), 0)
        chosen[...] = jnp.where(places_ref[...] == wanted, 1.0, 0.0).astype(low)
        rows = pl.ds(pl.multiple_of(m * span, span), span)
        window[...] = product(chosen[...], kv_here[:, :, rows, :].reshape(2 * wide, 2 * KVW)).astype(low)
        key_place = first_block * half_len + lax.broadcasted_iota(jnp.int32, bias.shape, 0)
        place_here = my_block * half_len + lax.rem(lax.broadcasted_iota(jnp.int32, bias.shape, 1), half_len)
        first = first_ref[m]
        start = jnp.where(place_here >= first, first, 0)
        bias[...] = jnp.where((key_place <= place_here) & (key_place >= start), 0.0, NEG_LARGE)
        here = pl.ds(pl.multiple_of(i * half_len, half_len), half_len)
        cosine = jnp.concatenate([cos_ref[here, :]] * (width // 128), axis=1)
        sine = jnp.concatenate([sin_ref[here, :]] * (width // 128), axis=1)
        d_keys, d_values = [], []
        for g in range(KV_HEADS):
            at = slice(g * width, (g + 1) * width)
            key = window[:, g * HEAD_DIM : (g + 1) * HEAD_DIM]
            value = window[:, KVW + g * HEAD_DIM : KVW + (g + 1) * HEAD_DIM]
            d_key, d_value, d_query = attend_back_heads(q_ref[here, at], d_heads[here, at], key, value, bias, half_len)
            d_keys.append(d_key)
            d_values.append(d_value)
            dq_ref[here, at] = (d_query * cosine - partner(d_query) * sine).astype(low)
        d_window = jnp.concatenate(d_keys + d_values, axis=1).astype(low)
        spread_back = product_tn(chosen[...], d_window)

        @pl.when(half == 0)
        def _():
            d_places[...] = spread_back

        @pl.when(half == 1)
        def _():
            both = (d_places[...] + spread_back).astype(low)
            dkv_ref[:, :, rows, :] = both.reshape(zs, 2, span, 2 * KVW)

        return carry

    lax.fori_loop(0, micro, attend_some, 0)
    both.finish()
    down.finish()
    down.start(3)
    lax.fori_loop(micro, 2 * micro, attend_some, 0)
    scatters["out"].stage_c(0)
    down.finish()
    down.total()
    down_ref[...] = held[0].astype(full)
    for one in arounds:
        one.finish()
    for one in scatters.values():
        one.end()


def back(order, first, dy, middle, gains, queries, cosine, sine, dx_part, out_part, both_part, down_part, out_all, kv_all,
         rest_part, last_part, come, zs, collective_id):
    many = dy.shape[0]
    micro = first.shape[0]
    span = many // micro
    wide = zs * span
    low, full = jnp.bfloat16, jnp.float32
    anywhere, here, smem = (pl.BlockSpec(memory_space=m) for m in (pl.ANY, pltpu.VMEM, pltpu.SMEM))
    shape, sem = jax.ShapeDtypeStruct, pltpu.SemaphoreType.DMA
    unit = down_part.shape[1]
    piece = shape(both_part.shape[1:], low)
    return pl.pallas_call(
        functools.partial(back_kernel, zs, micro),
        out_shape=[
            shape((many, D), low), shape((many, D), full), shape((many, D), low), shape(kv_all.shape, low),
            shape((8, D), full), shape((unit, D), full), piece, piece,
            shape((zs - 1,) + rest_part.shape[1:], low), shape((zs - 1,) + last_part.shape[1:], low),
        ],
        in_specs=[smem, here, smem] + [here] * 6 + [anywhere] * 12,
        out_specs=[here] * 6 + [anywhere] * 4,
        scratch_shapes=[
            pltpu.VMEM(out_all.shape, low),
            pltpu.VMEM(kv_all.shape, low),
            pltpu.VMEM((many, D), low),
            pltpu.VMEM((wide, 2 * wide), low),
            pltpu.VMEM((wide, 2 * KVW), low),
            pltpu.VMEM((wide, GROUP * span // 2), full),
            pltpu.VMEM((2 * wide, 2 * KVW), full),
            sem((6,)),
            pltpu.VMEM((2 * zs - 2, unit, D), low),
            pltpu.VMEM((2, unit, D), low),
            sem((2 * zs - 2, 2)), sem((2,)),
            pltpu.VMEM((2,) + piece.shape, low),
            pltpu.VMEM((2,) + piece.shape, low),
            sem((2 * zs - 2, 2)), sem((2,)), sem((2, zs - 1, 2)),
        ] + scatter_scratch(1, True, many, D, True) * 2,
        compiler_params=pltpu.CompilerParams(
            collective_id=collective_id, has_side_effects=True, vmem_limit_bytes=62 * MIB
        ),
        cost_estimate=LONG,
    )(order, places_of(order, span), first, dy, middle, gains, queries, cosine, sine, dx_part, out_part, both_part, down_part,
      out_all, kv_all, rest_part, last_part, *come)


def weights_kernel(zs, *refs):
    x_ref, attn_ref, d_middle_ref, d_attn_ref, gains_ref, gain_two_ref, cos_ref, sin_ref, dkv_ref = refs[:9]
    packed, both_part, both_up, both_down, g_out, g_query, rest_part, last_part, rest_in, last_in = refs[9:19]
    x_grad_ref, out_ref, query_ref, pack_ref, last_ref, moved_ref, rest_ref = refs[19:26]
    kv_w, d_kv, pack_g, sems, got, held, b_sems, bl_sem, rest_here, last_here, *more = refs[26:]
    exchange_sems, rest_sems, more = more[:3], more[3:6], more[6:]
    z = place()[0]
    low, full = jnp.bfloat16, jnp.float32
    greet(neighbours(zs, True, True))

    def into(ref):
        def take(at, value):
            ref[at, :] = value

        return take

    def next_refs(staged):
        nonlocal more
        mine, more = more[:SCATTER_REFS], more[SCATTER_REFS:]
        return mine if staged else [None, *mine[1:]]

    pairs = Scatter(zs, True, False, dkv_ref, into(d_kv), *next_refs(False))
    scatters = {
        "out": Scatter(zs, True, True, g_out, into(out_ref), *next_refs(True)),
        "query": Scatter(zs, True, True, g_query, into(query_ref), *next_refs(True)),
        "pack": Scatter(zs, True, True, pack_g, into(pack_ref), *next_refs(False)),
    }
    items = [(name, k) for k in range(1, zs) for name in ("out", "query")]
    items[4:4] = [("pack", 1)]
    items += [("pack", k) for k in range(2, zs)] + [("out", 0), ("query", 0), ("pack", 0)]
    rounds, schedules = scatter_plan(items)

    none = [None] * (zs - 3)
    chain = SumChain(zs, both_part, [*none, got.at[0], got.at[1], *none, got.at[2], got.at[3]], held, b_sems, bl_sem)
    loads = [
        pltpu.make_async_copy(both_up, got.at[0], sems.at[0]),
        pltpu.make_async_copy(both_down, got.at[2], sems.at[1]),
        pltpu.make_async_copy(packed.at[:, :, :, :, pl.ds(D, 2 * KVW)], kv_w, sems.at[2]),
    ]
    for load in loads:
        load.start()
    small = [
        pltpu.make_async_copy(rest_part.at[z], rest_here.at[0], sems.at[3]),
        pltpu.make_async_copy(last_part.at[z], last_here.at[0], sems.at[4]),
        pltpu.make_async_copy(rest_in, rest_here.at[pl.ds(1, zs - 1)], sems.at[5]),
        pltpu.make_async_copy(last_in, last_here.at[pl.ds(1, zs - 1)], sems.at[6]),
    ]
    for load in small:
        load.start()
    chain.fetch(zs - 1)
    pairs.begin([])
    scatters["out"].begin(schedules["out"])
    scatters["query"].begin(schedules["query"])
    for k in range(1, zs):
        pairs.stage_c(k)
    for load in loads:
        load.wait()
    chain.start(zs - 1)
    for load in small:
        load.wait()
    last_ref[...] = sum(last_here[n].astype(full) for n in range(zs))
    rest_here[0] = sum(rest_here[n].astype(full) for n in range(zs)).astype(low)
    rest = Exchange(rest_here.at[0], rest_ref, *rest_sems)
    rest.start()

    def keys_and_norm():
        pairs.stage_c(0)
        lanes = KVW // 128
        cosine = jnp.concatenate([cos_ref[...]] * lanes, axis=1)
        sine = jnp.concatenate([sin_ref[...]] * lanes, axis=1)
        d_key = d_kv[:, :KVW]
        d_lin = jnp.concatenate([d_key * cosine - partner(d_key) * sine, d_kv[:, KVW:]], axis=1).astype(low)
        d_attn = d_attn_ref[...] + product_nt(d_lin, kv_w[...].reshape(D, 2 * KVW))
        x = x_ref[...].astype(full)
        factor = rms_factor(x)
        normed = x * factor
        inner = d_attn * gains_ref[0:1, :]
        d_x = factor * (inner - normed * jnp.mean(inner * normed, axis=-1, keepdims=True))
        x_grad_ref[...] = (d_middle_ref[...] + d_x).astype(low)
        gain_one = jnp.sum(d_attn * normed, axis=0, keepdims=True)
        rows = lax.broadcasted_iota(jnp.int32, (128, D), 0)
        both = jnp.where(rows == 0, gain_one, jnp.where(rows == 1, gain_two_ref[0:1, :], 0.0))
        pack = jnp.concatenate([product_tn(attn_ref[...], d_lin), both.T], axis=1).astype(low)
        pack_g[...] = pack.reshape(pack_g.shape)
        scatters["pack"].begin([])

    for n, stages in enumerate(rounds):
        if n == 3:
            keys_and_norm()
        if n == len(rounds) - 3:
            chain.finish()
            chain.total()
            exchange = Exchange(held.at[0], moved_ref, *exchange_sems)
            exchange.start()
        for stage in stages:
            run_stage(scatters, *stage)
    for one in (rest, exchange):
        one.finish()
        one.end()
    for one in (pairs, *scatters.values()):
        one.end()


def weight_sums(x, attn_in, d_middle, d_attn, gains, gain_two, cosine, sine, d_kv, packed, both_part, both_up, both_down, g_out,
                g_query, rest_part, last_part, rest_in, last_in, zs, collective_id):
    many = x.shape[0]
    low, full = jnp.bfloat16, jnp.float32
    anywhere, here = (pl.BlockSpec(memory_space=m) for m in (pl.ANY, pltpu.VMEM))
    shape, sem = jax.ShapeDtypeStruct, pltpu.SemaphoreType.DMA
    wide = packed.shape[3]
    narrow = 2 * KVW + 128
    block = both_part.shape[1:]
    return pl.pallas_call(
        functools.partial(weights_kernel, zs),
        out_shape=[
            shape((many, D), low), shape((wide, D), full), shape((wide, D), full), shape((wide, narrow), full),
            shape(last_part.shape[1:], full), shape(block, low), shape(rest_part.shape[1:], low),
        ],
        in_specs=[here] * 9 + [anywhere] * 10,
        out_specs=[here] * 5 + [anywhere] * 2,
        scratch_shapes=[
            pltpu.VMEM(packed.shape[:4] + (2 * KVW,), low),
            pltpu.VMEM((many, 2 * KVW), full),
            pltpu.VMEM((zs, 2, 4, wide, narrow), low),
            sem((7,)),
            pltpu.VMEM((4,) + block, low),
            pltpu.VMEM((2,) + block, low),
            sem((2 * zs - 2, 2)), sem((2,)),
            pltpu.VMEM(rest_part.shape, low),
            pltpu.VMEM(last_part.shape, low),
        ] + EXCHANGE_SEMS * 2
        + scatter_scratch(zs, False, many, 2 * KVW, False)
        + scatter_scratch(zs, True, wide, D, True) * 2
        + scatter_scratch(zs, True, wide, narrow, False),
        compiler_params=pltpu.CompilerParams(
            collective_id=collective_id, has_side_effects=True, vmem_limit_bytes=62 * MIB
        ),
        cost_estimate=LONG,
    )(x, attn_in, d_middle, d_attn, gains, gain_two, cosine, sine, d_kv, packed, both_part, both_up, both_down, g_out,
      g_query, rest_part, last_part, rest_in, last_in)


class Links:
    def __init__(self, seq, rows):
        self.zs, self.rows = seq // 2, rows
        self.kernels = rows == 4 and self.zs == 4
        self.z_groups = [[2 * z + c for z in range(self.zs)] for c in range(2)]
        self.core_groups = [[2 * z, 2 * z + 1] for z in range(self.zs)]

    def gather_z(self, block):
        return lax.all_gather(block, "seq", axis=0, tiled=True, axis_index_groups=self.z_groups)

    def scatter_z(self, blocks):
        return lax.psum_scatter(blocks, "seq", scatter_dimension=0, tiled=True, axis_index_groups=self.z_groups)

    def exchange_xla(self, blocks):
        moved = lax.all_to_all(blocks, "rows", split_axis=1, concat_axis=1, tiled=True)
        return lax.all_to_all(moved, "seq", split_axis=0, concat_axis=0, tiled=True, axis_index_groups=self.core_groups)

    def gather(self, array, z_flag, planes):
        if planes:
            array = lax.all_gather(array, "rows", axis=0)
        array = lax.all_gather(array, "seq", axis=0, axis_index_groups=self.core_groups)
        return self.gather_z(array[None]) if z_flag else array

    def scatter(self, blocks, z_flag, planes):
        blocks = self.scatter_z(blocks)[0] if z_flag else blocks
        blocks = lax.psum_scatter(blocks, "seq", scatter_dimension=0, tiled=True, axis_index_groups=self.core_groups)[0]
        if planes:
            blocks = lax.psum_scatter(blocks, "rows", scatter_dimension=0, tiled=True)[0]
        return blocks.astype(jnp.float32)


def on_device(seq, rows, tokens, w_query, w_key, w_value, w_out, w_gate, w_up, w_down, gain_attn, gain_ffn, lengths, order, cotangent):
    links = Links(seq, rows)
    zs = links.zs
    micro, _, span, _ = tokens.shape
    half_len = span // 2
    many = micro * span
    low = jnp.bfloat16
    wide = w_gate.shape[0]
    unit = w_down.shape[0]

    both, rest = spread(w_gate, w_up, zs, rows)
    cut = split_unit(unit)
    flat, flat_rest = (2 * rows * wide, 2 * zs * cut), (2 * rows * wide, 2 * zs * (unit - cut))
    gains = jnp.pad(jnp.stack([gain_attn, gain_ffn], axis=1), ((0, 0), (0, 126)))
    pack = jnp.concatenate([w_query, w_key, w_value, gains], axis=1)
    dy_own = cotangent.reshape(many, D)
    own_tokens = tokens.reshape(many, D)
    x = own_tokens.astype(jnp.float32)
    first = lengths[:, 0, 0]
    slot_of = jnp.argmax(order[None, :] == jnp.arange(order.shape[0], dtype=jnp.int32)[:, None], axis=1).astype(jnp.int32)
    chained = links.kernels
    if chained:
        down_own, last_own = w_down[:cut], w_down[cut:]
        found = forward(order, first, own_tokens, pack, both, rest, down_own, last_own, w_out, dy_own, zs, 0)
        packed, both_own, kv, out_w, dy, ffn_in, rest_own, rest_got, last_got = found[:9]
        both_w = [b.reshape(flat) for b in (both_own, *found[9 : 7 + 2 * zs])]
        down_w = [down_own, *found[7 + 2 * zs : 5 + 4 * zs]]
        rest_w = [rest_own.reshape(flat_rest), rest_got.reshape(zs - 1, *flat_rest)]
        last_w = [last_own, last_got]
        queries, attn_in, attended, middle, gains, cosine, sine = found[5 + 4 * zs :]
        packed = packed.reshape(D, PACK)
    else:
        both_w = [links.gather_z(links.exchange_xla(both).reshape(flat))]
        rest_w = [links.gather_z(links.exchange_xla(rest).reshape(flat_rest))]
        down_w, last_w = [links.gather_z(w_down[:cut])], [links.gather_z(w_down[cut:])]
        packed, dy = links.gather(pack, True, True).reshape(D, PACK), links.gather(dy_own, False, True)
        gain_one, gain_two = packed[:, QKV].astype(jnp.float32), packed[:, QKV + 1].astype(jnp.float32)
        mine = slot_places(order, half_len, lax.axis_index("seq") * span + jnp.arange(span, dtype=jnp.int32))
        start = jnp.where(mine[None, :] >= first[:, None], first[:, None], 0)
        inverse = 10000.0 ** (-jnp.arange(HEAD_DIM // 2, dtype=jnp.float32) / (HEAD_DIM // 2))
        angles = ((mine[None, :] - start).astype(jnp.float32)[..., None] * inverse).reshape(many, HEAD_DIM // 2)
        cosine, sine = jnp.cos(angles), jnp.sin(angles)
        cosine, sine = jnp.tile(cosine, (1, 4)), jnp.tile(jnp.concatenate([-sine, sine], axis=1), (1, 2))
        attn_in = (x * rms_factor(x) * gain_one).astype(low)
        lin = product(attn_in, packed)
        kv_own = jnp.concatenate([turn(lin[:, D : D + KVW], cosine, sine), lin[:, D + KVW : QKV]], axis=1).astype(low)
        kv, out_w = links.gather(kv_own, True, False), links.gather(w_out, True, True)
        queries, attended = attend(order, slot_of, first, lin, cosine, sine, kv.reshape(seq, many, 2 * KVW))
        middle = x + product(attended, out_w.reshape(D, D))
        ffn_in = links.gather((middle * rms_factor(middle) * gain_two).astype(low), False, True)
    kv = kv.reshape(seq, many, 2 * KVW)
    out_w = out_w.reshape(D, D)
    dy = dy.reshape(2 * rows * many, D)

    ffn_in = ffn_in.reshape(2 * rows * many, D)
    shards = (zs, 2, rows, wide)
    if chained:
        hidden, d_both, grad_both, grad_down = ffn_first(ffn_in, dy, both_w, down_w, zs)
        grad_both, grad_down = grad_both.reshape(*shards, 2 * zs * cut), grad_down.reshape(zs, cut, D)
        result_part, d_ffn_part, grad_rest, grad_last, *come = ffn_second(
            ffn_in, dy, hidden, d_both, (both_w, down_w), (rest_w, last_w), zs, (grad_both, grad_down), 1
        )
    else:
        hidden, d_both, grad_both, grad_down = ffn_first(ffn_in, dy, both_w, down_w, zs)
        grad_both, grad_down = grad_both.reshape(*shards, 2 * zs * cut), grad_down.reshape(zs, cut, D)
        result_part, d_ffn_part, grad_rest, grad_last = ffn_second(
            ffn_in, dy, hidden, d_both, (both_w, down_w), (rest_w, last_w), zs
        )
    grad_rest, grad_last = grad_rest.reshape(*shards, 2 * zs * (unit - cut)), grad_last.reshape(zs, unit - cut, D)
    d_ffn_part, result_part = (part.reshape(2, rows, many, D) for part in (d_ffn_part, result_part))
    if chained:
        out_all, kv_all = out_w.reshape(*shards, D), kv.reshape(zs, 2, many, 2 * KVW)
        result, d_middle, d_query, d_kv, gain_two_grad, grad_down, both_up, both_down, rest_in, last_in = back(
            order, first, dy_own, middle, gains, queries, cosine, sine, d_ffn_part, result_part, grad_both, grad_down,
            out_all, kv_all, grad_rest, grad_last, come, zs, 2,
        )
        grad_out = product_tn(attended, d_middle.astype(low)).astype(low).reshape(*shards, D)
        grad_query = product_tn(attn_in, d_query).astype(low).reshape(*shards, D)
        d_attn = product_nt(d_query, packed[:, :D])
        x_grad, grad_out, grad_query, pack_grad, grad_last, grad_both, grad_rest = weight_sums(
            own_tokens, attn_in, d_middle, d_attn, gains, gain_two_grad, cosine, sine, d_kv, packed.reshape(*shards, PACK),
            grad_both, both_up, both_down, grad_out, grad_query, grad_rest, grad_last, rest_in, last_in, zs, 3,
        )
    else:
        d_ffn_in = links.scatter(d_ffn_part, False, True)
        result = (middle + links.scatter(result_part, False, True)).astype(low)
        grad_both, grad_rest = (links.exchange_xla(links.scatter_z(grad)[0]) for grad in (grad_both, grad_rest))
        grad_down, grad_last = (links.scatter_z(grad)[0].astype(jnp.float32) for grad in (grad_down, grad_last))
        factor_two = rms_factor(middle)
        d_part, grad_gain_two = norm_back(d_ffn_in, middle * factor_two, factor_two, gain_two)
        d_middle = dy_own.astype(jnp.float32) + d_part
        d_mid_low = d_middle.astype(low)
        grad_out = links.scatter(product_tn(attended, d_mid_low).astype(low).reshape(*shards, D), True, True)
        d_heads = product_nt(d_mid_low, out_w).astype(low)
        d_query, d_kv = attend_back(order, slot_of, first, queries, d_heads, cosine, sine, kv)
        grad_query = links.scatter(product_tn(attn_in, d_query).astype(low).reshape(*shards, D), True, True)
        d_kv = links.scatter(d_kv.reshape(zs, 2, many, 2 * KVW), True, False)
        d_key = turn(d_kv[:, :KVW], cosine, -sine)
        d_kv = jnp.concatenate([d_key.astype(low), d_kv[:, KVW:].astype(low)], axis=1)
        d_attn_in = product_nt(d_query, packed[:, :D]) + product_nt(d_kv, packed[:, D:QKV])
        factor_one = rms_factor(x)
        d_x, grad_gain_one = norm_back(d_attn_in, x * factor_one, factor_one, gain_one)
        x_grad = (d_middle + d_x).astype(low)
        gains_grad = jnp.pad(jnp.stack([grad_gain_one, grad_gain_two], axis=1), ((0, 0), (0, 126)))
        pack_grad = jnp.concatenate([product_tn(attn_in, d_kv), gains_grad], axis=1).astype(low)
        pack_grad = links.scatter(pack_grad.reshape(*shards, 2 * KVW + 128), True, True)
    grad_gate, grad_up = collect((grad_both, grad_rest), zs, rows, unit)
    grad_down = jnp.concatenate([grad_down, grad_last])

    return (
        result.reshape(tokens.shape),
        x_grad.reshape(tokens.shape),
        grad_query,
        pack_grad[:, :KVW],
        pack_grad[:, KVW : 2 * KVW],
        grad_out,
        grad_gate,
        grad_up,
        grad_down,
        pack_grad[:, 2 * KVW],
        pack_grad[:, 2 * KVW + 1],
    )


def solution(mesh):
    both = ("seq", "rows")
    row = P(None, "rows", "seq", None)
    weight, gain = P(both, None), P(both)
    return jax.shard_map(
        functools.partial(on_device, mesh.shape["seq"], mesh.shape["rows"]),
        mesh=mesh,
        in_specs=(row,) + (weight,) * 7 + (gain, gain, P(None, "rows", None), P(), row),
        out_specs=(row, row) + (weight,) * 7 + (gain, gain),
        check_vma=False,
    )
```

```python
import functools

import jax
import jax.numpy as jnp
from jax import lax
from jax.experimental import pallas as pl
from jax.experimental.pallas import tpu as pltpu
from jax.sharding import PartitionSpec as P

D = 2048
HEADS = 32
KV_HEADS = 4
HEAD_DIM = 64
GROUP = 8
KVW = 256
QKV = D + 2 * KVW
PACK = QKV + 128

EPSILON = 1e-05
NEG_LARGE = -1e30
MESH = pl.DeviceIdType.MESH
MIB = 1 << 20
LONG = pl.CostEstimate(flops=50_000_000_000, bytes_accessed=150 * MIB, transcendentals=0)


def product(left, right):
    return jnp.dot(left, right, preferred_element_type=jnp.float32)


def product_nt(left, right):
    return lax.dot_general(left, right, (((1,), (1,)), ((), ())), preferred_element_type=jnp.float32)


def product_tn(left, right):
    return lax.dot_general(left, right, (((0,), (0,)), ((), ())), preferred_element_type=jnp.float32)


def rms_factor(values):
    return lax.rsqrt(jnp.mean(values * values, axis=-1, keepdims=True) + EPSILON)


def norm_back(d_scaled, normed, factor, gain):
    inner = d_scaled * gain
    mean = jnp.mean(inner * normed, axis=-1, keepdims=True)
    return factor * (inner - normed * mean), jnp.sum(d_scaled * normed, axis=0)


def turn(tensor, cosine, sine):
    rows, lanes = tensor.shape
    half = HEAD_DIM // 2
    swapped = jnp.flip(tensor.reshape(rows, lanes // HEAD_DIM, 2, half), axis=2).reshape(rows, lanes)
    return tensor * jnp.tile(cosine, (1, lanes // 128)) + swapped * jnp.tile(sine, (1, lanes // 128))


def slot_places(order, half_len, slot_ids):
    matches = (slot_ids // half_len)[:, None] == jnp.arange(order.shape[0], dtype=jnp.int32)[None, :]
    return jnp.sum(jnp.where(matches, order[None, :], 0), axis=1) * half_len + slot_ids % half_len


def place():
    s, r = lax.axis_index("seq"), lax.axis_index("rows")
    return lax.div(s, 2), lax.rem(s, 2), r


def send(src, dst, ssem, rsem, device):
    return pltpu.make_async_remote_copy(
        src_ref=src, dst_ref=dst, send_sem=ssem, recv_sem=rsem, device_id=device, device_id_type=MESH
    )


def greet(devices):
    barrier = pltpu.get_barrier_semaphore()
    for device in devices:
        pl.semaphore_signal(barrier, inc=1, device_id=device, device_id_type=MESH)
    pl.semaphore_wait(barrier, len(devices))


def corners(r):
    return r, r + 1 - 2 * lax.rem(r, 2), lax.rem(r + 2, 4), 3 - r


def exchange_others():
    return [(cc, j) for j in (3, 1, 2, 0) for cc in range(2) if (cc, j) != (0, 0)]


class Exchange:
    def __init__(self, own, out, ssem, rsem, l_sem):
        z, c, r = place()
        line = corners(r)
        self.own, self.out, self.ssem, self.rsem, self.here = own, out, ssem, rsem, (c, r)
        self.others = [(1 - c if cc else c, line[j]) for cc, j in exchange_others()]
        self.devices = [(z * 2 + core, row) for core, row in self.others]
        self.local = pltpu.make_async_copy(own.at[c, r], out.at[c, r], l_sem)

    def start(self):
        self.copies = []
        for i, other in enumerate(self.others):
            copy = send(self.own.at[other], self.out.at[self.here], self.ssem.at[i], self.rsem.at[i], self.devices[i])
            copy.start()
            self.copies.append(copy)
        self.local.start()

    def finish(self):
        for i, other in enumerate(self.others):
            dst = self.out.at[other]
            send(dst, dst, self.ssem.at[i], self.rsem.at[i], self.devices[i]).wait_recv()
        self.local.wait()

    def end(self):
        for copy in self.copies:
            copy.wait_send()


class Line:
    def __init__(self, zs, way, lo, hi, src, dst, sems):
        z, c, r = place()
        lo, hi = (lo, min(hi, zs - 1)) if way == 1 else (max(lo, 1), hi)
        self.sends = (z >= lo) & (z < hi)
        self.gets = (z - way >= lo) & (z - way < hi)
        to = lax.rem(z + way + zs, zs)
        self.copy = send(src, dst, sems.at[0], sems.at[1], (to * 2 + c, r))

    def start(self):
        pl.when(self.sends)(self.copy.start)

    def finish(self):
        pl.when(self.sends)(self.copy.wait_send)
        pl.when(self.gets)(self.copy.wait_recv)


LINE_SEMS = pltpu.SemaphoreType.DMA((2,))
EXCHANGE_SEMS = [pltpu.SemaphoreType.DMA((7,)), pltpu.SemaphoreType.DMA((7,)), pltpu.SemaphoreType.DMA]


def neighbours(zs, planes, moved):
    z, c, r = place()
    line = corners(r)
    s = z * 2 + c
    devices = [(z * 2 + 1 - c, r)]
    if moved:
        devices = [(z * 2 + (1 - c if cc else c), line[j]) for cc, j in exchange_others()]
    elif planes:
        devices += [(s, line[1]), (s, line[2])]
    return devices + [(lax.rem(z + k, zs) * 2 + c, r) for k in range(1, zs)]


class Gather:
    def __init__(self, zs, z_flag, planes, own, out, z_ssem, z_rsem, f_ssem, f_rsem, h_ssem, h_rsem, c_ssem, c_rsem, l_sem):
        self.__dict__.update(locals())
        self.z, self.c, self.r = place()
        self.line = corners(self.r)
        self.s = self.z * 2 + self.c
        self.twin = (self.z * 2 + 1 - self.c, self.r)
        self.count = zs if z_flag else 1
        self.half = own.shape[0] // 2
        self.pending = []
        self.sent = []
        z = self.z
        self.kth = [0, jnp.where(z == 0, 3, 1), jnp.where((z == 0) | (z == 3), 2, 3), jnp.where(z == 0, 1, jnp.where(z == 3, 3, 2))]

    def start(self, copy):
        copy.start()
        self.pending.append(copy.wait_send)

    def slot(self, k, other, j):
        if not self.z_flag:
            return self.out.at[other, j]
        core = 1 - self.c if other else self.c
        zz = lax.rem(self.z - k + self.zs, self.zs)
        return self.out.at[zz, core, self.line[j]] if self.planes else self.out.at[zz, core]

    def z_copy(self, n, way, k, src, dst):
        to = (lax.rem(self.z + way + self.zs, self.zs) * 2 + self.c, self.r)
        return send(src, dst, self.z_ssem.at[n, 0 if way == 1 else 1], self.z_rsem.at[k], to)

    def hand_on(self, n, src, dst):
        z, k, zs = self.z, self.kth[n], self.zs
        up, down = (z < zs - 1, z > 0) if n == 0 else ((z >= k) & (z < zs - 1), (z < k) & (z > 0))
        for way, goes, step in ((1, up, 1), (-1, down, zs - 1)):
            copy = self.z_copy(n, way, lax.rem(k + step, zs), src, dst)
            pl.when(goes)(copy.start)
            self.sent.append((goes, copy))

    def near(self, k, j, src):
        dst = self.slot(k, 0, j) if src is None or not self.z_flag else self.slot(k, 0, 0)
        return send(dst if src is None else src, dst, self.f_ssem.at[k, j - 1], self.f_rsem.at[k, j - 1], (self.s, self.line[j]))

    def part(self, ref, j):
        return ref.at[pl.ds(self.half if j == 1 else 0, self.half)]

    def far(self, k, j, src):
        if src is None:
            src = dst = self.part(self.slot(k, 0, 3), j)
        else:
            dst = self.part(src if self.z_flag else self.out.at[0, 3], j)
            src = self.part(src, j)
        return send(src, dst, self.h_ssem.at[k, j - 1], self.h_rsem.at[k, j - 1], (self.s, self.line[3 - j]))

    def twin_copy(self, k, j, src):
        dst = self.slot(k, 0, j) if self.z_flag else self.out.at[1, j]
        return send(src, dst, self.c_ssem.at[k, j], self.c_rsem.at[k, j], self.twin)

    def to_twin(self, k, j, src):
        self.start(self.twin_copy(k, j, src))

    def from_twin(self, k, j):
        dst = self.slot(k, 1, j)
        send(dst, dst, self.c_ssem.at[k, j], self.c_rsem.at[k, j], self.twin).wait_recv()

    def launch(self):
        self.local = pltpu.make_async_copy(self.own, self.slot(0, 0, 0), self.l_sem)
        self.local.start()
        if self.count > 1 and self.planes:
            self.hand_on(0, self.own, self.slot(0, 0, 0))
        elif self.count > 1:
            for k in range(1, self.count):
                self.start(self.z_copy(k, k, k, self.own, self.slot(0, 0, 0)))

    def arrive(self, n):
        k = self.kth[n]
        src = self.slot(k, 0, 0)
        self.z_copy(n, 1, k, src, src).wait_recv()
        if self.planes:
            self.hand_on(n, src, src)

    def begin(self, n):
        k = self.kth[n]
        src = self.slot(k, 0, 0) if n else self.own
        if self.planes:
            for j in (1, 2):
                self.start(self.near(k, j, src))
        self.to_twin(k, 0, src)

    def forward(self, n):
        k = self.kth[n]
        for j in (1, 2):
            self.near(k, j, None).wait_recv()
            src = self.slot(k, 0, j)
            self.start(self.far(k, j, src))
            self.to_twin(k, j, src)

    def finish(self, n):
        k = self.kth[n]
        for j in (1, 2):
            self.far(k, j, None).wait_recv()
        self.to_twin(k, 3, self.slot(k, 0, 3))

    def complete(self, n):
        k = self.kth[n]
        if n == 0:
            self.local.wait()
        for j in range(4 if self.planes else 1):
            self.from_twin(k, j)

    def sent_all(self):
        for j in (1, 2):
            self.near(0, j, self.own).wait_send()
            self.far(0, j, self.slot(0, 0, j)).wait_send()
        for j in range(4):
            self.twin_copy(0, j, self.slot(0, 0, j) if j else self.own).wait_send()

    def end(self):
        for goes, copy in self.sent:
            pl.when(goes)(copy.wait_send)
        for wait in self.pending:
            wait()


def gather_sems(zs, z_flag):
    sem = pltpu.SemaphoreType.DMA
    n = zs if z_flag else 1
    return [sem((n, 2)), sem((n,)), sem((n, 2)), sem((n, 2)), sem((n, 2)), sem((n, 2)), sem((n, 4)), sem((n, 4)), sem]


class Chain:
    def __init__(self, zs, own, got, sems):
        self.zs, self.own, self.got, self.sems = zs, own, got, sems
        self.lines = []

    def start(self, k):
        zs = self.zs
        up, down = (self.own, self.own) if k == 1 else (self.got[k - 2], self.got[zs + k - 3])
        self.lines = [
            Line(zs, 1, k - 1, zs, up, self.got[k - 1], self.sems.at[k - 1]),
            Line(zs, -1, 0, zs - k + 1, down, self.got[zs + k - 2], self.sems.at[zs + k - 2]),
        ]
        for line in self.lines:
            line.start()

    def finish(self):
        for line in self.lines:
            line.finish()


class Scatter:
    def __init__(self, zs, z_flag, planes, given, final, stage, twin_in, half_in, full_in, z_in, l_sem, c_ssem, c_rsem, h_ssem,
                 h_rsem, f_ssem, f_rsem, z_ssem, z_rsem):
        self.__dict__.update(locals())
        self.z, self.c, self.r = place()
        self.line = corners(self.r)
        self.s = self.z * 2 + self.c
        self.twin = (self.z * 2 + 1 - self.c, self.r)
        self.rows = twin_in.shape[2]
        self.step = 16
        self.spots = (3, 1, 2, 0) if planes else (0,)
        self.zs = zs if z_flag else 1
        self.order = list(range(1, self.zs)) + [0]
        self.pending = []
        self.loads = []
        self.settled = 0

    def at_z(self, k):
        return (lax.rem(self.z + k, self.zs) * 2 + self.c, self.r)

    def block(self, k, other, j):
        if not self.z_flag:
            return self.given.at[other, j]
        zz, core = lax.rem(self.z + k, self.zs), 1 - self.c if other else self.c
        return self.given.at[zz, core, self.line[j]] if self.planes else self.given.at[zz, core]

    def start(self, copy):
        copy.start()
        self.pending.append(copy.wait_send)

    def begin(self, schedule):
        for k in self.order:
            for j in self.spots:
                self.start(self.twin_copy(k, j, self.block(k, 1, j)))
        if self.stage is not None:
            self.loads = [
                pltpu.make_async_copy(self.block(k, 0, j), self.stage.at[n % 2], self.l_sem.at[n % 2])
                for n, (k, j) in enumerate(schedule)
            ]
            for load in self.loads[:2]:
                load.start()

    def twin_copy(self, k, j, src):
        dst = self.twin_in.at[k, j]
        return send(dst if src is None else src, dst, self.c_ssem.at[k, j], self.c_rsem.at[k, j], self.twin)

    def settle(self, k, j, parts):
        own = self.block(k, 0, j)
        n = self.settled
        if self.stage is not None:
            self.loads[n].wait()
            own = self.stage.at[n % 2]
        self.twin_copy(k, j, None).wait_recv()
        step = self.step
        for first, last, more in parts:

            def body(i, carry, first=first, more=more):
                at = pl.ds(pl.multiple_of(first + i * step, step), step)
                value = own[at, :].astype(jnp.float32) + self.twin_in[k, j, at, :].astype(jnp.float32)
                for ref, offset in more:
                    there = pl.ds(pl.multiple_of(first - offset + i * step, step), step)
                    value = value + ref[there, :].astype(jnp.float32)
                if k == 0 and j == 0:
                    self.final(at, value)
                else:
                    self.twin_in[k, j, at, :] = value.astype(self.twin_in.dtype)
                return carry

            lax.fori_loop(0, (last - first) // step, body, 0)
        if n + 2 < len(self.loads):
            self.loads[n + 2].start()
        self.settled = n + 1

    def half_copy(self, k, n, src):
        dst = self.half_in.at[k, n]
        return send(dst if src is None else src, dst, self.h_ssem.at[k, n], self.h_rsem.at[k, n], (self.s, self.line[n + 1]))

    def full_copy(self, k, j, src):
        dst = self.full_in.at[k, j - 1]
        return send(dst if src is None else src, dst, self.f_ssem.at[k, j - 1], self.f_rsem.at[k, j - 1], (self.s, self.line[j]))

    def z_copy(self, k, src):
        dst = self.z_in.at[k]
        return send(dst if src is None else src, dst, self.z_ssem.at[k], self.z_rsem.at[k], self.at_z(k))

    def stage_a(self, k):
        half = self.rows // 2
        self.settle(k, 3, [(0, self.rows, [])])
        self.start(self.half_copy(k, 1, self.twin_in.at[k, 3, pl.ds(half, half)]))
        self.start(self.half_copy(k, 0, self.twin_in.at[k, 3, pl.ds(0, half)]))

    def stage_b(self, k):
        half = self.rows // 2
        for j in (1, 2):
            n = 2 - j
            self.half_copy(k, n, None).wait_recv()
            more = [(self.half_in.at[k, n], half if n else 0)]
            self.settle(k, j, [(0, half, [] if n else more), (half, self.rows, more if n else [])])
            self.start(self.full_copy(k, j, self.twin_in.at[k, j]))

    def stage_c(self, k):
        more = []
        if self.planes:
            for j in (1, 2):
                self.full_copy(k, j, None).wait_recv()
                more.append((self.full_in.at[k, j - 1], 0))
        if not k:
            for other in range(1, self.zs):
                self.z_copy(other, None).wait_recv()
                more.append((self.z_in.at[other], 0))
        self.settle(k, 0, [(0, self.rows, more)])
        if k:
            self.start(self.z_copy(k, self.twin_in.at[k, 0]))

    def end(self):
        for wait in self.pending:
            wait()


def scatter_scratch(zs, planes, rows, columns, staged):
    sem = pltpu.SemaphoreType.DMA
    low, least = jnp.bfloat16, (1, 2, 16, 128)
    spots = 4 if planes else 1
    return [
        pltpu.VMEM((2, rows, columns) if staged else (16, 128), low),
        pltpu.VMEM((zs, spots, rows, columns), low),
        pltpu.VMEM((zs, 2, rows // 2, columns) if planes else least, low),
        pltpu.VMEM((zs, 2, rows, columns) if planes else least, low),
        pltpu.VMEM((zs, rows, columns) if zs > 1 else least[1:], low),
        sem((2,)), sem((zs, 4)), sem((zs, 4)), sem((zs, 2)), sem((zs, 2)), sem((zs, 2)), sem((zs, 2)), sem((zs,)), sem((zs,)),
    ]


SCATTER_REFS = 14


def scatter_plan(items):
    rounds = []
    for n in range(len(items) + 2):
        rounds.append([])
        for back, stage in enumerate(("a", "b", "c")):
            if 0 <= n - back < len(items):
                name, k = items[n - back]
                if stage != "c" or k:
                    rounds[-1].append((name, stage, k))
    rounds.append([(name, "c", 0) for name, k in items if not k])
    places = {"a": (3,), "b": (1, 2), "c": (0,)}
    schedules = {}
    for name, stage, k in sum(rounds, []):
        schedules.setdefault(name, []).extend((k, j) for j in places[stage])
    return rounds, schedules


def run_stage(scatters, name, stage, k):
    {"a": Scatter.stage_a, "b": Scatter.stage_b, "c": Scatter.stage_c}[stage](scatters[name], k)


class SumChain:
    def __init__(self, zs, parts, got, held, sems, l_sem):
        self.__dict__.update(locals())
        self.z = place()[0]

    def own(self, to):
        return self.parts.at[lax.rem(self.z + to + self.zs, self.zs)]

    def fetch(self, k):
        self.loads = [
            pltpu.make_async_copy(self.own(-k), self.held.at[0], self.l_sem.at[0]),
            pltpu.make_async_copy(self.own(k), self.held.at[1], self.l_sem.at[1]),
        ]
        for load in self.loads:
            load.start()

    def add(self, into, more):
        ref = self.got[into]
        ref[...] = (ref[...].astype(jnp.float32) + self.held[more].astype(jnp.float32)).astype(ref.dtype)

    def start(self, k):
        zs, z, got = self.zs, self.z, self.got
        up, down = k - 1, zs - 2 + k
        self.lines = [
            Line(zs, 1, 0, 1, self.own(-k), got[up], self.sems.at[up]),
            Line(zs, -1, zs - 1, zs, self.own(k), got[down], self.sems.at[down]),
        ]
        if k > 1:
            for load in self.loads:
                load.wait()
            pl.when((z >= 1) & (z < k))(functools.partial(self.add, up - 1, 0))
            pl.when((z >= zs - k) & (z < zs - 1))(functools.partial(self.add, down - 1, 1))
            self.lines += [
                Line(zs, 1, 1, k, got[up - 1], got[up], self.sems.at[up]),
                Line(zs, -1, zs - k, zs - 1, got[down - 1], got[down], self.sems.at[down]),
            ]
        for line in self.lines:
            line.start()
        if k < zs - 1 and self.got[up + 1] is not None:
            self.fetch(k + 1)
        elif k == zs - 1:
            self.loads = [pltpu.make_async_copy(self.own(0), self.held.at[0], self.l_sem.at[0])]
            self.loads[0].start()

    def finish(self):
        for line in self.lines:
            line.finish()

    def total(self):
        zs, z = self.zs, self.z
        self.loads[0].wait()

        def add(come):
            self.held[0] = (self.held[0].astype(jnp.float32) + self.got[come][...].astype(jnp.float32)).astype(self.held.dtype)

        pl.when(z > 0)(functools.partial(add, zs - 2))
        pl.when(z < zs - 1)(functools.partial(add, 2 * zs - 3))


def partner(tensor):
    lanes = tensor.shape[-1]
    half = HEAD_DIM // 2
    lane = lax.broadcasted_iota(jnp.int32, tensor.shape, tensor.ndim - 1)
    ahead = pltpu.roll(tensor, lanes - half, tensor.ndim - 1)
    behind = pltpu.roll(tensor, half, tensor.ndim - 1)
    return jnp.where(lax.rem(lane, HEAD_DIM) < half, ahead, behind)


def first_of(my_block, half_blocks):
    return jnp.where(my_block >= half_blocks, half_blocks, 0)


def chosen_slots(places, first_block, half_len, wide):
    wanted = first_block * half_len + lax.broadcasted_iota(jnp.int32, (wide, 2 * wide), 0)
    return jnp.where(places == wanted, 1.0, 0.0).astype(jnp.bfloat16)


def stack_heads(block, first):
    return jnp.concatenate(
        [block[:, (first + h) * HEAD_DIM : (first + h + 1) * HEAD_DIM] for h in range(GROUP)], axis=0
    )


def unstack_heads(stacked, span):
    return jnp.concatenate([stacked[h * span : (h + 1) * span] for h in range(GROUP)], axis=1)


def load_window(inverse_ref, kv_ref, window, first_block):
    half_len = kv_ref.shape[1] // 2
    for n in range(window.shape[0] // half_len):
        slot = inverse_ref[first_block + n]
        at = pl.ds(pl.multiple_of(lax.rem(slot, 2) * half_len, half_len), half_len)
        window[n * half_len : (n + 1) * half_len, :] = kv_ref[lax.div(slot, 2), at, :]


def window_of(order_ref, first_ref, count, half_len):
    m, half = pl.program_id(0), pl.program_id(1)
    my_block = order_ref[lax.axis_index("seq") * 2 + half]
    half_blocks = count // half_len // 2
    first_block = jnp.where(my_block >= half_blocks, half_blocks, 0)
    return first_block, my_block * half_len, first_ref[m]


def attend_kernel(order_ref, inverse_ref, first_ref, lin_ref, cos_ref, sin_ref, kv_ref, q_ref, out_ref, window, bias):
    span = lin_ref.shape[0]
    wide = window.shape[0]
    first_block, my_place, first = window_of(order_ref, first_ref, 2 * wide, span)
    load_window(inverse_ref, kv_ref, window, first_block)
    key_place = first_block * span + lax.broadcasted_iota(jnp.int32, (span, wide), 1)
    place_here = my_place + lax.broadcasted_iota(jnp.int32, (span, wide), 0)
    start = jnp.where(place_here >= first, first, 0)
    bias[...] = jnp.where((key_place <= place_here) & (key_place >= start), 0.0, NEG_LARGE)
    width = GROUP * HEAD_DIM
    cosine = jnp.concatenate([cos_ref[...]] * (width // 128), axis=1)
    sine = jnp.concatenate([sin_ref[...]] * (width // 128), axis=1)
    for g in range(KV_HEADS):
        at = slice(g * width, (g + 1) * width)
        lin = lin_ref[:, at]
        query = (lin * cosine + partner(lin) * sine).astype(jnp.bfloat16) * jnp.bfloat16(HEAD_DIM ** -0.5)
        q_ref[:, at] = query
        key = window[:, g * HEAD_DIM : (g + 1) * HEAD_DIM]
        value = window[:, KVW + g * HEAD_DIM : KVW + (g + 1) * HEAD_DIM]
        scores = product_nt(stack_heads(query, 0), key).reshape(GROUP, span, wide) + bias[...][None]
        exps = jnp.exp(scores - jnp.max(scores, axis=-1, keepdims=True))
        total = jnp.sum(exps, axis=-1, keepdims=True).reshape(GROUP * span, 1)
        mixed = product(exps.astype(jnp.bfloat16).reshape(GROUP * span, wide), value) / total
        out_ref[:, at] = unstack_heads(mixed, span).astype(jnp.bfloat16)


def attend_back_heads(queries, d_heads, key, value, bias, span):
    query, d_mixed = stack_heads(queries, 0), stack_heads(d_heads, 0)
    scores = product_nt(key, query) + bias[...]
    exps = jnp.exp(scores - jnp.max(scores, axis=0, keepdims=True))
    probs = exps * (1.0 / jnp.sum(exps, axis=0, keepdims=True))
    weighted = probs * product_nt(value, d_mixed)
    delta = jnp.sum(weighted, axis=0, keepdims=True)
    d_scores = (weighted - probs * delta).astype(jnp.bfloat16)
    d_query = unstack_heads(product_tn(d_scores, key) * HEAD_DIM ** -0.5, span)
    return product(d_scores, query), product(probs.astype(jnp.bfloat16), d_mixed), d_query


def attend_back_kernel(order_ref, inverse_ref, first_ref, q_ref, d_ref, cos_ref, sin_ref, kv_ref, dq_ref, dkv_ref, window, bias, sums):
    span = q_ref.shape[0]
    wide = window.shape[0]
    rows = GROUP * span
    half = pl.program_id(1)
    first_block, my_place, first = window_of(order_ref, first_ref, 2 * wide, span)
    load_window(inverse_ref, kv_ref, window, first_block)
    key_place = first_block * span + lax.broadcasted_iota(jnp.int32, (wide, rows), 0)
    place_here = my_place + lax.rem(lax.broadcasted_iota(jnp.int32, (wide, rows), 1), span)
    start = jnp.where(place_here >= first, first, 0)
    bias[...] = jnp.where((key_place <= place_here) & (key_place >= start), 0.0, NEG_LARGE)

    @pl.when(half == 0)
    def _():
        sums[...] = jnp.zeros_like(sums)

    width = GROUP * HEAD_DIM
    cosine = jnp.concatenate([cos_ref[...]] * (width // 128), axis=1)
    sine = jnp.concatenate([sin_ref[...]] * (width // 128), axis=1)
    d_keys, d_values = [], []
    for g in range(KV_HEADS):
        at = slice(g * width, (g + 1) * width)
        key = window[:, g * HEAD_DIM : (g + 1) * HEAD_DIM]
        value = window[:, KVW + g * HEAD_DIM : KVW + (g + 1) * HEAD_DIM]
        d_key, d_value, d_query = attend_back_heads(q_ref[:, at], d_ref[:, at], key, value, bias, span)
        d_keys.append(d_key)
        d_values.append(d_value)
        dq_ref[:, at] = (d_query * cosine - partner(d_query) * sine).astype(jnp.bfloat16)
    d_window = jnp.concatenate(d_keys + d_values, axis=1)
    for n in range(wide // span):
        slot = inverse_ref[first_block + n]
        to = pl.ds(pl.multiple_of(lax.rem(slot, 2) * span, span), span)
        sums[lax.div(slot, 2), to, :] += d_window[n * span : (n + 1) * span]

    @pl.when(half == 1)
    def _():
        dkv_ref[...] = sums[...].astype(jnp.bfloat16)


def attention_specs(seq, micro, span):
    half_len = span // 2

    def rows(width):
        return pl.BlockSpec((half_len, width), lambda m, h, *_: (m * 2 + h, 0))

    whole = pl.BlockSpec((seq, span, 2 * KVW), lambda m, h, *_: (0, m, 0))
    return half_len, rows, whole


def attend(order, inverse, first, lin, cosine, sine, kv):
    seq, many, _ = kv.shape
    micro = first.shape[0]
    span = many // micro
    half_len, rows, whole = attention_specs(seq, micro, span)
    wide = seq * span // 2
    return pl.pallas_call(
        attend_kernel,
        grid_spec=pltpu.PrefetchScalarGridSpec(
            num_scalar_prefetch=3,
            grid=(micro, 2),
            in_specs=[rows(D), rows(128), rows(128), whole],
            out_specs=[rows(D), rows(D)],
            scratch_shapes=[pltpu.VMEM((wide, 2 * KVW), jnp.bfloat16), pltpu.VMEM((half_len, wide), jnp.float32)],
        ),
        out_shape=[jax.ShapeDtypeStruct((many, D), jnp.bfloat16)] * 2,
        compiler_params=pltpu.CompilerParams(vmem_limit_bytes=48 * MIB),
        cost_estimate=pl.CostEstimate(flops=8 * many * wide * D, bytes_accessed=16 * MIB, transcendentals=many * wide * HEADS),
    )(order, inverse, first, lin, cosine, sine, kv)


def attend_back(order, inverse, first, queries, d_heads, cosine, sine, kv):
    seq, many, _ = kv.shape
    micro = first.shape[0]
    span = many // micro
    half_len, rows, whole = attention_specs(seq, micro, span)
    wide = seq * span // 2
    return pl.pallas_call(
        attend_back_kernel,
        grid_spec=pltpu.PrefetchScalarGridSpec(
            num_scalar_prefetch=3,
            grid=(micro, 2),
            in_specs=[rows(D), rows(D), rows(128), rows(128), whole],
            out_specs=[rows(D), whole],
            scratch_shapes=[
                pltpu.VMEM((wide, 2 * KVW), jnp.bfloat16),
                pltpu.VMEM((wide, GROUP * half_len), jnp.float32),
                pltpu.VMEM((seq, span, 2 * KVW), jnp.float32),
            ],
        ),
        out_shape=[jax.ShapeDtypeStruct((many, D), jnp.bfloat16), jax.ShapeDtypeStruct(kv.shape, jnp.bfloat16)],
        compiler_params=pltpu.CompilerParams(vmem_limit_bytes=56 * MIB),
        cost_estimate=pl.CostEstimate(flops=20 * many * wide * D, bytes_accessed=24 * MIB, transcendentals=many * wide * HEADS),
    )(order, inverse, first, queries, d_heads, cosine, sine, kv)


def assemble(zs, pieces, whole, sem):
    if len(pieces) == 1:
        copy = pltpu.make_async_copy(pieces[0], whole, sem.at[0])
        copy.start()
        return [copy]
    z = lax.div(lax.axis_index("seq"), 2)
    size = whole.shape[0] // zs

    def rows(zz):
        return whole.at[pl.ds(pl.multiple_of(zz * size, size), size)]

    if len(pieces) == 2:
        pieces = [pieces[0], *(pieces[1].at[k] for k in range(zs - 1))]
    copies = [pltpu.make_async_copy(pieces[0], rows(z), sem.at[0])]
    copies[0].start()
    for k in range(1, zs):
        to = rows(lax.rem(z - k + zs, zs))
        below = pltpu.make_async_copy(pieces[k], to, sem.at[k])
        if len(pieces) == zs:
            below.start()
        else:
            above = pltpu.make_async_copy(pieces[2 * zs - 1 - k], to, sem.at[k])
            pl.when(z >= k)(below.start)
            pl.when(z < k)(above.start)
        copies.append(below)
    return copies


class Around:
    def __init__(self, zs, block, got, sems):
        z, c, r = place()
        self.copies = [
            send(block(k), got.at[k - 1], sems.at[k - 1, 0], sems.at[k - 1, 1], (lax.rem(z + k, zs) * 2 + c, r))
            for k in range(1, zs)
        ]

    def start(self):
        for copy in self.copies:
            copy.start()

    def finish(self):
        for copy in self.copies:
            copy.wait()


def swiglu(lin, d_hidden):
    n = d_hidden.shape[1]
    gate, upper = lin[:, :n], lin[:, n:]
    sig = 1.0 / (1.0 + jnp.exp(-gate))
    act = gate * sig
    d_gate = d_hidden * upper * (sig * (1.0 + gate * (1.0 - sig)))
    d_both = jnp.concatenate([d_gate.astype(jnp.bfloat16), (d_hidden * act).astype(jnp.bfloat16)], axis=1)
    return (act * upper).astype(jnp.bfloat16), d_both


def add_gradients(x, dy, hidden, d_both, both_sum, down_sum):
    for at in range(0, D, 256):
        both_sum[at : at + 256, :] += product_tn(x[:, at : at + 256], d_both)
    part = hidden.shape[1] // 4
    for at in range(0, hidden.shape[1], part):
        down_sum[at : at + part, :] += product_tn(hidden[:, at : at + part], dy)


def put_gradients(sums, staged, out, sem):
    copies = []
    for n in range(2):
        staged[n][...] = sums[n][...].astype(jnp.bfloat16)
        copies.append(pltpu.make_async_copy(staged[n], out[n], sem.at[n, 0]))
        copies[-1].start()
    for copy in copies:
        copy.wait()


def ffn_first_kernel(zs, count, linked, *refs):
    x_ref, dy_ref = refs[:2]
    both_pieces, down_pieces = refs[2 : 2 + count], refs[2 + count : 2 + 2 * count]
    refs = refs[2 + 2 * count :]
    if linked:
        rest_own, last_own, x_out_ref, rest_got, last_got, *refs = refs
    hidden_ref, d_both_ref, g_both_ref, g_down_ref, both_w, down_w, both_sum, down_sum, sem, *more = refs
    step, last = pl.program_id(0), pl.num_programs(0) - 1
    gathered, arounds = None, []
    if linked:
        x_all, a_sems, *g_sems = more
        gathered = Gather(zs, False, True, x_ref, x_all, *g_sems)
        arounds = [
            Around(zs, lambda k: rest_own, rest_got, a_sems.at[0]), Around(zs, lambda k: last_own, last_got, a_sems.at[1])
        ]

    @pl.when(step == 0)
    def _():
        copies = assemble(zs, both_pieces, both_w, sem.at[0]) + assemble(zs, down_pieces, down_w, sem.at[1])
        if linked:
            greet(neighbours(zs, True, False))
            gathered.launch()
            gathered.begin(0)
            for one in arounds:
                one.start()
        both_sum[...] = jnp.zeros_like(both_sum)
        down_sum[...] = jnp.zeros_like(down_sum)
        for copy in copies:
            copy.wait()
        if linked:
            gathered.local.wait()

    if linked:
        waits = [
            lambda: gathered.from_twin(0, 0), lambda: gathered.forward(0), lambda: gathered.from_twin(0, 1), None,
            lambda: gathered.from_twin(0, 2), lambda: gathered.finish(0), lambda: gathered.from_twin(0, 3),
        ]
        for n, wait in enumerate(waits):
            if wait is not None:
                pl.when(step == n + 1)(wait)
        x = x_all[lax.rem(step, 2), lax.div(step, 2)]
        x_out_ref[...] = x
    else:
        x = x_ref[...]
    dy = dy_ref[...]
    hidden, d_both = swiglu(product(x, both_w[...]), product_nt(dy, down_w[...]))
    hidden_ref[...] = hidden
    d_both_ref[...] = d_both
    add_gradients(x, dy, hidden, d_both, both_sum, down_sum)

    @pl.when(step == last)
    def _():
        put_gradients((both_sum, down_sum), (both_w, down_w), (g_both_ref, g_down_ref), sem)
        for one in arounds:
            one.finish()
        if linked:
            gathered.sent_all()


def ffn_second_kernel(zs, counts, linked, *refs):
    x_ref, dy_ref, hidden_ref, d_both_ref = refs[:4]
    refs = refs[4:]
    pieces = []
    for count in counts:
        pieces += [refs[:count], refs[count : 2 * count]]
        refs = refs[2 * count :]
    if linked:
        g_both_one, g_down_one, *refs = refs
    out_ref, dx_ref, g_both_ref, g_down_ref, *refs = refs
    if linked:
        *got, both_one, down_one, both_w, down_w, both_sum, down_sum, stage, sem, z_sem = refs
    else:
        got, (both_one, down_one, both_w, down_w, both_sum, down_sum, stage, sem) = [], refs
    n, wide = stage.shape[1] // 2, down_w.shape[0]
    down_rows = down_w.at[pl.ds(0, n)]
    step, last = pl.program_id(0), pl.num_programs(0) - 1
    lines = []
    if linked:
        z = lax.div(lax.axis_index("seq"), 2)
        for at, parts in ((0, g_both_one), (2, g_down_one)):
            lines += [
                Line(zs, 1, 0, 1, parts.at[lax.rem(z + zs - 1, zs)], got[at], z_sem.at[at]),
                Line(zs, -1, zs - 1, zs, parts.at[lax.rem(z + 1, zs)], got[at + 1], z_sem.at[at + 1]),
            ]

    @pl.when(step == 0)
    def _():
        copies = []
        for which, whole in enumerate((both_one, down_one, stage, down_rows)):
            copies += assemble(zs, pieces[which], whole, sem.at[which])
        if linked:
            greet(neighbours(zs, False, False))
            for line in lines:
                line.start()
        both_sum[...] = jnp.zeros_like(both_sum)
        down_sum[...] = jnp.zeros_like(down_sum)
        if wide > n:
            both_w[...] = jnp.zeros_like(both_w)
            down_w[n:, :] = jnp.zeros((wide - n, D), down_w.dtype)
        for copy in copies:
            copy.wait()
        both_w[:, :n] = stage[:, :n]
        both_w[:, wide : wide + n] = stage[:, n:]

    x, dy = x_ref[...], dy_ref[...]
    hidden, d_both = swiglu(product(x, both_w[...]), product_nt(dy, down_w[...]))
    dx_ref[...] = (product_nt(d_both_ref[...], both_one[...]) + product_nt(d_both, both_w[...])).astype(jnp.bfloat16)
    out_ref[...] = (product(hidden_ref[...], down_one[...]) + product(hidden, down_w[...])).astype(jnp.bfloat16)
    add_gradients(x, dy, hidden, d_both, both_sum, down_sum)

    @pl.when(step == last)
    def _():
        stage[:, :n] = both_sum[:, :n].astype(jnp.bfloat16)
        stage[:, n:] = both_sum[:, wide : wide + n].astype(jnp.bfloat16)
        down_w[...] = down_sum[...].astype(jnp.bfloat16)
        copies = [
            pltpu.make_async_copy(stage, g_both_ref, sem.at[0, 0]), pltpu.make_async_copy(down_rows, g_down_ref, sem.at[1, 0])
        ]
        for copy in copies:
            copy.start()
        for copy in copies:
            copy.wait()
        for line in lines:
            line.finish()


def ffn_first(x, dy, both_pieces, down_pieces, zs, others=(), collective_id=None):
    count, n = len(both_pieces), down_pieces[0].shape[0] * (zs if len(down_pieces) > 1 else 1)
    block, low, full = 256, jnp.bfloat16, jnp.float32
    sem, shape = pltpu.SemaphoreType.DMA, jax.ShapeDtypeStruct
    anywhere = pl.BlockSpec(memory_space=pl.ANY)
    linked = bool(others)
    total = dy.shape[0]

    def tokens(width):
        if linked:
            return pl.BlockSpec((block, width), lambda i: (i % 2 * 4 + i // 2, 0))
        return pl.BlockSpec((block, width), lambda i: (i, 0))

    extra_specs, extra_shapes, extra_scratch, params = [], [], [], {}
    if linked:
        extra_specs = [tokens(D)] + [anywhere] * 2
        extra_shapes = [shape(dy.shape, low)] + [shape((zs - 1,) + other.shape, low) for other in others]
        extra_scratch = [pltpu.VMEM((2, 4) + x.shape, low), sem((2, zs - 1, 2))] + gather_sems(zs, False)
        params = dict(collective_id=collective_id, has_side_effects=True)
    return pl.pallas_call(
        functools.partial(ffn_first_kernel, zs, count, linked),
        grid=(total // block,),
        in_specs=[anywhere if linked else tokens(D), tokens(D)] + [anywhere] * (2 * count + len(others)),
        out_specs=extra_specs + [tokens(n), tokens(2 * n)] + [anywhere] * 2,
        out_shape=extra_shapes
        + [shape((total, n), low), shape((total, 2 * n), low), shape((D, 2 * n), low), shape((n, D), low)],
        scratch_shapes=[
            pltpu.VMEM((D, 2 * n), low), pltpu.VMEM((n, D), low), pltpu.VMEM((D, 2 * n), full), pltpu.VMEM((n, D), full),
            sem((2, zs)),
        ] + extra_scratch,
        compiler_params=pltpu.CompilerParams(vmem_limit_bytes=60 * MIB, **params),
        cost_estimate=LONG,
    )(x, dy, *both_pieces, *down_pieces, *others)


def ffn_second(x, dy, hidden, d_both, one, two, zs, parts=(), collective_id=None):
    counts = (len(one[0]), len(two[0]))
    wides = [down[0].shape[0] * (zs if len(down) > 1 else 1) for _, down in (one, two)]
    n = wides[1]
    wide = -(-n // 128) * 128
    block, low, full = 256, jnp.bfloat16, jnp.float32
    sem, shape = pltpu.SemaphoreType.DMA, jax.ShapeDtypeStruct
    anywhere = pl.BlockSpec(memory_space=pl.ANY)

    def tokens(width):
        return pl.BlockSpec((block, width), lambda i: (i, 0))

    linked = bool(parts)
    params = dict(collective_id=collective_id, has_side_effects=True) if linked else {}
    return pl.pallas_call(
        functools.partial(ffn_second_kernel, zs, counts, linked),
        grid=(x.shape[0] // block,),
        in_specs=[tokens(D)] * 2 + [tokens(wides[0]), tokens(2 * wides[0])] + [anywhere] * (2 * sum(counts) + len(parts)),
        out_specs=[tokens(D)] * 2 + [anywhere] * (2 + 2 * len(parts)),
        out_shape=[shape(x.shape, low)] * 2 + [shape((D, 2 * n), low), shape((n, D), low)]
        + [shape(part.shape[1:], low) for part in parts for _ in range(2)],
        scratch_shapes=[
            pltpu.VMEM((D, 2 * wides[0]), low), pltpu.VMEM((wides[0], D), low),
            pltpu.VMEM((D, 2 * wide), low), pltpu.VMEM((wide, D), low),
            pltpu.VMEM((D, 2 * wide), full), pltpu.VMEM((wide, D), full), pltpu.VMEM((D, 2 * n), low),
            sem((4, zs)),
        ] + [sem((4, 2))] * linked,
        compiler_params=pltpu.CompilerParams(vmem_limit_bytes=56 * MIB, **params),
        cost_estimate=LONG,
    )(x, dy, hidden, d_both, *one[0], *one[1], *two[0], *two[1], *parts)


def split_unit(unit):
    return unit * 3 // 4 // 16 * 16


def portions(unit):
    first = split_unit(unit)
    return (0, first), (first, unit - first)


def spread_kernel(zs, rows, unit, gate_ref, up_ref, *out):
    for (begin, size), ref in zip(portions(unit), out):
        for c in range(2):
            for r in range(rows):
                for n, weight in enumerate((gate_ref, up_ref)):
                    for z in range(zs):
                        at = ((z * 2 + c) * rows + r) * unit + begin
                        to = (n * zs + z) * size
                        ref[c, r, :, to : to + size] = weight[:, at : at + size]


def spread(gate, up, zs, rows):
    wide, part = gate.shape
    unit = part // (zs * 2 * rows)
    return pl.pallas_call(
        functools.partial(spread_kernel, zs, rows, unit),
        out_shape=[jax.ShapeDtypeStruct((2, rows, wide, 2 * zs * size), gate.dtype) for _, size in portions(unit)],
    )(gate, up)


def collect_kernel(zs, rows, unit, *refs):
    given, outs = refs[:2], refs[2:]
    for n, out in enumerate(outs):
        for (begin, size), ref in zip(portions(unit), given):
            for c in range(2):
                for r in range(rows):
                    for z in range(zs):
                        at = ((z * 2 + c) * rows + r) * unit + begin
                        to = (n * zs + z) * size
                        out[:, at : at + size] = ref[c, r, :, to : to + size].astype(jnp.float32)


def collect(blocks, zs, rows, unit):
    shape = jax.ShapeDtypeStruct((blocks[0].shape[2], unit * zs * 2 * rows), jnp.float32)
    return pl.pallas_call(functools.partial(collect_kernel, zs, rows, unit), out_shape=[shape, shape])(*blocks)


def forward_kernel(zs, micro, *refs):
    order_ref, places_ref, first_ref, freq_ref, x_ref, pack_ref, both_ref, down_ref, out_ref, dy_ref, rest_ref = refs[:11]
    refs = refs[1:]
    packed, both_own, kv_all, out_all, dy_all, rest_own = refs[10:16]
    steps = 2 * zs - 2
    both_got, down_got = refs[16 : 16 + steps], refs[16 + steps : 16 + 2 * steps]
    q_ref, attn_ref, attended_ref, ffn_own, middle_ref, gains_ref, cos_ref, sin_ref = refs[16 + 2 * steps : 24 + 2 * steps]
    (staged, lin, kv_own, kv_here, window, chosen, bias, out_w, sems, *more) = refs[24 + 2 * steps :]
    low = jnp.bfloat16
    z, c, r = place()
    many = x_ref.shape[0]
    span = many // micro
    half_len = span // 2
    rows = D // zs
    greet(neighbours(zs, True, True))

    exchange = Exchange(both_ref, both_own, *more[:3])
    rest = Exchange(rest_ref, rest_own, *more[3:6])
    more = more[:3] + more[6:]
    both_chain, down_chain = Chain(zs, both_own, both_got, more[3]), Chain(zs, down_ref, down_got, more[4])
    more = more[5:]
    weights = Gather(zs, True, True, pack_ref, packed, *more[:9])
    outs = Gather(zs, True, True, out_ref, out_all, *more[9:18])
    pairs = Gather(zs, True, False, kv_own, kv_all, *more[18:27])
    dys = Gather(zs, False, True, dy_ref, dy_all, *more[27:36])

    weights.launch()
    exchange.start()
    weights.begin(0)
    outs.launch()

    lane = lax.broadcasted_iota(jnp.int32, (half_len, 128), 1)
    for i in range(2 * micro):
        place_here = order_ref[(z * 2 + c) * 2 + i % 2] * half_len + lax.broadcasted_iota(jnp.int32, (half_len, 128), 0)
        start = jnp.where(place_here >= first_ref[i // 2], first_ref[i // 2], 0)
        angle = (place_here - start).astype(jnp.float32) * freq_ref[...]
        cos_ref[i * half_len : (i + 1) * half_len, :] = jnp.cos(angle)
        sine = jnp.sin(angle)
        sin_ref[i * half_len : (i + 1) * half_len, :] = jnp.where(lax.rem(lane, HEAD_DIM) < HEAD_DIM // 2, -sine, sine)
    x = x_ref[...].astype(jnp.float32)
    factor = rms_factor(x)
    wide = window.shape[0]
    half_blocks = wide // half_len
    for half in range(2):
        my_block = order_ref[(z * 2 + c) * 2 + half]
        chosen[half] = chosen_slots(places_ref[...], first_of(my_block, half_blocks), half_len, wide)

    loads = {}

    def load(n):
        weights.complete(n)
        zz = lax.rem(z - weights.kth[n] + zs, zs)
        loads[n] = pltpu.make_async_copy(packed.at[zz], staged.at[n % 2], sems.at[n % 2])
        loads[n].start()

    def project(n):
        loads[n].wait()
        zz = lax.rem(z - weights.kth[n] + zs, zs)
        at = pl.ds(pl.multiple_of(zz * rows, rows), rows)
        block = staged[n % 2].reshape(rows, PACK)
        gains = block[:, QKV:].astype(jnp.float32).T[:8]
        gains_ref[:, at] = gains
        attn_in = (x_ref[:, at].astype(jnp.float32) * factor * gains[0:1]).astype(low)
        attn_ref[:, at] = attn_in
        value = product(attn_in, block[:, :QKV])
        lin[...] = value if n == 0 else lin[...] + value

    weights.arrive(1)
    weights.begin(1)
    weights.forward(0)
    weights.arrive(2)
    weights.begin(2)
    weights.forward(1)
    weights.finish(0)
    weights.arrive(3)
    weights.begin(3)
    down_chain.start(1)
    exchange.finish()
    both_chain.start(1)
    outs.arrive(1)
    weights.forward(2)
    weights.finish(1)
    load(0)
    outs.arrive(2)
    weights.forward(3)
    weights.finish(2)
    outs.begin(0)
    load(1)
    project(0)
    outs.arrive(3)
    outs.begin(1)
    project(1)
    weights.finish(3)
    rest.start()
    dys.launch()
    dys.begin(0)
    load(2)
    load(3)
    project(2)
    project(3)

    width = GROUP * HEAD_DIM
    cosine = jnp.concatenate([cos_ref[...]] * (width // 128), axis=1)
    sine = jnp.concatenate([sin_ref[...]] * (width // 128), axis=1)

    def turned(block, w):
        return block * cosine[:, :w] + partner(block) * sine[:, :w]

    kv_own[:, :KVW] = turned(lin[:, D : D + KVW], KVW).astype(low)
    kv_own[:, KVW:] = lin[:, D + KVW :].astype(low)
    pairs.launch()
    pairs.begin(0)
    for g in range(KV_HEADS):
        at = slice(g * width, (g + 1) * width)
        q_ref[:, at] = turned(lin[:, at], width).astype(low) * low(HEAD_DIM ** -0.5)
    outs.forward(0)
    outs.begin(2)
    both_chain.finish()
    down_chain.finish()
    both_chain.start(2)
    down_chain.start(2)
    for k in range(1, zs):
        pairs.arrive(k)
        pairs.begin(k)
    outs.forward(1)
    outs.finish(0)
    outs.begin(3)
    for k in range(zs):
        pairs.complete(k)
    kv_load = pltpu.make_async_copy(kv_all, kv_here, sems.at[2])
    kv_load.start()
    outs.forward(2)
    outs.finish(1)
    kv_load.wait()

    def attend_some(i, carry):
        m, half = lax.div(i, 2), lax.rem(i, 2)
        my_block = order_ref[(z * 2 + c) * 2 + half]
        first_block = first_of(my_block, half_blocks)
        at = pl.ds(pl.multiple_of(m * span, span), span)
        window[...] = product(chosen[half], kv_here[:, :, at, :].reshape(2 * wide, 2 * KVW)).astype(low)
        key_place = first_block * half_len + lax.broadcasted_iota(jnp.int32, (half_len, wide), 1)
        place_here = my_block * half_len + lax.broadcasted_iota(jnp.int32, (half_len, wide), 0)
        first = first_ref[m]
        start = jnp.where(place_here >= first, first, 0)
        bias[...] = jnp.where((key_place <= place_here) & (key_place >= start), 0.0, NEG_LARGE)
        here = pl.ds(pl.multiple_of(i * half_len, half_len), half_len)
        for g in range(KV_HEADS):
            at = slice(g * width, (g + 1) * width)
            key = window[:, g * HEAD_DIM : (g + 1) * HEAD_DIM]
            value = window[:, KVW + g * HEAD_DIM : KVW + (g + 1) * HEAD_DIM]
            scores = product_nt(stack_heads(q_ref[here, at], 0), key).reshape(GROUP, half_len, wide) + bias[...][None]
            exps = jnp.exp(scores - jnp.max(scores, axis=-1, keepdims=True))
            total = jnp.sum(exps, axis=-1, keepdims=True).reshape(GROUP * half_len, 1)
            mixed = product(exps.astype(low).reshape(GROUP * half_len, wide), value) / total
            attended_ref[here, at] = unstack_heads(mixed, half_len).astype(low)
        return carry

    lax.fori_loop(0, 2 * micro, attend_some, 0)
    outs.forward(3)
    outs.finish(2)
    outs.finish(3)
    dys.forward(0)
    for k in range(zs):
        outs.complete(k)
    out_load = pltpu.make_async_copy(out_all, out_w, sems.at[3])
    out_load.start()
    out_load.wait()
    middle = x_ref[...].astype(jnp.float32) + product(attended_ref[...], out_w[...].reshape(D, D))
    middle_ref[...] = middle
    ffn_own[...] = (middle * rms_factor(middle) * gains_ref[1:2, :]).astype(low)
    both_chain.finish()
    down_chain.finish()
    both_chain.start(3)
    down_chain.start(3)
    dys.finish(0)
    dys.complete(0)
    rest.finish()
    both_chain.finish()
    down_chain.finish()
    rest.end()
    exchange.end()
    for one in (weights, outs, pairs, dys):
        one.end()


def places_of(order, span):
    return (order[:, None] * (span // 2) + jnp.arange(span // 2, dtype=jnp.int32)).reshape(1, -1)


def forward(order, first, tokens, pack, both, rest, down, w_out, dy, zs, collective_id):
    many = tokens.shape[0]
    micro = first.shape[0]
    seq = 2 * zs
    wide = seq * (many // micro) // 2
    low, full = jnp.bfloat16, jnp.float32
    freq = 10000.0 ** (-(jnp.arange(128, dtype=jnp.int32) % (HEAD_DIM // 2)).astype(full) / (HEAD_DIM // 2))
    anywhere, here, smem = (pl.BlockSpec(memory_space=m) for m in (pl.ANY, pltpu.VMEM, pltpu.SMEM))
    shape = jax.ShapeDtypeStruct
    out_any = [
        shape((zs, 2, 4) + pack.shape, low),
        shape(both.shape, low),
        shape((zs, 2, many, 2 * KVW), low),
        shape((zs, 2, 4) + w_out.shape, low),
        shape((2, 4) + dy.shape, low),
        shape(rest.shape, low),
    ] + [shape(both.shape, low)] * (2 * zs - 2) + [shape(down.shape, low)] * (2 * zs - 2)
    out_here = [shape((many, D), t) for t in (low, low, low, low, full)] + [shape((8, D), full)] + [shape((many, 128), full)] * 2
    sem = pltpu.SemaphoreType.DMA
    found = pl.pallas_call(
        functools.partial(forward_kernel, zs, micro),
        out_shape=out_any + out_here,
        in_specs=[smem, here, smem] + [here] * 2 + [anywhere] * 6,
        out_specs=[anywhere] * len(out_any) + [here] * len(out_here),
        scratch_shapes=[
            pltpu.VMEM((2, 2, 4) + pack.shape, low),
            pltpu.VMEM((many, QKV), full),
            pltpu.VMEM((many, 2 * KVW), low),
            pltpu.VMEM((zs, 2, many, 2 * KVW), low),
            pltpu.VMEM((wide, 2 * KVW), low),
            pltpu.VMEM((2, wide, 2 * wide), low),
            pltpu.VMEM((many // micro // 2, wide), full),
            pltpu.VMEM((zs, 2, 4) + w_out.shape, low),
            sem((4,)),
        ] + EXCHANGE_SEMS * 2 + [sem((2 * zs - 2, 2))] * 2 + gather_sems(zs, True) * 3 + gather_sems(zs, False),
        compiler_params=pltpu.CompilerParams(
            collective_id=collective_id, has_side_effects=True, vmem_limit_bytes=56 * MIB
        ),
        cost_estimate=LONG,
    )(order, places_of(order, many // micro), first, freq.reshape(1, 128), tokens, pack, both, down, w_out, dy, rest)
    return found


def back_kernel(zs, micro, *refs):
    (order_ref, places_ref, first_ref, dy_ref, middle_ref, gains_ref, q_ref, cos_ref, sin_ref) = refs[:9]
    dx_part, out_part, both_part, down_part, out_all, kv_all, rest_part, last_part, *come = refs[9:21]
    result_ref, d_middle_ref, dq_ref, dkv_ref, gain_ref, down_ref, both_up, both_down, rest_in, last_in = refs[21:31]
    out_w, kv_here, d_heads, chosen, window, bias, d_places, sems, got, held, d_sems, dl_sem, *more = refs[31:]
    b_got, b_held, b_sems, bl_sem, r_sems, *more = more
    low, full = jnp.bfloat16, jnp.float32
    z, c, r = place()
    many = dy_ref.shape[0]
    span = many // micro
    half_len = span // 2
    greet(neighbours(zs, True, False))

    def take_d_ffn(at, value):
        d_middle_ref[at, :] = value

    def take_result(at, value):
        result_ref[at, :] = (middle_ref[at, :] + value).astype(low)

    scatters = {
        "dx": Scatter(1, False, True, dx_part, take_d_ffn, *more[:SCATTER_REFS]),
        "out": Scatter(1, False, True, out_part, take_result, *more[SCATTER_REFS : 2 * SCATTER_REFS]),
    }
    down = SumChain(zs, down_part, [got.at[n] for n in range(2 * zs - 2)], held, d_sems, dl_sem)
    none = [None] * (zs - 3)
    both = SumChain(
        zs, both_part, [b_got.at[0], both_up, *none, b_got.at[1], both_down, *none], b_held, b_sems, bl_sem
    )
    arounds = [
        Around(zs, lambda k: rest_part.at[lax.rem(z + k, zs)], rest_in, r_sems.at[0]),
        Around(zs, lambda k: last_part.at[lax.rem(z + k, zs)], last_in, r_sems.at[1]),
    ]
    comes = [
        pltpu.make_async_copy(src, dst, sems.at[2 + n])
        for n, (src, dst) in enumerate(zip(come, (b_got.at[0], b_got.at[1], got.at[0], got.at[zs - 1])))
    ]
    for copy in comes:
        copy.start()
    both.fetch(2)
    down.fetch(2)
    schedule = [(0, 3), (0, 1), (0, 2), (0, 0)]
    scatters["dx"].begin(schedule)
    for one in arounds:
        one.start()
    loads = [pltpu.make_async_copy(out_all, out_w, sems.at[0]), pltpu.make_async_copy(kv_all, kv_here, sems.at[1])]
    for load in loads:
        load.start()
    scatters["dx"].stage_a(0)
    for copy in comes:
        copy.wait()
    both.start(2)
    down.start(2)
    scatters["out"].begin(schedule)
    scatters["dx"].stage_b(0)
    scatters["out"].stage_a(0)
    scatters["dx"].stage_c(0)
    scatters["out"].stage_b(0)

    gain_ref[0:1, :] = jnp.zeros((1, D), full)

    def norm_some(i, carry):
        at = pl.ds(pl.multiple_of(i * half_len, half_len), half_len)
        middle, d_ffn = middle_ref[at, :], d_middle_ref[at, :]
        factor = rms_factor(middle)
        normed = middle * factor
        inner = d_ffn * gains_ref[1:2, :]
        d_norm = factor * (inner - normed * jnp.mean(inner * normed, axis=-1, keepdims=True))
        d_middle_ref[at, :] = dy_ref[at, :].astype(full) + d_norm
        gain_ref[0:1, :] += jnp.sum(d_ffn * normed, axis=0, keepdims=True)
        return carry

    lax.fori_loop(0, many // half_len, norm_some, 0)
    for load in loads:
        load.wait()
    d_heads[...] = product_nt(d_middle_ref[...].astype(low), out_w[...].reshape(D, D)).astype(low)

    wide = window.shape[0]
    half_blocks = wide // half_len
    width = GROUP * HEAD_DIM

    def attend_some(i, carry):
        m, half = lax.div(i, 2), lax.rem(i, 2)
        my_block = order_ref[(z * 2 + c) * 2 + half]
        first_block = jnp.where(my_block >= half_blocks, half_blocks, 0)
        wanted = first_block * half_len + lax.broadcasted_iota(jnp.int32, (wide, 2 * wide), 0)
        chosen[...] = jnp.where(places_ref[...] == wanted, 1.0, 0.0).astype(low)
        rows = pl.ds(pl.multiple_of(m * span, span), span)
        window[...] = product(chosen[...], kv_here[:, :, rows, :].reshape(2 * wide, 2 * KVW)).astype(low)
        key_place = first_block * half_len + lax.broadcasted_iota(jnp.int32, bias.shape, 0)
        place_here = my_block * half_len + lax.rem(lax.broadcasted_iota(jnp.int32, bias.shape, 1), half_len)
        first = first_ref[m]
        start = jnp.where(place_here >= first, first, 0)
        bias[...] = jnp.where((key_place <= place_here) & (key_place >= start), 0.0, NEG_LARGE)
        here = pl.ds(pl.multiple_of(i * half_len, half_len), half_len)
        cosine = jnp.concatenate([cos_ref[here, :]] * (width // 128), axis=1)
        sine = jnp.concatenate([sin_ref[here, :]] * (width // 128), axis=1)
        d_keys, d_values = [], []
        for g in range(KV_HEADS):
            at = slice(g * width, (g + 1) * width)
            key = window[:, g * HEAD_DIM : (g + 1) * HEAD_DIM]
            value = window[:, KVW + g * HEAD_DIM : KVW + (g + 1) * HEAD_DIM]
            d_key, d_value, d_query = attend_back_heads(q_ref[here, at], d_heads[here, at], key, value, bias, half_len)
            d_keys.append(d_key)
            d_values.append(d_value)
            dq_ref[here, at] = (d_query * cosine - partner(d_query) * sine).astype(low)
        d_window = jnp.concatenate(d_keys + d_values, axis=1).astype(low)
        spread_back = product_tn(chosen[...], d_window)

        @pl.when(half == 0)
        def _():
            d_places[...] = spread_back

        @pl.when(half == 1)
        def _():
            both = (d_places[...] + spread_back).astype(low)
            dkv_ref[:, :, rows, :] = both.reshape(zs, 2, span, 2 * KVW)

        return carry

    lax.fori_loop(0, micro, attend_some, 0)
    both.finish()
    down.finish()
    down.start(3)
    lax.fori_loop(micro, 2 * micro, attend_some, 0)
    scatters["out"].stage_c(0)
    down.finish()
    down.total()
    down_ref[...] = held[0].astype(full)
    for one in arounds:
        one.finish()
    for one in scatters.values():
        one.end()


def back(order, first, dy, middle, gains, queries, cosine, sine, dx_part, out_part, both_part, down_part, out_all, kv_all,
         rest_part, last_part, come, zs, collective_id):
    many = dy.shape[0]
    micro = first.shape[0]
    span = many // micro
    wide = zs * span
    low, full = jnp.bfloat16, jnp.float32
    anywhere, here, smem = (pl.BlockSpec(memory_space=m) for m in (pl.ANY, pltpu.VMEM, pltpu.SMEM))
    shape, sem = jax.ShapeDtypeStruct, pltpu.SemaphoreType.DMA
    unit = down_part.shape[1]
    piece = shape(both_part.shape[1:], low)
    return pl.pallas_call(
        functools.partial(back_kernel, zs, micro),
        out_shape=[
            shape((many, D), low), shape((many, D), full), shape((many, D), low), shape(kv_all.shape, low),
            shape((8, D), full), shape((unit, D), full), piece, piece,
            shape((zs - 1,) + rest_part.shape[1:], low), shape((zs - 1,) + last_part.shape[1:], low),
        ],
        in_specs=[smem, here, smem] + [here] * 6 + [anywhere] * 12,
        out_specs=[here] * 6 + [anywhere] * 4,
        scratch_shapes=[
            pltpu.VMEM(out_all.shape, low),
            pltpu.VMEM(kv_all.shape, low),
            pltpu.VMEM((many, D), low),
            pltpu.VMEM((wide, 2 * wide), low),
            pltpu.VMEM((wide, 2 * KVW), low),
            pltpu.VMEM((wide, GROUP * span // 2), full),
            pltpu.VMEM((2 * wide, 2 * KVW), full),
            sem((6,)),
            pltpu.VMEM((2 * zs - 2, unit, D), low),
            pltpu.VMEM((2, unit, D), low),
            sem((2 * zs - 2, 2)), sem((2,)),
            pltpu.VMEM((2,) + piece.shape, low),
            pltpu.VMEM((2,) + piece.shape, low),
            sem((2 * zs - 2, 2)), sem((2,)), sem((2, zs - 1, 2)),
        ] + scatter_scratch(1, True, many, D, True) * 2,
        compiler_params=pltpu.CompilerParams(
            collective_id=collective_id, has_side_effects=True, vmem_limit_bytes=62 * MIB
        ),
        cost_estimate=LONG,
    )(order, places_of(order, span), first, dy, middle, gains, queries, cosine, sine, dx_part, out_part, both_part, down_part,
      out_all, kv_all, rest_part, last_part, *come)


def products_kernel(attended_ref, attn_ref, d_middle_ref, dq_ref, packed_ref, out_ref, query_ref, d_attn_ref):
    low = jnp.bfloat16
    out_ref[...] = product_tn(attended_ref[...], d_middle_ref[...].astype(low)).astype(low)
    query_ref[...] = product_tn(attn_ref[...], dq_ref[...]).astype(low)
    d_attn_ref[...] = product_nt(dq_ref[...], packed_ref[...])


def products(attended, attn_in, d_middle, d_query, packed):
    many, block = attended.shape[0], 256
    low, shape = jnp.bfloat16, jax.ShapeDtypeStruct
    narrow = pl.BlockSpec((many, block), lambda i: (0, i))
    tall = pl.BlockSpec((block, D), lambda i: (i, 0))
    whole = pl.BlockSpec((many, D), lambda i: (0, 0))
    return pl.pallas_call(
        products_kernel,
        grid=(D // block,),
        in_specs=[narrow, narrow, whole, whole, tall],
        out_specs=[tall, tall, narrow],
        out_shape=[shape((D, D), low), shape((D, D), low), shape((many, D), jnp.float32)],
        compiler_params=pltpu.CompilerParams(vmem_limit_bytes=32 * MIB),
        cost_estimate=pl.CostEstimate(flops=6 * many * D * D, bytes_accessed=30 * MIB, transcendentals=0),
    )(attended, attn_in, d_middle, d_query, packed)


def weights_kernel(zs, *refs):
    x_ref, attn_ref, d_middle_ref, d_attn_ref, gains_ref, gain_two_ref, cos_ref, sin_ref, dkv_ref = refs[:9]
    packed, both_part, both_up, both_down, g_out, g_query, rest_part, last_part, rest_in, last_in = refs[9:19]
    x_grad_ref, out_ref, query_ref, pack_ref, last_ref, moved_ref, rest_ref = refs[19:26]
    kv_w, d_kv, pack_g, sems, got, held, b_sems, bl_sem, rest_here, last_here, *more = refs[26:]
    exchange_sems, rest_sems, more = more[:3], more[3:6], more[6:]
    z = place()[0]
    low, full = jnp.bfloat16, jnp.float32
    greet(neighbours(zs, True, True))

    def into(ref):
        def take(at, value):
            ref[at, :] = value

        return take

    def next_refs(staged):
        nonlocal more
        mine, more = more[:SCATTER_REFS], more[SCATTER_REFS:]
        return mine if staged else [None, *mine[1:]]

    pairs = Scatter(zs, True, False, dkv_ref, into(d_kv), *next_refs(False))
    scatters = {
        "out": Scatter(zs, True, True, g_out, into(out_ref), *next_refs(True)),
        "query": Scatter(zs, True, True, g_query, into(query_ref), *next_refs(True)),
        "pack": Scatter(zs, True, True, pack_g, into(pack_ref), *next_refs(False)),
    }
    items = [(name, k) for k in range(1, zs) for name in ("out", "query")]
    items[4:4] = [("pack", 1)]
    items += [("pack", k) for k in range(2, zs)] + [("out", 0), ("query", 0), ("pack", 0)]
    rounds, schedules = scatter_plan(items)

    none = [None] * (zs - 3)
    chain = SumChain(zs, both_part, [*none, got.at[0], got.at[1], *none, got.at[2], got.at[3]], held, b_sems, bl_sem)
    loads = [
        pltpu.make_async_copy(both_up, got.at[0], sems.at[0]),
        pltpu.make_async_copy(both_down, got.at[2], sems.at[1]),
        pltpu.make_async_copy(packed.at[:, :, :, :, pl.ds(D, 2 * KVW)], kv_w, sems.at[2]),
    ]
    for load in loads:
        load.start()
    small = [
        pltpu.make_async_copy(rest_part.at[z], rest_here.at[0], sems.at[3]),
        pltpu.make_async_copy(last_part.at[z], last_here.at[0], sems.at[4]),
        pltpu.make_async_copy(rest_in, rest_here.at[pl.ds(1, zs - 1)], sems.at[5]),
        pltpu.make_async_copy(last_in, last_here.at[pl.ds(1, zs - 1)], sems.at[6]),
    ]
    for load in small:
        load.start()
    chain.fetch(zs - 1)
    pairs.begin([])
    scatters["out"].begin(schedules["out"])
    scatters["query"].begin(schedules["query"])
    for k in range(1, zs):
        pairs.stage_c(k)
    for load in loads:
        load.wait()
    chain.start(zs - 1)
    for load in small:
        load.wait()
    last_ref[...] = sum(last_here[n].astype(full) for n in range(zs))
    rest_here[0] = sum(rest_here[n].astype(full) for n in range(zs)).astype(low)
    rest = Exchange(rest_here.at[0], rest_ref, *rest_sems)
    rest.start()

    def keys_and_norm():
        pairs.stage_c(0)
        lanes = KVW // 128
        cosine = jnp.concatenate([cos_ref[...]] * lanes, axis=1)
        sine = jnp.concatenate([sin_ref[...]] * lanes, axis=1)
        d_key = d_kv[:, :KVW]
        d_lin = jnp.concatenate([d_key * cosine - partner(d_key) * sine, d_kv[:, KVW:]], axis=1).astype(low)
        d_attn = d_attn_ref[...] + product_nt(d_lin, kv_w[...].reshape(D, 2 * KVW))
        x = x_ref[...].astype(full)
        factor = rms_factor(x)
        normed = x * factor
        inner = d_attn * gains_ref[0:1, :]
        d_x = factor * (inner - normed * jnp.mean(inner * normed, axis=-1, keepdims=True))
        x_grad_ref[...] = (d_middle_ref[...] + d_x).astype(low)
        gain_one = jnp.sum(d_attn * normed, axis=0, keepdims=True)
        rows = lax.broadcasted_iota(jnp.int32, (128, D), 0)
        both = jnp.where(rows == 0, gain_one, jnp.where(rows == 1, gain_two_ref[0:1, :], 0.0))
        pack = jnp.concatenate([product_tn(attn_ref[...], d_lin), both.T], axis=1).astype(low)
        pack_g[...] = pack.reshape(pack_g.shape)
        scatters["pack"].begin([])

    for n, stages in enumerate(rounds):
        if n == 3:
            keys_and_norm()
        if n == len(rounds) - 3:
            chain.finish()
            chain.total()
            exchange = Exchange(held.at[0], moved_ref, *exchange_sems)
            exchange.start()
        for stage in stages:
            run_stage(scatters, *stage)
    for one in (rest, exchange):
        one.finish()
        one.end()
    for one in (pairs, *scatters.values()):
        one.end()


def weight_sums(x, attn_in, d_middle, d_attn, gains, gain_two, cosine, sine, d_kv, packed, both_part, both_up, both_down, g_out,
                g_query, rest_part, last_part, rest_in, last_in, zs, collective_id):
    many = x.shape[0]
    low, full = jnp.bfloat16, jnp.float32
    anywhere, here = (pl.BlockSpec(memory_space=m) for m in (pl.ANY, pltpu.VMEM))
    shape, sem = jax.ShapeDtypeStruct, pltpu.SemaphoreType.DMA
    wide = packed.shape[3]
    narrow = 2 * KVW + 128
    block = both_part.shape[1:]
    return pl.pallas_call(
        functools.partial(weights_kernel, zs),
        out_shape=[
            shape((many, D), low), shape((wide, D), full), shape((wide, D), full), shape((wide, narrow), full),
            shape(last_part.shape[1:], full), shape(block, low), shape(rest_part.shape[1:], low),
        ],
        in_specs=[here] * 9 + [anywhere] * 10,
        out_specs=[here] * 5 + [anywhere] * 2,
        scratch_shapes=[
            pltpu.VMEM(packed.shape[:4] + (2 * KVW,), low),
            pltpu.VMEM((many, 2 * KVW), full),
            pltpu.VMEM((zs, 2, 4, wide, narrow), low),
            sem((7,)),
            pltpu.VMEM((4,) + block, low),
            pltpu.VMEM((2,) + block, low),
            sem((2 * zs - 2, 2)), sem((2,)),
            pltpu.VMEM(rest_part.shape, low),
            pltpu.VMEM(last_part.shape, low),
        ] + EXCHANGE_SEMS * 2
        + scatter_scratch(zs, False, many, 2 * KVW, False)
        + scatter_scratch(zs, True, wide, D, True) * 2
        + scatter_scratch(zs, True, wide, narrow, False),
        compiler_params=pltpu.CompilerParams(
            collective_id=collective_id, has_side_effects=True, vmem_limit_bytes=62 * MIB
        ),
        cost_estimate=LONG,
    )(x, attn_in, d_middle, d_attn, gains, gain_two, cosine, sine, d_kv, packed, both_part, both_up, both_down, g_out,
      g_query, rest_part, last_part, rest_in, last_in)


class Links:
    def __init__(self, seq, rows):
        self.zs, self.rows = seq // 2, rows
        self.kernels = rows == 4 and self.zs == 4
        self.z_groups = [[2 * z + c for z in range(self.zs)] for c in range(2)]
        self.core_groups = [[2 * z, 2 * z + 1] for z in range(self.zs)]

    def gather_z(self, block):
        return lax.all_gather(block, "seq", axis=0, tiled=True, axis_index_groups=self.z_groups)

    def scatter_z(self, blocks):
        return lax.psum_scatter(blocks, "seq", scatter_dimension=0, tiled=True, axis_index_groups=self.z_groups)

    def exchange_xla(self, blocks):
        moved = lax.all_to_all(blocks, "rows", split_axis=1, concat_axis=1, tiled=True)
        return lax.all_to_all(moved, "seq", split_axis=0, concat_axis=0, tiled=True, axis_index_groups=self.core_groups)

    def gather(self, array, z_flag, planes):
        if planes:
            array = lax.all_gather(array, "rows", axis=0)
        array = lax.all_gather(array, "seq", axis=0, axis_index_groups=self.core_groups)
        return self.gather_z(array[None]) if z_flag else array

    def scatter(self, blocks, z_flag, planes):
        blocks = self.scatter_z(blocks)[0] if z_flag else blocks
        blocks = lax.psum_scatter(blocks, "seq", scatter_dimension=0, tiled=True, axis_index_groups=self.core_groups)[0]
        if planes:
            blocks = lax.psum_scatter(blocks, "rows", scatter_dimension=0, tiled=True)[0]
        return blocks.astype(jnp.float32)


def on_device(seq, rows, tokens, w_query, w_key, w_value, w_out, w_gate, w_up, w_down, gain_attn, gain_ffn, lengths, order, cotangent):
    links = Links(seq, rows)
    zs = links.zs
    micro, _, span, _ = tokens.shape
    half_len = span // 2
    many = micro * span
    low = jnp.bfloat16
    wide = w_gate.shape[0]
    unit = w_down.shape[0]

    both, rest = spread(w_gate, w_up, zs, rows)
    cut = split_unit(unit)
    flat, flat_rest = (2 * rows * wide, 2 * zs * cut), (2 * rows * wide, 2 * zs * (unit - cut))
    gains = jnp.pad(jnp.stack([gain_attn, gain_ffn], axis=1), ((0, 0), (0, 126)))
    pack = jnp.concatenate([w_query, w_key, w_value, gains], axis=1)
    dy_own = cotangent.reshape(many, D)
    own_tokens = tokens.reshape(many, D)
    x = own_tokens.astype(jnp.float32)
    first = lengths[:, 0, 0]
    slot_of = jnp.argmax(order[None, :] == jnp.arange(order.shape[0], dtype=jnp.int32)[:, None], axis=1).astype(jnp.int32)
    chained = links.kernels
    if chained:
        down_own, last_own = w_down[:cut], w_down[cut:]
        found = forward(order, first, own_tokens, pack, both, rest, down_own, w_out, dy_own, zs, 0)
        packed, both_own, kv, out_w, dy, rest_own = found[:6]
        both_w = [b.reshape(flat) for b in (both_own, *found[6 : 4 + 2 * zs])]
        down_w = [down_own, *found[4 + 2 * zs : 2 + 4 * zs]]
        rest_own = rest_own.reshape(flat_rest)
        queries, attn_in, attended, ffn_in, middle, gains, cosine, sine = found[2 + 4 * zs :]
        packed = packed.reshape(D, PACK)
    else:
        both_w = [links.gather_z(links.exchange_xla(both).reshape(flat))]
        rest_w = [links.gather_z(links.exchange_xla(rest).reshape(flat_rest))]
        down_w, last_w = [links.gather_z(w_down[:cut])], [links.gather_z(w_down[cut:])]
        packed, dy = links.gather(pack, True, True).reshape(D, PACK), links.gather(dy_own, False, True)
        gain_one, gain_two = packed[:, QKV].astype(jnp.float32), packed[:, QKV + 1].astype(jnp.float32)
        mine = slot_places(order, half_len, lax.axis_index("seq") * span + jnp.arange(span, dtype=jnp.int32))
        start = jnp.where(mine[None, :] >= first[:, None], first[:, None], 0)
        inverse = 10000.0 ** (-jnp.arange(HEAD_DIM // 2, dtype=jnp.float32) / (HEAD_DIM // 2))
        angles = ((mine[None, :] - start).astype(jnp.float32)[..., None] * inverse).reshape(many, HEAD_DIM // 2)
        cosine, sine = jnp.cos(angles), jnp.sin(angles)
        cosine, sine = jnp.tile(cosine, (1, 4)), jnp.tile(jnp.concatenate([-sine, sine], axis=1), (1, 2))
        attn_in = (x * rms_factor(x) * gain_one).astype(low)
        lin = product(attn_in, packed)
        kv_own = jnp.concatenate([turn(lin[:, D : D + KVW], cosine, sine), lin[:, D + KVW : QKV]], axis=1).astype(low)
        kv, out_w = links.gather(kv_own, True, False), links.gather(w_out, True, True)
        queries, attended = attend(order, slot_of, first, lin, cosine, sine, kv.reshape(seq, many, 2 * KVW))
        middle = x + product(attended, out_w.reshape(D, D))
        ffn_in = links.gather((middle * rms_factor(middle) * gain_two).astype(low), False, True).reshape(2 * rows * many, D)
    kv = kv.reshape(seq, many, 2 * KVW)
    out_w = out_w.reshape(D, D)
    dy = dy.reshape(2 * rows * many, D)

    shards = (zs, 2, rows, wide)
    if chained:
        ffn_in, rest_got, last_got, hidden, d_both, grad_both, grad_down = ffn_first(
            ffn_in, dy, both_w, down_w, zs, (rest_own, last_own), 1
        )
        rest_w, last_w = [rest_own, rest_got], [last_own, last_got]
        grad_both, grad_down = grad_both.reshape(*shards, 2 * zs * cut), grad_down.reshape(zs, cut, D)
        result_part, d_ffn_part, grad_rest, grad_last, *come = ffn_second(
            ffn_in, dy, hidden, d_both, (both_w, down_w), (rest_w, last_w), zs, (grad_both, grad_down), 2
        )
    else:
        hidden, d_both, grad_both, grad_down = ffn_first(ffn_in, dy, both_w, down_w, zs)
        grad_both, grad_down = grad_both.reshape(*shards, 2 * zs * cut), grad_down.reshape(zs, cut, D)
        result_part, d_ffn_part, grad_rest, grad_last = ffn_second(
            ffn_in, dy, hidden, d_both, (both_w, down_w), (rest_w, last_w), zs
        )
    grad_rest, grad_last = grad_rest.reshape(*shards, 2 * zs * (unit - cut)), grad_last.reshape(zs, unit - cut, D)
    d_ffn_part, result_part = (part.reshape(2, rows, many, D) for part in (d_ffn_part, result_part))
    if chained:
        out_all, kv_all = out_w.reshape(*shards, D), kv.reshape(zs, 2, many, 2 * KVW)
        result, d_middle, d_query, d_kv, gain_two_grad, grad_down, both_up, both_down, rest_in, last_in = back(
            order, first, dy_own, middle, gains, queries, cosine, sine, d_ffn_part, result_part, grad_both, grad_down,
            out_all, kv_all, grad_rest, grad_last, come, zs, 3,
        )
        grad_out, grad_query, d_attn = products(attended, attn_in, d_middle, d_query, packed)
        grad_out, grad_query = grad_out.reshape(*shards, D), grad_query.reshape(*shards, D)
        x_grad, grad_out, grad_query, pack_grad, grad_last, grad_both, grad_rest = weight_sums(
            own_tokens, attn_in, d_middle, d_attn, gains, gain_two_grad, cosine, sine, d_kv, packed.reshape(*shards, PACK),
            grad_both, both_up, both_down, grad_out, grad_query, grad_rest, grad_last, rest_in, last_in, zs, 4,
        )
    else:
        d_ffn_in = links.scatter(d_ffn_part, False, True)
        result = (middle + links.scatter(result_part, False, True)).astype(low)
        grad_both, grad_rest = (links.exchange_xla(links.scatter_z(grad)[0]) for grad in (grad_both, grad_rest))
        grad_down, grad_last = (links.scatter_z(grad)[0].astype(jnp.float32) for grad in (grad_down, grad_last))
        factor_two = rms_factor(middle)
        d_part, grad_gain_two = norm_back(d_ffn_in, middle * factor_two, factor_two, gain_two)
        d_middle = dy_own.astype(jnp.float32) + d_part
        d_mid_low = d_middle.astype(low)
        grad_out = links.scatter(product_tn(attended, d_mid_low).astype(low).reshape(*shards, D), True, True)
        d_heads = product_nt(d_mid_low, out_w).astype(low)
        d_query, d_kv = attend_back(order, slot_of, first, queries, d_heads, cosine, sine, kv)
        grad_query = links.scatter(product_tn(attn_in, d_query).astype(low).reshape(*shards, D), True, True)
        d_kv = links.scatter(d_kv.reshape(zs, 2, many, 2 * KVW), True, False)
        d_key = turn(d_kv[:, :KVW], cosine, -sine)
        d_kv = jnp.concatenate([d_key.astype(low), d_kv[:, KVW:].astype(low)], axis=1)
        d_attn_in = product_nt(d_query, packed[:, :D]) + product_nt(d_kv, packed[:, D:QKV])
        factor_one = rms_factor(x)
        d_x, grad_gain_one = norm_back(d_attn_in, x * factor_one, factor_one, gain_one)
        x_grad = (d_middle + d_x).astype(low)
        gains_grad = jnp.pad(jnp.stack([grad_gain_one, grad_gain_two], axis=1), ((0, 0), (0, 126)))
        pack_grad = jnp.concatenate([product_tn(attn_in, d_kv), gains_grad], axis=1).astype(low)
        pack_grad = links.scatter(pack_grad.reshape(*shards, 2 * KVW + 128), True, True)
    grad_gate, grad_up = collect((grad_both, grad_rest), zs, rows, unit)
    grad_down = jnp.concatenate([grad_down, grad_last])

    return (
        result.reshape(tokens.shape),
        x_grad.reshape(tokens.shape),
        grad_query,
        pack_grad[:, :KVW],
        pack_grad[:, KVW : 2 * KVW],
        grad_out,
        grad_gate,
        grad_up,
        grad_down,
        pack_grad[:, 2 * KVW],
        pack_grad[:, 2 * KVW + 1],
    )


def solution(mesh):
    both = ("seq", "rows")
    row = P(None, "rows", "seq", None)
    weight, gain = P(both, None), P(both)
    return jax.shard_map(
        functools.partial(on_device, mesh.shape["seq"], mesh.shape["rows"]),
        mesh=mesh,
        in_specs=(row,) + (weight,) * 7 + (gain, gain, P(None, "rows", None), P(), row),
        out_specs=(row, row) + (weight,) * 7 + (gain, gain),
        check_vma=False,
    )
```

```python
import functools

import jax
import jax.numpy as jnp
from jax import lax
from jax.experimental import pallas as pl
from jax.experimental.pallas import tpu as pltpu
from jax.sharding import PartitionSpec as P

D = 2048
HEADS = 32
KV_HEADS = 4
HEAD_DIM = 64
GROUP = 8
KVW = 256
QKV = D + 2 * KVW
PACK = QKV + 128

EPSILON = 1e-05
NEG_LARGE = -1e30
MESH = pl.DeviceIdType.MESH
MIB = 1 << 20
LONG = pl.CostEstimate(flops=50_000_000_000, bytes_accessed=150 * MIB, transcendentals=0)


def product(left, right):
    return jnp.dot(left, right, preferred_element_type=jnp.float32)


def product_nt(left, right):
    return lax.dot_general(left, right, (((1,), (1,)), ((), ())), preferred_element_type=jnp.float32)


def product_tn(left, right):
    return lax.dot_general(left, right, (((0,), (0,)), ((), ())), preferred_element_type=jnp.float32)


def rms_factor(values):
    return lax.rsqrt(jnp.mean(values * values, axis=-1, keepdims=True) + EPSILON)


def norm_back(d_scaled, normed, factor, gain):
    inner = d_scaled * gain
    mean = jnp.mean(inner * normed, axis=-1, keepdims=True)
    return factor * (inner - normed * mean), jnp.sum(d_scaled * normed, axis=0)


def turn(tensor, cosine, sine):
    rows, lanes = tensor.shape
    half = HEAD_DIM // 2
    swapped = jnp.flip(tensor.reshape(rows, lanes // HEAD_DIM, 2, half), axis=2).reshape(rows, lanes)
    return tensor * jnp.tile(cosine, (1, lanes // 128)) + swapped * jnp.tile(sine, (1, lanes // 128))


def slot_places(order, half_len, slot_ids):
    matches = (slot_ids // half_len)[:, None] == jnp.arange(order.shape[0], dtype=jnp.int32)[None, :]
    return jnp.sum(jnp.where(matches, order[None, :], 0), axis=1) * half_len + slot_ids % half_len


def place():
    s, r = lax.axis_index("seq"), lax.axis_index("rows")
    return lax.div(s, 2), lax.rem(s, 2), r


def send(src, dst, ssem, rsem, device):
    return pltpu.make_async_remote_copy(
        src_ref=src, dst_ref=dst, send_sem=ssem, recv_sem=rsem, device_id=device, device_id_type=MESH
    )


def greet(devices):
    barrier = pltpu.get_barrier_semaphore()
    for device in devices:
        pl.semaphore_signal(barrier, inc=1, device_id=device, device_id_type=MESH)
    pl.semaphore_wait(barrier, len(devices))


def corners(r):
    return r, r + 1 - 2 * lax.rem(r, 2), lax.rem(r + 2, 4), 3 - r


def exchange_others():
    return [(cc, j) for j in (3, 1, 2, 0) for cc in range(2) if (cc, j) != (0, 0)]


class Exchange:
    def __init__(self, own, out, ssem, rsem, l_sem):
        z, c, r = place()
        line = corners(r)
        self.own, self.out, self.ssem, self.rsem, self.here = own, out, ssem, rsem, (c, r)
        self.others = [(1 - c if cc else c, line[j]) for cc, j in exchange_others()]
        self.devices = [(z * 2 + core, row) for core, row in self.others]
        self.local = pltpu.make_async_copy(own.at[c, r], out.at[c, r], l_sem)

    def start(self):
        self.copies = []
        for i, other in enumerate(self.others):
            copy = send(self.own.at[other], self.out.at[self.here], self.ssem.at[i], self.rsem.at[i], self.devices[i])
            copy.start()
            self.copies.append(copy)
        self.local.start()

    def finish(self):
        for i, other in enumerate(self.others):
            dst = self.out.at[other]
            send(dst, dst, self.ssem.at[i], self.rsem.at[i], self.devices[i]).wait_recv()
        self.local.wait()

    def end(self):
        for copy in self.copies:
            copy.wait_send()


class Line:
    def __init__(self, zs, way, lo, hi, src, dst, sems):
        z, c, r = place()
        lo, hi = (lo, min(hi, zs - 1)) if way == 1 else (max(lo, 1), hi)
        self.sends = (z >= lo) & (z < hi)
        self.gets = (z - way >= lo) & (z - way < hi)
        to = lax.rem(z + way + zs, zs)
        self.copy = send(src, dst, sems.at[0], sems.at[1], (to * 2 + c, r))

    def start(self):
        pl.when(self.sends)(self.copy.start)

    def finish(self):
        pl.when(self.sends)(self.copy.wait_send)
        pl.when(self.gets)(self.copy.wait_recv)


LINE_SEMS = pltpu.SemaphoreType.DMA((2,))
EXCHANGE_SEMS = [pltpu.SemaphoreType.DMA((7,)), pltpu.SemaphoreType.DMA((7,)), pltpu.SemaphoreType.DMA]


def neighbours(zs, planes, moved):
    z, c, r = place()
    line = corners(r)
    s = z * 2 + c
    devices = [(z * 2 + 1 - c, r)]
    if moved:
        devices = [(z * 2 + (1 - c if cc else c), line[j]) for cc, j in exchange_others()]
    elif planes:
        devices += [(s, line[1]), (s, line[2])]
    return devices + [(lax.rem(z + k, zs) * 2 + c, r) for k in range(1, zs)]


class Gather:
    def __init__(self, zs, z_flag, planes, own, out, z_ssem, z_rsem, f_ssem, f_rsem, h_ssem, h_rsem, c_ssem, c_rsem, l_sem):
        self.__dict__.update(locals())
        self.z, self.c, self.r = place()
        self.line = corners(self.r)
        self.s = self.z * 2 + self.c
        self.twin = (self.z * 2 + 1 - self.c, self.r)
        self.count = zs if z_flag else 1
        self.half = own.shape[0] // 2
        self.pending = []
        self.sent = []
        z = self.z
        self.kth = [0, jnp.where(z == 0, 3, 1), jnp.where((z == 0) | (z == 3), 2, 3), jnp.where(z == 0, 1, jnp.where(z == 3, 3, 2))]

    def start(self, copy):
        copy.start()
        self.pending.append(copy.wait_send)

    def slot(self, k, other, j):
        if not self.z_flag:
            return self.out.at[other, j]
        core = 1 - self.c if other else self.c
        zz = lax.rem(self.z - k + self.zs, self.zs)
        return self.out.at[zz, core, self.line[j]] if self.planes else self.out.at[zz, core]

    def z_copy(self, n, way, k, src, dst):
        to = (lax.rem(self.z + way + self.zs, self.zs) * 2 + self.c, self.r)
        return send(src, dst, self.z_ssem.at[n, 0 if way == 1 else 1], self.z_rsem.at[k], to)

    def hand_on(self, n, src, dst):
        z, k, zs = self.z, self.kth[n], self.zs
        up, down = (z < zs - 1, z > 0) if n == 0 else ((z >= k) & (z < zs - 1), (z < k) & (z > 0))
        for way, goes, step in ((1, up, 1), (-1, down, zs - 1)):
            copy = self.z_copy(n, way, lax.rem(k + step, zs), src, dst)
            pl.when(goes)(copy.start)
            self.sent.append((goes, copy))

    def near(self, k, j, src):
        dst = self.slot(k, 0, j) if src is None or not self.z_flag else self.slot(k, 0, 0)
        return send(dst if src is None else src, dst, self.f_ssem.at[k, j - 1], self.f_rsem.at[k, j - 1], (self.s, self.line[j]))

    def part(self, ref, j):
        return ref.at[pl.ds(self.half if j == 1 else 0, self.half)]

    def far(self, k, j, src):
        if src is None:
            src = dst = self.part(self.slot(k, 0, 3), j)
        else:
            dst = self.part(src if self.z_flag else self.out.at[0, 3], j)
            src = self.part(src, j)
        return send(src, dst, self.h_ssem.at[k, j - 1], self.h_rsem.at[k, j - 1], (self.s, self.line[3 - j]))

    def twin_copy(self, k, j, src):
        dst = self.slot(k, 0, j) if self.z_flag else self.out.at[1, j]
        return send(src, dst, self.c_ssem.at[k, j], self.c_rsem.at[k, j], self.twin)

    def to_twin(self, k, j, src):
        self.start(self.twin_copy(k, j, src))

    def from_twin(self, k, j):
        dst = self.slot(k, 1, j)
        send(dst, dst, self.c_ssem.at[k, j], self.c_rsem.at[k, j], self.twin).wait_recv()

    def launch(self):
        self.local = pltpu.make_async_copy(self.own, self.slot(0, 0, 0), self.l_sem)
        self.local.start()
        if self.count > 1 and self.planes:
            self.hand_on(0, self.own, self.slot(0, 0, 0))
        elif self.count > 1:
            for k in range(1, self.count):
                self.start(self.z_copy(k, k, k, self.own, self.slot(0, 0, 0)))

    def arrive(self, n):
        k = self.kth[n]
        src = self.slot(k, 0, 0)
        self.z_copy(n, 1, k, src, src).wait_recv()
        if self.planes:
            self.hand_on(n, src, src)

    def begin(self, n):
        k = self.kth[n]
        src = self.slot(k, 0, 0) if n else self.own
        if self.planes:
            for j in (1, 2):
                self.start(self.near(k, j, src))
        self.to_twin(k, 0, src)

    def forward(self, n):
        k = self.kth[n]
        for j in (1, 2):
            self.near(k, j, None).wait_recv()
            src = self.slot(k, 0, j)
            self.start(self.far(k, j, src))
            self.to_twin(k, j, src)

    def finish(self, n):
        k = self.kth[n]
        for j in (1, 2):
            self.far(k, j, None).wait_recv()
        self.to_twin(k, 3, self.slot(k, 0, 3))

    def complete(self, n):
        k = self.kth[n]
        if n == 0:
            self.local.wait()
        for j in range(4 if self.planes else 1):
            self.from_twin(k, j)

    def sent_all(self):
        for j in (1, 2):
            self.near(0, j, self.own).wait_send()
            self.far(0, j, self.slot(0, 0, j)).wait_send()
        for j in range(4):
            self.twin_copy(0, j, self.slot(0, 0, j) if j else self.own).wait_send()

    def end(self):
        for goes, copy in self.sent:
            pl.when(goes)(copy.wait_send)
        for wait in self.pending:
            wait()


def gather_sems(zs, z_flag):
    sem = pltpu.SemaphoreType.DMA
    n = zs if z_flag else 1
    return [sem((n, 2)), sem((n,)), sem((n, 2)), sem((n, 2)), sem((n, 2)), sem((n, 2)), sem((n, 4)), sem((n, 4)), sem]


class Chain:
    def __init__(self, zs, own, got, sems):
        self.zs, self.own, self.got, self.sems = zs, own, got, sems
        self.lines = []

    def start(self, k):
        zs = self.zs
        up, down = (self.own, self.own) if k == 1 else (self.got[k - 2], self.got[zs + k - 3])
        self.lines = [
            Line(zs, 1, k - 1, zs, up, self.got[k - 1], self.sems.at[k - 1]),
            Line(zs, -1, 0, zs - k + 1, down, self.got[zs + k - 2], self.sems.at[zs + k - 2]),
        ]
        for line in self.lines:
            line.start()

    def finish(self):
        for line in self.lines:
            line.finish()


class Scatter:
    def __init__(self, zs, z_flag, planes, given, final, stage, twin_in, half_in, full_in, z_in, l_sem, c_ssem, c_rsem, h_ssem,
                 h_rsem, f_ssem, f_rsem, z_ssem, z_rsem):
        self.__dict__.update(locals())
        self.z, self.c, self.r = place()
        self.line = corners(self.r)
        self.s = self.z * 2 + self.c
        self.twin = (self.z * 2 + 1 - self.c, self.r)
        self.rows = twin_in.shape[2]
        self.step = 16
        self.spots = (3, 1, 2, 0) if planes else (0,)
        self.zs = zs if z_flag else 1
        self.order = list(range(1, self.zs)) + [0]
        self.pending = []
        self.loads = []
        self.settled = 0

    def at_z(self, k):
        return (lax.rem(self.z + k, self.zs) * 2 + self.c, self.r)

    def block(self, k, other, j):
        if not self.z_flag:
            return self.given.at[other, j]
        zz, core = lax.rem(self.z + k, self.zs), 1 - self.c if other else self.c
        return self.given.at[zz, core, self.line[j]] if self.planes else self.given.at[zz, core]

    def start(self, copy):
        copy.start()
        self.pending.append(copy.wait_send)

    def begin(self, schedule):
        for k in self.order:
            for j in self.spots:
                self.start(self.twin_copy(k, j, self.block(k, 1, j)))
        if self.stage is not None:
            self.loads = [
                pltpu.make_async_copy(self.block(k, 0, j), self.stage.at[n % 2], self.l_sem.at[n % 2])
                for n, (k, j) in enumerate(schedule)
            ]
            for load in self.loads[:2]:
                load.start()

    def twin_copy(self, k, j, src):
        dst = self.twin_in.at[k, j]
        return send(dst if src is None else src, dst, self.c_ssem.at[k, j], self.c_rsem.at[k, j], self.twin)

    def settle(self, k, j, parts):
        own = self.block(k, 0, j)
        n = self.settled
        if self.stage is not None:
            self.loads[n].wait()
            own = self.stage.at[n % 2]
        self.twin_copy(k, j, None).wait_recv()
        step = self.step
        for first, last, more in parts:

            def body(i, carry, first=first, more=more):
                at = pl.ds(pl.multiple_of(first + i * step, step), step)
                value = own[at, :].astype(jnp.float32) + self.twin_in[k, j, at, :].astype(jnp.float32)
                for ref, offset in more:
                    there = pl.ds(pl.multiple_of(first - offset + i * step, step), step)
                    value = value + ref[there, :].astype(jnp.float32)
                if k == 0 and j == 0:
                    self.final(at, value)
                else:
                    self.twin_in[k, j, at, :] = value.astype(self.twin_in.dtype)
                return carry

            lax.fori_loop(0, (last - first) // step, body, 0)
        if n + 2 < len(self.loads):
            self.loads[n + 2].start()
        self.settled = n + 1

    def half_copy(self, k, n, src):
        dst = self.half_in.at[k, n]
        return send(dst if src is None else src, dst, self.h_ssem.at[k, n], self.h_rsem.at[k, n], (self.s, self.line[n + 1]))

    def full_copy(self, k, j, src):
        dst = self.full_in.at[k, j - 1]
        return send(dst if src is None else src, dst, self.f_ssem.at[k, j - 1], self.f_rsem.at[k, j - 1], (self.s, self.line[j]))

    def z_copy(self, k, src):
        dst = self.z_in.at[k]
        return send(dst if src is None else src, dst, self.z_ssem.at[k], self.z_rsem.at[k], self.at_z(k))

    def stage_a(self, k):
        half = self.rows // 2
        self.settle(k, 3, [(0, self.rows, [])])
        self.start(self.half_copy(k, 1, self.twin_in.at[k, 3, pl.ds(half, half)]))
        self.start(self.half_copy(k, 0, self.twin_in.at[k, 3, pl.ds(0, half)]))

    def stage_b(self, k):
        half = self.rows // 2
        for j in (1, 2):
            n = 2 - j
            self.half_copy(k, n, None).wait_recv()
            more = [(self.half_in.at[k, n], half if n else 0)]
            self.settle(k, j, [(0, half, [] if n else more), (half, self.rows, more if n else [])])
            self.start(self.full_copy(k, j, self.twin_in.at[k, j]))

    def stage_c(self, k):
        more = []
        if self.planes:
            for j in (1, 2):
                self.full_copy(k, j, None).wait_recv()
                more.append((self.full_in.at[k, j - 1], 0))
        if not k:
            for other in range(1, self.zs):
                self.z_copy(other, None).wait_recv()
                more.append((self.z_in.at[other], 0))
        self.settle(k, 0, [(0, self.rows, more)])
        if k:
            self.start(self.z_copy(k, self.twin_in.at[k, 0]))

    def end(self):
        for wait in self.pending:
            wait()


def scatter_scratch(zs, planes, rows, columns, staged):
    sem = pltpu.SemaphoreType.DMA
    low, least = jnp.bfloat16, (1, 2, 16, 128)
    spots = 4 if planes else 1
    return [
        pltpu.VMEM((2, rows, columns) if staged else (16, 128), low),
        pltpu.VMEM((zs, spots, rows, columns), low),
        pltpu.VMEM((zs, 2, rows // 2, columns) if planes else least, low),
        pltpu.VMEM((zs, 2, rows, columns) if planes else least, low),
        pltpu.VMEM((zs, rows, columns) if zs > 1 else least[1:], low),
        sem((2,)), sem((zs, 4)), sem((zs, 4)), sem((zs, 2)), sem((zs, 2)), sem((zs, 2)), sem((zs, 2)), sem((zs,)), sem((zs,)),
    ]


SCATTER_REFS = 14


def scatter_plan(items):
    rounds = []
    for n in range(len(items) + 2):
        rounds.append([])
        for back, stage in enumerate(("a", "b", "c")):
            if 0 <= n - back < len(items):
                name, k = items[n - back]
                if stage != "c" or k:
                    rounds[-1].append((name, stage, k))
    rounds.append([(name, "c", 0) for name, k in items if not k])
    places = {"a": (3,), "b": (1, 2), "c": (0,)}
    schedules = {}
    for name, stage, k in sum(rounds, []):
        schedules.setdefault(name, []).extend((k, j) for j in places[stage])
    return rounds, schedules


def run_stage(scatters, name, stage, k):
    {"a": Scatter.stage_a, "b": Scatter.stage_b, "c": Scatter.stage_c}[stage](scatters[name], k)


class SumChain:
    def __init__(self, zs, parts, got, held, sems, l_sem):
        self.__dict__.update(locals())
        self.z = place()[0]

    def own(self, to):
        return self.parts.at[lax.rem(self.z + to + self.zs, self.zs)]

    def fetch(self, k):
        self.loads = [
            pltpu.make_async_copy(self.own(-k), self.held.at[0], self.l_sem.at[0]),
            pltpu.make_async_copy(self.own(k), self.held.at[1], self.l_sem.at[1]),
        ]
        for load in self.loads:
            load.start()

    def add(self, into, more):
        ref = self.got[into]
        ref[...] = (ref[...].astype(jnp.float32) + self.held[more].astype(jnp.float32)).astype(ref.dtype)

    def lines_of(self, k):
        zs, got = self.zs, self.got
        up, down = k - 1, zs - 2 + k
        lines = [
            Line(zs, 1, 0, 1, self.own(-k), got[up], self.sems.at[up]),
            Line(zs, -1, zs - 1, zs, self.own(k), got[down], self.sems.at[down]),
        ]
        if k > 1:
            lines += [
                Line(zs, 1, 1, k, got[up - 1], got[up], self.sems.at[up]),
                Line(zs, -1, zs - k, zs - 1, got[down - 1], got[down], self.sems.at[down]),
            ]
        return lines

    def start(self, k):
        zs, z = self.zs, self.z
        up, down = k - 1, zs - 2 + k
        if k > 1:
            for load in self.loads:
                load.wait()
            pl.when((z >= 1) & (z < k))(functools.partial(self.add, up - 1, 0))
            pl.when((z >= zs - k) & (z < zs - 1))(functools.partial(self.add, down - 1, 1))
        self.lines = self.lines_of(k)
        for line in self.lines:
            line.start()
        if k == zs - 1:
            self.loads = [pltpu.make_async_copy(self.own(0), self.held.at[0], self.l_sem.at[0])]
            self.loads[0].start()

    def finish(self, k=None):
        for line in self.lines if k is None else self.lines_of(k):
            line.finish()

    def total(self):
        zs, z = self.zs, self.z
        self.loads[0].wait()

        def add(come):
            self.held[0] = (self.held[0].astype(jnp.float32) + self.got[come][...].astype(jnp.float32)).astype(self.held.dtype)

        pl.when(z > 0)(functools.partial(add, zs - 2))
        pl.when(z < zs - 1)(functools.partial(add, 2 * zs - 3))


def partner(tensor):
    lanes = tensor.shape[-1]
    half = HEAD_DIM // 2
    lane = lax.broadcasted_iota(jnp.int32, tensor.shape, tensor.ndim - 1)
    ahead = pltpu.roll(tensor, lanes - half, tensor.ndim - 1)
    behind = pltpu.roll(tensor, half, tensor.ndim - 1)
    return jnp.where(lax.rem(lane, HEAD_DIM) < half, ahead, behind)


def first_of(my_block, half_blocks):
    return jnp.where(my_block >= half_blocks, half_blocks, 0)


def chosen_slots(places, first_block, half_len, wide):
    wanted = first_block * half_len + lax.broadcasted_iota(jnp.int32, (wide, 2 * wide), 0)
    return jnp.where(places == wanted, 1.0, 0.0).astype(jnp.bfloat16)


def stack_heads(block, first):
    return jnp.concatenate(
        [block[:, (first + h) * HEAD_DIM : (first + h + 1) * HEAD_DIM] for h in range(GROUP)], axis=0
    )


def unstack_heads(stacked, span):
    return jnp.concatenate([stacked[h * span : (h + 1) * span] for h in range(GROUP)], axis=1)


def load_window(inverse_ref, kv_ref, window, first_block):
    half_len = kv_ref.shape[1] // 2
    for n in range(window.shape[0] // half_len):
        slot = inverse_ref[first_block + n]
        at = pl.ds(pl.multiple_of(lax.rem(slot, 2) * half_len, half_len), half_len)
        window[n * half_len : (n + 1) * half_len, :] = kv_ref[lax.div(slot, 2), at, :]


def window_of(order_ref, first_ref, count, half_len):
    m, half = pl.program_id(0), pl.program_id(1)
    my_block = order_ref[lax.axis_index("seq") * 2 + half]
    half_blocks = count // half_len // 2
    first_block = jnp.where(my_block >= half_blocks, half_blocks, 0)
    return first_block, my_block * half_len, first_ref[m]


def attend_kernel(order_ref, inverse_ref, first_ref, lin_ref, cos_ref, sin_ref, kv_ref, q_ref, out_ref, window, bias):
    span = lin_ref.shape[0]
    wide = window.shape[0]
    first_block, my_place, first = window_of(order_ref, first_ref, 2 * wide, span)
    load_window(inverse_ref, kv_ref, window, first_block)
    key_place = first_block * span + lax.broadcasted_iota(jnp.int32, (span, wide), 1)
    place_here = my_place + lax.broadcasted_iota(jnp.int32, (span, wide), 0)
    start = jnp.where(place_here >= first, first, 0)
    bias[...] = jnp.where((key_place <= place_here) & (key_place >= start), 0.0, NEG_LARGE)
    width = GROUP * HEAD_DIM
    cosine = jnp.concatenate([cos_ref[...]] * (width // 128), axis=1)
    sine = jnp.concatenate([sin_ref[...]] * (width // 128), axis=1)
    for g in range(KV_HEADS):
        at = slice(g * width, (g + 1) * width)
        lin = lin_ref[:, at]
        query = (lin * cosine + partner(lin) * sine).astype(jnp.bfloat16) * jnp.bfloat16(HEAD_DIM ** -0.5)
        q_ref[:, at] = query
        key = window[:, g * HEAD_DIM : (g + 1) * HEAD_DIM]
        value = window[:, KVW + g * HEAD_DIM : KVW + (g + 1) * HEAD_DIM]
        scores = product_nt(stack_heads(query, 0), key).reshape(GROUP, span, wide) + bias[...][None]
        exps = jnp.exp(scores - jnp.max(scores, axis=-1, keepdims=True))
        total = jnp.sum(exps, axis=-1, keepdims=True).reshape(GROUP * span, 1)
        mixed = product(exps.astype(jnp.bfloat16).reshape(GROUP * span, wide), value) / total
        out_ref[:, at] = unstack_heads(mixed, span).astype(jnp.bfloat16)


def attend_back_heads(queries, d_heads, key, value, bias, span):
    query, d_mixed = stack_heads(queries, 0), stack_heads(d_heads, 0)
    scores = product_nt(key, query) + bias[...]
    exps = jnp.exp(scores - jnp.max(scores, axis=0, keepdims=True))
    probs = exps * (1.0 / jnp.sum(exps, axis=0, keepdims=True))
    weighted = probs * product_nt(value, d_mixed)
    delta = jnp.sum(weighted, axis=0, keepdims=True)
    d_scores = (weighted - probs * delta).astype(jnp.bfloat16)
    d_query = unstack_heads(product_tn(d_scores, key) * HEAD_DIM ** -0.5, span)
    return product(d_scores, query), product(probs.astype(jnp.bfloat16), d_mixed), d_query


def attend_back_kernel(order_ref, inverse_ref, first_ref, q_ref, d_ref, cos_ref, sin_ref, kv_ref, dq_ref, dkv_ref, window, bias, sums):
    span = q_ref.shape[0]
    wide = window.shape[0]
    rows = GROUP * span
    half = pl.program_id(1)
    first_block, my_place, first = window_of(order_ref, first_ref, 2 * wide, span)
    load_window(inverse_ref, kv_ref, window, first_block)
    key_place = first_block * span + lax.broadcasted_iota(jnp.int32, (wide, rows), 0)
    place_here = my_place + lax.rem(lax.broadcasted_iota(jnp.int32, (wide, rows), 1), span)
    start = jnp.where(place_here >= first, first, 0)
    bias[...] = jnp.where((key_place <= place_here) & (key_place >= start), 0.0, NEG_LARGE)

    @pl.when(half == 0)
    def _():
        sums[...] = jnp.zeros_like(sums)

    width = GROUP * HEAD_DIM
    cosine = jnp.concatenate([cos_ref[...]] * (width // 128), axis=1)
    sine = jnp.concatenate([sin_ref[...]] * (width // 128), axis=1)
    d_keys, d_values = [], []
    for g in range(KV_HEADS):
        at = slice(g * width, (g + 1) * width)
        key = window[:, g * HEAD_DIM : (g + 1) * HEAD_DIM]
        value = window[:, KVW + g * HEAD_DIM : KVW + (g + 1) * HEAD_DIM]
        d_key, d_value, d_query = attend_back_heads(q_ref[:, at], d_ref[:, at], key, value, bias, span)
        d_keys.append(d_key)
        d_values.append(d_value)
        dq_ref[:, at] = (d_query * cosine - partner(d_query) * sine).astype(jnp.bfloat16)
    d_window = jnp.concatenate(d_keys + d_values, axis=1)
    for n in range(wide // span):
        slot = inverse_ref[first_block + n]
        to = pl.ds(pl.multiple_of(lax.rem(slot, 2) * span, span), span)
        sums[lax.div(slot, 2), to, :] += d_window[n * span : (n + 1) * span]

    @pl.when(half == 1)
    def _():
        dkv_ref[...] = sums[...].astype(jnp.bfloat16)


def attention_specs(seq, micro, span):
    half_len = span // 2

    def rows(width):
        return pl.BlockSpec((half_len, width), lambda m, h, *_: (m * 2 + h, 0))

    whole = pl.BlockSpec((seq, span, 2 * KVW), lambda m, h, *_: (0, m, 0))
    return half_len, rows, whole


def attend(order, inverse, first, lin, cosine, sine, kv):
    seq, many, _ = kv.shape
    micro = first.shape[0]
    span = many // micro
    half_len, rows, whole = attention_specs(seq, micro, span)
    wide = seq * span // 2
    return pl.pallas_call(
        attend_kernel,
        grid_spec=pltpu.PrefetchScalarGridSpec(
            num_scalar_prefetch=3,
            grid=(micro, 2),
            in_specs=[rows(D), rows(128), rows(128), whole],
            out_specs=[rows(D), rows(D)],
            scratch_shapes=[pltpu.VMEM((wide, 2 * KVW), jnp.bfloat16), pltpu.VMEM((half_len, wide), jnp.float32)],
        ),
        out_shape=[jax.ShapeDtypeStruct((many, D), jnp.bfloat16)] * 2,
        compiler_params=pltpu.CompilerParams(vmem_limit_bytes=48 * MIB),
        cost_estimate=pl.CostEstimate(flops=8 * many * wide * D, bytes_accessed=16 * MIB, transcendentals=many * wide * HEADS),
    )(order, inverse, first, lin, cosine, sine, kv)


def attend_back(order, inverse, first, queries, d_heads, cosine, sine, kv):
    seq, many, _ = kv.shape
    micro = first.shape[0]
    span = many // micro
    half_len, rows, whole = attention_specs(seq, micro, span)
    wide = seq * span // 2
    return pl.pallas_call(
        attend_back_kernel,
        grid_spec=pltpu.PrefetchScalarGridSpec(
            num_scalar_prefetch=3,
            grid=(micro, 2),
            in_specs=[rows(D), rows(D), rows(128), rows(128), whole],
            out_specs=[rows(D), whole],
            scratch_shapes=[
                pltpu.VMEM((wide, 2 * KVW), jnp.bfloat16),
                pltpu.VMEM((wide, GROUP * half_len), jnp.float32),
                pltpu.VMEM((seq, span, 2 * KVW), jnp.float32),
            ],
        ),
        out_shape=[jax.ShapeDtypeStruct((many, D), jnp.bfloat16), jax.ShapeDtypeStruct(kv.shape, jnp.bfloat16)],
        compiler_params=pltpu.CompilerParams(vmem_limit_bytes=56 * MIB),
        cost_estimate=pl.CostEstimate(flops=20 * many * wide * D, bytes_accessed=24 * MIB, transcendentals=many * wide * HEADS),
    )(order, inverse, first, queries, d_heads, cosine, sine, kv)


def assemble(zs, pieces, whole, sem):
    if len(pieces) == 1:
        copy = pltpu.make_async_copy(pieces[0], whole, sem.at[0])
        copy.start()
        return [copy]
    z = lax.div(lax.axis_index("seq"), 2)
    size = whole.shape[0] // zs

    def rows(zz):
        return whole.at[pl.ds(pl.multiple_of(zz * size, size), size)]

    if len(pieces) == 2:
        pieces = [pieces[0], *(pieces[1].at[k] for k in range(zs - 1))]
    copies = [pltpu.make_async_copy(pieces[0], rows(z), sem.at[0])]
    copies[0].start()
    for k in range(1, zs):
        to = rows(lax.rem(z - k + zs, zs))
        below = pltpu.make_async_copy(pieces[k], to, sem.at[k])
        if len(pieces) == zs:
            below.start()
        else:
            above = pltpu.make_async_copy(pieces[2 * zs - 1 - k], to, sem.at[k])
            pl.when(z >= k)(below.start)
            pl.when(z < k)(above.start)
        copies.append(below)
    return copies


class Around:
    def __init__(self, zs, block, got, sems):
        z, c, r = place()
        self.copies = [
            send(block(k), got.at[k - 1], sems.at[k - 1, 0], sems.at[k - 1, 1], (lax.rem(z + k, zs) * 2 + c, r))
            for k in range(1, zs)
        ]

    def start(self):
        for copy in self.copies:
            copy.start()

    def finish(self):
        for copy in self.copies:
            copy.wait()


def swiglu(lin, d_hidden):
    n = d_hidden.shape[1]
    gate, upper = lin[:, :n], lin[:, n:]
    sig = 1.0 / (1.0 + jnp.exp(-gate))
    act = gate * sig
    d_gate = d_hidden * upper * (sig * (1.0 + gate * (1.0 - sig)))
    d_both = jnp.concatenate([d_gate.astype(jnp.bfloat16), (d_hidden * act).astype(jnp.bfloat16)], axis=1)
    return (act * upper).astype(jnp.bfloat16), d_both


def add_gradients(x, dy, hidden, d_both, both_sum, down_sum):
    for at in range(0, D, 256):
        both_sum[at : at + 256, :] += product_tn(x[:, at : at + 256], d_both)
    part = hidden.shape[1] // 4
    for at in range(0, hidden.shape[1], part):
        down_sum[at : at + part, :] += product_tn(hidden[:, at : at + part], dy)


def put_gradients(sums, staged, out, sem):
    copies = []
    for n in range(2):
        staged[n][...] = sums[n][...].astype(jnp.bfloat16)
        copies.append(pltpu.make_async_copy(staged[n], out[n], sem.at[n, 0]))
        copies[-1].start()
    for copy in copies:
        copy.wait()


def ffn_first_kernel(zs, count, linked, *refs):
    x_ref, dy_ref = refs[:2]
    both_pieces, down_pieces = refs[2 : 2 + count], refs[2 + count : 2 + 2 * count]
    refs = refs[2 + 2 * count :]
    if linked:
        rest_own, last_own, x_out_ref, rest_got, last_got, *refs = refs
    hidden_ref, d_both_ref, g_both_ref, g_down_ref, both_w, down_w, both_sum, down_sum, sem, *more = refs
    step, last = pl.program_id(0), pl.num_programs(0) - 1
    gathered, arounds = None, []
    if linked:
        x_all, a_sems, *g_sems = more
        gathered = Gather(zs, False, True, x_ref, x_all, *g_sems)
        arounds = [
            Around(zs, lambda k: rest_own, rest_got, a_sems.at[0]), Around(zs, lambda k: last_own, last_got, a_sems.at[1])
        ]

    @pl.when(step == 0)
    def _():
        copies = assemble(zs, both_pieces, both_w, sem.at[0]) + assemble(zs, down_pieces, down_w, sem.at[1])
        if linked:
            greet(neighbours(zs, True, False))
            gathered.launch()
            gathered.begin(0)
            for one in arounds:
                one.start()
        both_sum[...] = jnp.zeros_like(both_sum)
        down_sum[...] = jnp.zeros_like(down_sum)
        for copy in copies:
            copy.wait()
        if linked:
            gathered.local.wait()

    if linked:
        waits = [
            lambda: gathered.from_twin(0, 0), lambda: gathered.forward(0), lambda: gathered.from_twin(0, 1), None,
            lambda: gathered.from_twin(0, 2), lambda: gathered.finish(0), lambda: gathered.from_twin(0, 3),
        ]
        for n, wait in enumerate(waits):
            if wait is not None:
                pl.when(step == n + 1)(wait)
        x = x_all[lax.rem(step, 2), lax.div(step, 2)]
        x_out_ref[...] = x
    else:
        x = x_ref[...]
    dy = dy_ref[...]
    hidden, d_both = swiglu(product(x, both_w[...]), product_nt(dy, down_w[...]))
    hidden_ref[...] = hidden
    d_both_ref[...] = d_both
    add_gradients(x, dy, hidden, d_both, both_sum, down_sum)

    @pl.when(step == last)
    def _():
        put_gradients((both_sum, down_sum), (both_w, down_w), (g_both_ref, g_down_ref), sem)
        for one in arounds:
            one.finish()
        if linked:
            gathered.sent_all()


def ffn_second_kernel(zs, counts, linked, *refs):
    x_ref, dy_ref, hidden_ref, d_both_ref = refs[:4]
    refs = refs[4:]
    pieces = []
    for count in counts:
        pieces += [refs[:count], refs[count : 2 * count]]
        refs = refs[2 * count :]
    if linked:
        g_both_one, g_down_one, *refs = refs
    out_ref, dx_ref, g_both_ref, g_down_ref, *refs = refs
    if linked:
        *got, both_one, down_one, both_w, down_w, both_sum, down_sum, stage, sem, z_sem, come, held, d_sems, dl_sem = refs
    else:
        got, (both_one, down_one, both_w, down_w, both_sum, down_sum, stage, sem) = [], refs
    n, wide = stage.shape[1] // 2, down_w.shape[0]
    down_rows = down_w.at[pl.ds(0, n)]
    step, last = pl.program_id(0), pl.num_programs(0) - 1
    lines = []
    if linked:
        z = lax.div(lax.axis_index("seq"), 2)
        lines = [
            Line(zs, 1, 0, 1, g_both_one.at[lax.rem(z + zs - 1, zs)], got[0], z_sem.at[0]),
            Line(zs, -1, zs - 1, zs, g_both_one.at[lax.rem(z + 1, zs)], got[1], z_sem.at[1]),
        ]
        none = [None] * (zs - 3)
        down = SumChain(zs, g_down_one, [come.at[0], got[2], *none, come.at[1], got[3], *none], held, d_sems, dl_sem)

    @pl.when(step == 0)
    def _():
        copies = []
        for which, whole in enumerate((both_one, down_one, stage, down_rows)):
            copies += assemble(zs, pieces[which], whole, sem.at[which])
        if linked:
            greet(neighbours(zs, False, False))
            down.start(1)
        both_sum[...] = jnp.zeros_like(both_sum)
        down_sum[...] = jnp.zeros_like(down_sum)
        if wide > n:
            both_w[...] = jnp.zeros_like(both_w)
            down_w[n:, :] = jnp.zeros((wide - n, D), down_w.dtype)
        for copy in copies:
            copy.wait()
        both_w[:, :n] = stage[:, :n]
        both_w[:, wide : wide + n] = stage[:, n:]

    if linked:

        @pl.when(step == last - 5)
        def _():
            down.finish(1)
            for line in lines:
                line.start()
            down.fetch(2)
            down.start(2)

    x, dy = x_ref[...], dy_ref[...]
    hidden, d_both = swiglu(product(x, both_w[...]), product_nt(dy, down_w[...]))
    dx_ref[...] = (product_nt(d_both_ref[...], both_one[...]) + product_nt(d_both, both_w[...])).astype(jnp.bfloat16)
    out_ref[...] = (product(hidden_ref[...], down_one[...]) + product(hidden, down_w[...])).astype(jnp.bfloat16)
    add_gradients(x, dy, hidden, d_both, both_sum, down_sum)

    @pl.when(step == last)
    def _():
        stage[:, :n] = both_sum[:, :n].astype(jnp.bfloat16)
        stage[:, n:] = both_sum[:, wide : wide + n].astype(jnp.bfloat16)
        down_w[...] = down_sum[...].astype(jnp.bfloat16)
        copies = [
            pltpu.make_async_copy(stage, g_both_ref, sem.at[0, 0]), pltpu.make_async_copy(down_rows, g_down_ref, sem.at[1, 0])
        ]
        for copy in copies:
            copy.start()
        for copy in copies:
            copy.wait()
        for line in lines:
            line.finish()
        if linked:
            down.finish(2)


def ffn_first(x, dy, both_pieces, down_pieces, zs, others=(), collective_id=None):
    count, n = len(both_pieces), down_pieces[0].shape[0] * (zs if len(down_pieces) > 1 else 1)
    block, low, full = 256, jnp.bfloat16, jnp.float32
    sem, shape = pltpu.SemaphoreType.DMA, jax.ShapeDtypeStruct
    anywhere = pl.BlockSpec(memory_space=pl.ANY)
    linked = bool(others)
    total = dy.shape[0]

    def tokens(width):
        if linked:
            return pl.BlockSpec((block, width), lambda i: (i % 2 * 4 + i // 2, 0))
        return pl.BlockSpec((block, width), lambda i: (i, 0))

    extra_specs, extra_shapes, extra_scratch, params = [], [], [], {}
    if linked:
        extra_specs = [tokens(D)] + [anywhere] * 2
        extra_shapes = [shape(dy.shape, low)] + [shape((zs - 1,) + other.shape, low) for other in others]
        extra_scratch = [pltpu.VMEM((2, 4) + x.shape, low), sem((2, zs - 1, 2))] + gather_sems(zs, False)
        params = dict(collective_id=collective_id, has_side_effects=True)
    return pl.pallas_call(
        functools.partial(ffn_first_kernel, zs, count, linked),
        grid=(total // block,),
        in_specs=[anywhere if linked else tokens(D), tokens(D)] + [anywhere] * (2 * count + len(others)),
        out_specs=extra_specs + [tokens(n), tokens(2 * n)] + [anywhere] * 2,
        out_shape=extra_shapes
        + [shape((total, n), low), shape((total, 2 * n), low), shape((D, 2 * n), low), shape((n, D), low)],
        scratch_shapes=[
            pltpu.VMEM((D, 2 * n), low), pltpu.VMEM((n, D), low), pltpu.VMEM((D, 2 * n), full), pltpu.VMEM((n, D), full),
            sem((2, zs)),
        ] + extra_scratch,
        compiler_params=pltpu.CompilerParams(vmem_limit_bytes=60 * MIB, **params),
        cost_estimate=LONG,
    )(x, dy, *both_pieces, *down_pieces, *others)


def ffn_second(x, dy, hidden, d_both, one, two, zs, parts=(), collective_id=None):
    counts = (len(one[0]), len(two[0]))
    wides = [down[0].shape[0] * (zs if len(down) > 1 else 1) for _, down in (one, two)]
    n = wides[1]
    wide = -(-n // 128) * 128
    block, low, full = 256, jnp.bfloat16, jnp.float32
    sem, shape = pltpu.SemaphoreType.DMA, jax.ShapeDtypeStruct
    anywhere = pl.BlockSpec(memory_space=pl.ANY)

    def tokens(width):
        return pl.BlockSpec((block, width), lambda i: (i, 0))

    linked = bool(parts)
    extra = []
    if linked:
        held = pltpu.VMEM((2,) + parts[1].shape[1:], low)
        extra = [sem((2, 2)), held, held, sem((2 * zs - 2, 2)), sem((2,))]
    params = dict(collective_id=collective_id, has_side_effects=True) if linked else {}
    return pl.pallas_call(
        functools.partial(ffn_second_kernel, zs, counts, linked),
        grid=(x.shape[0] // block,),
        in_specs=[tokens(D)] * 2 + [tokens(wides[0]), tokens(2 * wides[0])] + [anywhere] * (2 * sum(counts) + len(parts)),
        out_specs=[tokens(D)] * 2 + [anywhere] * (2 + 2 * len(parts)),
        out_shape=[shape(x.shape, low)] * 2 + [shape((D, 2 * n), low), shape((n, D), low)]
        + [shape(part.shape[1:], low) for part in parts for _ in range(2)],
        scratch_shapes=[
            pltpu.VMEM((D, 2 * wides[0]), low), pltpu.VMEM((wides[0], D), low),
            pltpu.VMEM((D, 2 * wide), low), pltpu.VMEM((wide, D), low),
            pltpu.VMEM((D, 2 * wide), full), pltpu.VMEM((wide, D), full), pltpu.VMEM((D, 2 * n), low),
            sem((4, zs)),
        ] + extra,
        compiler_params=pltpu.CompilerParams(vmem_limit_bytes=56 * MIB, **params),
        cost_estimate=LONG,
    )(x, dy, hidden, d_both, *one[0], *one[1], *two[0], *two[1], *parts)


def split_unit(unit):
    return unit * 3 // 4 // 16 * 16


def portions(unit):
    first = split_unit(unit)
    return (0, first), (first, unit - first)


def gain_columns(one, two, rows):
    row = lax.broadcasted_iota(jnp.int32, (128, rows), 0)
    return jnp.where(row == 0, one, jnp.where(row == 1, two, 0.0)).T


def spread_kernel(zs, rows, unit, gate_ref, up_ref, query_ref, key_ref, value_ref, one_ref, two_ref, down_ref, *out):
    for (begin, size), ref in zip(portions(unit), out):
        for c in range(2):
            for r in range(rows):
                for n, weight in enumerate((gate_ref, up_ref)):
                    for z in range(zs):
                        at = ((z * 2 + c) * rows + r) * unit + begin
                        to = (n * zs + z) * size
                        ref[c, r, :, to : to + size] = weight[:, at : at + size]
    pack_ref, down_one, down_two = out[2:]
    pack_ref[:, :D] = query_ref[...]
    pack_ref[:, D : D + KVW] = key_ref[...]
    pack_ref[:, D + KVW : QKV] = value_ref[...]
    gains = gain_columns(one_ref[...].astype(jnp.float32), two_ref[...].astype(jnp.float32), pack_ref.shape[0])
    pack_ref[:, QKV:] = gains.astype(pack_ref.dtype)
    cut = down_one.shape[0]
    down_one[...] = down_ref[:cut, :]
    down_two[...] = down_ref[cut:, :]


def spread(gate, up, query, key, value, one, two, down, zs, rows):
    wide, part = gate.shape
    unit = part // (zs * 2 * rows)
    shape, low = jax.ShapeDtypeStruct, gate.dtype
    return pl.pallas_call(
        functools.partial(spread_kernel, zs, rows, unit),
        out_shape=[shape((2, rows, wide, 2 * zs * size), low) for _, size in portions(unit)]
        + [shape((wide, PACK), low)]
        + [shape((size, D), low) for _, size in portions(unit)],
    )(gate, up, query, key, value, one.reshape(1, -1), two.reshape(1, -1), down)


def collect_kernel(zs, rows, unit, *refs):
    given, (pack_ref, down_one, down_two), outs = refs[:2], refs[2:5], refs[5:]
    for n, out in enumerate(outs[:2]):
        for (begin, size), ref in zip(portions(unit), given):
            for c in range(2):
                for r in range(rows):
                    for z in range(zs):
                        at = ((z * 2 + c) * rows + r) * unit + begin
                        to = (n * zs + z) * size
                        out[:, at : at + size] = ref[c, r, :, to : to + size].astype(jnp.float32)
    key_ref, value_ref, gains_ref, down_ref = outs[2:]
    key_ref[...] = pack_ref[:, :KVW]
    value_ref[...] = pack_ref[:, KVW : 2 * KVW]
    gains_ref[...] = pack_ref[:, 2 * KVW :].T[:8]
    cut = down_one.shape[0]
    down_ref[:cut, :] = down_one[...]
    down_ref[cut:, :] = down_two[...]


def collect(blocks, pack, downs, zs, rows, unit):
    wide = blocks[0].shape[2]
    shape, full = jax.ShapeDtypeStruct, jnp.float32
    whole = shape((wide, unit * zs * 2 * rows), full)
    narrow = shape((wide, KVW), full)
    return pl.pallas_call(
        functools.partial(collect_kernel, zs, rows, unit),
        out_shape=[whole, whole, narrow, narrow, shape((8, wide), full), shape((unit, D), full)],
    )(*blocks, pack, *downs)


def forward_kernel(zs, micro, *refs):
    order_ref, places_ref, first_ref, freq_ref, x_ref, pack_ref, both_ref, down_ref, out_ref, dy_ref, rest_ref = refs[:11]
    refs = refs[1:]
    packed, both_own, kv_all, out_all, dy_all, rest_own = refs[10:16]
    steps = 2 * zs - 2
    both_got, down_got = refs[16 : 16 + steps], refs[16 + steps : 16 + 2 * steps]
    q_ref, attn_ref, attended_ref, ffn_own, middle_ref, gains_ref, cos_ref, sin_ref = refs[16 + 2 * steps : 24 + 2 * steps]
    (staged, lin, kv_own, kv_here, window, chosen, bias, out_w, sems, *more) = refs[24 + 2 * steps :]
    low = jnp.bfloat16
    z, c, r = place()
    many = x_ref.shape[0]
    span = many // micro
    half_len = span // 2
    rows = D // zs
    greet(neighbours(zs, True, True))

    exchange = Exchange(both_ref, both_own, *more[:3])
    rest = Exchange(rest_ref, rest_own, *more[3:6])
    more = more[:3] + more[6:]
    both_chain, down_chain = Chain(zs, both_own, both_got, more[3]), Chain(zs, down_ref, down_got, more[4])
    more = more[5:]
    weights = Gather(zs, True, True, pack_ref, packed, *more[:9])
    outs = Gather(zs, True, True, out_ref, out_all, *more[9:18])
    pairs = Gather(zs, True, False, kv_own, kv_all, *more[18:27])
    dys = Gather(zs, False, True, dy_ref, dy_all, *more[27:36])

    weights.launch()
    exchange.start()
    weights.begin(0)
    outs.launch()

    lane = lax.broadcasted_iota(jnp.int32, (half_len, 128), 1)
    for i in range(2 * micro):
        place_here = order_ref[(z * 2 + c) * 2 + i % 2] * half_len + lax.broadcasted_iota(jnp.int32, (half_len, 128), 0)
        start = jnp.where(place_here >= first_ref[i // 2], first_ref[i // 2], 0)
        angle = (place_here - start).astype(jnp.float32) * freq_ref[...]
        cos_ref[i * half_len : (i + 1) * half_len, :] = jnp.cos(angle)
        sine = jnp.sin(angle)
        sin_ref[i * half_len : (i + 1) * half_len, :] = jnp.where(lax.rem(lane, HEAD_DIM) < HEAD_DIM // 2, -sine, sine)
    x = x_ref[...].astype(jnp.float32)
    factor = rms_factor(x)
    wide = window.shape[0]
    half_blocks = wide // half_len
    for half in range(2):
        my_block = order_ref[(z * 2 + c) * 2 + half]
        chosen[half] = chosen_slots(places_ref[...], first_of(my_block, half_blocks), half_len, wide)

    loads = {}

    def load(n):
        weights.complete(n)
        zz = lax.rem(z - weights.kth[n] + zs, zs)
        loads[n] = pltpu.make_async_copy(packed.at[zz], staged.at[n % 2], sems.at[n % 2])
        loads[n].start()

    def project(n):
        loads[n].wait()
        zz = lax.rem(z - weights.kth[n] + zs, zs)
        at = pl.ds(pl.multiple_of(zz * rows, rows), rows)
        block = staged[n % 2].reshape(rows, PACK)
        gains = block[:, QKV:].astype(jnp.float32).T[:8]
        gains_ref[:, at] = gains
        attn_in = (x_ref[:, at].astype(jnp.float32) * factor * gains[0:1]).astype(low)
        attn_ref[:, at] = attn_in
        value = product(attn_in, block[:, :QKV])
        lin[...] = value if n == 0 else lin[...] + value

    weights.arrive(1)
    weights.begin(1)
    weights.forward(0)
    weights.arrive(2)
    weights.begin(2)
    weights.forward(1)
    weights.finish(0)
    weights.arrive(3)
    weights.begin(3)
    down_chain.start(1)
    exchange.finish()
    both_chain.start(1)
    outs.arrive(1)
    weights.forward(2)
    weights.finish(1)
    load(0)
    outs.arrive(2)
    weights.forward(3)
    weights.finish(2)
    outs.begin(0)
    load(1)
    project(0)
    outs.arrive(3)
    outs.begin(1)
    project(1)
    weights.finish(3)
    rest.start()
    dys.launch()
    dys.begin(0)
    load(2)
    load(3)
    project(2)
    project(3)

    width = GROUP * HEAD_DIM
    cosine = jnp.concatenate([cos_ref[...]] * (width // 128), axis=1)
    sine = jnp.concatenate([sin_ref[...]] * (width // 128), axis=1)

    def turned(block, w):
        return block * cosine[:, :w] + partner(block) * sine[:, :w]

    kv_own[:, :KVW] = turned(lin[:, D : D + KVW], KVW).astype(low)
    kv_own[:, KVW:] = lin[:, D + KVW :].astype(low)
    pairs.launch()
    pairs.begin(0)
    for g in range(KV_HEADS):
        at = slice(g * width, (g + 1) * width)
        q_ref[:, at] = turned(lin[:, at], width).astype(low) * low(HEAD_DIM ** -0.5)
    outs.forward(0)
    outs.begin(2)
    both_chain.finish()
    down_chain.finish()
    both_chain.start(2)
    down_chain.start(2)
    for k in range(1, zs):
        pairs.arrive(k)
        pairs.begin(k)
    outs.forward(1)
    outs.finish(0)
    outs.begin(3)
    for k in range(zs):
        pairs.complete(k)
    kv_load = pltpu.make_async_copy(kv_all, kv_here, sems.at[2])
    kv_load.start()
    outs.forward(2)
    outs.finish(1)
    kv_load.wait()

    def attend_some(i, carry):
        m, half = lax.div(i, 2), lax.rem(i, 2)
        my_block = order_ref[(z * 2 + c) * 2 + half]
        first_block = first_of(my_block, half_blocks)
        at = pl.ds(pl.multiple_of(m * span, span), span)
        window[...] = product(chosen[half], kv_here[:, :, at, :].reshape(2 * wide, 2 * KVW)).astype(low)
        key_place = first_block * half_len + lax.broadcasted_iota(jnp.int32, (half_len, wide), 1)
        place_here = my_block * half_len + lax.broadcasted_iota(jnp.int32, (half_len, wide), 0)
        first = first_ref[m]
        start = jnp.where(place_here >= first, first, 0)
        bias[...] = jnp.where((key_place <= place_here) & (key_place >= start), 0.0, NEG_LARGE)
        here = pl.ds(pl.multiple_of(i * half_len, half_len), half_len)
        for g in range(KV_HEADS):
            at = slice(g * width, (g + 1) * width)
            key = window[:, g * HEAD_DIM : (g + 1) * HEAD_DIM]
            value = window[:, KVW + g * HEAD_DIM : KVW + (g + 1) * HEAD_DIM]
            scores = product_nt(stack_heads(q_ref[here, at], 0), key).reshape(GROUP, half_len, wide) + bias[...][None]
            exps = jnp.exp(scores - jnp.max(scores, axis=-1, keepdims=True))
            total = jnp.sum(exps, axis=-1, keepdims=True).reshape(GROUP * half_len, 1)
            mixed = product(exps.astype(low).reshape(GROUP * half_len, wide), value) / total
            attended_ref[here, at] = unstack_heads(mixed, half_len).astype(low)
        return carry

    lax.fori_loop(0, 2 * micro, attend_some, 0)
    outs.forward(3)
    outs.finish(2)
    outs.finish(3)
    dys.forward(0)
    for k in range(zs):
        outs.complete(k)
    out_load = pltpu.make_async_copy(out_all, out_w, sems.at[3])
    out_load.start()
    out_load.wait()
    middle = x_ref[...].astype(jnp.float32) + product(attended_ref[...], out_w[...].reshape(D, D))
    middle_ref[...] = middle
    ffn_own[...] = (middle * rms_factor(middle) * gains_ref[1:2, :]).astype(low)
    both_chain.finish()
    down_chain.finish()
    both_chain.start(3)
    down_chain.start(3)
    dys.finish(0)
    dys.complete(0)
    rest.finish()
    both_chain.finish()
    down_chain.finish()
    rest.end()
    exchange.end()
    for one in (weights, outs, pairs, dys):
        one.end()


def places_of(order, span):
    return (order[:, None] * (span // 2) + jnp.arange(span // 2, dtype=jnp.int32)).reshape(1, -1)


def forward(order, first, tokens, pack, both, rest, down, w_out, dy, zs, collective_id):
    many = tokens.shape[0]
    micro = first.shape[0]
    seq = 2 * zs
    wide = seq * (many // micro) // 2
    low, full = jnp.bfloat16, jnp.float32
    freq = 10000.0 ** (-(jnp.arange(128, dtype=jnp.int32) % (HEAD_DIM // 2)).astype(full) / (HEAD_DIM // 2))
    anywhere, here, smem = (pl.BlockSpec(memory_space=m) for m in (pl.ANY, pltpu.VMEM, pltpu.SMEM))
    shape = jax.ShapeDtypeStruct
    out_any = [
        shape((zs, 2, 4) + pack.shape, low),
        shape(both.shape, low),
        shape((zs, 2, many, 2 * KVW), low),
        shape((zs, 2, 4) + w_out.shape, low),
        shape((2, 4) + dy.shape, low),
        shape(rest.shape, low),
    ] + [shape(both.shape, low)] * (2 * zs - 2) + [shape(down.shape, low)] * (2 * zs - 2)
    out_here = [shape((many, D), t) for t in (low, low, low, low, full)] + [shape((8, D), full)] + [shape((many, 128), full)] * 2
    sem = pltpu.SemaphoreType.DMA
    found = pl.pallas_call(
        functools.partial(forward_kernel, zs, micro),
        out_shape=out_any + out_here,
        in_specs=[smem, here, smem] + [here] * 2 + [anywhere] * 6,
        out_specs=[anywhere] * len(out_any) + [here] * len(out_here),
        scratch_shapes=[
            pltpu.VMEM((2, 2, 4) + pack.shape, low),
            pltpu.VMEM((many, QKV), full),
            pltpu.VMEM((many, 2 * KVW), low),
            pltpu.VMEM((zs, 2, many, 2 * KVW), low),
            pltpu.VMEM((wide, 2 * KVW), low),
            pltpu.VMEM((2, wide, 2 * wide), low),
            pltpu.VMEM((many // micro // 2, wide), full),
            pltpu.VMEM((zs, 2, 4) + w_out.shape, low),
            sem((4,)),
        ] + EXCHANGE_SEMS * 2 + [sem((2 * zs - 2, 2))] * 2 + gather_sems(zs, True) * 3 + gather_sems(zs, False),
        compiler_params=pltpu.CompilerParams(
            collective_id=collective_id, has_side_effects=True, vmem_limit_bytes=56 * MIB
        ),
        cost_estimate=LONG,
    )(order, places_of(order, many // micro), first, freq.reshape(1, 128), tokens, pack, both, down, w_out, dy, rest)
    return found


def back_kernel(zs, micro, *refs):
    (order_ref, places_ref, first_ref, dy_ref, middle_ref, gains_ref, q_ref, cos_ref, sin_ref) = refs[:9]
    dx_part, out_part, both_part, down_part, out_all, kv_all, rest_part, last_part, *come = refs[9:21]
    result_ref, d_middle_ref, dq_ref, dkv_ref, gain_ref, down_ref, both_up, both_down, rest_in, last_in = refs[21:31]
    out_w, kv_here, d_heads, chosen, window, bias, d_places, sems, got, held, d_sems, dl_sem, *more = refs[31:]
    b_got, b_held, b_sems, bl_sem, r_sems, *more = more
    low, full = jnp.bfloat16, jnp.float32
    z, c, r = place()
    many = dy_ref.shape[0]
    span = many // micro
    half_len = span // 2
    greet(neighbours(zs, True, False))

    def take_d_ffn(at, value):
        d_middle_ref[at, :] = value

    def take_result(at, value):
        result_ref[at, :] = (middle_ref[at, :] + value).astype(low)

    scatters = {
        "dx": Scatter(1, False, True, dx_part, take_d_ffn, *more[:SCATTER_REFS]),
        "out": Scatter(1, False, True, out_part, take_result, *more[SCATTER_REFS : 2 * SCATTER_REFS]),
    }
    none = [None] * (zs - 3)
    down = SumChain(zs, down_part, [*none, got.at[0], got.at[1], *none, got.at[2], got.at[3]], held, d_sems, dl_sem)
    both = SumChain(
        zs, both_part, [b_got.at[0], both_up, *none, b_got.at[1], both_down, *none], b_held, b_sems, bl_sem
    )
    arounds = [
        Around(zs, lambda k: rest_part.at[lax.rem(z + k, zs)], rest_in, r_sems.at[0]),
        Around(zs, lambda k: last_part.at[lax.rem(z + k, zs)], last_in, r_sems.at[1]),
    ]
    comes = [
        pltpu.make_async_copy(src, dst, sems.at[2 + n])
        for n, (src, dst) in enumerate(zip(come, (b_got.at[0], b_got.at[1], got.at[0], got.at[2])))
    ]
    for copy in comes:
        copy.start()
    both.fetch(2)
    down.fetch(zs - 1)
    schedule = [(0, 3), (0, 1), (0, 2), (0, 0)]
    scatters["dx"].begin(schedule)
    for one in arounds:
        one.start()
    loads = [pltpu.make_async_copy(out_all, out_w, sems.at[0]), pltpu.make_async_copy(kv_all, kv_here, sems.at[1])]
    for load in loads:
        load.start()
    scatters["dx"].stage_a(0)
    for copy in comes:
        copy.wait()
    both.start(2)
    down.start(zs - 1)
    scatters["out"].begin(schedule)
    scatters["dx"].stage_b(0)
    scatters["out"].stage_a(0)
    scatters["dx"].stage_c(0)
    scatters["out"].stage_b(0)

    gain_ref[0:1, :] = jnp.zeros((1, D), full)

    def norm_some(i, carry):
        at = pl.ds(pl.multiple_of(i * half_len, half_len), half_len)
        middle, d_ffn = middle_ref[at, :], d_middle_ref[at, :]
        factor = rms_factor(middle)
        normed = middle * factor
        inner = d_ffn * gains_ref[1:2, :]
        d_norm = factor * (inner - normed * jnp.mean(inner * normed, axis=-1, keepdims=True))
        d_middle_ref[at, :] = dy_ref[at, :].astype(full) + d_norm
        gain_ref[0:1, :] += jnp.sum(d_ffn * normed, axis=0, keepdims=True)
        return carry

    lax.fori_loop(0, many // half_len, norm_some, 0)
    for load in loads:
        load.wait()
    d_heads[...] = product_nt(d_middle_ref[...].astype(low), out_w[...].reshape(D, D)).astype(low)

    wide = window.shape[0]
    half_blocks = wide // half_len
    width = GROUP * HEAD_DIM

    def attend_some(i, carry):
        m, half = lax.div(i, 2), lax.rem(i, 2)
        my_block = order_ref[(z * 2 + c) * 2 + half]
        first_block = jnp.where(my_block >= half_blocks, half_blocks, 0)
        wanted = first_block * half_len + lax.broadcasted_iota(jnp.int32, (wide, 2 * wide), 0)
        chosen[...] = jnp.where(places_ref[...] == wanted, 1.0, 0.0).astype(low)
        rows = pl.ds(pl.multiple_of(m * span, span), span)
        window[...] = product(chosen[...], kv_here[:, :, rows, :].reshape(2 * wide, 2 * KVW)).astype(low)
        key_place = first_block * half_len + lax.broadcasted_iota(jnp.int32, bias.shape, 0)
        place_here = my_block * half_len + lax.rem(lax.broadcasted_iota(jnp.int32, bias.shape, 1), half_len)
        first = first_ref[m]
        start = jnp.where(place_here >= first, first, 0)
        bias[...] = jnp.where((key_place <= place_here) & (key_place >= start), 0.0, NEG_LARGE)
        here = pl.ds(pl.multiple_of(i * half_len, half_len), half_len)
        cosine = jnp.concatenate([cos_ref[here, :]] * (width // 128), axis=1)
        sine = jnp.concatenate([sin_ref[here, :]] * (width // 128), axis=1)
        d_keys, d_values = [], []
        for g in range(KV_HEADS):
            at = slice(g * width, (g + 1) * width)
            key = window[:, g * HEAD_DIM : (g + 1) * HEAD_DIM]
            value = window[:, KVW + g * HEAD_DIM : KVW + (g + 1) * HEAD_DIM]
            d_key, d_value, d_query = attend_back_heads(q_ref[here, at], d_heads[here, at], key, value, bias, half_len)
            d_keys.append(d_key)
            d_values.append(d_value)
            dq_ref[here, at] = (d_query * cosine - partner(d_query) * sine).astype(low)
        d_window = jnp.concatenate(d_keys + d_values, axis=1).astype(low)
        spread_back = product_tn(chosen[...], d_window)

        @pl.when(half == 0)
        def _():
            d_places[...] = spread_back

        @pl.when(half == 1)
        def _():
            both = (d_places[...] + spread_back).astype(low)
            dkv_ref[:, :, rows, :] = both.reshape(zs, 2, span, 2 * KVW)

        return carry

    lax.fori_loop(0, 2 * micro, attend_some, 0)
    scatters["out"].stage_c(0)
    both.finish()
    down.finish()
    down.total()
    down_ref[...] = held[0].astype(full)
    for one in arounds:
        one.finish()
    for one in scatters.values():
        one.end()


def back(order, first, dy, middle, gains, queries, cosine, sine, dx_part, out_part, both_part, down_part, out_all, kv_all,
         rest_part, last_part, come, zs, collective_id):
    many = dy.shape[0]
    micro = first.shape[0]
    span = many // micro
    wide = zs * span
    low, full = jnp.bfloat16, jnp.float32
    anywhere, here, smem = (pl.BlockSpec(memory_space=m) for m in (pl.ANY, pltpu.VMEM, pltpu.SMEM))
    shape, sem = jax.ShapeDtypeStruct, pltpu.SemaphoreType.DMA
    unit = down_part.shape[1]
    piece = shape(both_part.shape[1:], low)
    return pl.pallas_call(
        functools.partial(back_kernel, zs, micro),
        out_shape=[
            shape((many, D), low), shape((many, D), full), shape((many, D), low), shape(kv_all.shape, low),
            shape((8, D), full), shape((unit, D), full), piece, piece,
            shape((zs - 1,) + rest_part.shape[1:], low), shape((zs - 1,) + last_part.shape[1:], low),
        ],
        in_specs=[smem, here, smem] + [here] * 6 + [anywhere] * 12,
        out_specs=[here] * 6 + [anywhere] * 4,
        scratch_shapes=[
            pltpu.VMEM(out_all.shape, low),
            pltpu.VMEM(kv_all.shape, low),
            pltpu.VMEM((many, D), low),
            pltpu.VMEM((wide, 2 * wide), low),
            pltpu.VMEM((wide, 2 * KVW), low),
            pltpu.VMEM((wide, GROUP * span // 2), full),
            pltpu.VMEM((2 * wide, 2 * KVW), full),
            sem((6,)),
            pltpu.VMEM((4, unit, D), low),
            pltpu.VMEM((2, unit, D), low),
            sem((2 * zs - 2, 2)), sem((2,)),
            pltpu.VMEM((2,) + piece.shape, low),
            pltpu.VMEM((2,) + piece.shape, low),
            sem((2 * zs - 2, 2)), sem((2,)), sem((2, zs - 1, 2)),
        ] + scatter_scratch(1, True, many, D, True) * 2,
        compiler_params=pltpu.CompilerParams(
            collective_id=collective_id, has_side_effects=True, vmem_limit_bytes=62 * MIB
        ),
        cost_estimate=LONG,
    )(order, places_of(order, span), first, dy, middle, gains, queries, cosine, sine, dx_part, out_part, both_part, down_part,
      out_all, kv_all, rest_part, last_part, *come)


def products_kernel(attended_ref, attn_ref, d_middle_ref, dq_ref, packed_ref, out_ref, query_ref, d_attn_ref):
    low = jnp.bfloat16
    out_ref[...] = product_tn(attended_ref[...], d_middle_ref[...].astype(low)).astype(low)
    query_ref[...] = product_tn(attn_ref[...], dq_ref[...]).astype(low)
    d_attn_ref[...] = product_nt(dq_ref[...], packed_ref[...])


def products(attended, attn_in, d_middle, d_query, packed):
    many, block = attended.shape[0], 256
    low, shape = jnp.bfloat16, jax.ShapeDtypeStruct
    narrow = pl.BlockSpec((many, block), lambda i: (0, i))
    tall = pl.BlockSpec((block, D), lambda i: (i, 0))
    whole = pl.BlockSpec((many, D), lambda i: (0, 0))
    return pl.pallas_call(
        products_kernel,
        grid=(D // block,),
        in_specs=[narrow, narrow, whole, whole, tall],
        out_specs=[tall, tall, narrow],
        out_shape=[shape((D, D), low), shape((D, D), low), shape((many, D), jnp.float32)],
        compiler_params=pltpu.CompilerParams(vmem_limit_bytes=60 * MIB),
        cost_estimate=pl.CostEstimate(flops=6 * many * D * D, bytes_accessed=30 * MIB, transcendentals=0),
    )(attended, attn_in, d_middle, d_query, packed)


def weights_kernel(zs, *refs):
    x_ref, attn_ref, d_middle_ref, d_attn_ref, gains_ref, gain_two_ref, cos_ref, sin_ref, dkv_ref = refs[:9]
    packed, both_part, both_up, both_down, g_out, g_query, rest_part, last_part, rest_in, last_in = refs[9:19]
    x_grad_ref, out_ref, query_ref, pack_ref, last_ref, moved_ref, rest_ref = refs[19:26]
    kv_w, d_kv, pack_g, sems, got, held, b_sems, bl_sem, rest_here, last_here, *more = refs[26:]
    exchange_sems, rest_sems, more = more[:3], more[3:6], more[6:]
    z = place()[0]
    low, full = jnp.bfloat16, jnp.float32
    greet(neighbours(zs, True, True))

    def into(ref):
        def take(at, value):
            ref[at, :] = value

        return take

    def next_refs(staged):
        nonlocal more
        mine, more = more[:SCATTER_REFS], more[SCATTER_REFS:]
        return mine if staged else [None, *mine[1:]]

    pairs = Scatter(zs, True, False, dkv_ref, into(d_kv), *next_refs(False))
    scatters = {
        "out": Scatter(zs, True, True, g_out, into(out_ref), *next_refs(True)),
        "query": Scatter(zs, True, True, g_query, into(query_ref), *next_refs(True)),
        "pack": Scatter(zs, True, True, pack_g, into(pack_ref), *next_refs(False)),
    }
    items = [(name, k) for k in range(1, zs) for name in ("out", "query")]
    items[4:4] = [("pack", 1)]
    items += [("pack", k) for k in range(2, zs)] + [("out", 0), ("query", 0), ("pack", 0)]
    rounds, schedules = scatter_plan(items)

    none = [None] * (zs - 3)
    chain = SumChain(zs, both_part, [*none, got.at[0], got.at[1], *none, got.at[2], got.at[3]], held, b_sems, bl_sem)
    loads = [
        pltpu.make_async_copy(both_up, got.at[0], sems.at[0]),
        pltpu.make_async_copy(both_down, got.at[2], sems.at[1]),
        pltpu.make_async_copy(packed.at[:, :, :, :, pl.ds(D, 2 * KVW)], kv_w, sems.at[2]),
    ]
    for load in loads:
        load.start()
    small = [
        pltpu.make_async_copy(rest_part.at[z], rest_here.at[0], sems.at[3]),
        pltpu.make_async_copy(last_part.at[z], last_here.at[0], sems.at[4]),
        pltpu.make_async_copy(rest_in, rest_here.at[pl.ds(1, zs - 1)], sems.at[5]),
        pltpu.make_async_copy(last_in, last_here.at[pl.ds(1, zs - 1)], sems.at[6]),
    ]
    for load in small:
        load.start()
    chain.fetch(zs - 1)
    pairs.begin([])
    scatters["out"].begin(schedules["out"])
    scatters["query"].begin(schedules["query"])
    for k in range(1, zs):
        pairs.stage_c(k)
    for load in loads:
        load.wait()
    chain.start(zs - 1)
    for load in small:
        load.wait()
    last_ref[...] = sum(last_here[n].astype(full) for n in range(zs))
    rest_here[0] = sum(rest_here[n].astype(full) for n in range(zs)).astype(low)
    rest = Exchange(rest_here.at[0], rest_ref, *rest_sems)
    rest.start()

    def keys_and_norm():
        pairs.stage_c(0)
        lanes = KVW // 128
        cosine = jnp.concatenate([cos_ref[...]] * lanes, axis=1)
        sine = jnp.concatenate([sin_ref[...]] * lanes, axis=1)
        d_key = d_kv[:, :KVW]
        d_lin = jnp.concatenate([d_key * cosine - partner(d_key) * sine, d_kv[:, KVW:]], axis=1).astype(low)
        d_attn = d_attn_ref[...] + product_nt(d_lin, kv_w[...].reshape(D, 2 * KVW))
        x = x_ref[...].astype(full)
        factor = rms_factor(x)
        normed = x * factor
        inner = d_attn * gains_ref[0:1, :]
        d_x = factor * (inner - normed * jnp.mean(inner * normed, axis=-1, keepdims=True))
        x_grad_ref[...] = (d_middle_ref[...] + d_x).astype(low)
        gain_one = jnp.sum(d_attn * normed, axis=0, keepdims=True)
        rows = lax.broadcasted_iota(jnp.int32, (128, D), 0)
        both = jnp.where(rows == 0, gain_one, jnp.where(rows == 1, gain_two_ref[0:1, :], 0.0))
        pack = jnp.concatenate([product_tn(attn_ref[...], d_lin), both.T], axis=1).astype(low)
        pack_g[...] = pack.reshape(pack_g.shape)
        scatters["pack"].begin([])

    for n, stages in enumerate(rounds):
        if n == 3:
            keys_and_norm()
        if n == len(rounds) - 3:
            chain.finish()
            chain.total()
            exchange = Exchange(held.at[0], moved_ref, *exchange_sems)
            exchange.start()
        for stage in stages:
            run_stage(scatters, *stage)
    for one in (rest, exchange):
        one.finish()
        one.end()
    for one in (pairs, *scatters.values()):
        one.end()


def weight_sums(x, attn_in, d_middle, d_attn, gains, gain_two, cosine, sine, d_kv, packed, both_part, both_up, both_down, g_out,
                g_query, rest_part, last_part, rest_in, last_in, zs, collective_id):
    many = x.shape[0]
    low, full = jnp.bfloat16, jnp.float32
    anywhere, here = (pl.BlockSpec(memory_space=m) for m in (pl.ANY, pltpu.VMEM))
    shape, sem = jax.ShapeDtypeStruct, pltpu.SemaphoreType.DMA
    wide = packed.shape[3]
    narrow = 2 * KVW + 128
    block = both_part.shape[1:]
    return pl.pallas_call(
        functools.partial(weights_kernel, zs),
        out_shape=[
            shape((many, D), low), shape((wide, D), full), shape((wide, D), full), shape((wide, narrow), full),
            shape(last_part.shape[1:], full), shape(block, low), shape(rest_part.shape[1:], low),
        ],
        in_specs=[here] * 9 + [anywhere] * 10,
        out_specs=[here] * 5 + [anywhere] * 2,
        scratch_shapes=[
            pltpu.VMEM(packed.shape[:4] + (2 * KVW,), low),
            pltpu.VMEM((many, 2 * KVW), full),
            pltpu.VMEM((zs, 2, 4, wide, narrow), low),
            sem((7,)),
            pltpu.VMEM((4,) + block, low),
            pltpu.VMEM((2,) + block, low),
            sem((2 * zs - 2, 2)), sem((2,)),
            pltpu.VMEM(rest_part.shape, low),
            pltpu.VMEM(last_part.shape, low),
        ] + EXCHANGE_SEMS * 2
        + scatter_scratch(zs, False, many, 2 * KVW, False)
        + scatter_scratch(zs, True, wide, D, True) * 2
        + scatter_scratch(zs, True, wide, narrow, False),
        compiler_params=pltpu.CompilerParams(
            collective_id=collective_id, has_side_effects=True, vmem_limit_bytes=62 * MIB
        ),
        cost_estimate=LONG,
    )(x, attn_in, d_middle, d_attn, gains, gain_two, cosine, sine, d_kv, packed, both_part, both_up, both_down, g_out,
      g_query, rest_part, last_part, rest_in, last_in)


class Links:
    def __init__(self, seq, rows):
        self.zs, self.rows = seq // 2, rows
        self.kernels = rows == 4 and self.zs == 4
        self.z_groups = [[2 * z + c for z in range(self.zs)] for c in range(2)]
        self.core_groups = [[2 * z, 2 * z + 1] for z in range(self.zs)]

    def gather_z(self, block):
        return lax.all_gather(block, "seq", axis=0, tiled=True, axis_index_groups=self.z_groups)

    def scatter_z(self, blocks):
        return lax.psum_scatter(blocks, "seq", scatter_dimension=0, tiled=True, axis_index_groups=self.z_groups)

    def exchange_xla(self, blocks):
        moved = lax.all_to_all(blocks, "rows", split_axis=1, concat_axis=1, tiled=True)
        return lax.all_to_all(moved, "seq", split_axis=0, concat_axis=0, tiled=True, axis_index_groups=self.core_groups)

    def gather(self, array, z_flag, planes):
        if planes:
            array = lax.all_gather(array, "rows", axis=0)
        array = lax.all_gather(array, "seq", axis=0, axis_index_groups=self.core_groups)
        return self.gather_z(array[None]) if z_flag else array

    def scatter(self, blocks, z_flag, planes):
        blocks = self.scatter_z(blocks)[0] if z_flag else blocks
        blocks = lax.psum_scatter(blocks, "seq", scatter_dimension=0, tiled=True, axis_index_groups=self.core_groups)[0]
        if planes:
            blocks = lax.psum_scatter(blocks, "rows", scatter_dimension=0, tiled=True)[0]
        return blocks.astype(jnp.float32)


def on_device(seq, rows, tokens, w_query, w_key, w_value, w_out, w_gate, w_up, w_down, gain_attn, gain_ffn, lengths, order, cotangent):
    links = Links(seq, rows)
    zs = links.zs
    micro, _, span, _ = tokens.shape
    half_len = span // 2
    many = micro * span
    low = jnp.bfloat16
    wide = w_gate.shape[0]
    unit = w_down.shape[0]

    both, rest, pack, down_own, last_own = spread(
        w_gate, w_up, w_query, w_key, w_value, gain_attn, gain_ffn, w_down, zs, rows
    )
    cut = split_unit(unit)
    flat, flat_rest = (2 * rows * wide, 2 * zs * cut), (2 * rows * wide, 2 * zs * (unit - cut))
    dy_own = cotangent.reshape(many, D)
    own_tokens = tokens.reshape(many, D)
    x = own_tokens.astype(jnp.float32)
    first = lengths[:, 0, 0]
    slot_of = jnp.argmax(order[None, :] == jnp.arange(order.shape[0], dtype=jnp.int32)[:, None], axis=1).astype(jnp.int32)
    chained = links.kernels
    if chained:
        found = forward(order, first, own_tokens, pack, both, rest, down_own, w_out, dy_own, zs, 0)
        packed, both_own, kv, out_w, dy, rest_own = found[:6]
        both_w = [b.reshape(flat) for b in (both_own, *found[6 : 4 + 2 * zs])]
        down_w = [down_own, *found[4 + 2 * zs : 2 + 4 * zs]]
        rest_own = rest_own.reshape(flat_rest)
        queries, attn_in, attended, ffn_in, middle, gains, cosine, sine = found[2 + 4 * zs :]
        packed = packed.reshape(D, PACK)
    else:
        both_w = [links.gather_z(links.exchange_xla(both).reshape(flat))]
        rest_w = [links.gather_z(links.exchange_xla(rest).reshape(flat_rest))]
        down_w, last_w = [links.gather_z(down_own)], [links.gather_z(last_own)]
        packed, dy = links.gather(pack, True, True).reshape(D, PACK), links.gather(dy_own, False, True)
        gain_one, gain_two = packed[:, QKV].astype(jnp.float32), packed[:, QKV + 1].astype(jnp.float32)
        mine = slot_places(order, half_len, lax.axis_index("seq") * span + jnp.arange(span, dtype=jnp.int32))
        start = jnp.where(mine[None, :] >= first[:, None], first[:, None], 0)
        inverse = 10000.0 ** (-jnp.arange(HEAD_DIM // 2, dtype=jnp.float32) / (HEAD_DIM // 2))
        angles = ((mine[None, :] - start).astype(jnp.float32)[..., None] * inverse).reshape(many, HEAD_DIM // 2)
        cosine, sine = jnp.cos(angles), jnp.sin(angles)
        cosine, sine = jnp.tile(cosine, (1, 4)), jnp.tile(jnp.concatenate([-sine, sine], axis=1), (1, 2))
        attn_in = (x * rms_factor(x) * gain_one).astype(low)
        lin = product(attn_in, packed)
        kv_own = jnp.concatenate([turn(lin[:, D : D + KVW], cosine, sine), lin[:, D + KVW : QKV]], axis=1).astype(low)
        kv, out_w = links.gather(kv_own, True, False), links.gather(w_out, True, True)
        queries, attended = attend(order, slot_of, first, lin, cosine, sine, kv.reshape(seq, many, 2 * KVW))
        middle = x + product(attended, out_w.reshape(D, D))
        ffn_in = links.gather((middle * rms_factor(middle) * gain_two).astype(low), False, True).reshape(2 * rows * many, D)
    kv = kv.reshape(seq, many, 2 * KVW)
    out_w = out_w.reshape(D, D)
    dy = dy.reshape(2 * rows * many, D)

    shards = (zs, 2, rows, wide)
    if chained:
        ffn_in, rest_got, last_got, hidden, d_both, grad_both, grad_down = ffn_first(
            ffn_in, dy, both_w, down_w, zs, (rest_own, last_own), 1
        )
        rest_w, last_w = [rest_own, rest_got], [last_own, last_got]
        grad_both, grad_down = grad_both.reshape(*shards, 2 * zs * cut), grad_down.reshape(zs, cut, D)
        result_part, d_ffn_part, grad_rest, grad_last, *come = ffn_second(
            ffn_in, dy, hidden, d_both, (both_w, down_w), (rest_w, last_w), zs, (grad_both, grad_down), 2
        )
    else:
        hidden, d_both, grad_both, grad_down = ffn_first(ffn_in, dy, both_w, down_w, zs)
        grad_both, grad_down = grad_both.reshape(*shards, 2 * zs * cut), grad_down.reshape(zs, cut, D)
        result_part, d_ffn_part, grad_rest, grad_last = ffn_second(
            ffn_in, dy, hidden, d_both, (both_w, down_w), (rest_w, last_w), zs
        )
    grad_rest, grad_last = grad_rest.reshape(*shards, 2 * zs * (unit - cut)), grad_last.reshape(zs, unit - cut, D)
    d_ffn_part, result_part = (part.reshape(2, rows, many, D) for part in (d_ffn_part, result_part))
    if chained:
        out_all, kv_all = out_w.reshape(*shards, D), kv.reshape(zs, 2, many, 2 * KVW)
        result, d_middle, d_query, d_kv, gain_two_grad, grad_down, both_up, both_down, rest_in, last_in = back(
            order, first, dy_own, middle, gains, queries, cosine, sine, d_ffn_part, result_part, grad_both, grad_down,
            out_all, kv_all, grad_rest, grad_last, come, zs, 3,
        )
        grad_out, grad_query, d_attn = products(attended, attn_in, d_middle, d_query, packed)
        grad_out, grad_query = grad_out.reshape(*shards, D), grad_query.reshape(*shards, D)
        x_grad, grad_out, grad_query, pack_grad, grad_last, grad_both, grad_rest = weight_sums(
            own_tokens, attn_in, d_middle, d_attn, gains, gain_two_grad, cosine, sine, d_kv, packed.reshape(*shards, PACK),
            grad_both, both_up, both_down, grad_out, grad_query, grad_rest, grad_last, rest_in, last_in, zs, 4,
        )
    else:
        d_ffn_in = links.scatter(d_ffn_part, False, True)
        result = (middle + links.scatter(result_part, False, True)).astype(low)
        grad_both, grad_rest = (links.exchange_xla(links.scatter_z(grad)[0]) for grad in (grad_both, grad_rest))
        grad_down, grad_last = (links.scatter_z(grad)[0].astype(jnp.float32) for grad in (grad_down, grad_last))
        factor_two = rms_factor(middle)
        d_part, grad_gain_two = norm_back(d_ffn_in, middle * factor_two, factor_two, gain_two)
        d_middle = dy_own.astype(jnp.float32) + d_part
        d_mid_low = d_middle.astype(low)
        grad_out = links.scatter(product_tn(attended, d_mid_low).astype(low).reshape(*shards, D), True, True)
        d_heads = product_nt(d_mid_low, out_w).astype(low)
        d_query, d_kv = attend_back(order, slot_of, first, queries, d_heads, cosine, sine, kv)
        grad_query = links.scatter(product_tn(attn_in, d_query).astype(low).reshape(*shards, D), True, True)
        d_kv = links.scatter(d_kv.reshape(zs, 2, many, 2 * KVW), True, False)
        d_key = turn(d_kv[:, :KVW], cosine, -sine)
        d_kv = jnp.concatenate([d_key.astype(low), d_kv[:, KVW:].astype(low)], axis=1)
        d_attn_in = product_nt(d_query, packed[:, :D]) + product_nt(d_kv, packed[:, D:QKV])
        factor_one = rms_factor(x)
        d_x, grad_gain_one = norm_back(d_attn_in, x * factor_one, factor_one, gain_one)
        x_grad = (d_middle + d_x).astype(low)
        gains_grad = jnp.pad(jnp.stack([grad_gain_one, grad_gain_two], axis=1), ((0, 0), (0, 126)))
        pack_grad = jnp.concatenate([product_tn(attn_in, d_kv), gains_grad], axis=1).astype(low)
        pack_grad = links.scatter(pack_grad.reshape(*shards, 2 * KVW + 128), True, True)
    grad_gate, grad_up, grad_key, grad_value, gains_grad, grad_down = collect(
        (grad_both, grad_rest), pack_grad, (grad_down, grad_last), zs, rows, unit
    )
    return (
        result.reshape(tokens.shape),
        x_grad.reshape(tokens.shape),
        grad_query,
        grad_key,
        grad_value,
        grad_out,
        grad_gate,
        grad_up,
        grad_down,
        gains_grad[0],
        gains_grad[1],
    )


def solution(mesh):
    both = ("seq", "rows")
    row = P(None, "rows", "seq", None)
    weight, gain = P(both, None), P(both)
    return jax.shard_map(
        functools.partial(on_device, mesh.shape["seq"], mesh.shape["rows"]),
        mesh=mesh,
        in_specs=(row,) + (weight,) * 7 + (gain, gain, P(None, "rows", None), P(), row),
        out_specs=(row, row) + (weight,) * 7 + (gain, gain),
        check_vma=False,
    )
```

```python
import functools

import jax
import jax.numpy as jnp
import numpy as np
from jax import lax
from jax.experimental import pallas as pl
from jax.experimental.pallas import tpu as pltpu
from jax.sharding import PartitionSpec as P

D = 2048
HEADS = 32
KV_HEADS = 4
HEAD_DIM = 64
GROUP = 8
KVW = 256
QKV = D + 2 * KVW
PACK = QKV + 128

EPSILON = 1e-05
NEG_LARGE = -1e30
MESH = pl.DeviceIdType.MESH
MIB = 1 << 20
LONG = pl.CostEstimate(flops=50_000_000_000, bytes_accessed=150 * MIB, transcendentals=0)


def product(left, right):
    return jnp.dot(left, right, preferred_element_type=jnp.float32)


def product_nt(left, right):
    return lax.dot_general(left, right, (((1,), (1,)), ((), ())), preferred_element_type=jnp.float32)


def product_tn(left, right):
    return lax.dot_general(left, right, (((0,), (0,)), ((), ())), preferred_element_type=jnp.float32)


def rms_factor(values):
    return lax.rsqrt(jnp.mean(values * values, axis=-1, keepdims=True) + EPSILON)


def norm_back(d_scaled, normed, factor, gain):
    inner = d_scaled * gain
    mean = jnp.mean(inner * normed, axis=-1, keepdims=True)
    return factor * (inner - normed * mean), jnp.sum(d_scaled * normed, axis=0)


def turn(tensor, cosine, sine):
    rows, lanes = tensor.shape
    half = HEAD_DIM // 2
    swapped = jnp.flip(tensor.reshape(rows, lanes // HEAD_DIM, 2, half), axis=2).reshape(rows, lanes)
    return tensor * jnp.tile(cosine, (1, lanes // 128)) + swapped * jnp.tile(sine, (1, lanes // 128))


def slot_places(order, half_len, slot_ids):
    matches = (slot_ids // half_len)[:, None] == jnp.arange(order.shape[0], dtype=jnp.int32)[None, :]
    return jnp.sum(jnp.where(matches, order[None, :], 0), axis=1) * half_len + slot_ids % half_len


def place():
    s, r = lax.axis_index("seq"), lax.axis_index("rows")
    return lax.div(s, 2), lax.rem(s, 2), r


def send(src, dst, ssem, rsem, device):
    return pltpu.make_async_remote_copy(
        src_ref=src, dst_ref=dst, send_sem=ssem, recv_sem=rsem, device_id=device, device_id_type=MESH
    )


def greet(devices):
    barrier = pltpu.get_barrier_semaphore()
    for device in devices:
        pl.semaphore_signal(barrier, inc=1, device_id=device, device_id_type=MESH)
    pl.semaphore_wait(barrier, len(devices))


def corners(r):
    return r, r + 1 - 2 * lax.rem(r, 2), lax.rem(r + 2, 4), 3 - r


def exchange_others():
    return [(cc, j) for j in (3, 1, 2, 0) for cc in range(2) if (cc, j) != (0, 0)]


class Exchange:
    def __init__(self, own, out, ssem, rsem, l_sem):
        z, c, r = place()
        line = corners(r)
        self.own, self.out, self.ssem, self.rsem, self.here = own, out, ssem, rsem, (c, r)
        self.others = [(1 - c if cc else c, line[j]) for cc, j in exchange_others()]
        self.devices = [(z * 2 + core, row) for core, row in self.others]
        self.local = pltpu.make_async_copy(own.at[c, r], out.at[c, r], l_sem)

    def start(self):
        self.copies = []
        for i, other in enumerate(self.others):
            copy = send(self.own.at[other], self.out.at[self.here], self.ssem.at[i], self.rsem.at[i], self.devices[i])
            copy.start()
            self.copies.append(copy)
        self.local.start()

    def finish(self):
        for i, other in enumerate(self.others):
            dst = self.out.at[other]
            send(dst, dst, self.ssem.at[i], self.rsem.at[i], self.devices[i]).wait_recv()
        self.local.wait()

    def end(self):
        for copy in self.copies:
            copy.wait_send()


class Line:
    def __init__(self, zs, way, lo, hi, src, dst, sems):
        z, c, r = place()
        lo, hi = (lo, min(hi, zs - 1)) if way == 1 else (max(lo, 1), hi)
        self.sends = (z >= lo) & (z < hi)
        self.gets = (z - way >= lo) & (z - way < hi)
        to = lax.rem(z + way + zs, zs)
        self.copy = send(src, dst, sems.at[0], sems.at[1], (to * 2 + c, r))

    def start(self):
        pl.when(self.sends)(self.copy.start)

    def finish(self):
        pl.when(self.sends)(self.copy.wait_send)
        pl.when(self.gets)(self.copy.wait_recv)


LINE_SEMS = pltpu.SemaphoreType.DMA((2,))
EXCHANGE_SEMS = [pltpu.SemaphoreType.DMA((7,)), pltpu.SemaphoreType.DMA((7,)), pltpu.SemaphoreType.DMA]


def neighbours(zs, planes, moved):
    z, c, r = place()
    line = corners(r)
    s = z * 2 + c
    devices = [(z * 2 + 1 - c, r)]
    if moved:
        devices = [(z * 2 + (1 - c if cc else c), line[j]) for cc, j in exchange_others()]
    elif planes:
        devices += [(s, line[1]), (s, line[2])]
    return devices + [(lax.rem(z + k, zs) * 2 + c, r) for k in range(1, zs)]


class Gather:
    def __init__(self, zs, z_flag, planes, own, out, z_ssem, z_rsem, f_ssem, f_rsem, h_ssem, h_rsem, c_ssem, c_rsem, l_sem):
        self.__dict__.update(locals())
        self.z, self.c, self.r = place()
        self.line = corners(self.r)
        self.s = self.z * 2 + self.c
        self.twin = (self.z * 2 + 1 - self.c, self.r)
        self.count = zs if z_flag else 1
        self.half = own.shape[0] // 2
        self.pending = []
        self.sent = []
        z = self.z
        self.kth = [0, jnp.where(z == 0, 3, 1), jnp.where((z == 0) | (z == 3), 2, 3), jnp.where(z == 0, 1, jnp.where(z == 3, 3, 2))]

    def start(self, copy):
        copy.start()
        self.pending.append(copy.wait_send)

    def slot(self, k, other, j):
        if not self.z_flag:
            return self.out.at[other, j]
        core = 1 - self.c if other else self.c
        zz = lax.rem(self.z - k + self.zs, self.zs)
        return self.out.at[zz, core, self.line[j]] if self.planes else self.out.at[zz, core]

    def z_copy(self, n, way, k, src, dst):
        to = (lax.rem(self.z + way + self.zs, self.zs) * 2 + self.c, self.r)
        return send(src, dst, self.z_ssem.at[n, 0 if way == 1 else 1], self.z_rsem.at[k], to)

    def hand_on(self, n, src, dst):
        z, k, zs = self.z, self.kth[n], self.zs
        up, down = (z < zs - 1, z > 0) if n == 0 else ((z >= k) & (z < zs - 1), (z < k) & (z > 0))
        for way, goes, step in ((1, up, 1), (-1, down, zs - 1)):
            copy = self.z_copy(n, way, lax.rem(k + step, zs), src, dst)
            pl.when(goes)(copy.start)
            self.sent.append((goes, copy))

    def near(self, k, j, src):
        dst = self.slot(k, 0, j) if src is None or not self.z_flag else self.slot(k, 0, 0)
        return send(dst if src is None else src, dst, self.f_ssem.at[k, j - 1], self.f_rsem.at[k, j - 1], (self.s, self.line[j]))

    def part(self, ref, j):
        return ref.at[pl.ds(self.half if j == 1 else 0, self.half)]

    def far(self, k, j, src):
        if src is None:
            src = dst = self.part(self.slot(k, 0, 3), j)
        else:
            dst = self.part(src if self.z_flag else self.out.at[0, 3], j)
            src = self.part(src, j)
        return send(src, dst, self.h_ssem.at[k, j - 1], self.h_rsem.at[k, j - 1], (self.s, self.line[3 - j]))

    def twin_copy(self, k, j, src):
        dst = self.slot(k, 0, j) if self.z_flag else self.out.at[1, j]
        return send(src, dst, self.c_ssem.at[k, j], self.c_rsem.at[k, j], self.twin)

    def to_twin(self, k, j, src):
        self.start(self.twin_copy(k, j, src))

    def from_twin(self, k, j):
        dst = self.slot(k, 1, j)
        send(dst, dst, self.c_ssem.at[k, j], self.c_rsem.at[k, j], self.twin).wait_recv()

    def launch(self):
        self.local = pltpu.make_async_copy(self.own, self.slot(0, 0, 0), self.l_sem)
        self.local.start()
        if self.count > 1 and self.planes:
            self.hand_on(0, self.own, self.slot(0, 0, 0))
        elif self.count > 1:
            for k in range(1, self.count):
                self.start(self.z_copy(k, k, k, self.own, self.slot(0, 0, 0)))

    def arrive(self, n):
        k = self.kth[n]
        src = self.slot(k, 0, 0)
        self.z_copy(n, 1, k, src, src).wait_recv()
        if self.planes:
            self.hand_on(n, src, src)

    def begin(self, n):
        k = self.kth[n]
        src = self.slot(k, 0, 0) if n else self.own
        if self.planes:
            for j in (1, 2):
                self.start(self.near(k, j, src))
        self.to_twin(k, 0, src)

    def forward(self, n):
        k = self.kth[n]
        for j in (1, 2):
            self.near(k, j, None).wait_recv()
            src = self.slot(k, 0, j)
            self.start(self.far(k, j, src))
            self.to_twin(k, j, src)

    def finish(self, n):
        k = self.kth[n]
        for j in (1, 2):
            self.far(k, j, None).wait_recv()
        self.to_twin(k, 3, self.slot(k, 0, 3))

    def complete(self, n):
        k = self.kth[n]
        if n == 0:
            self.local.wait()
        for j in range(4 if self.planes else 1):
            self.from_twin(k, j)

    def sent_all(self):
        for j in (1, 2):
            self.near(0, j, self.own).wait_send()
            self.far(0, j, self.slot(0, 0, j)).wait_send()
        for j in range(4):
            self.twin_copy(0, j, self.slot(0, 0, j) if j else self.own).wait_send()

    def end(self):
        for goes, copy in self.sent:
            pl.when(goes)(copy.wait_send)
        for wait in self.pending:
            wait()


def gather_sems(zs, z_flag):
    sem = pltpu.SemaphoreType.DMA
    n = zs if z_flag else 1
    return [sem((n, 2)), sem((n,)), sem((n, 2)), sem((n, 2)), sem((n, 2)), sem((n, 2)), sem((n, 4)), sem((n, 4)), sem]


class Chain:
    def __init__(self, zs, own, got, sems):
        self.zs, self.own, self.got, self.sems = zs, own, got, sems
        self.lines = []

    def start(self, k):
        zs = self.zs
        up, down = (self.own, self.own) if k == 1 else (self.got[k - 2], self.got[zs + k - 3])
        self.lines = [
            Line(zs, 1, k - 1, zs, up, self.got[k - 1], self.sems.at[k - 1]),
            Line(zs, -1, 0, zs - k + 1, down, self.got[zs + k - 2], self.sems.at[zs + k - 2]),
        ]
        for line in self.lines:
            line.start()

    def finish(self):
        for line in self.lines:
            line.finish()


class Scatter:
    def __init__(self, zs, z_flag, planes, given, final, stage, twin_in, half_in, full_in, z_in, l_sem, c_ssem, c_rsem, h_ssem,
                 h_rsem, f_ssem, f_rsem, z_ssem, z_rsem):
        self.__dict__.update(locals())
        self.z, self.c, self.r = place()
        self.line = corners(self.r)
        self.s = self.z * 2 + self.c
        self.twin = (self.z * 2 + 1 - self.c, self.r)
        self.rows = twin_in.shape[2]
        self.step = 16
        self.spots = (3, 1, 2, 0) if planes else (0,)
        self.zs = zs if z_flag else 1
        self.order = list(range(1, self.zs)) + [0]
        self.pending = []
        self.loads = []
        self.settled = 0

    def at_z(self, k):
        return (lax.rem(self.z + k, self.zs) * 2 + self.c, self.r)

    def block(self, k, other, j):
        if not self.z_flag:
            return self.given.at[other, j]
        zz, core = lax.rem(self.z + k, self.zs), 1 - self.c if other else self.c
        return self.given.at[zz, core, self.line[j]] if self.planes else self.given.at[zz, core]

    def start(self, copy):
        copy.start()
        self.pending.append(copy.wait_send)

    def begin(self, schedule):
        for k in self.order:
            for j in self.spots:
                self.start(self.twin_copy(k, j, self.block(k, 1, j)))
        if self.stage is not None:
            self.loads = [
                pltpu.make_async_copy(self.block(k, 0, j), self.stage.at[n % 2], self.l_sem.at[n % 2])
                for n, (k, j) in enumerate(schedule)
            ]
            for load in self.loads[:2]:
                load.start()

    def twin_copy(self, k, j, src):
        dst = self.twin_in.at[k, j]
        return send(dst if src is None else src, dst, self.c_ssem.at[k, j], self.c_rsem.at[k, j], self.twin)

    def settle(self, k, j, parts):
        own = self.block(k, 0, j)
        n = self.settled
        if self.stage is not None:
            self.loads[n].wait()
            own = self.stage.at[n % 2]
        self.twin_copy(k, j, None).wait_recv()
        step = self.step
        for first, last, more in parts:

            def body(i, carry, first=first, more=more):
                at = pl.ds(pl.multiple_of(first + i * step, step), step)
                value = own[at, :].astype(jnp.float32) + self.twin_in[k, j, at, :].astype(jnp.float32)
                for ref, offset in more:
                    there = pl.ds(pl.multiple_of(first - offset + i * step, step), step)
                    value = value + ref[there, :].astype(jnp.float32)
                if k == 0 and j == 0:
                    self.final(at, value)
                else:
                    self.twin_in[k, j, at, :] = value.astype(self.twin_in.dtype)
                return carry

            lax.fori_loop(0, (last - first) // step, body, 0)
        if n + 2 < len(self.loads):
            self.loads[n + 2].start()
        self.settled = n + 1

    def half_copy(self, k, n, src):
        dst = self.half_in.at[k, n]
        return send(dst if src is None else src, dst, self.h_ssem.at[k, n], self.h_rsem.at[k, n], (self.s, self.line[n + 1]))

    def full_copy(self, k, j, src):
        dst = self.full_in.at[k, j - 1]
        return send(dst if src is None else src, dst, self.f_ssem.at[k, j - 1], self.f_rsem.at[k, j - 1], (self.s, self.line[j]))

    def z_copy(self, k, src):
        dst = self.z_in.at[k]
        return send(dst if src is None else src, dst, self.z_ssem.at[k], self.z_rsem.at[k], self.at_z(k))

    def stage_a(self, k):
        half = self.rows // 2
        self.settle(k, 3, [(0, self.rows, [])])
        self.start(self.half_copy(k, 1, self.twin_in.at[k, 3, pl.ds(half, half)]))
        self.start(self.half_copy(k, 0, self.twin_in.at[k, 3, pl.ds(0, half)]))

    def stage_b(self, k):
        half = self.rows // 2
        for j in (1, 2):
            n = 2 - j
            self.half_copy(k, n, None).wait_recv()
            more = [(self.half_in.at[k, n], half if n else 0)]
            self.settle(k, j, [(0, half, [] if n else more), (half, self.rows, more if n else [])])
            self.start(self.full_copy(k, j, self.twin_in.at[k, j]))

    def stage_c(self, k):
        more = []
        if self.planes:
            for j in (1, 2):
                self.full_copy(k, j, None).wait_recv()
                more.append((self.full_in.at[k, j - 1], 0))
        if not k:
            for other in range(1, self.zs):
                self.z_copy(other, None).wait_recv()
                more.append((self.z_in.at[other], 0))
        self.settle(k, 0, [(0, self.rows, more)])
        if k:
            self.start(self.z_copy(k, self.twin_in.at[k, 0]))

    def end(self):
        for wait in self.pending:
            wait()


def scatter_scratch(zs, planes, rows, columns, staged):
    sem = pltpu.SemaphoreType.DMA
    low, least = jnp.bfloat16, (1, 2, 16, 128)
    spots = 4 if planes else 1
    return [
        pltpu.VMEM((2, rows, columns) if staged else (16, 128), low),
        pltpu.VMEM((zs, spots, rows, columns), low),
        pltpu.VMEM((zs, 2, rows // 2, columns) if planes else least, low),
        pltpu.VMEM((zs, 2, rows, columns) if planes else least, low),
        pltpu.VMEM((zs, rows, columns) if zs > 1 else least[1:], low),
        sem((2,)), sem((zs, 4)), sem((zs, 4)), sem((zs, 2)), sem((zs, 2)), sem((zs, 2)), sem((zs, 2)), sem((zs,)), sem((zs,)),
    ]


SCATTER_REFS = 14


def scatter_plan(items):
    rounds = []
    for n in range(len(items) + 2):
        rounds.append([])
        for back, stage in enumerate(("a", "b", "c")):
            if 0 <= n - back < len(items):
                name, k = items[n - back]
                if stage != "c" or k:
                    rounds[-1].append((name, stage, k))
    rounds.append([(name, "c", 0) for name, k in items if not k])
    places = {"a": (3,), "b": (1, 2), "c": (0,)}
    schedules = {}
    for name, stage, k in sum(rounds, []):
        schedules.setdefault(name, []).extend((k, j) for j in places[stage])
    return rounds, schedules


def run_stage(scatters, name, stage, k):
    {"a": Scatter.stage_a, "b": Scatter.stage_b, "c": Scatter.stage_c}[stage](scatters[name], k)


class SumChain:
    def __init__(self, zs, parts, got, held, sems, l_sem):
        self.__dict__.update(locals())
        self.z = place()[0]

    def own(self, to):
        return self.parts.at[lax.rem(self.z + to + self.zs, self.zs)]

    def fetch(self, k):
        self.loads = [
            pltpu.make_async_copy(self.own(-k), self.held.at[0], self.l_sem.at[0]),
            pltpu.make_async_copy(self.own(k), self.held.at[1], self.l_sem.at[1]),
        ]
        for load in self.loads:
            load.start()

    def add(self, into, more):
        ref = self.got[into]
        ref[...] = (ref[...].astype(jnp.float32) + self.held[more].astype(jnp.float32)).astype(ref.dtype)

    def lines_of(self, k):
        zs, got = self.zs, self.got
        up, down = k - 1, zs - 2 + k
        lines = [
            Line(zs, 1, 0, 1, self.own(-k), got[up], self.sems.at[up]),
            Line(zs, -1, zs - 1, zs, self.own(k), got[down], self.sems.at[down]),
        ]
        if k > 1:
            lines += [
                Line(zs, 1, 1, k, got[up - 1], got[up], self.sems.at[up]),
                Line(zs, -1, zs - k, zs - 1, got[down - 1], got[down], self.sems.at[down]),
            ]
        return lines

    def start(self, k):
        zs, z = self.zs, self.z
        up, down = k - 1, zs - 2 + k
        if k > 1:
            for load in self.loads:
                load.wait()
            pl.when((z >= 1) & (z < k))(functools.partial(self.add, up - 1, 0))
            pl.when((z >= zs - k) & (z < zs - 1))(functools.partial(self.add, down - 1, 1))
        self.lines = self.lines_of(k)
        for line in self.lines:
            line.start()
        if k == zs - 1:
            self.loads = [pltpu.make_async_copy(self.own(0), self.held.at[0], self.l_sem.at[0])]
            self.loads[0].start()

    def finish(self, k=None):
        for line in self.lines if k is None else self.lines_of(k):
            line.finish()

    def total(self):
        zs, z = self.zs, self.z
        self.loads[0].wait()

        def add(come):
            self.held[0] = (self.held[0].astype(jnp.float32) + self.got[come][...].astype(jnp.float32)).astype(self.held.dtype)

        pl.when(z > 0)(functools.partial(add, zs - 2))
        pl.when(z < zs - 1)(functools.partial(add, 2 * zs - 3))


def partner(tensor):
    lanes = tensor.shape[-1]
    half = HEAD_DIM // 2
    lane = lax.broadcasted_iota(jnp.int32, tensor.shape, tensor.ndim - 1)
    ahead = pltpu.roll(tensor, lanes - half, tensor.ndim - 1)
    behind = pltpu.roll(tensor, half, tensor.ndim - 1)
    return jnp.where(lax.rem(lane, HEAD_DIM) < half, ahead, behind)


def first_of(my_block, half_blocks):
    return jnp.where(my_block >= half_blocks, half_blocks, 0)


def chosen_slots(places, first_block, half_len, wide):
    wanted = first_block * half_len + lax.broadcasted_iota(jnp.int32, (wide, 2 * wide), 0)
    return jnp.where(places == wanted, 1.0, 0.0).astype(jnp.bfloat16)


def stack_heads(block, first):
    return jnp.concatenate(
        [block[:, (first + h) * HEAD_DIM : (first + h + 1) * HEAD_DIM] for h in range(GROUP)], axis=0
    )


def unstack_heads(stacked, span):
    return jnp.concatenate([stacked[h * span : (h + 1) * span] for h in range(GROUP)], axis=1)


def load_window(inverse_ref, kv_ref, window, first_block):
    half_len = kv_ref.shape[1] // 2
    for n in range(window.shape[0] // half_len):
        slot = inverse_ref[first_block + n]
        at = pl.ds(pl.multiple_of(lax.rem(slot, 2) * half_len, half_len), half_len)
        window[n * half_len : (n + 1) * half_len, :] = kv_ref[lax.div(slot, 2), at, :]


def window_of(order_ref, first_ref, count, half_len):
    m, half = pl.program_id(0), pl.program_id(1)
    my_block = order_ref[lax.axis_index("seq") * 2 + half]
    half_blocks = count // half_len // 2
    first_block = jnp.where(my_block >= half_blocks, half_blocks, 0)
    return first_block, my_block * half_len, first_ref[m]


def attend_kernel(order_ref, inverse_ref, first_ref, lin_ref, cos_ref, sin_ref, kv_ref, q_ref, out_ref, window, bias):
    span = lin_ref.shape[0]
    wide = window.shape[0]
    first_block, my_place, first = window_of(order_ref, first_ref, 2 * wide, span)
    load_window(inverse_ref, kv_ref, window, first_block)
    key_place = first_block * span + lax.broadcasted_iota(jnp.int32, (span, wide), 1)
    place_here = my_place + lax.broadcasted_iota(jnp.int32, (span, wide), 0)
    start = jnp.where(place_here >= first, first, 0)
    bias[...] = jnp.where((key_place <= place_here) & (key_place >= start), 0.0, NEG_LARGE)
    width = GROUP * HEAD_DIM
    cosine = jnp.concatenate([cos_ref[...]] * (width // 128), axis=1)
    sine = jnp.concatenate([sin_ref[...]] * (width // 128), axis=1)
    for g in range(KV_HEADS):
        at = slice(g * width, (g + 1) * width)
        lin = lin_ref[:, at]
        query = (lin * cosine + partner(lin) * sine).astype(jnp.bfloat16) * jnp.bfloat16(HEAD_DIM ** -0.5)
        q_ref[:, at] = query
        key = window[:, g * HEAD_DIM : (g + 1) * HEAD_DIM]
        value = window[:, KVW + g * HEAD_DIM : KVW + (g + 1) * HEAD_DIM]
        scores = product_nt(stack_heads(query, 0), key).reshape(GROUP, span, wide) + bias[...][None]
        exps = jnp.exp(scores - jnp.max(scores, axis=-1, keepdims=True))
        total = jnp.sum(exps, axis=-1, keepdims=True).reshape(GROUP * span, 1)
        mixed = product(exps.astype(jnp.bfloat16).reshape(GROUP * span, wide), value) / total
        out_ref[:, at] = unstack_heads(mixed, span).astype(jnp.bfloat16)


def attend_back_heads(queries, d_heads, key, value, bias, span):
    query, d_mixed = stack_heads(queries, 0), stack_heads(d_heads, 0)
    scores = product_nt(key, query) + bias[...]
    exps = jnp.exp(scores - jnp.max(scores, axis=0, keepdims=True))
    probs = exps * (1.0 / jnp.sum(exps, axis=0, keepdims=True))
    weighted = probs * product_nt(value, d_mixed)
    delta = jnp.sum(weighted, axis=0, keepdims=True)
    d_scores = (weighted - probs * delta).astype(jnp.bfloat16)
    d_query = unstack_heads(product_tn(d_scores, key) * HEAD_DIM ** -0.5, span)
    return product(d_scores, query), product(probs.astype(jnp.bfloat16), d_mixed), d_query


def attend_back_kernel(order_ref, inverse_ref, first_ref, q_ref, d_ref, cos_ref, sin_ref, kv_ref, dq_ref, dkv_ref, window, bias, sums):
    span = q_ref.shape[0]
    wide = window.shape[0]
    rows = GROUP * span
    half = pl.program_id(1)
    first_block, my_place, first = window_of(order_ref, first_ref, 2 * wide, span)
    load_window(inverse_ref, kv_ref, window, first_block)
    key_place = first_block * span + lax.broadcasted_iota(jnp.int32, (wide, rows), 0)
    place_here = my_place + lax.rem(lax.broadcasted_iota(jnp.int32, (wide, rows), 1), span)
    start = jnp.where(place_here >= first, first, 0)
    bias[...] = jnp.where((key_place <= place_here) & (key_place >= start), 0.0, NEG_LARGE)

    @pl.when(half == 0)
    def _():
        sums[...] = jnp.zeros_like(sums)

    width = GROUP * HEAD_DIM
    cosine = jnp.concatenate([cos_ref[...]] * (width // 128), axis=1)
    sine = jnp.concatenate([sin_ref[...]] * (width // 128), axis=1)
    d_keys, d_values = [], []
    for g in range(KV_HEADS):
        at = slice(g * width, (g + 1) * width)
        key = window[:, g * HEAD_DIM : (g + 1) * HEAD_DIM]
        value = window[:, KVW + g * HEAD_DIM : KVW + (g + 1) * HEAD_DIM]
        d_key, d_value, d_query = attend_back_heads(q_ref[:, at], d_ref[:, at], key, value, bias, span)
        d_keys.append(d_key)
        d_values.append(d_value)
        dq_ref[:, at] = (d_query * cosine - partner(d_query) * sine).astype(jnp.bfloat16)
    d_window = jnp.concatenate(d_keys + d_values, axis=1)
    for n in range(wide // span):
        slot = inverse_ref[first_block + n]
        to = pl.ds(pl.multiple_of(lax.rem(slot, 2) * span, span), span)
        sums[lax.div(slot, 2), to, :] += d_window[n * span : (n + 1) * span]

    @pl.when(half == 1)
    def _():
        dkv_ref[...] = sums[...].astype(jnp.bfloat16)


def attention_specs(seq, micro, span):
    half_len = span // 2

    def rows(width):
        return pl.BlockSpec((half_len, width), lambda m, h, *_: (m * 2 + h, 0))

    whole = pl.BlockSpec((seq, span, 2 * KVW), lambda m, h, *_: (0, m, 0))
    return half_len, rows, whole


def attend(order, inverse, first, lin, cosine, sine, kv):
    seq, many, _ = kv.shape
    micro = first.shape[0]
    span = many // micro
    half_len, rows, whole = attention_specs(seq, micro, span)
    wide = seq * span // 2
    return pl.pallas_call(
        attend_kernel,
        grid_spec=pltpu.PrefetchScalarGridSpec(
            num_scalar_prefetch=3,
            grid=(micro, 2),
            in_specs=[rows(D), rows(128), rows(128), whole],
            out_specs=[rows(D), rows(D)],
            scratch_shapes=[pltpu.VMEM((wide, 2 * KVW), jnp.bfloat16), pltpu.VMEM((half_len, wide), jnp.float32)],
        ),
        out_shape=[jax.ShapeDtypeStruct((many, D), jnp.bfloat16)] * 2,
        compiler_params=pltpu.CompilerParams(vmem_limit_bytes=48 * MIB),
        cost_estimate=pl.CostEstimate(flops=8 * many * wide * D, bytes_accessed=16 * MIB, transcendentals=many * wide * HEADS),
    )(order, inverse, first, lin, cosine, sine, kv)


def attend_back(order, inverse, first, queries, d_heads, cosine, sine, kv):
    seq, many, _ = kv.shape
    micro = first.shape[0]
    span = many // micro
    half_len, rows, whole = attention_specs(seq, micro, span)
    wide = seq * span // 2
    return pl.pallas_call(
        attend_back_kernel,
        grid_spec=pltpu.PrefetchScalarGridSpec(
            num_scalar_prefetch=3,
            grid=(micro, 2),
            in_specs=[rows(D), rows(D), rows(128), rows(128), whole],
            out_specs=[rows(D), whole],
            scratch_shapes=[
                pltpu.VMEM((wide, 2 * KVW), jnp.bfloat16),
                pltpu.VMEM((wide, GROUP * half_len), jnp.float32),
                pltpu.VMEM((seq, span, 2 * KVW), jnp.float32),
            ],
        ),
        out_shape=[jax.ShapeDtypeStruct((many, D), jnp.bfloat16), jax.ShapeDtypeStruct(kv.shape, jnp.bfloat16)],
        compiler_params=pltpu.CompilerParams(vmem_limit_bytes=56 * MIB),
        cost_estimate=pl.CostEstimate(flops=20 * many * wide * D, bytes_accessed=24 * MIB, transcendentals=many * wide * HEADS),
    )(order, inverse, first, queries, d_heads, cosine, sine, kv)


def assemble(zs, pieces, whole, sem):
    if len(pieces) == 1:
        copy = pltpu.make_async_copy(pieces[0], whole, sem.at[0])
        copy.start()
        return [copy]
    z = lax.div(lax.axis_index("seq"), 2)
    size = whole.shape[0] // zs

    def rows(zz):
        return whole.at[pl.ds(pl.multiple_of(zz * size, size), size)]

    if len(pieces) == 2:
        pieces = [pieces[0], *(pieces[1].at[k] for k in range(zs - 1))]
    copies = [pltpu.make_async_copy(pieces[0], rows(z), sem.at[0])]
    copies[0].start()
    for k in range(1, zs):
        to = rows(lax.rem(z - k + zs, zs))
        below = pltpu.make_async_copy(pieces[k], to, sem.at[k])
        if len(pieces) == zs:
            below.start()
        else:
            above = pltpu.make_async_copy(pieces[2 * zs - 1 - k], to, sem.at[k])
            pl.when(z >= k)(below.start)
            pl.when(z < k)(above.start)
        copies.append(below)
    return copies


class Around:
    def __init__(self, zs, block, got, sems):
        z, c, r = place()
        self.copies = [
            send(block(k), got.at[k - 1], sems.at[k - 1, 0], sems.at[k - 1, 1], (lax.rem(z + k, zs) * 2 + c, r))
            for k in range(1, zs)
        ]

    def start(self):
        for copy in self.copies:
            copy.start()

    def finish(self):
        for copy in self.copies:
            copy.wait()


def swiglu(lin, d_hidden):
    n = d_hidden.shape[1]
    gate, upper = lin[:, :n], lin[:, n:]
    sig = 1.0 / (1.0 + jnp.exp(-gate))
    act = gate * sig
    d_gate = d_hidden * upper * (sig * (1.0 + gate * (1.0 - sig)))
    d_both = jnp.concatenate([d_gate.astype(jnp.bfloat16), (d_hidden * act).astype(jnp.bfloat16)], axis=1)
    return (act * upper).astype(jnp.bfloat16), d_both


def add_gradients(x, dy, hidden, d_both, both_sum, down_sum):
    for at in range(0, D, 256):
        both_sum[at : at + 256, :] += product_tn(x[:, at : at + 256], d_both)
    part = hidden.shape[1] // 4
    for at in range(0, hidden.shape[1], part):
        down_sum[at : at + part, :] += product_tn(hidden[:, at : at + part], dy)


def put_gradients(sums, staged, out, sem):
    copies = []
    for n in range(2):
        staged[n][...] = sums[n][...].astype(jnp.bfloat16)
        copies.append(pltpu.make_async_copy(staged[n], out[n], sem.at[n, 0]))
        copies[-1].start()
    for copy in copies:
        copy.wait()


def ffn_first_kernel(zs, count, linked, *refs):
    x_ref, dy_ref = refs[:2]
    both_pieces, down_pieces = refs[2 : 2 + count], refs[2 + count : 2 + 2 * count]
    refs = refs[2 + 2 * count :]
    if linked:
        rest_own, last_own, x_out_ref, rest_got, last_got, *refs = refs
    hidden_ref, d_both_ref, g_both_ref, g_down_ref, both_w, down_w, both_sum, down_sum, sem, *more = refs
    step, last = pl.program_id(0), pl.num_programs(0) - 1
    gathered, arounds = None, []
    if linked:
        x_all, a_sems, *g_sems = more
        gathered = Gather(zs, False, True, x_ref, x_all, *g_sems)
        arounds = [
            Around(zs, lambda k: rest_own, rest_got, a_sems.at[0]), Around(zs, lambda k: last_own, last_got, a_sems.at[1])
        ]

    @pl.when(step == 0)
    def _():
        copies = assemble(zs, both_pieces, both_w, sem.at[0]) + assemble(zs, down_pieces, down_w, sem.at[1])
        if linked:
            greet(neighbours(zs, True, False))
            gathered.launch()
            gathered.begin(0)
            for one in arounds:
                one.start()
        both_sum[...] = jnp.zeros_like(both_sum)
        down_sum[...] = jnp.zeros_like(down_sum)
        for copy in copies:
            copy.wait()
        if linked:
            gathered.local.wait()

    if linked:
        waits = [
            lambda: gathered.from_twin(0, 0), lambda: gathered.forward(0), lambda: gathered.from_twin(0, 1), None,
            lambda: gathered.from_twin(0, 2), lambda: gathered.finish(0), lambda: gathered.from_twin(0, 3),
        ]
        for n, wait in enumerate(waits):
            if wait is not None:
                pl.when(step == n + 1)(wait)
        x = x_all[lax.rem(step, 2), lax.div(step, 2)]
        x_out_ref[...] = x
    else:
        x = x_ref[...]
    dy = dy_ref[...]
    hidden, d_both = swiglu(product(x, both_w[...]), product_nt(dy, down_w[...]))
    hidden_ref[...] = hidden
    d_both_ref[...] = d_both
    add_gradients(x, dy, hidden, d_both, both_sum, down_sum)

    @pl.when(step == last)
    def _():
        put_gradients((both_sum, down_sum), (both_w, down_w), (g_both_ref, g_down_ref), sem)
        for one in arounds:
            one.finish()
        if linked:
            gathered.sent_all()


def ffn_second_kernel(zs, counts, linked, *refs):
    x_ref, dy_ref, hidden_ref, d_both_ref = refs[:4]
    refs = refs[4:]
    pieces = []
    for count in counts:
        pieces += [refs[:count], refs[count : 2 * count]]
        refs = refs[2 * count :]
    if linked:
        g_both_one, g_down_one, *refs = refs
    out_ref, dx_ref, g_both_ref, g_down_ref, *refs = refs
    if linked:
        *got, both_one, down_one, both_w, down_w, both_sum, down_sum, stage, sem, z_sem, come, held, d_sems, dl_sem = refs
    else:
        got, (both_one, down_one, both_w, down_w, both_sum, down_sum, stage, sem) = [], refs
    n, wide = stage.shape[1] // 2, down_w.shape[0]
    down_rows = down_w.at[pl.ds(0, n)]
    step, last = pl.program_id(0), pl.num_programs(0) - 1
    lines = []
    if linked:
        z = lax.div(lax.axis_index("seq"), 2)
        lines = [
            Line(zs, 1, 0, 1, g_both_one.at[lax.rem(z + zs - 1, zs)], got[0], z_sem.at[0]),
            Line(zs, -1, zs - 1, zs, g_both_one.at[lax.rem(z + 1, zs)], got[1], z_sem.at[1]),
        ]
        none = [None] * (zs - 3)
        down = SumChain(zs, g_down_one, [come.at[0], got[2], *none, come.at[1], got[3], *none], held, d_sems, dl_sem)

    @pl.when(step == 0)
    def _():
        copies = []
        for which, whole in enumerate((both_one, down_one, stage, down_rows)):
            copies += assemble(zs, pieces[which], whole, sem.at[which])
        if linked:
            greet(neighbours(zs, False, False))
            down.start(1)
        both_sum[...] = jnp.zeros_like(both_sum)
        down_sum[...] = jnp.zeros_like(down_sum)
        if wide > n:
            both_w[...] = jnp.zeros_like(both_w)
            down_w[n:, :] = jnp.zeros((wide - n, D), down_w.dtype)
        for copy in copies:
            copy.wait()
        both_w[:, :n] = stage[:, :n]
        both_w[:, wide : wide + n] = stage[:, n:]

    if linked:

        @pl.when(step == last - 5)
        def _():
            down.finish(1)
            for line in lines:
                line.start()
            down.fetch(2)
            down.start(2)

    x, dy = x_ref[...], dy_ref[...]
    hidden, d_both = swiglu(product(x, both_w[...]), product_nt(dy, down_w[...]))
    dx_ref[...] = (product_nt(d_both_ref[...], both_one[...]) + product_nt(d_both, both_w[...])).astype(jnp.bfloat16)
    out_ref[...] = (product(hidden_ref[...], down_one[...]) + product(hidden, down_w[...])).astype(jnp.bfloat16)
    add_gradients(x, dy, hidden, d_both, both_sum, down_sum)

    @pl.when(step == last)
    def _():
        stage[:, :n] = both_sum[:, :n].astype(jnp.bfloat16)
        stage[:, n:] = both_sum[:, wide : wide + n].astype(jnp.bfloat16)
        down_w[...] = down_sum[...].astype(jnp.bfloat16)
        copies = [
            pltpu.make_async_copy(stage, g_both_ref, sem.at[0, 0]), pltpu.make_async_copy(down_rows, g_down_ref, sem.at[1, 0])
        ]
        for copy in copies:
            copy.start()
        for copy in copies:
            copy.wait()
        for line in lines:
            line.finish()
        if linked:
            down.finish(2)


def ffn_first(x, dy, both_pieces, down_pieces, zs, others=(), collective_id=None):
    count, n = len(both_pieces), down_pieces[0].shape[0] * (zs if len(down_pieces) > 1 else 1)
    block, low, full = 256, jnp.bfloat16, jnp.float32
    sem, shape = pltpu.SemaphoreType.DMA, jax.ShapeDtypeStruct
    anywhere = pl.BlockSpec(memory_space=pl.ANY)
    linked = bool(others)
    total = dy.shape[0]

    def tokens(width):
        if linked:
            return pl.BlockSpec((block, width), lambda i: (i % 2 * 4 + i // 2, 0))
        return pl.BlockSpec((block, width), lambda i: (i, 0))

    extra_specs, extra_shapes, extra_scratch, params = [], [], [], {}
    if linked:
        extra_specs = [tokens(D)] + [anywhere] * 2
        extra_shapes = [shape(dy.shape, low)] + [shape((zs - 1,) + other.shape, low) for other in others]
        extra_scratch = [pltpu.VMEM((2, 4) + x.shape, low), sem((2, zs - 1, 2))] + gather_sems(zs, False)
        params = dict(collective_id=collective_id, has_side_effects=True)
    return pl.pallas_call(
        functools.partial(ffn_first_kernel, zs, count, linked),
        grid=(total // block,),
        in_specs=[anywhere if linked else tokens(D), tokens(D)] + [anywhere] * (2 * count + len(others)),
        out_specs=extra_specs + [tokens(n), tokens(2 * n)] + [anywhere] * 2,
        out_shape=extra_shapes
        + [shape((total, n), low), shape((total, 2 * n), low), shape((D, 2 * n), low), shape((n, D), low)],
        scratch_shapes=[
            pltpu.VMEM((D, 2 * n), low), pltpu.VMEM((n, D), low), pltpu.VMEM((D, 2 * n), full), pltpu.VMEM((n, D), full),
            sem((2, zs)),
        ] + extra_scratch,
        compiler_params=pltpu.CompilerParams(vmem_limit_bytes=60 * MIB, **params),
        cost_estimate=LONG,
    )(x, dy, *both_pieces, *down_pieces, *others)


def ffn_second(x, dy, hidden, d_both, one, two, zs, parts=(), collective_id=None):
    counts = (len(one[0]), len(two[0]))
    wides = [down[0].shape[0] * (zs if len(down) > 1 else 1) for _, down in (one, two)]
    n = wides[1]
    wide = -(-n // 128) * 128
    block, low, full = 256, jnp.bfloat16, jnp.float32
    sem, shape = pltpu.SemaphoreType.DMA, jax.ShapeDtypeStruct
    anywhere = pl.BlockSpec(memory_space=pl.ANY)

    def tokens(width):
        return pl.BlockSpec((block, width), lambda i: (i, 0))

    linked = bool(parts)
    extra = []
    if linked:
        held = pltpu.VMEM((2,) + parts[1].shape[1:], low)
        extra = [sem((2, 2)), held, held, sem((2 * zs - 2, 2)), sem((2,))]
    params = dict(collective_id=collective_id, has_side_effects=True) if linked else {}
    return pl.pallas_call(
        functools.partial(ffn_second_kernel, zs, counts, linked),
        grid=(x.shape[0] // block,),
        in_specs=[tokens(D)] * 2 + [tokens(wides[0]), tokens(2 * wides[0])] + [anywhere] * (2 * sum(counts) + len(parts)),
        out_specs=[tokens(D)] * 2 + [anywhere] * (2 + 2 * len(parts)),
        out_shape=[shape(x.shape, low)] * 2 + [shape((D, 2 * n), low), shape((n, D), low)]
        + [shape(part.shape[1:], low) for part in parts for _ in range(2)],
        scratch_shapes=[
            pltpu.VMEM((D, 2 * wides[0]), low), pltpu.VMEM((wides[0], D), low),
            pltpu.VMEM((D, 2 * wide), low), pltpu.VMEM((wide, D), low),
            pltpu.VMEM((D, 2 * wide), full), pltpu.VMEM((wide, D), full), pltpu.VMEM((D, 2 * n), low),
            sem((4, zs)),
        ] + extra,
        compiler_params=pltpu.CompilerParams(vmem_limit_bytes=56 * MIB, **params),
        cost_estimate=LONG,
    )(x, dy, hidden, d_both, *one[0], *one[1], *two[0], *two[1], *parts)


def split_unit(unit):
    return unit * 3 // 4 // 16 * 16


def portions(unit):
    first = split_unit(unit)
    return (0, first), (first, unit - first)


def gain_columns(one, two, rows):
    row = lax.broadcasted_iota(jnp.int32, (128, rows), 0)
    return jnp.where(row == 0, one, jnp.where(row == 1, two, 0.0)).T


def spread_kernel(zs, rows, unit, gate_ref, up_ref, query_ref, key_ref, value_ref, one_ref, two_ref, down_ref, *out):
    for (begin, size), ref in zip(portions(unit), out):
        for c in range(2):
            for r in range(rows):
                for n, weight in enumerate((gate_ref, up_ref)):
                    for z in range(zs):
                        at = ((z * 2 + c) * rows + r) * unit + begin
                        to = (n * zs + z) * size
                        ref[c, r, :, to : to + size] = weight[:, at : at + size]
    pack_ref, down_one, down_two = out[2:]
    pack_ref[:, :D] = query_ref[...]
    pack_ref[:, D : D + KVW] = key_ref[...]
    pack_ref[:, D + KVW : QKV] = value_ref[...]
    gains = gain_columns(one_ref[...].astype(jnp.float32), two_ref[...].astype(jnp.float32), pack_ref.shape[0])
    pack_ref[:, QKV:] = gains.astype(pack_ref.dtype)
    cut = down_one.shape[0]
    down_one[...] = down_ref[:cut, :]
    down_two[...] = down_ref[cut:, :]


def spread(gate, up, query, key, value, one, two, down, zs, rows):
    wide, part = gate.shape
    unit = part // (zs * 2 * rows)
    shape, low = jax.ShapeDtypeStruct, gate.dtype
    return pl.pallas_call(
        functools.partial(spread_kernel, zs, rows, unit),
        out_shape=[shape((2, rows, wide, 2 * zs * size), low) for _, size in portions(unit)]
        + [shape((wide, PACK), low)]
        + [shape((size, D), low) for _, size in portions(unit)],
    )(gate, up, query, key, value, one.reshape(1, -1), two.reshape(1, -1), down)


def collect_kernel(zs, rows, unit, *refs):
    given, (pack_ref, down_one, down_two), outs = refs[:2], refs[2:5], refs[5:]
    for n, out in enumerate(outs[:2]):
        for (begin, size), ref in zip(portions(unit), given):
            for c in range(2):
                for r in range(rows):
                    for z in range(zs):
                        at = ((z * 2 + c) * rows + r) * unit + begin
                        to = (n * zs + z) * size
                        out[:, at : at + size] = ref[c, r, :, to : to + size].astype(jnp.float32)
    key_ref, value_ref, one_ref, two_ref, down_ref = outs[2:]
    key_ref[...] = pack_ref[:, :KVW]
    value_ref[...] = pack_ref[:, KVW : 2 * KVW]
    gains = pack_ref[:, 2 * KVW :].T
    one_ref[...] = gains[0:1]
    two_ref[...] = gains[1:2]
    cut = down_one.shape[0]
    down_ref[:cut, :] = down_one[...]
    down_ref[cut:, :] = down_two[...]


def collect(blocks, pack, downs, zs, rows, unit):
    wide = blocks[0].shape[2]
    shape, full = jax.ShapeDtypeStruct, jnp.float32
    whole = shape((wide, unit * zs * 2 * rows), full)
    narrow = shape((wide, KVW), full)
    return pl.pallas_call(
        functools.partial(collect_kernel, zs, rows, unit),
        out_shape=[whole, whole, narrow, narrow, shape((1, wide), full), shape((1, wide), full), shape((unit, D), full)],
    )(*blocks, pack, *downs)


def forward_kernel(zs, micro, *refs):
    order_ref, places_ref, first_ref, freq_ref, x_ref, pack_ref, both_ref, down_ref, out_ref, dy_ref, rest_ref = refs[:11]
    refs = refs[1:]
    packed, both_own, kv_all, out_all, dy_all, rest_own = refs[10:16]
    steps = 2 * zs - 2
    both_got, down_got = refs[16 : 16 + steps], refs[16 + steps : 16 + 2 * steps]
    q_ref, attn_ref, attended_ref, ffn_own, middle_ref, gains_ref, cos_ref, sin_ref = refs[16 + 2 * steps : 24 + 2 * steps]
    (staged, lin, kv_own, kv_here, window, chosen, bias, out_w, sems, *more) = refs[24 + 2 * steps :]
    low = jnp.bfloat16
    z, c, r = place()
    many = x_ref.shape[0]
    span = many // micro
    half_len = span // 2
    rows = D // zs
    greet(neighbours(zs, True, True))

    exchange = Exchange(both_ref, both_own, *more[:3])
    rest = Exchange(rest_ref, rest_own, *more[3:6])
    more = more[:3] + more[6:]
    both_chain, down_chain = Chain(zs, both_own, both_got, more[3]), Chain(zs, down_ref, down_got, more[4])
    more = more[5:]
    weights = Gather(zs, True, True, pack_ref, packed, *more[:9])
    outs = Gather(zs, True, True, out_ref, out_all, *more[9:18])
    pairs = Gather(zs, True, False, kv_own, kv_all, *more[18:27])
    dys = Gather(zs, False, True, dy_ref, dy_all, *more[27:36])

    weights.launch()
    exchange.start()
    weights.begin(0)
    outs.launch()

    lane = lax.broadcasted_iota(jnp.int32, (half_len, 128), 1)
    for i in range(2 * micro):
        place_here = order_ref[(z * 2 + c) * 2 + i % 2] * half_len + lax.broadcasted_iota(jnp.int32, (half_len, 128), 0)
        start = jnp.where(place_here >= first_ref[i // 2, 0], first_ref[i // 2, 0], 0)
        angle = (place_here - start).astype(jnp.float32) * freq_ref[...]
        cos_ref[i * half_len : (i + 1) * half_len, :] = jnp.cos(angle)
        sine = jnp.sin(angle)
        sin_ref[i * half_len : (i + 1) * half_len, :] = jnp.where(lax.rem(lane, HEAD_DIM) < HEAD_DIM // 2, -sine, sine)
    x = x_ref[...].astype(jnp.float32)
    factor = rms_factor(x)
    wide = window.shape[0]
    half_blocks = wide // half_len
    for half in range(2):
        my_block = order_ref[(z * 2 + c) * 2 + half]
        chosen[half] = chosen_slots(places_ref[...], first_of(my_block, half_blocks), half_len, wide)

    loads = {}

    def load(n):
        weights.complete(n)
        zz = lax.rem(z - weights.kth[n] + zs, zs)
        loads[n] = pltpu.make_async_copy(packed.at[zz], staged.at[n % 2], sems.at[n % 2])
        loads[n].start()

    def project(n):
        loads[n].wait()
        zz = lax.rem(z - weights.kth[n] + zs, zs)
        at = pl.ds(pl.multiple_of(zz * rows, rows), rows)
        block = staged[n % 2].reshape(rows, PACK)
        gains = block[:, QKV:].astype(jnp.float32).T[:8]
        gains_ref[:, at] = gains
        attn_in = (x_ref[:, at].astype(jnp.float32) * factor * gains[0:1]).astype(low)
        attn_ref[:, at] = attn_in
        value = product(attn_in, block[:, :QKV])
        lin[...] = value if n == 0 else lin[...] + value

    weights.arrive(1)
    weights.begin(1)
    weights.forward(0)
    weights.arrive(2)
    weights.begin(2)
    weights.forward(1)
    weights.finish(0)
    weights.arrive(3)
    weights.begin(3)
    down_chain.start(1)
    exchange.finish()
    both_chain.start(1)
    outs.arrive(1)
    weights.forward(2)
    weights.finish(1)
    load(0)
    outs.arrive(2)
    weights.forward(3)
    weights.finish(2)
    outs.begin(0)
    load(1)
    project(0)
    outs.arrive(3)
    outs.begin(1)
    project(1)
    weights.finish(3)
    rest.start()
    dys.launch()
    dys.begin(0)
    load(2)
    load(3)
    project(2)
    project(3)

    width = GROUP * HEAD_DIM
    cosine = jnp.concatenate([cos_ref[...]] * (width // 128), axis=1)
    sine = jnp.concatenate([sin_ref[...]] * (width // 128), axis=1)

    def turned(block, w):
        return block * cosine[:, :w] + partner(block) * sine[:, :w]

    kv_own[:, :KVW] = turned(lin[:, D : D + KVW], KVW).astype(low)
    kv_own[:, KVW:] = lin[:, D + KVW :].astype(low)
    pairs.launch()
    pairs.begin(0)
    for g in range(KV_HEADS):
        at = slice(g * width, (g + 1) * width)
        q_ref[:, at] = turned(lin[:, at], width).astype(low) * low(HEAD_DIM ** -0.5)
    outs.forward(0)
    outs.begin(2)
    both_chain.finish()
    down_chain.finish()
    both_chain.start(2)
    down_chain.start(2)
    for k in range(1, zs):
        pairs.arrive(k)
        pairs.begin(k)
    outs.forward(1)
    outs.finish(0)
    outs.begin(3)
    for k in range(zs):
        pairs.complete(k)
    kv_load = pltpu.make_async_copy(kv_all, kv_here, sems.at[2])
    kv_load.start()
    outs.forward(2)
    outs.finish(1)
    kv_load.wait()

    def attend_some(i, carry):
        m, half = lax.div(i, 2), lax.rem(i, 2)
        my_block = order_ref[(z * 2 + c) * 2 + half]
        first_block = first_of(my_block, half_blocks)
        at = pl.ds(pl.multiple_of(m * span, span), span)
        window[...] = product(chosen[half], kv_here[:, :, at, :].reshape(2 * wide, 2 * KVW)).astype(low)
        key_place = first_block * half_len + lax.broadcasted_iota(jnp.int32, (half_len, wide), 1)
        place_here = my_block * half_len + lax.broadcasted_iota(jnp.int32, (half_len, wide), 0)
        first = first_ref[m, 0]
        start = jnp.where(place_here >= first, first, 0)
        bias[...] = jnp.where((key_place <= place_here) & (key_place >= start), 0.0, NEG_LARGE)
        here = pl.ds(pl.multiple_of(i * half_len, half_len), half_len)
        for g in range(KV_HEADS):
            at = slice(g * width, (g + 1) * width)
            key = window[:, g * HEAD_DIM : (g + 1) * HEAD_DIM]
            value = window[:, KVW + g * HEAD_DIM : KVW + (g + 1) * HEAD_DIM]
            scores = product_nt(stack_heads(q_ref[here, at], 0), key).reshape(GROUP, half_len, wide) + bias[...][None]
            exps = jnp.exp(scores - jnp.max(scores, axis=-1, keepdims=True))
            total = jnp.sum(exps, axis=-1, keepdims=True).reshape(GROUP * half_len, 1)
            mixed = product(exps.astype(low).reshape(GROUP * half_len, wide), value) / total
            attended_ref[here, at] = unstack_heads(mixed, half_len).astype(low)
        return carry

    lax.fori_loop(0, 2 * micro, attend_some, 0)
    outs.forward(3)
    outs.finish(2)
    outs.finish(3)
    dys.forward(0)
    for k in range(zs):
        outs.complete(k)
    out_load = pltpu.make_async_copy(out_all, out_w, sems.at[3])
    out_load.start()
    out_load.wait()
    middle = x_ref[...].astype(jnp.float32) + product(attended_ref[...], out_w[...].reshape(D, D))
    middle_ref[...] = middle
    ffn_own[...] = (middle * rms_factor(middle) * gains_ref[1:2, :]).astype(low)
    both_chain.finish()
    down_chain.finish()
    both_chain.start(3)
    down_chain.start(3)
    dys.finish(0)
    dys.complete(0)
    rest.finish()
    both_chain.finish()
    down_chain.finish()
    rest.end()
    exchange.end()
    for one in (weights, outs, pairs, dys):
        one.end()


def places_of(order, span):
    return (order[:, None] * (span // 2) + jnp.arange(span // 2, dtype=jnp.int32)).reshape(1, -1)


def forward(order, first, tokens, pack, both, rest, down, w_out, dy, zs, collective_id):
    many = tokens.shape[0]
    micro = first.shape[0]
    seq = 2 * zs
    wide = seq * (many // micro) // 2
    low, full = jnp.bfloat16, jnp.float32
    turns = np.arange(128) % (HEAD_DIM // 2) / (HEAD_DIM // 2)
    freq = jnp.asarray((10000.0 ** -turns).astype(np.float32))
    anywhere, here, smem = (pl.BlockSpec(memory_space=m) for m in (pl.ANY, pltpu.VMEM, pltpu.SMEM))
    shape = jax.ShapeDtypeStruct
    out_any = [
        shape((zs, 2, 4) + pack.shape, low),
        shape(both.shape, low),
        shape((zs, 2, many, 2 * KVW), low),
        shape((zs, 2, 4) + w_out.shape, low),
        shape((2, 4) + dy.shape, low),
        shape(rest.shape, low),
    ] + [shape(both.shape, low)] * (2 * zs - 2) + [shape(down.shape, low)] * (2 * zs - 2)
    out_here = [shape((many, D), t) for t in (low, low, low, low, full)] + [shape((8, D), full)] + [shape((many, 128), full)] * 2
    sem = pltpu.SemaphoreType.DMA
    found = pl.pallas_call(
        functools.partial(forward_kernel, zs, micro),
        out_shape=out_any + out_here,
        in_specs=[smem, here, smem] + [here] * 2 + [anywhere] * 6,
        out_specs=[anywhere] * len(out_any) + [here] * len(out_here),
        scratch_shapes=[
            pltpu.VMEM((2, 2, 4) + pack.shape, low),
            pltpu.VMEM((many, QKV), full),
            pltpu.VMEM((many, 2 * KVW), low),
            pltpu.VMEM((zs, 2, many, 2 * KVW), low),
            pltpu.VMEM((wide, 2 * KVW), low),
            pltpu.VMEM((2, wide, 2 * wide), low),
            pltpu.VMEM((many // micro // 2, wide), full),
            pltpu.VMEM((zs, 2, 4) + w_out.shape, low),
            sem((4,)),
        ] + EXCHANGE_SEMS * 2 + [sem((2 * zs - 2, 2))] * 2 + gather_sems(zs, True) * 3 + gather_sems(zs, False),
        compiler_params=pltpu.CompilerParams(
            collective_id=collective_id, has_side_effects=True, vmem_limit_bytes=56 * MIB
        ),
        cost_estimate=LONG,
    )(order, places_of(order, many // micro), first, freq.reshape(1, 128), tokens, pack, both, down, w_out, dy, rest)
    return found


def back_kernel(zs, micro, *refs):
    (order_ref, places_ref, first_ref, dy_ref, middle_ref, gains_ref, q_ref, cos_ref, sin_ref) = refs[:9]
    dx_part, out_part, both_part, down_part, out_all, kv_all, rest_part, last_part, *come = refs[9:21]
    result_ref, d_middle_ref, dq_ref, dkv_ref, gain_ref, down_ref, both_up, both_down, rest_in, last_in = refs[21:31]
    out_w, kv_here, d_heads, chosen, window, bias, d_places, sems, got, held, d_sems, dl_sem, *more = refs[31:]
    b_got, b_held, b_sems, bl_sem, r_sems, *more = more
    low, full = jnp.bfloat16, jnp.float32
    z, c, r = place()
    many = dy_ref.shape[0]
    span = many // micro
    half_len = span // 2
    greet(neighbours(zs, True, False))

    def take_d_ffn(at, value):
        d_middle_ref[at, :] = value

    def take_result(at, value):
        result_ref[at, :] = (middle_ref[at, :] + value).astype(low)

    scatters = {
        "dx": Scatter(1, False, True, dx_part, take_d_ffn, *more[:SCATTER_REFS]),
        "out": Scatter(1, False, True, out_part, take_result, *more[SCATTER_REFS : 2 * SCATTER_REFS]),
    }
    none = [None] * (zs - 3)
    down = SumChain(zs, down_part, [*none, got.at[0], got.at[1], *none, got.at[2], got.at[3]], held, d_sems, dl_sem)
    both = SumChain(
        zs, both_part, [b_got.at[0], both_up, *none, b_got.at[1], both_down, *none], b_held, b_sems, bl_sem
    )
    arounds = [
        Around(zs, lambda k: rest_part.at[lax.rem(z + k, zs)], rest_in, r_sems.at[0]),
        Around(zs, lambda k: last_part.at[lax.rem(z + k, zs)], last_in, r_sems.at[1]),
    ]
    comes = [
        pltpu.make_async_copy(src, dst, sems.at[2 + n])
        for n, (src, dst) in enumerate(zip(come, (b_got.at[0], b_got.at[1], got.at[0], got.at[2])))
    ]
    for copy in comes:
        copy.start()
    both.fetch(2)
    down.fetch(zs - 1)
    schedule = [(0, 3), (0, 1), (0, 2), (0, 0)]
    scatters["dx"].begin(schedule)
    for one in arounds:
        one.start()
    loads = [pltpu.make_async_copy(out_all, out_w, sems.at[0]), pltpu.make_async_copy(kv_all, kv_here, sems.at[1])]
    for load in loads:
        load.start()
    scatters["dx"].stage_a(0)
    for copy in comes:
        copy.wait()
    both.start(2)
    down.start(zs - 1)
    scatters["out"].begin(schedule)
    scatters["dx"].stage_b(0)
    scatters["out"].stage_a(0)
    scatters["dx"].stage_c(0)
    scatters["out"].stage_b(0)

    gain_ref[0:1, :] = jnp.zeros((1, D), full)

    def norm_some(i, carry):
        at = pl.ds(pl.multiple_of(i * half_len, half_len), half_len)
        middle, d_ffn = middle_ref[at, :], d_middle_ref[at, :]
        factor = rms_factor(middle)
        normed = middle * factor
        inner = d_ffn * gains_ref[1:2, :]
        d_norm = factor * (inner - normed * jnp.mean(inner * normed, axis=-1, keepdims=True))
        d_middle_ref[at, :] = dy_ref[at, :].astype(full) + d_norm
        gain_ref[0:1, :] += jnp.sum(d_ffn * normed, axis=0, keepdims=True)
        return carry

    lax.fori_loop(0, many // half_len, norm_some, 0)
    for load in loads:
        load.wait()
    d_heads[...] = product_nt(d_middle_ref[...].astype(low), out_w[...].reshape(D, D)).astype(low)

    wide = window.shape[0]
    half_blocks = wide // half_len
    width = GROUP * HEAD_DIM

    def attend_some(i, carry):
        m, half = lax.div(i, 2), lax.rem(i, 2)
        my_block = order_ref[(z * 2 + c) * 2 + half]
        first_block = jnp.where(my_block >= half_blocks, half_blocks, 0)
        wanted = first_block * half_len + lax.broadcasted_iota(jnp.int32, (wide, 2 * wide), 0)
        chosen[...] = jnp.where(places_ref[...] == wanted, 1.0, 0.0).astype(low)
        rows = pl.ds(pl.multiple_of(m * span, span), span)
        window[...] = product(chosen[...], kv_here[:, :, rows, :].reshape(2 * wide, 2 * KVW)).astype(low)
        key_place = first_block * half_len + lax.broadcasted_iota(jnp.int32, bias.shape, 0)
        place_here = my_block * half_len + lax.rem(lax.broadcasted_iota(jnp.int32, bias.shape, 1), half_len)
        first = first_ref[m, 0]
        start = jnp.where(place_here >= first, first, 0)
        bias[...] = jnp.where((key_place <= place_here) & (key_place >= start), 0.0, NEG_LARGE)
        here = pl.ds(pl.multiple_of(i * half_len, half_len), half_len)
        cosine = jnp.concatenate([cos_ref[here, :]] * (width // 128), axis=1)
        sine = jnp.concatenate([sin_ref[here, :]] * (width // 128), axis=1)
        d_keys, d_values = [], []
        for g in range(KV_HEADS):
            at = slice(g * width, (g + 1) * width)
            key = window[:, g * HEAD_DIM : (g + 1) * HEAD_DIM]
            value = window[:, KVW + g * HEAD_DIM : KVW + (g + 1) * HEAD_DIM]
            d_key, d_value, d_query = attend_back_heads(q_ref[here, at], d_heads[here, at], key, value, bias, half_len)
            d_keys.append(d_key)
            d_values.append(d_value)
            dq_ref[here, at] = (d_query * cosine - partner(d_query) * sine).astype(low)
        d_window = jnp.concatenate(d_keys + d_values, axis=1).astype(low)
        spread_back = product_tn(chosen[...], d_window)

        @pl.when(half == 0)
        def _():
            d_places[...] = spread_back

        @pl.when(half == 1)
        def _():
            both = (d_places[...] + spread_back).astype(low)
            dkv_ref[:, :, rows, :] = both.reshape(zs, 2, span, 2 * KVW)

        return carry

    lax.fori_loop(0, 2 * micro, attend_some, 0)
    scatters["out"].stage_c(0)
    both.finish()
    down.finish()
    down.total()
    down_ref[...] = held[0].astype(full)
    for one in arounds:
        one.finish()
    for one in scatters.values():
        one.end()


def back(order, first, dy, middle, gains, queries, cosine, sine, dx_part, out_part, both_part, down_part, out_all, kv_all,
         rest_part, last_part, come, zs, collective_id):
    many = dy.shape[0]
    micro = first.shape[0]
    span = many // micro
    wide = zs * span
    low, full = jnp.bfloat16, jnp.float32
    anywhere, here, smem = (pl.BlockSpec(memory_space=m) for m in (pl.ANY, pltpu.VMEM, pltpu.SMEM))
    shape, sem = jax.ShapeDtypeStruct, pltpu.SemaphoreType.DMA
    unit = down_part.shape[1]
    piece = shape(both_part.shape[1:], low)
    return pl.pallas_call(
        functools.partial(back_kernel, zs, micro),
        out_shape=[
            shape((many, D), low), shape((many, D), full), shape((many, D), low), shape(kv_all.shape, low),
            shape((8, D), full), shape((unit, D), full), piece, piece,
            shape((zs - 1,) + rest_part.shape[1:], low), shape((zs - 1,) + last_part.shape[1:], low),
        ],
        in_specs=[smem, here, smem] + [here] * 6 + [anywhere] * 12,
        out_specs=[here] * 6 + [anywhere] * 4,
        scratch_shapes=[
            pltpu.VMEM(out_all.shape, low),
            pltpu.VMEM(kv_all.shape, low),
            pltpu.VMEM((many, D), low),
            pltpu.VMEM((wide, 2 * wide), low),
            pltpu.VMEM((wide, 2 * KVW), low),
            pltpu.VMEM((wide, GROUP * span // 2), full),
            pltpu.VMEM((2 * wide, 2 * KVW), full),
            sem((6,)),
            pltpu.VMEM((4, unit, D), low),
            pltpu.VMEM((2, unit, D), low),
            sem((2 * zs - 2, 2)), sem((2,)),
            pltpu.VMEM((2,) + piece.shape, low),
            pltpu.VMEM((2,) + piece.shape, low),
            sem((2 * zs - 2, 2)), sem((2,)), sem((2, zs - 1, 2)),
        ] + scatter_scratch(1, True, many, D, True) * 2,
        compiler_params=pltpu.CompilerParams(
            collective_id=collective_id, has_side_effects=True, vmem_limit_bytes=62 * MIB
        ),
        cost_estimate=LONG,
    )(order, places_of(order, span), first, dy, middle, gains, queries, cosine, sine, dx_part, out_part, both_part, down_part,
      out_all, kv_all, rest_part, last_part, *come)


def products_kernel(attended_ref, attn_ref, d_middle_ref, dq_ref, packed_ref, out_ref, query_ref, d_attn_ref):
    low = jnp.bfloat16
    out_ref[...] = product_tn(attended_ref[...], d_middle_ref[...].astype(low)).astype(low)
    query_ref[...] = product_tn(attn_ref[...], dq_ref[...]).astype(low)
    d_attn_ref[...] = product_nt(dq_ref[...], packed_ref[...])


def products(attended, attn_in, d_middle, d_query, packed):
    many, block = attended.shape[0], 512
    low, shape = jnp.bfloat16, jax.ShapeDtypeStruct
    narrow = pl.BlockSpec((many, block), lambda i: (0, i))
    tall = pl.BlockSpec((block, D), lambda i: (i, 0))
    whole = pl.BlockSpec((many, D), lambda i: (0, 0))
    return pl.pallas_call(
        products_kernel,
        grid=(D // block,),
        in_specs=[narrow, narrow, whole, whole, tall],
        out_specs=[tall, tall, narrow],
        out_shape=[shape((D, D), low), shape((D, D), low), shape((many, D), jnp.float32)],
        compiler_params=pltpu.CompilerParams(vmem_limit_bytes=60 * MIB),
        cost_estimate=pl.CostEstimate(flops=6 * many * D * D, bytes_accessed=30 * MIB, transcendentals=0),
    )(attended, attn_in, d_middle, d_query, packed)


def weights_kernel(zs, *refs):
    x_ref, attn_ref, d_middle_ref, d_attn_ref, gains_ref, gain_two_ref, cos_ref, sin_ref, dkv_ref = refs[:9]
    packed, both_part, both_up, both_down, g_out, g_query, rest_part, last_part, rest_in, last_in = refs[9:19]
    x_grad_ref, out_ref, query_ref, pack_ref, last_ref, moved_ref, rest_ref = refs[19:26]
    kv_w, d_kv, pack_g, sems, got, held, b_sems, bl_sem, rest_here, last_here, *more = refs[26:]
    exchange_sems, rest_sems, more = more[:3], more[3:6], more[6:]
    z = place()[0]
    low, full = jnp.bfloat16, jnp.float32
    greet(neighbours(zs, True, True))

    def into(ref):
        def take(at, value):
            ref[at, :] = value

        return take

    def next_refs(staged):
        nonlocal more
        mine, more = more[:SCATTER_REFS], more[SCATTER_REFS:]
        return mine if staged else [None, *mine[1:]]

    pairs = Scatter(zs, True, False, dkv_ref, into(d_kv), *next_refs(False))
    scatters = {
        "out": Scatter(zs, True, True, g_out, into(out_ref), *next_refs(True)),
        "query": Scatter(zs, True, True, g_query, into(query_ref), *next_refs(True)),
        "pack": Scatter(zs, True, True, pack_g, into(pack_ref), *next_refs(False)),
    }
    items = [(name, k) for k in range(1, zs) for name in ("out", "query")]
    items[4:4] = [("pack", 1)]
    items += [("pack", k) for k in range(2, zs)] + [("out", 0), ("query", 0), ("pack", 0)]
    rounds, schedules = scatter_plan(items)

    none = [None] * (zs - 3)
    chain = SumChain(zs, both_part, [*none, got.at[0], got.at[1], *none, got.at[2], got.at[3]], held, b_sems, bl_sem)
    loads = [
        pltpu.make_async_copy(both_up, got.at[0], sems.at[0]),
        pltpu.make_async_copy(both_down, got.at[2], sems.at[1]),
        pltpu.make_async_copy(packed.at[:, :, :, :, pl.ds(D, 2 * KVW)], kv_w, sems.at[2]),
    ]
    for load in loads:
        load.start()
    small = [
        pltpu.make_async_copy(rest_part.at[z], rest_here.at[0], sems.at[3]),
        pltpu.make_async_copy(last_part.at[z], last_here.at[0], sems.at[4]),
        pltpu.make_async_copy(rest_in, rest_here.at[pl.ds(1, zs - 1)], sems.at[5]),
        pltpu.make_async_copy(last_in, last_here.at[pl.ds(1, zs - 1)], sems.at[6]),
    ]
    for load in small:
        load.start()
    chain.fetch(zs - 1)
    pairs.begin([])
    scatters["out"].begin(schedules["out"])
    scatters["query"].begin(schedules["query"])
    for k in range(1, zs):
        pairs.stage_c(k)
    for load in loads:
        load.wait()
    chain.start(zs - 1)
    for load in small:
        load.wait()
    last_ref[...] = sum(last_here[n].astype(full) for n in range(zs))
    rest_here[0] = sum(rest_here[n].astype(full) for n in range(zs)).astype(low)
    rest = Exchange(rest_here.at[0], rest_ref, *rest_sems)
    rest.start()

    def keys_and_norm():
        pairs.stage_c(0)
        lanes = KVW // 128
        cosine = jnp.concatenate([cos_ref[...]] * lanes, axis=1)
        sine = jnp.concatenate([sin_ref[...]] * lanes, axis=1)
        d_key = d_kv[:, :KVW]
        d_lin = jnp.concatenate([d_key * cosine - partner(d_key) * sine, d_kv[:, KVW:]], axis=1).astype(low)
        d_attn = d_attn_ref[...] + product_nt(d_lin, kv_w[...].reshape(D, 2 * KVW))
        x = x_ref[...].astype(full)
        factor = rms_factor(x)
        normed = x * factor
        inner = d_attn * gains_ref[0:1, :]
        d_x = factor * (inner - normed * jnp.mean(inner * normed, axis=-1, keepdims=True))
        x_grad_ref[...] = (d_middle_ref[...] + d_x).astype(low)
        gain_one = jnp.sum(d_attn * normed, axis=0, keepdims=True)
        rows = lax.broadcasted_iota(jnp.int32, (128, D), 0)
        both = jnp.where(rows == 0, gain_one, jnp.where(rows == 1, gain_two_ref[0:1, :], 0.0))
        pack = jnp.concatenate([product_tn(attn_ref[...], d_lin), both.T], axis=1).astype(low)
        pack_g[...] = pack.reshape(pack_g.shape)
        scatters["pack"].begin([])

    for n, stages in enumerate(rounds):
        if n == 3:
            keys_and_norm()
        if n == len(rounds) - 3:
            chain.finish()
            chain.total()
            exchange = Exchange(held.at[0], moved_ref, *exchange_sems)
            exchange.start()
        for stage in stages:
            run_stage(scatters, *stage)
    for one in (rest, exchange):
        one.finish()
        one.end()
    for one in (pairs, *scatters.values()):
        one.end()


def weight_sums(x, attn_in, d_middle, d_attn, gains, gain_two, cosine, sine, d_kv, packed, both_part, both_up, both_down, g_out,
                g_query, rest_part, last_part, rest_in, last_in, zs, collective_id):
    many = x.shape[0]
    low, full = jnp.bfloat16, jnp.float32
    anywhere, here = (pl.BlockSpec(memory_space=m) for m in (pl.ANY, pltpu.VMEM))
    shape, sem = jax.ShapeDtypeStruct, pltpu.SemaphoreType.DMA
    wide = packed.shape[3]
    narrow = 2 * KVW + 128
    block = both_part.shape[1:]
    return pl.pallas_call(
        functools.partial(weights_kernel, zs),
        out_shape=[
            shape((many, D), low), shape((wide, D), full), shape((wide, D), full), shape((wide, narrow), full),
            shape(last_part.shape[1:], full), shape(block, low), shape(rest_part.shape[1:], low),
        ],
        in_specs=[here] * 9 + [anywhere] * 10,
        out_specs=[here] * 5 + [anywhere] * 2,
        scratch_shapes=[
            pltpu.VMEM(packed.shape[:4] + (2 * KVW,), low),
            pltpu.VMEM((many, 2 * KVW), full),
            pltpu.VMEM((zs, 2, 4, wide, narrow), low),
            sem((7,)),
            pltpu.VMEM((4,) + block, low),
            pltpu.VMEM((2,) + block, low),
            sem((2 * zs - 2, 2)), sem((2,)),
            pltpu.VMEM(rest_part.shape, low),
            pltpu.VMEM(last_part.shape, low),
        ] + EXCHANGE_SEMS * 2
        + scatter_scratch(zs, False, many, 2 * KVW, False)
        + scatter_scratch(zs, True, wide, D, True) * 2
        + scatter_scratch(zs, True, wide, narrow, False),
        compiler_params=pltpu.CompilerParams(
            collective_id=collective_id, has_side_effects=True, vmem_limit_bytes=62 * MIB
        ),
        cost_estimate=LONG,
    )(x, attn_in, d_middle, d_attn, gains, gain_two, cosine, sine, d_kv, packed, both_part, both_up, both_down, g_out,
      g_query, rest_part, last_part, rest_in, last_in)


class Links:
    def __init__(self, seq, rows):
        self.zs, self.rows = seq // 2, rows
        self.kernels = rows == 4 and self.zs == 4
        self.z_groups = [[2 * z + c for z in range(self.zs)] for c in range(2)]
        self.core_groups = [[2 * z, 2 * z + 1] for z in range(self.zs)]

    def gather_z(self, block):
        return lax.all_gather(block, "seq", axis=0, tiled=True, axis_index_groups=self.z_groups)

    def scatter_z(self, blocks):
        return lax.psum_scatter(blocks, "seq", scatter_dimension=0, tiled=True, axis_index_groups=self.z_groups)

    def exchange_xla(self, blocks):
        moved = lax.all_to_all(blocks, "rows", split_axis=1, concat_axis=1, tiled=True)
        return lax.all_to_all(moved, "seq", split_axis=0, concat_axis=0, tiled=True, axis_index_groups=self.core_groups)

    def gather(self, array, z_flag, planes):
        if planes:
            array = lax.all_gather(array, "rows", axis=0)
        array = lax.all_gather(array, "seq", axis=0, axis_index_groups=self.core_groups)
        return self.gather_z(array[None]) if z_flag else array

    def scatter(self, blocks, z_flag, planes):
        blocks = self.scatter_z(blocks)[0] if z_flag else blocks
        blocks = lax.psum_scatter(blocks, "seq", scatter_dimension=0, tiled=True, axis_index_groups=self.core_groups)[0]
        if planes:
            blocks = lax.psum_scatter(blocks, "rows", scatter_dimension=0, tiled=True)[0]
        return blocks.astype(jnp.float32)


def on_device(seq, rows, tokens, w_query, w_key, w_value, w_out, w_gate, w_up, w_down, gain_attn, gain_ffn, lengths, order, cotangent):
    links = Links(seq, rows)
    zs = links.zs
    micro, _, span, _ = tokens.shape
    half_len = span // 2
    many = micro * span
    low = jnp.bfloat16
    wide = w_gate.shape[0]
    unit = w_down.shape[0]

    both, rest, pack, down_own, last_own = spread(
        w_gate, w_up, w_query, w_key, w_value, gain_attn, gain_ffn, w_down, zs, rows
    )
    cut = split_unit(unit)
    flat, flat_rest = (2 * rows * wide, 2 * zs * cut), (2 * rows * wide, 2 * zs * (unit - cut))
    dy_own = cotangent.reshape(many, D)
    own_tokens = tokens.reshape(many, D)
    x = own_tokens.astype(jnp.float32)
    first = lengths[:, 0, 0]
    slot_of = jnp.argmax(order[None, :] == jnp.arange(order.shape[0], dtype=jnp.int32)[:, None], axis=1).astype(jnp.int32)
    chained = links.kernels
    if chained:
        found = forward(order, lengths[:, 0], own_tokens, pack, both, rest, down_own, w_out, dy_own, zs, 0)
        packed, both_own, kv, out_w, dy, rest_own = found[:6]
        both_w = [b.reshape(flat) for b in (both_own, *found[6 : 4 + 2 * zs])]
        down_w = [down_own, *found[4 + 2 * zs : 2 + 4 * zs]]
        rest_own = rest_own.reshape(flat_rest)
        queries, attn_in, attended, ffn_in, middle, gains, cosine, sine = found[2 + 4 * zs :]
        packed = packed.reshape(D, PACK)
    else:
        both_w = [links.gather_z(links.exchange_xla(both).reshape(flat))]
        rest_w = [links.gather_z(links.exchange_xla(rest).reshape(flat_rest))]
        down_w, last_w = [links.gather_z(down_own)], [links.gather_z(last_own)]
        packed, dy = links.gather(pack, True, True).reshape(D, PACK), links.gather(dy_own, False, True)
        gain_one, gain_two = packed[:, QKV].astype(jnp.float32), packed[:, QKV + 1].astype(jnp.float32)
        mine = slot_places(order, half_len, lax.axis_index("seq") * span + jnp.arange(span, dtype=jnp.int32))
        start = jnp.where(mine[None, :] >= first[:, None], first[:, None], 0)
        inverse = 10000.0 ** (-jnp.arange(HEAD_DIM // 2, dtype=jnp.float32) / (HEAD_DIM // 2))
        angles = ((mine[None, :] - start).astype(jnp.float32)[..., None] * inverse).reshape(many, HEAD_DIM // 2)
        cosine, sine = jnp.cos(angles), jnp.sin(angles)
        cosine, sine = jnp.tile(cosine, (1, 4)), jnp.tile(jnp.concatenate([-sine, sine], axis=1), (1, 2))
        attn_in = (x * rms_factor(x) * gain_one).astype(low)
        lin = product(attn_in, packed)
        kv_own = jnp.concatenate([turn(lin[:, D : D + KVW], cosine, sine), lin[:, D + KVW : QKV]], axis=1).astype(low)
        kv, out_w = links.gather(kv_own, True, False), links.gather(w_out, True, True)
        queries, attended = attend(order, slot_of, first, lin, cosine, sine, kv.reshape(seq, many, 2 * KVW))
        middle = x + product(attended, out_w.reshape(D, D))
        ffn_in = links.gather((middle * rms_factor(middle) * gain_two).astype(low), False, True).reshape(2 * rows * many, D)
    kv = kv.reshape(seq, many, 2 * KVW)
    out_w = out_w.reshape(D, D)
    dy = dy.reshape(2 * rows * many, D)

    shards = (zs, 2, rows, wide)
    if chained:
        ffn_in, rest_got, last_got, hidden, d_both, grad_both, grad_down = ffn_first(
            ffn_in, dy, both_w, down_w, zs, (rest_own, last_own), 1
        )
        rest_w, last_w = [rest_own, rest_got], [last_own, last_got]
        grad_both, grad_down = grad_both.reshape(*shards, 2 * zs * cut), grad_down.reshape(zs, cut, D)
        result_part, d_ffn_part, grad_rest, grad_last, *come = ffn_second(
            ffn_in, dy, hidden, d_both, (both_w, down_w), (rest_w, last_w), zs, (grad_both, grad_down), 2
        )
    else:
        hidden, d_both, grad_both, grad_down = ffn_first(ffn_in, dy, both_w, down_w, zs)
        grad_both, grad_down = grad_both.reshape(*shards, 2 * zs * cut), grad_down.reshape(zs, cut, D)
        result_part, d_ffn_part, grad_rest, grad_last = ffn_second(
            ffn_in, dy, hidden, d_both, (both_w, down_w), (rest_w, last_w), zs
        )
    grad_rest, grad_last = grad_rest.reshape(*shards, 2 * zs * (unit - cut)), grad_last.reshape(zs, unit - cut, D)
    d_ffn_part, result_part = (part.reshape(2, rows, many, D) for part in (d_ffn_part, result_part))
    if chained:
        out_all, kv_all = out_w.reshape(*shards, D), kv.reshape(zs, 2, many, 2 * KVW)
        result, d_middle, d_query, d_kv, gain_two_grad, grad_down, both_up, both_down, rest_in, last_in = back(
            order, lengths[:, 0], dy_own, middle, gains, queries, cosine, sine, d_ffn_part, result_part, grad_both, grad_down,
            out_all, kv_all, grad_rest, grad_last, come, zs, 3,
        )
        grad_out, grad_query, d_attn = products(attended, attn_in, d_middle, d_query, packed)
        grad_out, grad_query = grad_out.reshape(*shards, D), grad_query.reshape(*shards, D)
        x_grad, grad_out, grad_query, pack_grad, grad_last, grad_both, grad_rest = weight_sums(
            own_tokens, attn_in, d_middle, d_attn, gains, gain_two_grad, cosine, sine, d_kv, packed.reshape(*shards, PACK),
            grad_both, both_up, both_down, grad_out, grad_query, grad_rest, grad_last, rest_in, last_in, zs, 4,
        )
    else:
        d_ffn_in = links.scatter(d_ffn_part, False, True)
        result = (middle + links.scatter(result_part, False, True)).astype(low)
        grad_both, grad_rest = (links.exchange_xla(links.scatter_z(grad)[0]) for grad in (grad_both, grad_rest))
        grad_down, grad_last = (links.scatter_z(grad)[0].astype(jnp.float32) for grad in (grad_down, grad_last))
        factor_two = rms_factor(middle)
        d_part, grad_gain_two = norm_back(d_ffn_in, middle * factor_two, factor_two, gain_two)
        d_middle = dy_own.astype(jnp.float32) + d_part
        d_mid_low = d_middle.astype(low)
        grad_out = links.scatter(product_tn(attended, d_mid_low).astype(low).reshape(*shards, D), True, True)
        d_heads = product_nt(d_mid_low, out_w).astype(low)
        d_query, d_kv = attend_back(order, slot_of, first, queries, d_heads, cosine, sine, kv)
        grad_query = links.scatter(product_tn(attn_in, d_query).astype(low).reshape(*shards, D), True, True)
        d_kv = links.scatter(d_kv.reshape(zs, 2, many, 2 * KVW), True, False)
        d_key = turn(d_kv[:, :KVW], cosine, -sine)
        d_kv = jnp.concatenate([d_key.astype(low), d_kv[:, KVW:].astype(low)], axis=1)
        d_attn_in = product_nt(d_query, packed[:, :D]) + product_nt(d_kv, packed[:, D:QKV])
        factor_one = rms_factor(x)
        d_x, grad_gain_one = norm_back(d_attn_in, x * factor_one, factor_one, gain_one)
        x_grad = (d_middle + d_x).astype(low)
        gains_grad = jnp.pad(jnp.stack([grad_gain_one, grad_gain_two], axis=1), ((0, 0), (0, 126)))
        pack_grad = jnp.concatenate([product_tn(attn_in, d_kv), gains_grad], axis=1).astype(low)
        pack_grad = links.scatter(pack_grad.reshape(*shards, 2 * KVW + 128), True, True)
    grad_gate, grad_up, grad_key, grad_value, grad_one, grad_two, grad_down = collect(
        (grad_both, grad_rest), pack_grad, (grad_down, grad_last), zs, rows, unit
    )
    return (
        result.reshape(tokens.shape),
        x_grad.reshape(tokens.shape),
        grad_query,
        grad_key,
        grad_value,
        grad_out,
        grad_gate,
        grad_up,
        grad_down,
        grad_one.reshape(-1),
        grad_two.reshape(-1),
    )


def solution(mesh):
    both = ("seq", "rows")
    row = P(None, "rows", "seq", None)
    weight, gain = P(both, None), P(both)
    return jax.shard_map(
        functools.partial(on_device, mesh.shape["seq"], mesh.shape["rows"]),
        mesh=mesh,
        in_specs=(row,) + (weight,) * 7 + (gain, gain, P(None, "rows", None), P(), row),
        out_specs=(row, row) + (weight,) * 7 + (gain, gain),
        check_vma=False,
    )
```

```python
import functools

import jax
import jax.numpy as jnp
import numpy as np
from jax import lax
from jax.experimental import pallas as pl
from jax.experimental.pallas import tpu as pltpu
from jax.sharding import PartitionSpec as P

D = 2048
HEADS = 32
KV_HEADS = 4
HEAD_DIM = 64
GROUP = 8
KVW = 256
QKV = D + 2 * KVW
PACK = QKV + 128

EPSILON = 1e-05
NEG_LARGE = -1e30
MESH = pl.DeviceIdType.MESH
MIB = 1 << 20
LONG = pl.CostEstimate(flops=50_000_000_000, bytes_accessed=150 * MIB, transcendentals=0)


def product(left, right):
    return jnp.dot(left, right, preferred_element_type=jnp.float32)


def product_nt(left, right):
    return lax.dot_general(left, right, (((1,), (1,)), ((), ())), preferred_element_type=jnp.float32)


def product_tn(left, right):
    return lax.dot_general(left, right, (((0,), (0,)), ((), ())), preferred_element_type=jnp.float32)


def rms_factor(values):
    return lax.rsqrt(jnp.mean(values * values, axis=-1, keepdims=True) + EPSILON)


def norm_back(d_scaled, normed, factor, gain):
    inner = d_scaled * gain
    mean = jnp.mean(inner * normed, axis=-1, keepdims=True)
    return factor * (inner - normed * mean), jnp.sum(d_scaled * normed, axis=0)


def turn(tensor, cosine, sine):
    rows, lanes = tensor.shape
    half = HEAD_DIM // 2
    swapped = jnp.flip(tensor.reshape(rows, lanes // HEAD_DIM, 2, half), axis=2).reshape(rows, lanes)
    return tensor * jnp.tile(cosine, (1, lanes // 128)) + swapped * jnp.tile(sine, (1, lanes // 128))


def slot_places(order, half_len, slot_ids):
    matches = (slot_ids // half_len)[:, None] == jnp.arange(order.shape[0], dtype=jnp.int32)[None, :]
    return jnp.sum(jnp.where(matches, order[None, :], 0), axis=1) * half_len + slot_ids % half_len


def place():
    s, r = lax.axis_index("seq"), lax.axis_index("rows")
    return lax.div(s, 2), lax.rem(s, 2), r


def send(src, dst, ssem, rsem, device):
    return pltpu.make_async_remote_copy(
        src_ref=src, dst_ref=dst, send_sem=ssem, recv_sem=rsem, device_id=device, device_id_type=MESH
    )


def greet(devices):
    barrier = pltpu.get_barrier_semaphore()
    for device in devices:
        pl.semaphore_signal(barrier, inc=1, device_id=device, device_id_type=MESH)
    pl.semaphore_wait(barrier, len(devices))


def corners(r):
    return r, r + 1 - 2 * lax.rem(r, 2), lax.rem(r + 2, 4), 3 - r


def exchange_others():
    return [(cc, j) for j in (3, 1, 2, 0) for cc in range(2) if (cc, j) != (0, 0)]


class Exchange:
    def __init__(self, own, out, ssem, rsem, l_sem):
        z, c, r = place()
        line = corners(r)
        self.own, self.out, self.ssem, self.rsem, self.here = own, out, ssem, rsem, (c, r)
        self.others = [(1 - c if cc else c, line[j]) for cc, j in exchange_others()]
        self.devices = [(z * 2 + core, row) for core, row in self.others]
        self.local = pltpu.make_async_copy(own.at[c, r], out.at[c, r], l_sem)

    def start(self):
        self.copies = []
        for i, other in enumerate(self.others):
            copy = send(self.own.at[other], self.out.at[self.here], self.ssem.at[i], self.rsem.at[i], self.devices[i])
            copy.start()
            self.copies.append(copy)
        self.local.start()

    def finish(self):
        for i, other in enumerate(self.others):
            dst = self.out.at[other]
            send(dst, dst, self.ssem.at[i], self.rsem.at[i], self.devices[i]).wait_recv()
        self.local.wait()

    def end(self):
        for copy in self.copies:
            copy.wait_send()


class Line:
    def __init__(self, zs, way, lo, hi, src, dst, sems):
        z, c, r = place()
        lo, hi = (lo, min(hi, zs - 1)) if way == 1 else (max(lo, 1), hi)
        self.sends = (z >= lo) & (z < hi)
        self.gets = (z - way >= lo) & (z - way < hi)
        to = lax.rem(z + way + zs, zs)
        self.copy = send(src, dst, sems.at[0], sems.at[1], (to * 2 + c, r))

    def start(self):
        pl.when(self.sends)(self.copy.start)

    def finish(self):
        pl.when(self.sends)(self.copy.wait_send)
        pl.when(self.gets)(self.copy.wait_recv)


LINE_SEMS = pltpu.SemaphoreType.DMA((2,))
EXCHANGE_SEMS = [pltpu.SemaphoreType.DMA((7,)), pltpu.SemaphoreType.DMA((7,)), pltpu.SemaphoreType.DMA]


def neighbours(zs, planes, moved):
    z, c, r = place()
    line = corners(r)
    s = z * 2 + c
    devices = [(z * 2 + 1 - c, r)]
    if moved:
        devices = [(z * 2 + (1 - c if cc else c), line[j]) for cc, j in exchange_others()]
    elif planes:
        devices += [(s, line[1]), (s, line[2])]
    return devices + [(lax.rem(z + k, zs) * 2 + c, r) for k in range(1, zs)]


class Gather:
    def __init__(self, zs, z_flag, planes, own, out, z_ssem, z_rsem, f_ssem, f_rsem, h_ssem, h_rsem, c_ssem, c_rsem, l_sem):
        self.__dict__.update(locals())
        self.z, self.c, self.r = place()
        self.line = corners(self.r)
        self.s = self.z * 2 + self.c
        self.twin = (self.z * 2 + 1 - self.c, self.r)
        self.count = zs if z_flag else 1
        self.half = own.shape[0] // 2
        self.pending = []
        self.sent = []
        z = self.z
        self.kth = [0, jnp.where(z == 0, 3, 1), jnp.where((z == 0) | (z == 3), 2, 3), jnp.where(z == 0, 1, jnp.where(z == 3, 3, 2))]

    def start(self, copy):
        copy.start()
        self.pending.append(copy.wait_send)

    def slot(self, k, other, j):
        if not self.z_flag:
            return self.out.at[other, j]
        core = 1 - self.c if other else self.c
        zz = lax.rem(self.z - k + self.zs, self.zs)
        return self.out.at[zz, core, self.line[j]] if self.planes else self.out.at[zz, core]

    def z_copy(self, n, way, k, src, dst):
        to = (lax.rem(self.z + way + self.zs, self.zs) * 2 + self.c, self.r)
        return send(src, dst, self.z_ssem.at[n, 0 if way == 1 else 1], self.z_rsem.at[k], to)

    def hand_on(self, n, src, dst):
        z, k, zs = self.z, self.kth[n], self.zs
        up, down = (z < zs - 1, z > 0) if n == 0 else ((z >= k) & (z < zs - 1), (z < k) & (z > 0))
        for way, goes, step in ((1, up, 1), (-1, down, zs - 1)):
            copy = self.z_copy(n, way, lax.rem(k + step, zs), src, dst)
            pl.when(goes)(copy.start)
            self.sent.append((goes, copy))

    def near(self, k, j, src):
        dst = self.slot(k, 0, j) if src is None or not self.z_flag else self.slot(k, 0, 0)
        return send(dst if src is None else src, dst, self.f_ssem.at[k, j - 1], self.f_rsem.at[k, j - 1], (self.s, self.line[j]))

    def part(self, ref, j):
        return ref.at[pl.ds(self.half if j == 1 else 0, self.half)]

    def far(self, k, j, src):
        if src is None:
            src = dst = self.part(self.slot(k, 0, 3), j)
        else:
            dst = self.part(src if self.z_flag else self.out.at[0, 3], j)
            src = self.part(src, j)
        return send(src, dst, self.h_ssem.at[k, j - 1], self.h_rsem.at[k, j - 1], (self.s, self.line[3 - j]))

    def twin_copy(self, k, j, src):
        dst = self.slot(k, 0, j) if self.z_flag else self.out.at[1, j]
        return send(src, dst, self.c_ssem.at[k, j], self.c_rsem.at[k, j], self.twin)

    def to_twin(self, k, j, src):
        self.start(self.twin_copy(k, j, src))

    def from_twin(self, k, j):
        dst = self.slot(k, 1, j)
        send(dst, dst, self.c_ssem.at[k, j], self.c_rsem.at[k, j], self.twin).wait_recv()

    def launch(self):
        self.local = pltpu.make_async_copy(self.own, self.slot(0, 0, 0), self.l_sem)
        self.local.start()
        if self.count > 1 and self.planes:
            self.hand_on(0, self.own, self.slot(0, 0, 0))
        elif self.count > 1:
            for k in range(1, self.count):
                self.start(self.z_copy(k, k, k, self.own, self.slot(0, 0, 0)))

    def arrive(self, n):
        k = self.kth[n]
        src = self.slot(k, 0, 0)
        self.z_copy(n, 1, k, src, src).wait_recv()
        if self.planes:
            self.hand_on(n, src, src)

    def begin(self, n):
        k = self.kth[n]
        src = self.slot(k, 0, 0) if n else self.own
        if self.planes:
            for j in (1, 2):
                self.start(self.near(k, j, src))
        self.to_twin(k, 0, src)

    def forward(self, n):
        k = self.kth[n]
        for j in (1, 2):
            self.near(k, j, None).wait_recv()
            src = self.slot(k, 0, j)
            self.start(self.far(k, j, src))
            self.to_twin(k, j, src)

    def finish(self, n):
        k = self.kth[n]
        for j in (1, 2):
            self.far(k, j, None).wait_recv()
        self.to_twin(k, 3, self.slot(k, 0, 3))

    def complete(self, n):
        k = self.kth[n]
        if n == 0:
            self.local.wait()
        for j in range(4 if self.planes else 1):
            self.from_twin(k, j)

    def sent_all(self):
        for j in (1, 2):
            self.near(0, j, self.own).wait_send()
            self.far(0, j, self.slot(0, 0, j)).wait_send()
        for j in range(4):
            self.twin_copy(0, j, self.slot(0, 0, j) if j else self.own).wait_send()

    def end(self):
        for goes, copy in self.sent:
            pl.when(goes)(copy.wait_send)
        for wait in self.pending:
            wait()


def gather_sems(zs, z_flag):
    sem = pltpu.SemaphoreType.DMA
    n = zs if z_flag else 1
    return [sem((n, 2)), sem((n,)), sem((n, 2)), sem((n, 2)), sem((n, 2)), sem((n, 2)), sem((n, 4)), sem((n, 4)), sem]


class Chain:
    def __init__(self, zs, own, got, sems):
        self.zs, self.own, self.got, self.sems = zs, own, got, sems
        self.lines = []

    def start(self, k):
        zs = self.zs
        up, down = (self.own, self.own) if k == 1 else (self.got[k - 2], self.got[zs + k - 3])
        self.lines = [
            Line(zs, 1, k - 1, zs, up, self.got[k - 1], self.sems.at[k - 1]),
            Line(zs, -1, 0, zs - k + 1, down, self.got[zs + k - 2], self.sems.at[zs + k - 2]),
        ]
        for line in self.lines:
            line.start()

    def finish(self):
        for line in self.lines:
            line.finish()


class Scatter:
    def __init__(self, zs, z_flag, planes, given, final, stage, twin_in, half_in, full_in, z_in, l_sem, c_ssem, c_rsem, h_ssem,
                 h_rsem, f_ssem, f_rsem, z_ssem, z_rsem):
        self.__dict__.update(locals())
        self.z, self.c, self.r = place()
        self.line = corners(self.r)
        self.s = self.z * 2 + self.c
        self.twin = (self.z * 2 + 1 - self.c, self.r)
        self.rows = twin_in.shape[2]
        self.step = 16
        self.spots = (3, 1, 2, 0) if planes else (0,)
        self.zs = zs if z_flag else 1
        self.order = list(range(1, self.zs)) + [0]
        self.pending = []
        self.loads = []
        self.settled = 0

    def at_z(self, k):
        return (lax.rem(self.z + k, self.zs) * 2 + self.c, self.r)

    def block(self, k, other, j):
        if not self.z_flag:
            return self.given.at[other, j]
        zz, core = lax.rem(self.z + k, self.zs), 1 - self.c if other else self.c
        return self.given.at[zz, core, self.line[j]] if self.planes else self.given.at[zz, core]

    def start(self, copy):
        copy.start()
        self.pending.append(copy.wait_send)

    def begin(self, schedule):
        for k in self.order:
            for j in self.spots:
                self.start(self.twin_copy(k, j, self.block(k, 1, j)))
        if self.stage is not None:
            self.loads = [
                pltpu.make_async_copy(self.block(k, 0, j), self.stage.at[n % 2], self.l_sem.at[n % 2])
                for n, (k, j) in enumerate(schedule)
            ]
            for load in self.loads[:2]:
                load.start()

    def twin_copy(self, k, j, src):
        dst = self.twin_in.at[k, j]
        return send(dst if src is None else src, dst, self.c_ssem.at[k, j], self.c_rsem.at[k, j], self.twin)

    def settle(self, k, j, parts):
        own = self.block(k, 0, j)
        n = self.settled
        if self.stage is not None:
            self.loads[n].wait()
            own = self.stage.at[n % 2]
        self.twin_copy(k, j, None).wait_recv()
        step = self.step
        for first, last, more in parts:

            def body(i, carry, first=first, more=more):
                at = pl.ds(pl.multiple_of(first + i * step, step), step)
                value = own[at, :].astype(jnp.float32) + self.twin_in[k, j, at, :].astype(jnp.float32)
                for ref, offset in more:
                    there = pl.ds(pl.multiple_of(first - offset + i * step, step), step)
                    value = value + ref[there, :].astype(jnp.float32)
                if k == 0 and j == 0:
                    self.final(at, value)
                else:
                    self.twin_in[k, j, at, :] = value.astype(self.twin_in.dtype)
                return carry

            lax.fori_loop(0, (last - first) // step, body, 0)
        if n + 2 < len(self.loads):
            self.loads[n + 2].start()
        self.settled = n + 1

    def half_copy(self, k, n, src):
        dst = self.half_in.at[k, n]
        return send(dst if src is None else src, dst, self.h_ssem.at[k, n], self.h_rsem.at[k, n], (self.s, self.line[n + 1]))

    def full_copy(self, k, j, src):
        dst = self.full_in.at[k, j - 1]
        return send(dst if src is None else src, dst, self.f_ssem.at[k, j - 1], self.f_rsem.at[k, j - 1], (self.s, self.line[j]))

    def z_copy(self, k, src):
        dst = self.z_in.at[k]
        return send(dst if src is None else src, dst, self.z_ssem.at[k], self.z_rsem.at[k], self.at_z(k))

    def stage_a(self, k):
        half = self.rows // 2
        self.settle(k, 3, [(0, self.rows, [])])
        self.start(self.half_copy(k, 1, self.twin_in.at[k, 3, pl.ds(half, half)]))
        self.start(self.half_copy(k, 0, self.twin_in.at[k, 3, pl.ds(0, half)]))

    def stage_b(self, k):
        half = self.rows // 2
        for j in (1, 2):
            n = 2 - j
            self.half_copy(k, n, None).wait_recv()
            more = [(self.half_in.at[k, n], half if n else 0)]
            self.settle(k, j, [(0, half, [] if n else more), (half, self.rows, more if n else [])])
            self.start(self.full_copy(k, j, self.twin_in.at[k, j]))

    def stage_c(self, k):
        more = []
        if self.planes:
            for j in (1, 2):
                self.full_copy(k, j, None).wait_recv()
                more.append((self.full_in.at[k, j - 1], 0))
        if not k:
            for other in range(1, self.zs):
                self.z_copy(other, None).wait_recv()
                more.append((self.z_in.at[other], 0))
        self.settle(k, 0, [(0, self.rows, more)])
        if k:
            self.start(self.z_copy(k, self.twin_in.at[k, 0]))

    def end(self):
        for wait in self.pending:
            wait()


def scatter_scratch(zs, planes, rows, columns, staged):
    sem = pltpu.SemaphoreType.DMA
    low, least = jnp.bfloat16, (1, 2, 16, 128)
    spots = 4 if planes else 1
    return [
        pltpu.VMEM((2, rows, columns) if staged else (16, 128), low),
        pltpu.VMEM((zs, spots, rows, columns), low),
        pltpu.VMEM((zs, 2, rows // 2, columns) if planes else least, low),
        pltpu.VMEM((zs, 2, rows, columns) if planes else least, low),
        pltpu.VMEM((zs, rows, columns) if zs > 1 else least[1:], low),
        sem((2,)), sem((zs, 4)), sem((zs, 4)), sem((zs, 2)), sem((zs, 2)), sem((zs, 2)), sem((zs, 2)), sem((zs,)), sem((zs,)),
    ]


SCATTER_REFS = 14


def scatter_plan(items):
    rounds = []
    for n in range(len(items) + 2):
        rounds.append([])
        for back, stage in enumerate(("a", "b", "c")):
            if 0 <= n - back < len(items):
                name, k = items[n - back]
                if stage != "c" or k:
                    rounds[-1].append((name, stage, k))
    rounds.append([(name, "c", 0) for name, k in items if not k])
    places = {"a": (3,), "b": (1, 2), "c": (0,)}
    schedules = {}
    for name, stage, k in sum(rounds, []):
        schedules.setdefault(name, []).extend((k, j) for j in places[stage])
    return rounds, schedules


def run_stage(scatters, name, stage, k):
    {"a": Scatter.stage_a, "b": Scatter.stage_b, "c": Scatter.stage_c}[stage](scatters[name], k)


class SumChain:
    def __init__(self, zs, parts, got, held, sems, l_sem):
        self.__dict__.update(locals())
        self.z = place()[0]

    def own(self, to):
        return self.parts.at[lax.rem(self.z + to + self.zs, self.zs)]

    def fetch(self, k):
        self.loads = [
            pltpu.make_async_copy(self.own(-k), self.held.at[0], self.l_sem.at[0]),
            pltpu.make_async_copy(self.own(k), self.held.at[1], self.l_sem.at[1]),
        ]
        for load in self.loads:
            load.start()

    def add(self, into, more):
        ref = self.got[into]
        ref[...] = (ref[...].astype(jnp.float32) + self.held[more].astype(jnp.float32)).astype(ref.dtype)

    def lines_of(self, k):
        zs, got = self.zs, self.got
        up, down = k - 1, zs - 2 + k
        lines = [
            Line(zs, 1, 0, 1, self.own(-k), got[up], self.sems.at[up]),
            Line(zs, -1, zs - 1, zs, self.own(k), got[down], self.sems.at[down]),
        ]
        if k > 1:
            lines += [
                Line(zs, 1, 1, k, got[up - 1], got[up], self.sems.at[up]),
                Line(zs, -1, zs - k, zs - 1, got[down - 1], got[down], self.sems.at[down]),
            ]
        return lines

    def start(self, k):
        zs, z = self.zs, self.z
        up, down = k - 1, zs - 2 + k
        if k > 1:
            for load in self.loads:
                load.wait()
            pl.when((z >= 1) & (z < k))(functools.partial(self.add, up - 1, 0))
            pl.when((z >= zs - k) & (z < zs - 1))(functools.partial(self.add, down - 1, 1))
        self.lines = self.lines_of(k)
        for line in self.lines:
            line.start()
        if k == zs - 1:
            self.loads = [pltpu.make_async_copy(self.own(0), self.held.at[0], self.l_sem.at[0])]
            self.loads[0].start()

    def finish(self, k=None):
        for line in self.lines if k is None else self.lines_of(k):
            line.finish()

    def total(self):
        zs, z = self.zs, self.z
        self.loads[0].wait()

        def add(come):
            self.held[0] = (self.held[0].astype(jnp.float32) + self.got[come][...].astype(jnp.float32)).astype(self.held.dtype)

        pl.when(z > 0)(functools.partial(add, zs - 2))
        pl.when(z < zs - 1)(functools.partial(add, 2 * zs - 3))


def partner(tensor):
    lanes = tensor.shape[-1]
    half = HEAD_DIM // 2
    lane = lax.broadcasted_iota(jnp.int32, tensor.shape, tensor.ndim - 1)
    ahead = pltpu.roll(tensor, lanes - half, tensor.ndim - 1)
    behind = pltpu.roll(tensor, half, tensor.ndim - 1)
    return jnp.where(lax.rem(lane, HEAD_DIM) < half, ahead, behind)


def first_of(my_block, half_blocks):
    return jnp.where(my_block >= half_blocks, half_blocks, 0)


def chosen_slots(places, first_block, half_len, wide):
    wanted = first_block * half_len + lax.broadcasted_iota(jnp.int32, (wide, 2 * wide), 0)
    return jnp.where(places == wanted, 1.0, 0.0).astype(jnp.bfloat16)


def stack_heads(block, first):
    return jnp.concatenate(
        [block[:, (first + h) * HEAD_DIM : (first + h + 1) * HEAD_DIM] for h in range(GROUP)], axis=0
    )


def unstack_heads(stacked, span):
    return jnp.concatenate([stacked[h * span : (h + 1) * span] for h in range(GROUP)], axis=1)


def load_window(inverse_ref, kv_ref, window, first_block):
    half_len = kv_ref.shape[1] // 2
    for n in range(window.shape[0] // half_len):
        slot = inverse_ref[first_block + n]
        at = pl.ds(pl.multiple_of(lax.rem(slot, 2) * half_len, half_len), half_len)
        window[n * half_len : (n + 1) * half_len, :] = kv_ref[lax.div(slot, 2), at, :]


def window_of(order_ref, first_ref, count, half_len):
    m, half = pl.program_id(0), pl.program_id(1)
    my_block = order_ref[lax.axis_index("seq") * 2 + half]
    half_blocks = count // half_len // 2
    first_block = jnp.where(my_block >= half_blocks, half_blocks, 0)
    return first_block, my_block * half_len, first_ref[m]


def attend_kernel(order_ref, inverse_ref, first_ref, lin_ref, cos_ref, sin_ref, kv_ref, q_ref, out_ref, window, bias):
    span = lin_ref.shape[0]
    wide = window.shape[0]
    first_block, my_place, first = window_of(order_ref, first_ref, 2 * wide, span)
    load_window(inverse_ref, kv_ref, window, first_block)
    key_place = first_block * span + lax.broadcasted_iota(jnp.int32, (span, wide), 1)
    place_here = my_place + lax.broadcasted_iota(jnp.int32, (span, wide), 0)
    start = jnp.where(place_here >= first, first, 0)
    bias[...] = jnp.where((key_place <= place_here) & (key_place >= start), 0.0, NEG_LARGE)
    width = GROUP * HEAD_DIM
    cosine = jnp.concatenate([cos_ref[...]] * (width // 128), axis=1)
    sine = jnp.concatenate([sin_ref[...]] * (width // 128), axis=1)
    for g in range(KV_HEADS):
        at = slice(g * width, (g + 1) * width)
        lin = lin_ref[:, at]
        query = (lin * cosine + partner(lin) * sine).astype(jnp.bfloat16) * jnp.bfloat16(HEAD_DIM ** -0.5)
        q_ref[:, at] = query
        key = window[:, g * HEAD_DIM : (g + 1) * HEAD_DIM]
        value = window[:, KVW + g * HEAD_DIM : KVW + (g + 1) * HEAD_DIM]
        scores = product_nt(stack_heads(query, 0), key).reshape(GROUP, span, wide) + bias[...][None]
        exps = jnp.exp(scores - jnp.max(scores, axis=-1, keepdims=True))
        total = jnp.sum(exps, axis=-1, keepdims=True).reshape(GROUP * span, 1)
        mixed = product(exps.astype(jnp.bfloat16).reshape(GROUP * span, wide), value) / total
        out_ref[:, at] = unstack_heads(mixed, span).astype(jnp.bfloat16)


def attend_back_heads(queries, d_heads, key, value, bias, span):
    query, d_mixed = stack_heads(queries, 0), stack_heads(d_heads, 0)
    scores = product_nt(key, query) + bias[...]
    exps = jnp.exp(scores - jnp.max(scores, axis=0, keepdims=True))
    probs = exps * (1.0 / jnp.sum(exps, axis=0, keepdims=True))
    weighted = probs * product_nt(value, d_mixed)
    delta = jnp.sum(weighted, axis=0, keepdims=True)
    d_scores = (weighted - probs * delta).astype(jnp.bfloat16)
    d_query = unstack_heads(product_tn(d_scores, key) * HEAD_DIM ** -0.5, span)
    return product(d_scores, query), product(probs.astype(jnp.bfloat16), d_mixed), d_query


def attend_back_kernel(order_ref, inverse_ref, first_ref, q_ref, d_ref, cos_ref, sin_ref, kv_ref, dq_ref, dkv_ref, window, bias, sums):
    span = q_ref.shape[0]
    wide = window.shape[0]
    rows = GROUP * span
    half = pl.program_id(1)
    first_block, my_place, first = window_of(order_ref, first_ref, 2 * wide, span)
    load_window(inverse_ref, kv_ref, window, first_block)
    key_place = first_block * span + lax.broadcasted_iota(jnp.int32, (wide, rows), 0)
    place_here = my_place + lax.rem(lax.broadcasted_iota(jnp.int32, (wide, rows), 1), span)
    start = jnp.where(place_here >= first, first, 0)
    bias[...] = jnp.where((key_place <= place_here) & (key_place >= start), 0.0, NEG_LARGE)

    @pl.when(half == 0)
    def _():
        sums[...] = jnp.zeros_like(sums)

    width = GROUP * HEAD_DIM
    cosine = jnp.concatenate([cos_ref[...]] * (width // 128), axis=1)
    sine = jnp.concatenate([sin_ref[...]] * (width // 128), axis=1)
    d_keys, d_values = [], []
    for g in range(KV_HEADS):
        at = slice(g * width, (g + 1) * width)
        key = window[:, g * HEAD_DIM : (g + 1) * HEAD_DIM]
        value = window[:, KVW + g * HEAD_DIM : KVW + (g + 1) * HEAD_DIM]
        d_key, d_value, d_query = attend_back_heads(q_ref[:, at], d_ref[:, at], key, value, bias, span)
        d_keys.append(d_key)
        d_values.append(d_value)
        dq_ref[:, at] = (d_query * cosine - partner(d_query) * sine).astype(jnp.bfloat16)
    d_window = jnp.concatenate(d_keys + d_values, axis=1)
    for n in range(wide // span):
        slot = inverse_ref[first_block + n]
        to = pl.ds(pl.multiple_of(lax.rem(slot, 2) * span, span), span)
        sums[lax.div(slot, 2), to, :] += d_window[n * span : (n + 1) * span]

    @pl.when(half == 1)
    def _():
        dkv_ref[...] = sums[...].astype(jnp.bfloat16)


def attention_specs(seq, micro, span):
    half_len = span // 2

    def rows(width):
        return pl.BlockSpec((half_len, width), lambda m, h, *_: (m * 2 + h, 0))

    whole = pl.BlockSpec((seq, span, 2 * KVW), lambda m, h, *_: (0, m, 0))
    return half_len, rows, whole


def attend(order, inverse, first, lin, cosine, sine, kv):
    seq, many, _ = kv.shape
    micro = first.shape[0]
    span = many // micro
    half_len, rows, whole = attention_specs(seq, micro, span)
    wide = seq * span // 2
    return pl.pallas_call(
        attend_kernel,
        grid_spec=pltpu.PrefetchScalarGridSpec(
            num_scalar_prefetch=3,
            grid=(micro, 2),
            in_specs=[rows(D), rows(128), rows(128), whole],
            out_specs=[rows(D), rows(D)],
            scratch_shapes=[pltpu.VMEM((wide, 2 * KVW), jnp.bfloat16), pltpu.VMEM((half_len, wide), jnp.float32)],
        ),
        out_shape=[jax.ShapeDtypeStruct((many, D), jnp.bfloat16)] * 2,
        compiler_params=pltpu.CompilerParams(vmem_limit_bytes=48 * MIB),
        cost_estimate=pl.CostEstimate(flops=8 * many * wide * D, bytes_accessed=16 * MIB, transcendentals=many * wide * HEADS),
    )(order, inverse, first, lin, cosine, sine, kv)


def attend_back(order, inverse, first, queries, d_heads, cosine, sine, kv):
    seq, many, _ = kv.shape
    micro = first.shape[0]
    span = many // micro
    half_len, rows, whole = attention_specs(seq, micro, span)
    wide = seq * span // 2
    return pl.pallas_call(
        attend_back_kernel,
        grid_spec=pltpu.PrefetchScalarGridSpec(
            num_scalar_prefetch=3,
            grid=(micro, 2),
            in_specs=[rows(D), rows(D), rows(128), rows(128), whole],
            out_specs=[rows(D), whole],
            scratch_shapes=[
                pltpu.VMEM((wide, 2 * KVW), jnp.bfloat16),
                pltpu.VMEM((wide, GROUP * half_len), jnp.float32),
                pltpu.VMEM((seq, span, 2 * KVW), jnp.float32),
            ],
        ),
        out_shape=[jax.ShapeDtypeStruct((many, D), jnp.bfloat16), jax.ShapeDtypeStruct(kv.shape, jnp.bfloat16)],
        compiler_params=pltpu.CompilerParams(vmem_limit_bytes=56 * MIB),
        cost_estimate=pl.CostEstimate(flops=20 * many * wide * D, bytes_accessed=24 * MIB, transcendentals=many * wide * HEADS),
    )(order, inverse, first, queries, d_heads, cosine, sine, kv)


def assemble(zs, pieces, whole, sem):
    if len(pieces) == 1:
        copy = pltpu.make_async_copy(pieces[0], whole, sem.at[0])
        copy.start()
        return [copy]
    z = lax.div(lax.axis_index("seq"), 2)
    size = whole.shape[0] // zs

    def rows(zz):
        return whole.at[pl.ds(pl.multiple_of(zz * size, size), size)]

    if len(pieces) == 2:
        pieces = [pieces[0], *(pieces[1].at[k] for k in range(zs - 1))]
    copies = [pltpu.make_async_copy(pieces[0], rows(z), sem.at[0])]
    copies[0].start()
    for k in range(1, zs):
        to = rows(lax.rem(z - k + zs, zs))
        below = pltpu.make_async_copy(pieces[k], to, sem.at[k])
        if len(pieces) == zs:
            below.start()
        else:
            above = pltpu.make_async_copy(pieces[2 * zs - 1 - k], to, sem.at[k])
            pl.when(z >= k)(below.start)
            pl.when(z < k)(above.start)
        copies.append(below)
    return copies


class Around:
    def __init__(self, zs, block, got, sems):
        z, c, r = place()
        self.copies = [
            send(block(k), got.at[k - 1], sems.at[k - 1, 0], sems.at[k - 1, 1], (lax.rem(z + k, zs) * 2 + c, r))
            for k in range(1, zs)
        ]

    def start(self):
        for copy in self.copies:
            copy.start()

    def finish(self):
        for copy in self.copies:
            copy.wait()


def swiglu(lin, d_hidden):
    n = d_hidden.shape[1]
    gate, upper = lin[:, :n], lin[:, n:]
    sig = 1.0 / (1.0 + jnp.exp(-gate))
    act = gate * sig
    d_gate = d_hidden * upper * (sig * (1.0 + gate * (1.0 - sig)))
    d_both = jnp.concatenate([d_gate.astype(jnp.bfloat16), (d_hidden * act).astype(jnp.bfloat16)], axis=1)
    return (act * upper).astype(jnp.bfloat16), d_both


def add_gradients(x, dy, hidden, d_both, both_sum, down_sum):
    for at in range(0, D, 256):
        both_sum[at : at + 256, :] += product_tn(x[:, at : at + 256], d_both)
    part = hidden.shape[1] // 4
    for at in range(0, hidden.shape[1], part):
        down_sum[at : at + part, :] += product_tn(hidden[:, at : at + part], dy)


def put_gradients(sums, staged, out, sem):
    copies = []
    for n in range(2):
        staged[n][...] = sums[n][...].astype(jnp.bfloat16)
        copies.append(pltpu.make_async_copy(staged[n], out[n], sem.at[n, 0]))
        copies[-1].start()
    for copy in copies:
        copy.wait()


def ffn_first_kernel(zs, count, linked, *refs):
    x_ref, dy_ref = refs[:2]
    both_pieces, down_pieces = refs[2 : 2 + count], refs[2 + count : 2 + 2 * count]
    refs = refs[2 + 2 * count :]
    if linked:
        rest_own, last_own, x_out_ref, rest_got, last_got, *refs = refs
    hidden_ref, d_both_ref, g_both_ref, g_down_ref, both_w, down_w, both_sum, down_sum, sem, *more = refs
    step, last = pl.program_id(0), pl.num_programs(0) - 1
    gathered, arounds = None, []
    if linked:
        x_all, a_sems, *g_sems = more
        gathered = Gather(zs, False, True, x_ref, x_all, *g_sems)
        arounds = [
            Around(zs, lambda k: rest_own, rest_got, a_sems.at[0]), Around(zs, lambda k: last_own, last_got, a_sems.at[1])
        ]

    @pl.when(step == 0)
    def _():
        copies = assemble(zs, both_pieces, both_w, sem.at[0]) + assemble(zs, down_pieces, down_w, sem.at[1])
        if linked:
            greet(neighbours(zs, True, False))
            gathered.launch()
            gathered.begin(0)
            for one in arounds:
                one.start()
        both_sum[...] = jnp.zeros_like(both_sum)
        down_sum[...] = jnp.zeros_like(down_sum)
        for copy in copies:
            copy.wait()
        if linked:
            gathered.local.wait()

    if linked:
        waits = [
            lambda: gathered.from_twin(0, 0), lambda: gathered.forward(0), lambda: gathered.from_twin(0, 1), None,
            lambda: gathered.from_twin(0, 2), lambda: gathered.finish(0), lambda: gathered.from_twin(0, 3),
        ]
        for n, wait in enumerate(waits):
            if wait is not None:
                pl.when(step == n + 1)(wait)
        x = x_all[lax.rem(step, 2), lax.div(step, 2)]
        x_out_ref[...] = x
    else:
        x = x_ref[...]
    dy = dy_ref[...]
    hidden, d_both = swiglu(product(x, both_w[...]), product_nt(dy, down_w[...]))
    hidden_ref[...] = hidden
    d_both_ref[...] = d_both
    add_gradients(x, dy, hidden, d_both, both_sum, down_sum)

    @pl.when(step == last)
    def _():
        put_gradients((both_sum, down_sum), (both_w, down_w), (g_both_ref, g_down_ref), sem)
        for one in arounds:
            one.finish()
        if linked:
            gathered.sent_all()


def ffn_second_kernel(zs, counts, linked, *refs):
    x_ref, dy_ref, hidden_ref, d_both_ref = refs[:4]
    refs = refs[4:]
    pieces = []
    for count in counts:
        pieces += [refs[:count], refs[count : 2 * count]]
        refs = refs[2 * count :]
    if linked:
        g_both_one, g_down_one, *refs = refs
    out_ref, dx_ref, g_both_ref, g_down_ref, *refs = refs
    if linked:
        *got, both_one, down_one, both_w, down_w, both_sum, down_sum, stage, sem, z_sem, come, held, d_sems, dl_sem = refs
    else:
        got, (both_one, down_one, both_w, down_w, both_sum, down_sum, stage, sem) = [], refs
    n, wide = stage.shape[1] // 2, down_w.shape[0]
    down_rows = down_w.at[pl.ds(0, n)]
    step, last = pl.program_id(0), pl.num_programs(0) - 1
    lines = []
    if linked:
        z = lax.div(lax.axis_index("seq"), 2)
        lines = [
            Line(zs, 1, 0, 1, g_both_one.at[lax.rem(z + zs - 1, zs)], got[0], z_sem.at[0]),
            Line(zs, -1, zs - 1, zs, g_both_one.at[lax.rem(z + 1, zs)], got[1], z_sem.at[1]),
        ]
        none = [None] * (zs - 3)
        down = SumChain(zs, g_down_one, [come.at[0], got[2], *none, come.at[1], got[3], *none], held, d_sems, dl_sem)

    @pl.when(step == 0)
    def _():
        copies = []
        for which, whole in enumerate((both_one, down_one, stage, down_rows)):
            copies += assemble(zs, pieces[which], whole, sem.at[which])
        if linked:
            greet(neighbours(zs, False, False))
            down.start(1)
        both_sum[...] = jnp.zeros_like(both_sum)
        down_sum[...] = jnp.zeros_like(down_sum)
        if wide > n:
            both_w[...] = jnp.zeros_like(both_w)
            down_w[n:, :] = jnp.zeros((wide - n, D), down_w.dtype)
        for copy in copies:
            copy.wait()
        both_w[:, :n] = stage[:, :n]
        both_w[:, wide : wide + n] = stage[:, n:]

    if linked:

        @pl.when(step == last - 5)
        def _():
            down.finish(1)
            for line in lines:
                line.start()
            down.fetch(2)
            down.start(2)

    x, dy = x_ref[...], dy_ref[...]
    hidden, d_both = swiglu(product(x, both_w[...]), product_nt(dy, down_w[...]))
    dx_ref[...] = (product_nt(d_both_ref[...], both_one[...]) + product_nt(d_both, both_w[...])).astype(jnp.bfloat16)
    out_ref[...] = (product(hidden_ref[...], down_one[...]) + product(hidden, down_w[...])).astype(jnp.bfloat16)
    add_gradients(x, dy, hidden, d_both, both_sum, down_sum)

    @pl.when(step == last)
    def _():
        stage[:, :n] = both_sum[:, :n].astype(jnp.bfloat16)
        stage[:, n:] = both_sum[:, wide : wide + n].astype(jnp.bfloat16)
        down_w[...] = down_sum[...].astype(jnp.bfloat16)
        copies = [
            pltpu.make_async_copy(stage, g_both_ref, sem.at[0, 0]), pltpu.make_async_copy(down_rows, g_down_ref, sem.at[1, 0])
        ]
        for copy in copies:
            copy.start()
        for copy in copies:
            copy.wait()
        for line in lines:
            line.finish()
        if linked:
            down.finish(2)


def ffn_first(x, dy, both_pieces, down_pieces, zs, others=(), collective_id=None):
    count, n = len(both_pieces), down_pieces[0].shape[0] * (zs if len(down_pieces) > 1 else 1)
    block, low, full = 256, jnp.bfloat16, jnp.float32
    sem, shape = pltpu.SemaphoreType.DMA, jax.ShapeDtypeStruct
    anywhere = pl.BlockSpec(memory_space=pl.ANY)
    linked = bool(others)
    total = dy.shape[0]

    def tokens(width):
        if linked:
            return pl.BlockSpec((block, width), lambda i: (i % 2 * 4 + i // 2, 0))
        return pl.BlockSpec((block, width), lambda i: (i, 0))

    extra_specs, extra_shapes, extra_scratch, params = [], [], [], {}
    if linked:
        extra_specs = [tokens(D)] + [anywhere] * 2
        extra_shapes = [shape(dy.shape, low)] + [shape((zs - 1,) + other.shape, low) for other in others]
        extra_scratch = [pltpu.VMEM((2, 4) + x.shape, low), sem((2, zs - 1, 2))] + gather_sems(zs, False)
        params = dict(collective_id=collective_id, has_side_effects=True)
    return pl.pallas_call(
        functools.partial(ffn_first_kernel, zs, count, linked),
        grid=(total // block,),
        in_specs=[anywhere if linked else tokens(D), tokens(D)] + [anywhere] * (2 * count + len(others)),
        out_specs=extra_specs + [tokens(n), tokens(2 * n)] + [anywhere] * 2,
        out_shape=extra_shapes
        + [shape((total, n), low), shape((total, 2 * n), low), shape((D, 2 * n), low), shape((n, D), low)],
        scratch_shapes=[
            pltpu.VMEM((D, 2 * n), low), pltpu.VMEM((n, D), low), pltpu.VMEM((D, 2 * n), full), pltpu.VMEM((n, D), full),
            sem((2, zs)),
        ] + extra_scratch,
        compiler_params=pltpu.CompilerParams(vmem_limit_bytes=60 * MIB, **params),
        cost_estimate=LONG,
    )(x, dy, *both_pieces, *down_pieces, *others)


def ffn_second(x, dy, hidden, d_both, one, two, zs, parts=(), collective_id=None):
    counts = (len(one[0]), len(two[0]))
    wides = [down[0].shape[0] * (zs if len(down) > 1 else 1) for _, down in (one, two)]
    n = wides[1]
    wide = -(-n // 128) * 128
    block, low, full = 256, jnp.bfloat16, jnp.float32
    sem, shape = pltpu.SemaphoreType.DMA, jax.ShapeDtypeStruct
    anywhere = pl.BlockSpec(memory_space=pl.ANY)

    def tokens(width):
        return pl.BlockSpec((block, width), lambda i: (i, 0))

    linked = bool(parts)
    extra = []
    if linked:
        held = pltpu.VMEM((2,) + parts[1].shape[1:], low)
        extra = [sem((2, 2)), held, held, sem((2 * zs - 2, 2)), sem((2,))]
    params = dict(collective_id=collective_id, has_side_effects=True) if linked else {}
    return pl.pallas_call(
        functools.partial(ffn_second_kernel, zs, counts, linked),
        grid=(x.shape[0] // block,),
        in_specs=[tokens(D)] * 2 + [tokens(wides[0]), tokens(2 * wides[0])] + [anywhere] * (2 * sum(counts) + len(parts)),
        out_specs=[tokens(D)] * 2 + [anywhere] * (2 + 2 * len(parts)),
        out_shape=[shape(x.shape, low)] * 2 + [shape((D, 2 * n), low), shape((n, D), low)]
        + [shape(part.shape[1:], low) for part in parts for _ in range(2)],
        scratch_shapes=[
            pltpu.VMEM((D, 2 * wides[0]), low), pltpu.VMEM((wides[0], D), low),
            pltpu.VMEM((D, 2 * wide), low), pltpu.VMEM((wide, D), low),
            pltpu.VMEM((D, 2 * wide), full), pltpu.VMEM((wide, D), full), pltpu.VMEM((D, 2 * n), low),
            sem((4, zs)),
        ] + extra,
        compiler_params=pltpu.CompilerParams(vmem_limit_bytes=56 * MIB, **params),
        cost_estimate=LONG,
    )(x, dy, hidden, d_both, *one[0], *one[1], *two[0], *two[1], *parts)


def split_unit(unit):
    return unit * 3 // 4 // 16 * 16


def portions(unit):
    first = split_unit(unit)
    return (0, first), (first, unit - first)


def gain_columns(one, two, rows):
    row = lax.broadcasted_iota(jnp.int32, (128, rows), 0)
    return jnp.where(row == 0, one, jnp.where(row == 1, two, 0.0)).T


def spread_kernel(zs, rows, unit, gate_ref, up_ref, query_ref, key_ref, value_ref, one_ref, two_ref, down_ref, *out):
    for (begin, size), ref in zip(portions(unit), out):
        for c in range(2):
            for r in range(rows):
                for n, weight in enumerate((gate_ref, up_ref)):
                    for z in range(zs):
                        at = ((z * 2 + c) * rows + r) * unit + begin
                        to = (n * zs + z) * size
                        ref[c, r, :, to : to + size] = weight[:, at : at + size]
    pack_ref, down_one, down_two = out[2:]
    pack_ref[:, :D] = query_ref[...]
    pack_ref[:, D : D + KVW] = key_ref[...]
    pack_ref[:, D + KVW : QKV] = value_ref[...]
    gains = gain_columns(one_ref[...].astype(jnp.float32), two_ref[...].astype(jnp.float32), pack_ref.shape[0])
    pack_ref[:, QKV:] = gains.astype(pack_ref.dtype)
    cut = down_one.shape[0]
    down_one[...] = down_ref[:cut, :]
    down_two[...] = down_ref[cut:, :]


def spread(gate, up, query, key, value, one, two, down, zs, rows):
    wide, part = gate.shape
    unit = part // (zs * 2 * rows)
    shape, low = jax.ShapeDtypeStruct, gate.dtype
    return pl.pallas_call(
        functools.partial(spread_kernel, zs, rows, unit),
        out_shape=[shape((2, rows, wide, 2 * zs * size), low) for _, size in portions(unit)]
        + [shape((wide, PACK), low)]
        + [shape((size, D), low) for _, size in portions(unit)],
    )(gate, up, query, key, value, one.reshape(1, -1), two.reshape(1, -1), down)


def collect_kernel(zs, rows, unit, *refs):
    given, (pack_ref, down_one, down_two), outs = refs[:2], refs[2:5], refs[5:]
    for n, out in enumerate(outs[:2]):
        for (begin, size), ref in zip(portions(unit), given):
            for c in range(2):
                for r in range(rows):
                    for z in range(zs):
                        at = ((z * 2 + c) * rows + r) * unit + begin
                        to = (n * zs + z) * size
                        out[:, at : at + size] = ref[c, r, :, to : to + size].astype(jnp.float32)
    key_ref, value_ref, one_ref, two_ref, down_ref = outs[2:]
    key_ref[...] = pack_ref[:, :KVW]
    value_ref[...] = pack_ref[:, KVW : 2 * KVW]
    gains = pack_ref[:, 2 * KVW :].T
    one_ref[...] = gains[0:1]
    two_ref[...] = gains[1:2]
    cut = down_one.shape[0]
    down_ref[:cut, :] = down_one[...]
    down_ref[cut:, :] = down_two[...]


def collect(blocks, pack, downs, zs, rows, unit):
    wide = blocks[0].shape[2]
    shape, full = jax.ShapeDtypeStruct, jnp.float32
    whole = shape((wide, unit * zs * 2 * rows), full)
    narrow = shape((wide, KVW), full)
    return pl.pallas_call(
        functools.partial(collect_kernel, zs, rows, unit),
        out_shape=[whole, whole, narrow, narrow, shape((1, wide), full), shape((1, wide), full), shape((unit, D), full)],
    )(*blocks, pack, *downs)


def forward_kernel(zs, micro, *refs):
    order_ref, places_ref, first_ref, freq_ref, x_ref, pack_ref, both_ref, down_ref, out_ref, dy_ref, rest_ref = refs[:11]
    refs = refs[1:]
    packed, both_own, kv_all, out_all, dy_all, rest_own = refs[10:16]
    steps = 2 * zs - 2
    both_got, down_got = refs[16 : 16 + steps], refs[16 + steps : 16 + 2 * steps]
    q_ref, attn_ref, attended_ref, ffn_own, middle_ref, gains_ref, cos_ref, sin_ref = refs[16 + 2 * steps : 24 + 2 * steps]
    (staged, lin, kv_own, kv_here, window, chosen, bias, out_w, sems, *more) = refs[24 + 2 * steps :]
    low = jnp.bfloat16
    z, c, r = place()
    many = x_ref.shape[0]
    span = many // micro
    half_len = span // 2
    rows = D // zs
    greet(neighbours(zs, True, True))

    exchange = Exchange(both_ref, both_own, *more[:3])
    rest = Exchange(rest_ref, rest_own, *more[3:6])
    more = more[:3] + more[6:]
    both_chain, down_chain = Chain(zs, both_own, both_got, more[3]), Chain(zs, down_ref, down_got, more[4])
    more = more[5:]
    weights = Gather(zs, True, True, pack_ref, packed, *more[:9])
    outs = Gather(zs, True, True, out_ref, out_all, *more[9:18])
    pairs = Gather(zs, True, False, kv_own, kv_all, *more[18:27])
    dys = Gather(zs, False, True, dy_ref, dy_all, *more[27:36])

    weights.launch()
    exchange.start()
    weights.begin(0)
    outs.launch()

    lane = lax.broadcasted_iota(jnp.int32, (half_len, 128), 1)
    for i in range(2 * micro):
        place_here = order_ref[(z * 2 + c) * 2 + i % 2] * half_len + lax.broadcasted_iota(jnp.int32, (half_len, 128), 0)
        start = jnp.where(place_here >= first_ref[i // 2, 0], first_ref[i // 2, 0], 0)
        angle = (place_here - start).astype(jnp.float32) * freq_ref[...]
        cos_ref[i * half_len : (i + 1) * half_len, :] = jnp.cos(angle)
        sine = jnp.sin(angle)
        sin_ref[i * half_len : (i + 1) * half_len, :] = jnp.where(lax.rem(lane, HEAD_DIM) < HEAD_DIM // 2, -sine, sine)
    x = x_ref[...].astype(jnp.float32)
    factor = rms_factor(x)
    wide = window.shape[0]
    half_blocks = wide // half_len
    for half in range(2):
        my_block = order_ref[(z * 2 + c) * 2 + half]
        chosen[half] = chosen_slots(places_ref[...], first_of(my_block, half_blocks), half_len, wide)

    loads = {}

    def load(n):
        weights.complete(n)
        zz = lax.rem(z - weights.kth[n] + zs, zs)
        loads[n] = pltpu.make_async_copy(packed.at[zz], staged.at[n % 2], sems.at[n % 2])
        loads[n].start()

    def project(n):
        loads[n].wait()
        zz = lax.rem(z - weights.kth[n] + zs, zs)
        at = pl.ds(pl.multiple_of(zz * rows, rows), rows)
        block = staged[n % 2].reshape(rows, PACK)
        gains = block[:, QKV:].astype(jnp.float32).T[:8]
        gains_ref[:, at] = gains
        attn_in = (x_ref[:, at].astype(jnp.float32) * factor * gains[0:1]).astype(low)
        attn_ref[:, at] = attn_in
        value = product(attn_in, block[:, :QKV])
        lin[...] = value if n == 0 else lin[...] + value

    weights.arrive(1)
    weights.begin(1)
    weights.forward(0)
    weights.arrive(2)
    weights.begin(2)
    weights.forward(1)
    weights.finish(0)
    weights.arrive(3)
    weights.begin(3)
    down_chain.start(1)
    exchange.finish()
    both_chain.start(1)
    outs.arrive(1)
    weights.forward(2)
    weights.finish(1)
    load(0)
    outs.arrive(2)
    weights.forward(3)
    weights.finish(2)
    outs.begin(0)
    load(1)
    project(0)
    outs.arrive(3)
    outs.begin(1)
    project(1)
    weights.finish(3)
    rest.start()
    dys.launch()
    dys.begin(0)
    load(2)
    load(3)
    project(2)
    project(3)

    width = GROUP * HEAD_DIM
    cosine = jnp.concatenate([cos_ref[...]] * (width // 128), axis=1)
    sine = jnp.concatenate([sin_ref[...]] * (width // 128), axis=1)

    def turned(block, w):
        return block * cosine[:, :w] + partner(block) * sine[:, :w]

    kv_own[:, :KVW] = turned(lin[:, D : D + KVW], KVW).astype(low)
    kv_own[:, KVW:] = lin[:, D + KVW :].astype(low)
    pairs.launch()
    pairs.begin(0)
    for g in range(KV_HEADS):
        at = slice(g * width, (g + 1) * width)
        q_ref[:, at] = turned(lin[:, at], width).astype(low) * low(HEAD_DIM ** -0.5)
    outs.forward(0)
    outs.begin(2)
    both_chain.finish()
    down_chain.finish()
    both_chain.start(2)
    down_chain.start(2)
    for k in range(1, zs):
        pairs.arrive(k)
        pairs.begin(k)
    outs.forward(1)
    outs.finish(0)
    outs.begin(3)
    for k in range(zs):
        pairs.complete(k)
    kv_load = pltpu.make_async_copy(kv_all, kv_here, sems.at[2])
    kv_load.start()
    outs.forward(2)
    outs.finish(1)
    kv_load.wait()

    def attend_some(i, carry):
        m, half = lax.div(i, 2), lax.rem(i, 2)
        my_block = order_ref[(z * 2 + c) * 2 + half]
        first_block = first_of(my_block, half_blocks)
        at = pl.ds(pl.multiple_of(m * span, span), span)
        window[...] = product(chosen[half], kv_here[:, :, at, :].reshape(2 * wide, 2 * KVW)).astype(low)
        key_place = first_block * half_len + lax.broadcasted_iota(jnp.int32, (half_len, wide), 1)
        place_here = my_block * half_len + lax.broadcasted_iota(jnp.int32, (half_len, wide), 0)
        first = first_ref[m, 0]
        start = jnp.where(place_here >= first, first, 0)
        bias[...] = jnp.where((key_place <= place_here) & (key_place >= start), 0.0, NEG_LARGE)
        here = pl.ds(pl.multiple_of(i * half_len, half_len), half_len)
        for g in range(KV_HEADS):
            at = slice(g * width, (g + 1) * width)
            key = window[:, g * HEAD_DIM : (g + 1) * HEAD_DIM]
            value = window[:, KVW + g * HEAD_DIM : KVW + (g + 1) * HEAD_DIM]
            scores = product_nt(stack_heads(q_ref[here, at], 0), key).reshape(GROUP, half_len, wide) + bias[...][None]
            exps = jnp.exp(scores - jnp.max(scores, axis=-1, keepdims=True))
            total = jnp.sum(exps, axis=-1, keepdims=True).reshape(GROUP * half_len, 1)
            mixed = product(exps.astype(low).reshape(GROUP * half_len, wide), value) / total
            attended_ref[here, at] = unstack_heads(mixed, half_len).astype(low)
        return carry

    lax.fori_loop(0, 2 * micro, attend_some, 0)
    outs.forward(3)
    outs.finish(2)
    outs.finish(3)
    dys.forward(0)
    for k in range(zs):
        outs.complete(k)
    out_load = pltpu.make_async_copy(out_all, out_w, sems.at[3])
    out_load.start()
    out_load.wait()
    middle = x_ref[...].astype(jnp.float32) + product(attended_ref[...], out_w[...].reshape(D, D))
    middle_ref[...] = middle
    ffn_own[...] = (middle * rms_factor(middle) * gains_ref[1:2, :]).astype(low)
    both_chain.finish()
    down_chain.finish()
    both_chain.start(3)
    down_chain.start(3)
    dys.finish(0)
    dys.complete(0)
    rest.finish()
    both_chain.finish()
    down_chain.finish()
    rest.end()
    exchange.end()
    for one in (weights, outs, pairs, dys):
        one.end()


def places_of(order, span):
    return (order[:, None] * (span // 2) + jnp.arange(span // 2, dtype=jnp.int32)).reshape(1, -1)


def forward(order, first, tokens, pack, both, rest, down, w_out, dy, zs, collective_id):
    many = tokens.shape[0]
    micro = first.shape[0]
    seq = 2 * zs
    wide = seq * (many // micro) // 2
    low, full = jnp.bfloat16, jnp.float32
    turns = np.arange(128) % (HEAD_DIM // 2) / (HEAD_DIM // 2)
    freq = jnp.asarray((10000.0 ** -turns).astype(np.float32))
    anywhere, here, smem = (pl.BlockSpec(memory_space=m) for m in (pl.ANY, pltpu.VMEM, pltpu.SMEM))
    shape = jax.ShapeDtypeStruct
    out_any = [
        shape((zs, 2, 4) + pack.shape, low),
        shape(both.shape, low),
        shape((zs, 2, many, 2 * KVW), low),
        shape((zs, 2, 4) + w_out.shape, low),
        shape((2, 4) + dy.shape, low),
        shape(rest.shape, low),
    ] + [shape(both.shape, low)] * (2 * zs - 2) + [shape(down.shape, low)] * (2 * zs - 2)
    out_here = [shape((many, D), t) for t in (low, low, low, low, full)] + [shape((8, D), full)] + [shape((many, 128), full)] * 2
    sem = pltpu.SemaphoreType.DMA
    found = pl.pallas_call(
        functools.partial(forward_kernel, zs, micro),
        out_shape=out_any + out_here,
        in_specs=[smem, here, smem] + [here] * 2 + [anywhere] * 6,
        out_specs=[anywhere] * len(out_any) + [here] * len(out_here),
        scratch_shapes=[
            pltpu.VMEM((2, 2, 4) + pack.shape, low),
            pltpu.VMEM((many, QKV), full),
            pltpu.VMEM((many, 2 * KVW), low),
            pltpu.VMEM((zs, 2, many, 2 * KVW), low),
            pltpu.VMEM((wide, 2 * KVW), low),
            pltpu.VMEM((2, wide, 2 * wide), low),
            pltpu.VMEM((many // micro // 2, wide), full),
            pltpu.VMEM((zs, 2, 4) + w_out.shape, low),
            sem((4,)),
        ] + EXCHANGE_SEMS * 2 + [sem((2 * zs - 2, 2))] * 2 + gather_sems(zs, True) * 3 + gather_sems(zs, False),
        compiler_params=pltpu.CompilerParams(
            collective_id=collective_id, has_side_effects=True, vmem_limit_bytes=56 * MIB
        ),
        cost_estimate=LONG,
    )(order, places_of(order, many // micro), first, freq.reshape(1, 128), tokens, pack, both, down, w_out, dy, rest)
    return found


def back_kernel(zs, micro, *refs):
    (order_ref, places_ref, first_ref, dy_ref, middle_ref, gains_ref, q_ref, cos_ref, sin_ref) = refs[:9]
    dx_part, out_part, both_part, down_part, out_all, kv_all, rest_part, last_part, *come = refs[9:21]
    result_ref, d_middle_ref, dq_ref, dkv_ref, gain_ref, down_ref, both_up, both_down, rest_in, last_in = refs[21:31]
    out_w, kv_here, d_heads, chosen, window, bias, d_places, sems, got, held, d_sems, dl_sem, *more = refs[31:]
    b_got, b_held, b_sems, bl_sem, r_sems, *more = more
    low, full = jnp.bfloat16, jnp.float32
    z, c, r = place()
    many = dy_ref.shape[0]
    span = many // micro
    half_len = span // 2
    greet(neighbours(zs, True, False))

    def take_d_ffn(at, value):
        d_middle_ref[at, :] = value

    def take_result(at, value):
        result_ref[at, :] = (middle_ref[at, :] + value).astype(low)

    scatters = {
        "dx": Scatter(1, False, True, dx_part, take_d_ffn, *more[:SCATTER_REFS]),
        "out": Scatter(1, False, True, out_part, take_result, *more[SCATTER_REFS : 2 * SCATTER_REFS]),
    }
    none = [None] * (zs - 3)
    down = SumChain(zs, down_part, [*none, got.at[0], got.at[1], *none, got.at[2], got.at[3]], held, d_sems, dl_sem)
    both = SumChain(
        zs, both_part, [b_got.at[0], both_up, *none, b_got.at[1], both_down, *none], b_held, b_sems, bl_sem
    )
    arounds = [
        Around(zs, lambda k: rest_part.at[lax.rem(z + k, zs)], rest_in, r_sems.at[0]),
        Around(zs, lambda k: last_part.at[lax.rem(z + k, zs)], last_in, r_sems.at[1]),
    ]
    comes = [
        pltpu.make_async_copy(src, dst, sems.at[2 + n])
        for n, (src, dst) in enumerate(zip(come, (b_got.at[0], b_got.at[1], got.at[0], got.at[2])))
    ]
    for copy in comes:
        copy.start()
    both.fetch(2)
    down.fetch(zs - 1)
    schedule = [(0, 3), (0, 1), (0, 2), (0, 0)]
    scatters["dx"].begin(schedule)
    for one in arounds:
        one.start()
    loads = [pltpu.make_async_copy(out_all, out_w, sems.at[0]), pltpu.make_async_copy(kv_all, kv_here, sems.at[1])]
    for load in loads:
        load.start()
    scatters["dx"].stage_a(0)
    for copy in comes:
        copy.wait()
    both.start(2)
    down.start(zs - 1)
    scatters["out"].begin(schedule)
    scatters["dx"].stage_b(0)
    scatters["out"].stage_a(0)
    scatters["dx"].stage_c(0)
    scatters["out"].stage_b(0)

    gain_ref[0:1, :] = jnp.zeros((1, D), full)

    def norm_some(i, carry):
        at = pl.ds(pl.multiple_of(i * half_len, half_len), half_len)
        middle, d_ffn = middle_ref[at, :], d_middle_ref[at, :]
        factor = rms_factor(middle)
        normed = middle * factor
        inner = d_ffn * gains_ref[1:2, :]
        d_norm = factor * (inner - normed * jnp.mean(inner * normed, axis=-1, keepdims=True))
        d_middle_ref[at, :] = dy_ref[at, :].astype(full) + d_norm
        gain_ref[0:1, :] += jnp.sum(d_ffn * normed, axis=0, keepdims=True)
        return carry

    lax.fori_loop(0, many // half_len, norm_some, 0)
    for load in loads:
        load.wait()
    d_heads[...] = product_nt(d_middle_ref[...].astype(low), out_w[...].reshape(D, D)).astype(low)

    wide = window.shape[0]
    half_blocks = wide // half_len
    width = GROUP * HEAD_DIM

    def attend_some(i, carry):
        m, half = lax.div(i, 2), lax.rem(i, 2)
        my_block = order_ref[(z * 2 + c) * 2 + half]
        first_block = jnp.where(my_block >= half_blocks, half_blocks, 0)
        wanted = first_block * half_len + lax.broadcasted_iota(jnp.int32, (wide, 2 * wide), 0)
        chosen[...] = jnp.where(places_ref[...] == wanted, 1.0, 0.0).astype(low)
        rows = pl.ds(pl.multiple_of(m * span, span), span)
        window[...] = product(chosen[...], kv_here[:, :, rows, :].reshape(2 * wide, 2 * KVW)).astype(low)
        key_place = first_block * half_len + lax.broadcasted_iota(jnp.int32, bias.shape, 0)
        place_here = my_block * half_len + lax.rem(lax.broadcasted_iota(jnp.int32, bias.shape, 1), half_len)
        first = first_ref[m, 0]
        start = jnp.where(place_here >= first, first, 0)
        bias[...] = jnp.where((key_place <= place_here) & (key_place >= start), 0.0, NEG_LARGE)
        here = pl.ds(pl.multiple_of(i * half_len, half_len), half_len)
        cosine = jnp.concatenate([cos_ref[here, :]] * (width // 128), axis=1)
        sine = jnp.concatenate([sin_ref[here, :]] * (width // 128), axis=1)
        d_keys, d_values = [], []
        for g in range(KV_HEADS):
            at = slice(g * width, (g + 1) * width)
            key = window[:, g * HEAD_DIM : (g + 1) * HEAD_DIM]
            value = window[:, KVW + g * HEAD_DIM : KVW + (g + 1) * HEAD_DIM]
            d_key, d_value, d_query = attend_back_heads(q_ref[here, at], d_heads[here, at], key, value, bias, half_len)
            d_keys.append(d_key)
            d_values.append(d_value)
            dq_ref[here, at] = (d_query * cosine - partner(d_query) * sine).astype(low)
        d_window = jnp.concatenate(d_keys + d_values, axis=1).astype(low)
        spread_back = product_tn(chosen[...], d_window)

        @pl.when(half == 0)
        def _():
            d_places[...] = spread_back

        @pl.when(half == 1)
        def _():
            both = (d_places[...] + spread_back).astype(low)
            dkv_ref[:, :, rows, :] = both.reshape(zs, 2, span, 2 * KVW)

        return carry

    lax.fori_loop(0, 2 * micro, attend_some, 0)
    scatters["out"].stage_c(0)
    both.finish()
    down.finish()
    down.total()
    down_ref[...] = held[0].astype(full)
    for one in arounds:
        one.finish()
    for one in scatters.values():
        one.end()


def back(order, first, dy, middle, gains, queries, cosine, sine, dx_part, out_part, both_part, down_part, out_all, kv_all,
         rest_part, last_part, come, zs, collective_id):
    many = dy.shape[0]
    micro = first.shape[0]
    span = many // micro
    wide = zs * span
    low, full = jnp.bfloat16, jnp.float32
    anywhere, here, smem = (pl.BlockSpec(memory_space=m) for m in (pl.ANY, pltpu.VMEM, pltpu.SMEM))
    shape, sem = jax.ShapeDtypeStruct, pltpu.SemaphoreType.DMA
    unit = down_part.shape[1]
    piece = shape(both_part.shape[1:], low)
    return pl.pallas_call(
        functools.partial(back_kernel, zs, micro),
        out_shape=[
            shape((many, D), low), shape((many, D), full), shape((many, D), low), shape(kv_all.shape, low),
            shape((8, D), full), shape((unit, D), full), piece, piece,
            shape((zs - 1,) + rest_part.shape[1:], low), shape((zs - 1,) + last_part.shape[1:], low),
        ],
        in_specs=[smem, here, smem] + [here] * 6 + [anywhere] * 12,
        out_specs=[here] * 6 + [anywhere] * 4,
        scratch_shapes=[
            pltpu.VMEM(out_all.shape, low),
            pltpu.VMEM(kv_all.shape, low),
            pltpu.VMEM((many, D), low),
            pltpu.VMEM((wide, 2 * wide), low),
            pltpu.VMEM((wide, 2 * KVW), low),
            pltpu.VMEM((wide, GROUP * span // 2), full),
            pltpu.VMEM((2 * wide, 2 * KVW), full),
            sem((6,)),
            pltpu.VMEM((4, unit, D), low),
            pltpu.VMEM((2, unit, D), low),
            sem((2 * zs - 2, 2)), sem((2,)),
            pltpu.VMEM((2,) + piece.shape, low),
            pltpu.VMEM((2,) + piece.shape, low),
            sem((2 * zs - 2, 2)), sem((2,)), sem((2, zs - 1, 2)),
        ] + scatter_scratch(1, True, many, D, True) * 2,
        compiler_params=pltpu.CompilerParams(
            collective_id=collective_id, has_side_effects=True, vmem_limit_bytes=62 * MIB
        ),
        cost_estimate=LONG,
    )(order, places_of(order, span), first, dy, middle, gains, queries, cosine, sine, dx_part, out_part, both_part, down_part,
      out_all, kv_all, rest_part, last_part, *come)


def products_kernel(attended_ref, attn_ref, d_middle_ref, dq_ref, packed_ref, out_ref, query_ref, d_attn_ref):
    low = jnp.bfloat16
    out_ref[...] = product_tn(attended_ref[...], d_middle_ref[...].astype(low)).astype(low)
    query_ref[...] = product_tn(attn_ref[...], dq_ref[...]).astype(low)
    d_attn_ref[...] = product_nt(dq_ref[...], packed_ref[...])


def products(attended, attn_in, d_middle, d_query, packed):
    many, block = attended.shape[0], 512
    low, shape = jnp.bfloat16, jax.ShapeDtypeStruct
    narrow = pl.BlockSpec((many, block), lambda i: (0, i))
    tall = pl.BlockSpec((block, D), lambda i: (i, 0))
    whole = pl.BlockSpec((many, D), lambda i: (0, 0))
    return pl.pallas_call(
        products_kernel,
        grid=(D // block,),
        in_specs=[narrow, narrow, whole, whole, tall],
        out_specs=[tall, tall, narrow],
        out_shape=[shape((D, D), low), shape((D, D), low), shape((many, D), jnp.float32)],
        compiler_params=pltpu.CompilerParams(vmem_limit_bytes=60 * MIB),
        cost_estimate=pl.CostEstimate(flops=6 * many * D * D, bytes_accessed=30 * MIB, transcendentals=0),
    )(attended, attn_in, d_middle, d_query, packed)


def weights_kernel(zs, *refs):
    x_ref, attn_ref, d_middle_ref, d_attn_ref, gains_ref, gain_two_ref, cos_ref, sin_ref, dkv_ref = refs[:9]
    packed, both_part, both_up, both_down, g_out, g_query, rest_part, last_part, rest_in, last_in = refs[9:19]
    x_grad_ref, out_ref, query_ref, pack_ref, last_ref, moved_ref, rest_ref = refs[19:26]
    kv_w, d_kv, pack_g, sems, got, held, b_sems, bl_sem, rest_here, last_here, *more = refs[26:]
    exchange_sems, rest_sems, more = more[:3], more[3:6], more[6:]
    z = place()[0]
    low, full = jnp.bfloat16, jnp.float32
    greet(neighbours(zs, True, True))

    def into(ref):
        def take(at, value):
            ref[at, :] = value

        return take

    def next_refs(staged):
        nonlocal more
        mine, more = more[:SCATTER_REFS], more[SCATTER_REFS:]
        return mine if staged else [None, *mine[1:]]

    pairs = Scatter(zs, True, False, dkv_ref, into(d_kv), *next_refs(False))
    scatters = {
        "out": Scatter(zs, True, True, g_out, into(out_ref), *next_refs(True)),
        "query": Scatter(zs, True, True, g_query, into(query_ref), *next_refs(True)),
        "pack": Scatter(zs, True, True, pack_g, into(pack_ref), *next_refs(False)),
    }
    items = [(name, k) for k in range(1, zs) for name in ("out", "query")]
    items[4:4] = [("pack", 1)]
    items += [("pack", k) for k in range(2, zs)] + [("out", 0), ("query", 0), ("pack", 0)]
    rounds, schedules = scatter_plan(items)

    none = [None] * (zs - 3)
    chain = SumChain(zs, both_part, [*none, got.at[0], got.at[1], *none, got.at[2], got.at[3]], held, b_sems, bl_sem)
    loads = [
        pltpu.make_async_copy(both_up, got.at[0], sems.at[0]),
        pltpu.make_async_copy(both_down, got.at[2], sems.at[1]),
        pltpu.make_async_copy(packed.at[:, :, :, :, pl.ds(D, 2 * KVW)], kv_w, sems.at[2]),
    ]
    for load in loads:
        load.start()
    small = [
        pltpu.make_async_copy(rest_part.at[z], rest_here.at[0], sems.at[3]),
        pltpu.make_async_copy(last_part.at[z], last_here.at[0], sems.at[4]),
        pltpu.make_async_copy(rest_in, rest_here.at[pl.ds(1, zs - 1)], sems.at[5]),
        pltpu.make_async_copy(last_in, last_here.at[pl.ds(1, zs - 1)], sems.at[6]),
    ]
    for load in small:
        load.start()
    chain.fetch(zs - 1)
    pairs.begin([])
    scatters["out"].begin(schedules["out"])
    scatters["query"].begin(schedules["query"])
    for k in range(1, zs):
        pairs.stage_c(k)
    for load in loads:
        load.wait()
    chain.start(zs - 1)
    for load in small:
        load.wait()
    last_ref[...] = sum(last_here[n].astype(full) for n in range(zs))
    rest_here[0] = sum(rest_here[n].astype(full) for n in range(zs)).astype(low)
    rest = Exchange(rest_here.at[0], rest_ref, *rest_sems)
    rest.start()

    def keys_and_norm():
        pairs.stage_c(0)
        lanes = KVW // 128
        cosine = jnp.concatenate([cos_ref[...]] * lanes, axis=1)
        sine = jnp.concatenate([sin_ref[...]] * lanes, axis=1)
        d_key = d_kv[:, :KVW]
        d_lin = jnp.concatenate([d_key * cosine - partner(d_key) * sine, d_kv[:, KVW:]], axis=1).astype(low)
        d_attn = d_attn_ref[...] + product_nt(d_lin, kv_w[...].reshape(D, 2 * KVW))
        x = x_ref[...].astype(full)
        factor = rms_factor(x)
        normed = x * factor
        inner = d_attn * gains_ref[0:1, :]
        d_x = factor * (inner - normed * jnp.mean(inner * normed, axis=-1, keepdims=True))
        x_grad_ref[...] = (d_middle_ref[...] + d_x).astype(low)
        gain_one = jnp.sum(d_attn * normed, axis=0, keepdims=True)
        rows = lax.broadcasted_iota(jnp.int32, (128, D), 0)
        both = jnp.where(rows == 0, gain_one, jnp.where(rows == 1, gain_two_ref[0:1, :], 0.0))
        pack = jnp.concatenate([product_tn(attn_ref[...], d_lin), both.T], axis=1).astype(low)
        pack_g[...] = pack.reshape(pack_g.shape)
        scatters["pack"].begin([])

    for n, stages in enumerate(rounds):
        if n == 3:
            keys_and_norm()
        if n == len(rounds) - 2:
            chain.finish()
            chain.total()
            exchange = Exchange(held.at[0], moved_ref, *exchange_sems)
            exchange.start()
        for stage in stages:
            run_stage(scatters, *stage)
    for one in (rest, exchange):
        one.finish()
        one.end()
    for one in (pairs, *scatters.values()):
        one.end()


def weight_sums(x, attn_in, d_middle, d_attn, gains, gain_two, cosine, sine, d_kv, packed, both_part, both_up, both_down, g_out,
                g_query, rest_part, last_part, rest_in, last_in, zs, collective_id):
    many = x.shape[0]
    low, full = jnp.bfloat16, jnp.float32
    anywhere, here = (pl.BlockSpec(memory_space=m) for m in (pl.ANY, pltpu.VMEM))
    shape, sem = jax.ShapeDtypeStruct, pltpu.SemaphoreType.DMA
    wide = packed.shape[3]
    narrow = 2 * KVW + 128
    block = both_part.shape[1:]
    return pl.pallas_call(
        functools.partial(weights_kernel, zs),
        out_shape=[
            shape((many, D), low), shape((wide, D), full), shape((wide, D), full), shape((wide, narrow), full),
            shape(last_part.shape[1:], full), shape(block, low), shape(rest_part.shape[1:], low),
        ],
        in_specs=[here] * 9 + [anywhere] * 10,
        out_specs=[here] * 5 + [anywhere] * 2,
        scratch_shapes=[
            pltpu.VMEM(packed.shape[:4] + (2 * KVW,), low),
            pltpu.VMEM((many, 2 * KVW), full),
            pltpu.VMEM((zs, 2, 4, wide, narrow), low),
            sem((7,)),
            pltpu.VMEM((4,) + block, low),
            pltpu.VMEM((2,) + block, low),
            sem((2 * zs - 2, 2)), sem((2,)),
            pltpu.VMEM(rest_part.shape, low),
            pltpu.VMEM(last_part.shape, low),
        ] + EXCHANGE_SEMS * 2
        + scatter_scratch(zs, False, many, 2 * KVW, False)
        + scatter_scratch(zs, True, wide, D, True) * 2
        + scatter_scratch(zs, True, wide, narrow, False),
        compiler_params=pltpu.CompilerParams(
            collective_id=collective_id, has_side_effects=True, vmem_limit_bytes=62 * MIB
        ),
        cost_estimate=LONG,
    )(x, attn_in, d_middle, d_attn, gains, gain_two, cosine, sine, d_kv, packed, both_part, both_up, both_down, g_out,
      g_query, rest_part, last_part, rest_in, last_in)


class Links:
    def __init__(self, seq, rows):
        self.zs, self.rows = seq // 2, rows
        self.kernels = rows == 4 and self.zs == 4
        self.z_groups = [[2 * z + c for z in range(self.zs)] for c in range(2)]
        self.core_groups = [[2 * z, 2 * z + 1] for z in range(self.zs)]

    def gather_z(self, block):
        return lax.all_gather(block, "seq", axis=0, tiled=True, axis_index_groups=self.z_groups)

    def scatter_z(self, blocks):
        return lax.psum_scatter(blocks, "seq", scatter_dimension=0, tiled=True, axis_index_groups=self.z_groups)

    def exchange_xla(self, blocks):
        moved = lax.all_to_all(blocks, "rows", split_axis=1, concat_axis=1, tiled=True)
        return lax.all_to_all(moved, "seq", split_axis=0, concat_axis=0, tiled=True, axis_index_groups=self.core_groups)

    def gather(self, array, z_flag, planes):
        if planes:
            array = lax.all_gather(array, "rows", axis=0)
        array = lax.all_gather(array, "seq", axis=0, axis_index_groups=self.core_groups)
        return self.gather_z(array[None]) if z_flag else array

    def scatter(self, blocks, z_flag, planes):
        blocks = self.scatter_z(blocks)[0] if z_flag else blocks
        blocks = lax.psum_scatter(blocks, "seq", scatter_dimension=0, tiled=True, axis_index_groups=self.core_groups)[0]
        if planes:
            blocks = lax.psum_scatter(blocks, "rows", scatter_dimension=0, tiled=True)[0]
        return blocks.astype(jnp.float32)


def on_device(seq, rows, tokens, w_query, w_key, w_value, w_out, w_gate, w_up, w_down, gain_attn, gain_ffn, lengths, order, cotangent):
    links = Links(seq, rows)
    zs = links.zs
    micro, _, span, _ = tokens.shape
    half_len = span // 2
    many = micro * span
    low = jnp.bfloat16
    wide = w_gate.shape[0]
    unit = w_down.shape[0]

    both, rest, pack, down_own, last_own = spread(
        w_gate, w_up, w_query, w_key, w_value, gain_attn, gain_ffn, w_down, zs, rows
    )
    cut = split_unit(unit)
    flat, flat_rest = (2 * rows * wide, 2 * zs * cut), (2 * rows * wide, 2 * zs * (unit - cut))
    dy_own = cotangent.reshape(many, D)
    own_tokens = tokens.reshape(many, D)
    x = own_tokens.astype(jnp.float32)
    first = lengths[:, 0, 0]
    slot_of = jnp.argmax(order[None, :] == jnp.arange(order.shape[0], dtype=jnp.int32)[:, None], axis=1).astype(jnp.int32)
    chained = links.kernels
    if chained:
        found = forward(order, lengths[:, 0], own_tokens, pack, both, rest, down_own, w_out, dy_own, zs, 0)
        packed, both_own, kv, out_w, dy, rest_own = found[:6]
        both_w = [b.reshape(flat) for b in (both_own, *found[6 : 4 + 2 * zs])]
        down_w = [down_own, *found[4 + 2 * zs : 2 + 4 * zs]]
        rest_own = rest_own.reshape(flat_rest)
        queries, attn_in, attended, ffn_in, middle, gains, cosine, sine = found[2 + 4 * zs :]
        packed = packed.reshape(D, PACK)
    else:
        both_w = [links.gather_z(links.exchange_xla(both).reshape(flat))]
        rest_w = [links.gather_z(links.exchange_xla(rest).reshape(flat_rest))]
        down_w, last_w = [links.gather_z(down_own)], [links.gather_z(last_own)]
        packed, dy = links.gather(pack, True, True).reshape(D, PACK), links.gather(dy_own, False, True)
        gain_one, gain_two = packed[:, QKV].astype(jnp.float32), packed[:, QKV + 1].astype(jnp.float32)
        mine = slot_places(order, half_len, lax.axis_index("seq") * span + jnp.arange(span, dtype=jnp.int32))
        start = jnp.where(mine[None, :] >= first[:, None], first[:, None], 0)
        inverse = 10000.0 ** (-jnp.arange(HEAD_DIM // 2, dtype=jnp.float32) / (HEAD_DIM // 2))
        angles = ((mine[None, :] - start).astype(jnp.float32)[..., None] * inverse).reshape(many, HEAD_DIM // 2)
        cosine, sine = jnp.cos(angles), jnp.sin(angles)
        cosine, sine = jnp.tile(cosine, (1, 4)), jnp.tile(jnp.concatenate([-sine, sine], axis=1), (1, 2))
        attn_in = (x * rms_factor(x) * gain_one).astype(low)
        lin = product(attn_in, packed)
        kv_own = jnp.concatenate([turn(lin[:, D : D + KVW], cosine, sine), lin[:, D + KVW : QKV]], axis=1).astype(low)
        kv, out_w = links.gather(kv_own, True, False), links.gather(w_out, True, True)
        queries, attended = attend(order, slot_of, first, lin, cosine, sine, kv.reshape(seq, many, 2 * KVW))
        middle = x + product(attended, out_w.reshape(D, D))
        ffn_in = links.gather((middle * rms_factor(middle) * gain_two).astype(low), False, True).reshape(2 * rows * many, D)
    kv = kv.reshape(seq, many, 2 * KVW)
    out_w = out_w.reshape(D, D)
    dy = dy.reshape(2 * rows * many, D)

    shards = (zs, 2, rows, wide)
    if chained:
        ffn_in, rest_got, last_got, hidden, d_both, grad_both, grad_down = ffn_first(
            ffn_in, dy, both_w, down_w, zs, (rest_own, last_own), 1
        )
        rest_w, last_w = [rest_own, rest_got], [last_own, last_got]
        grad_both, grad_down = grad_both.reshape(*shards, 2 * zs * cut), grad_down.reshape(zs, cut, D)
        result_part, d_ffn_part, grad_rest, grad_last, *come = ffn_second(
            ffn_in, dy, hidden, d_both, (both_w, down_w), (rest_w, last_w), zs, (grad_both, grad_down), 2
        )
    else:
        hidden, d_both, grad_both, grad_down = ffn_first(ffn_in, dy, both_w, down_w, zs)
        grad_both, grad_down = grad_both.reshape(*shards, 2 * zs * cut), grad_down.reshape(zs, cut, D)
        result_part, d_ffn_part, grad_rest, grad_last = ffn_second(
            ffn_in, dy, hidden, d_both, (both_w, down_w), (rest_w, last_w), zs
        )
    grad_rest, grad_last = grad_rest.reshape(*shards, 2 * zs * (unit - cut)), grad_last.reshape(zs, unit - cut, D)
    d_ffn_part, result_part = (part.reshape(2, rows, many, D) for part in (d_ffn_part, result_part))
    if chained:
        out_all, kv_all = out_w.reshape(*shards, D), kv.reshape(zs, 2, many, 2 * KVW)
        result, d_middle, d_query, d_kv, gain_two_grad, grad_down, both_up, both_down, rest_in, last_in = back(
            order, lengths[:, 0], dy_own, middle, gains, queries, cosine, sine, d_ffn_part, result_part, grad_both, grad_down,
            out_all, kv_all, grad_rest, grad_last, come, zs, 3,
        )
        grad_out, grad_query, d_attn = products(attended, attn_in, d_middle, d_query, packed)
        grad_out, grad_query = grad_out.reshape(*shards, D), grad_query.reshape(*shards, D)
        x_grad, grad_out, grad_query, pack_grad, grad_last, grad_both, grad_rest = weight_sums(
            own_tokens, attn_in, d_middle, d_attn, gains, gain_two_grad, cosine, sine, d_kv, packed.reshape(*shards, PACK),
            grad_both, both_up, both_down, grad_out, grad_query, grad_rest, grad_last, rest_in, last_in, zs, 4,
        )
    else:
        d_ffn_in = links.scatter(d_ffn_part, False, True)
        result = (middle + links.scatter(result_part, False, True)).astype(low)
        grad_both, grad_rest = (links.exchange_xla(links.scatter_z(grad)[0]) for grad in (grad_both, grad_rest))
        grad_down, grad_last = (links.scatter_z(grad)[0].astype(jnp.float32) for grad in (grad_down, grad_last))
        factor_two = rms_factor(middle)
        d_part, grad_gain_two = norm_back(d_ffn_in, middle * factor_two, factor_two, gain_two)
        d_middle = dy_own.astype(jnp.float32) + d_part
        d_mid_low = d_middle.astype(low)
        grad_out = links.scatter(product_tn(attended, d_mid_low).astype(low).reshape(*shards, D), True, True)
        d_heads = product_nt(d_mid_low, out_w).astype(low)
        d_query, d_kv = attend_back(order, slot_of, first, queries, d_heads, cosine, sine, kv)
        grad_query = links.scatter(product_tn(attn_in, d_query).astype(low).reshape(*shards, D), True, True)
        d_kv = links.scatter(d_kv.reshape(zs, 2, many, 2 * KVW), True, False)
        d_key = turn(d_kv[:, :KVW], cosine, -sine)
        d_kv = jnp.concatenate([d_key.astype(low), d_kv[:, KVW:].astype(low)], axis=1)
        d_attn_in = product_nt(d_query, packed[:, :D]) + product_nt(d_kv, packed[:, D:QKV])
        factor_one = rms_factor(x)
        d_x, grad_gain_one = norm_back(d_attn_in, x * factor_one, factor_one, gain_one)
        x_grad = (d_middle + d_x).astype(low)
        gains_grad = jnp.pad(jnp.stack([grad_gain_one, grad_gain_two], axis=1), ((0, 0), (0, 126)))
        pack_grad = jnp.concatenate([product_tn(attn_in, d_kv), gains_grad], axis=1).astype(low)
        pack_grad = links.scatter(pack_grad.reshape(*shards, 2 * KVW + 128), True, True)
    grad_gate, grad_up, grad_key, grad_value, grad_one, grad_two, grad_down = collect(
        (grad_both, grad_rest), pack_grad, (grad_down, grad_last), zs, rows, unit
    )
    return (
        result.reshape(tokens.shape),
        x_grad.reshape(tokens.shape),
        grad_query,
        grad_key,
        grad_value,
        grad_out,
        grad_gate,
        grad_up,
        grad_down,
        grad_one.reshape(-1),
        grad_two.reshape(-1),
    )


def solution(mesh):
    both = ("seq", "rows")
    row = P(None, "rows", "seq", None)
    weight, gain = P(both, None), P(both)
    return jax.shard_map(
        functools.partial(on_device, mesh.shape["seq"], mesh.shape["rows"]),
        mesh=mesh,
        in_specs=(row,) + (weight,) * 7 + (gain, gain, P(None, "rows", None), P(), row),
        out_specs=(row, row) + (weight,) * 7 + (gain, gain),
        check_vma=False,
    )
```
